32 devices in a mesh: tm: 8 (over z, y), chan: 4 (over x, core).
Axes of the slice: x: 2, y: 2, z: 4, core: 2. Of those that a mesh axis runs over, the one named last changes fastest.
Arguments:
- tokens: bfloat16 [8, 2048, 2048], P(None, 'tm', 'chan'), may hold values from -6 to 6
- ln_gain: float32 [2048], replicated, may hold values from 0.5 to 1.5
- ln_bias: float32 [2048], replicated, may hold values from -1.5 to 1.5
- weights: bfloat16 [3, 2048, 2048], P(None, None, 'chan'), may hold values from -0.125 to 0.125
- mix_forget: float32 [2048], P('chan'), may hold values from -0.5 to 0.5
- mix_reset: float32 [2048], P('chan'), may hold values from -1 to 1
- bias_forget: float32 [2048], P('chan'), as said below
- bias_reset: float32 [2048], P('chan'), may hold values from -1 to 1
- state_bank: float32 [8, 2048], P(None, 'chan'), may hold values from -6 to 6
- selector: int32 [8], replicated, may hold values from 0 to 7
- resets: int32 [8, 16], replicated, may hold values from 1 to 2048, as said below
- cotangent: bfloat16 [8, 2048, 2048], P(None, 'tm', 'chan'), may hold values from -6 to 6
Outputs:
- activations: bfloat16 [8, 2048, 2048], P(None, 'tm', 'chan')
- final_states: float32 [8, 2048], P(None, 'chan')
- input_grad: float32 [8, 2048, 2048], P(None, 'tm', 'chan')
- weight_grad: float32 [3, 2048, 2048], P(None, None, 'chan')
- gain_grad: float32 [2048], P('chan')
- norm_bias_grad: float32 [2048], P('chan')
- mix_forget_grad: float32 [2048], P('chan')
- mix_reset_grad: float32 [2048], P('chan')
- bias_forget_grad: float32 [2048], P('chan')
- bias_reset_grad: float32 [2048], P('chan')
The draws below stay inside these ranges and needn't reach their ends.
Inputs may be any that keep to these rules, and one draw needn't show every extreme that they name: `resets`: each row lists 16 positions. In one row all entries equal 2048 (no reset in that row). Every other row begins sentences at o, o + 128, o + 256, ..., with its own offset o from 1 to 127. `bias_forget`: between 1.5 and ln(2048) + 2.
All inputs are finite; a program needn't handle non-finite values.
Results may differ from the reference program's by a relative error of at most 0.0052.
Values may be sent and summed in bfloat16 or wider, within the bound.
A program may use at most 192 MiB of HBM per device.

```python
import jax
import jax.numpy as jnp
from jax import lax

D = 2048
ROWS = 8
SENT = 128
BANK = 8
LEN = 2048


def draw_bias_forget(key, part):
    key = jax.random.fold_in(key, 23)
    first, second, third = jax.random.split(key, 3)
    share = 0.5
    slow = jax.random.uniform(first, (D,)) < share
    slow_value = jnp.log(LEN * 1.0) + jax.random.uniform(second, (D,), minval=1.0, maxval=2.0)
    fast_value = jax.random.uniform(third, (D,), minval=1.5, maxval=4.0)
    return jnp.where(slow, slow_value, fast_value).astype(jnp.float32)


def draw_resets(key, part):
    key = jax.random.fold_in(key, 11)
    first, second = jax.random.split(key)
    offsets = jax.random.randint(first, (ROWS,), 1, SENT)
    spanning = jax.random.randint(second, (), 0, ROWS)
    offsets = offsets.at[(spanning + 1) % ROWS].set(SENT - 1)
    offsets = offsets.at[(spanning + 2) % ROWS].set(1)
    starts = offsets[:, None] + SENT * jnp.arange(LEN // SENT, dtype=jnp.int32)[None, :]
    row_ids = jnp.arange(ROWS, dtype=jnp.int32)
    return jnp.where((row_ids == spanning)[:, None], LEN, starts).astype(jnp.int32)


def touch_ends(values, rng, least, high):
    longest = values.shape.index(max(values.shape))
    spots = []
    for shift in (0, 1):
        where = [jax.random.randint(jax.random.fold_in(rng, axis), (), 0, length) for axis, length in enumerate(values.shape)]
        where[longest] = (where[longest] + shift) % values.shape[longest]
        spots.append(tuple(where))
    return values.at[spots[0]].set(least).at[spots[1]].set(high)


def block_levels(own_key, dims, cuts, smallest, top_value):
    loudness = 1.0
    for position, parts in cuts:
        heights = jax.random.uniform(jax.random.fold_in(jax.random.fold_in(own_key, 6), position), (parts,), jnp.float32, smallest / len(cuts), top_value / len(cuts))
        loudness = loudness * jnp.repeat(jnp.exp(heights), dims[position] // parts).reshape((-1,) + (1,) * (len(dims) - 1 - position))
    return loudness


def noise(own_key, extent, width, limit, shards=(), kind=jnp.bfloat16):
    gain = block_levels(own_key, extent, shards, -0.22, 0.18) if shards else 1.0
    drawn = jax.random.normal(own_key, extent, jnp.float32) * width * gain
    return jnp.minimum(jnp.maximum(drawn, -limit), limit).astype(kind)


def setup_inputs(seed: int = 0) -> dict:
    key_list = jax.random.split(jax.random.key(seed), 13)
    tokens = noise(key_list[0], (ROWS, LEN, D), 1.0, 6.0, ((1, 8), (2, 4)))
    ln_gain = jnp.clip(1.0 + 0.1 * jax.random.normal(key_list[1], (D,), jnp.float32), 0.5, 1.5)
    ln_bias = noise(key_list[2], (D,), 0.3, 1.5, (), jnp.float32)
    weights = noise(key_list[3], (3, D, D), D ** -0.5, 0.125, ((2, 4),))
    mix_forget = jnp.clip(jax.random.uniform(key_list[4], (D,), jnp.float32, -0.5, 0.5) * block_levels(key_list[4], (D,), ((0, 4),), -0.4, 0.0), -0.5, 0.5)
    mix_reset = jnp.clip(jax.random.uniform(key_list[5], (D,), jnp.float32, -1.0, 1.0) * block_levels(key_list[5], (D,), ((0, 4),), -0.4, 0.0), -1.0, 1.0)
    bias_forget = draw_bias_forget(jax.random.fold_in(key_list[12], 71), 0)
    bias_reset = jnp.clip(jax.random.uniform(key_list[7], (D,), jnp.float32, -1.0, 1.0) * block_levels(key_list[7], (D,), ((0, 4),), -0.4, 0.0), -1.0, 1.0)
    state_bank = noise(key_list[8], (BANK, D), 1.5, 6.0, ((1, 4),), jnp.float32)
    selector = touch_ends(jax.random.randint(key_list[9], (ROWS,), 0, BANK), jax.random.fold_in(key_list[9], 1), 0, BANK - 1).astype(jnp.int32)
    resets = draw_resets(jax.random.fold_in(key_list[12], 71), 0)
    cotangent = noise(key_list[11], (ROWS, LEN, D), 1.0, 6.0, ((1, 8), (2, 4)))
    return dict(tokens=tokens, ln_gain=ln_gain, ln_bias=ln_bias, weights=weights, mix_forget=mix_forget, mix_reset=mix_reset, bias_forget=bias_forget, bias_reset=bias_reset, state_bank=state_bank, selector=selector, resets=resets, cotangent=cotangent)


EPSILON = 1e-05

@jax.custom_vjp
def low(v):
    return lax.optimization_barrier(v.astype(jnp.bfloat16)).astype(jnp.float32)

@jax.custom_vjp
def low_back(v):
    return v

def low_keep(v):
    return (low(v), None)

def low_pass(kept, grad):
    return (grad,)

def back_keep(v):
    return (v, None)

def back_low(kept, grad):
    return (low(grad),)
low.defvjp(low_keep, low_pass)
low_back.defvjp(back_keep, back_low)

def forward(tokens_wide, ln_gain, ln_bias, weights_wide, mix_forget, mix_reset, bias_forget, bias_reset, entry_state, keep_mask):
    row_mean = lax.optimization_barrier(jnp.mean(tokens_wide, axis=-1, keepdims=True))
    centered = tokens_wide - row_mean
    inv_scale = lax.rsqrt(lax.optimization_barrier(jnp.mean(centered * centered, axis=-1, keepdims=True)) + EPSILON)
    normed = centered * inv_scale * ln_gain + ln_bias
    lowered = low(normed)
    projected = low_back(jnp.einsum('rtd,kde->krte', lowered, weights_wide, precision=lax.Precision.HIGHEST))
    forget = jax.nn.sigmoid(projected[1] + mix_forget * normed + bias_forget)
    out_gate = jax.nn.sigmoid(projected[2] + mix_reset * normed + bias_reset)
    keep_rate = forget * keep_mask
    inject = (1.0 - forget) * projected[0]

    def advance(state, slices):
        state = slices[0] * state + slices[1]
        return (state, state)
    final_state, states = lax.scan(advance, entry_state, (jnp.swapaxes(keep_rate, 0, 1), jnp.swapaxes(inject, 0, 1)))
    states = jnp.swapaxes(states, 0, 1)
    result = out_gate * jnp.tanh(states) + (1.0 - out_gate) * tokens_wide
    return (result, final_state)

def reference(tokens, ln_gain, ln_bias, weights, mix_forget, mix_reset, bias_forget, bias_reset, state_bank, selector, resets, cotangent):
    positions = jnp.arange(LEN, dtype=jnp.int32)
    hits = jnp.any(resets[:, None, :] == positions[None, :, None], axis=-1)
    keep_mask = (1.0 - hits.astype(jnp.float32))[..., None]
    entry_state = state_bank[selector.astype(jnp.int32)]

    def layer_fn(tokens_wide, gain_in, bias_in, weights_wide, forget_mix, reset_mix, forget_bias, reset_bias):
        return forward(tokens_wide, gain_in, bias_in, weights_wide, forget_mix, reset_mix, forget_bias, reset_bias, entry_state, keep_mask)
    result, pullback, final_state = jax.vjp(layer_fn, tokens.astype(jnp.float32), ln_gain, ln_bias, weights.astype(jnp.float32), mix_forget, mix_reset, bias_forget, bias_reset, has_aux=True)
    grads = pullback(cotangent.astype(jnp.float32))
    return (result.astype(jnp.bfloat16), final_state, grads[0], grads[3], grads[1], grads[2], grads[4], grads[5], grads[6], grads[7])
```

```python
import jax
import jax.numpy as jnp
from jax import lax
from jax.experimental import pallas as pl
from jax.experimental.pallas import tpu as pltpu
from jax.sharding import PartitionSpec as P

EPSILON = 1e-05
CHUNK = 32
BLOCK = 16
LANE = 128
UNIT = 256
LAG = 2
SLICE = 7
VMEM_BYTES = 63 << 20
WIDEN = 512
FIRST = 5
MESH = pl.DeviceIdType.MESH
F32 = jnp.float32
BF16 = jnp.bfloat16


def sigmoid(v):
    return 1.0 / (1.0 + jnp.exp(-v))


def swapped(v, outer, inner):
    return jnp.swapaxes(v.reshape(outer, inner, v.shape[-1]), 0, 1).reshape(outer * inner, v.shape[-1])


def both(*conditions):
    out = conditions[0]
    for c in conditions[1:]:
        out = jnp.logical_and(out, c)
    return out


def ring_of(tm_count):
    return 12 if tm_count <= 8 else 3


def layer_kernel(
    tokens, weights, cotangent, gain, shift, mix_f, mix_r, bias_f, bias_r, bank, selector, resets,
    fin, in_grad, act, low_t, final, totals,
    raw, rx, low, low_t_buf, w_buf, cand, forget, gate, masked, own_tok, cot_raw, cot, mean, inv, keep_mask, grad_buf,
    act_buf, side, terms, out_buf, row_rx, more, sum_rx, mean_s, inv_s, part_s, entry, fore, back, flow, reset_rows,
    x_send, x_recv, s_send, s_recv, d_send, d_recv, own_sem, w_sem, cot_sem, act_sem, tr_sem, low_sem,
    fore_send, fore_recv, back_send, back_recv, ready_sem, out_sem, loc_sem, pair_send, pair_recv, red_send, red_recv,
    bc_send, bc_recv, swap_send, swap_recv, give_send, give_recv, sib_send, sib_recv, acr_send, acr_recv, row_send,
    row_recv, sum_send, sum_recv,
):
    rows, steps, width = tokens.shape
    full = gain.shape[-1]
    tm_count, tm = lax.axis_size("tm"), lax.axis_index("tm")
    chan_count, chan = lax.axis_size("chan"), lax.axis_index("chan")
    sibling = chan + 1 - 2 * lax.rem(chan, 2)
    across = lax.rem(chan + 2, 4)
    chunks = steps // CHUNK
    span = CHUNK * rows
    part = BLOCK * rows
    tiles = width // LANE
    blocks = CHUNK // BLOCK
    units = 3 * full // UNIT
    per_gate = full // UNIT
    pieces = UNIT // 4 // CHUNK

    def remote(src, dst, send, recv, target):
        return pltpu.make_async_remote_copy(src, dst, send, recv, device_id=target, device_id_type=MESH)

    def lanes(j):
        return slice(j * LANE, (j + 1) * LANE)

    def mine(ref, j):
        return ref[0:1, pl.ds(pl.multiple_of(chan * width + j * LANE, LANE), LANE)]

    def hat(at, j):
        return (own_tok[at, lanes(j)].astype(F32) - mean[at, :]) * inv[at, :]

    def normed(at, j):
        return hat(at, j) * mine(gain, j) + mine(shift, j)

    def rows_of(ch):
        return pl.ds(pl.multiple_of(ch * span, span), span)

    def piece(ch):
        return tokens.at[:, pl.ds(pl.multiple_of(ch * CHUNK, CHUNK), CHUNK), :]

    def raw_at(ch, block):
        return raw.at[pl.ds(pl.multiple_of((ch * chan_count + block) * rows, rows), rows)]

    def own_copy(ch):
        return pltpu.make_async_copy(piece(ch), raw_at(ch, chan), own_sem.at[ch])

    def x_copy(ch):
        return remote(piece(ch), raw_at(ch, chan), x_send.at[ch], x_recv.at[ch], (tm, across))

    def s_copy(ch):
        return remote(piece(ch), raw_at(ch, chan), s_send.at[ch], s_recv.at[ch], (tm, sibling))

    def d_copy(ch):
        return remote(raw_at(ch, across), raw_at(ch, across), d_send.at[ch], d_recv.at[ch], (tm, sibling))

    def cot_copy(ch):
        at = pl.ds(pl.multiple_of(ch * CHUNK, CHUNK), CHUNK)
        return pltpu.make_async_copy(cotangent.at[:, at, :], cot_raw.at[lax.rem(ch, 2)], cot_sem.at[lax.rem(ch, 2)])

    def act_copy(ch):
        at = pl.ds(pl.multiple_of(ch * CHUNK, CHUNK), CHUNK)
        return pltpu.make_async_copy(act_buf.at[lax.rem(ch, 2)], act.at[:, at, :], act_sem.at[lax.rem(ch, 2)])

    def tr_copy(ch):
        return pltpu.make_async_copy(low_t_buf, low_t.at[:, rows_of(ch)], tr_sem)

    def low_copy(u):
        at = pl.ds(pl.multiple_of(lax.rem(u, per_gate) * UNIT, UNIT), UNIT)
        return pltpu.make_async_copy(low_t.at[at], low.at[lax.rem(u, 2)], low_sem.at[lax.rem(u, 2)])

    w_copies = [pltpu.make_async_copy(weights.at[k], w_buf.at[k], w_sem.at[k]) for k in range(3)]

    barrier = pltpu.get_barrier_semaphore()
    for d in range(1, 4):
        pl.semaphore_signal(barrier, inc=1, device_id=(tm, lax.rem(chan + d, 4)), device_id_type=MESH)

    def greet(d, carry):
        pl.semaphore_signal(barrier, inc=1, device_id=(lax.rem(tm + d, tm_count), chan), device_id_type=MESH)
        return carry

    lax.fori_loop(1, tm_count, greet, 0)
    own_copy(0).start()
    own_copy(1).start()
    cot_copy(0).start()
    for copy in w_copies:
        copy.start()
    pl.semaphore_wait(barrier, tm_count + 2)
    for ch in range(2):
        x_copy(ch).start()
        s_copy(ch).start()

    count = resets.shape[1]
    for j in range(count):
        reset_rows[j] = jnp.broadcast_to(resets[:, j : j + 1], (rows, LANE))

    def mark(t, carry):
        at = tm * steps + t

        def compare(j, hit):
            return jnp.maximum(hit, jnp.where(reset_rows[j] == at, 1.0, 0.0))

        hit = lax.fori_loop(0, count, compare, jnp.zeros((rows, LANE), F32), unroll=16)
        keep_mask[pl.ds(pl.multiple_of(t * rows, rows), rows), :] = 1.0 - hit
        return carry

    lax.fori_loop(0, steps, mark, 0)
    for r in range(rows):
        entry[r : r + 1, :] = bank[pl.ds(selector[r], 1), :]

    def flip(ch):
        @pl.when(ch >= 1)
        def _():
            tr_copy(ch - 1).wait()

        def one(j, carry):
            cols = pl.ds(pl.multiple_of(j * 256, 256), 256)
            low_t_buf[cols, :] = jnp.transpose(low[lax.rem(ch, 2), :, cols])
            return carry

        lax.fori_loop(0, full // 256, one, 0)
        tr_copy(ch).start()

    def gather_step(ch, carry):
        a_run, b_run = carry

        @pl.when(ch + 2 < chunks)
        def _():
            own_copy(ch + 2).start()
            x_copy(ch + 2).start()
            s_copy(ch + 2).start()

        @pl.when(ch + 1 < chunks)
        def _():
            cot_copy(ch + 1).start()

        base = pl.multiple_of(ch * span, span)
        slot = lax.rem(ch, 2)

        cot_copy(ch).wait()
        for h in range(blocks):
            for j in range(tiles):
                v = cot_raw[slot, :, h * BLOCK : (h + 1) * BLOCK, lanes(j)].astype(F32).reshape(part, LANE)
                cot[pl.ds(pl.multiple_of(base + h * part, part), part), lanes(j)] = swapped(v, rows, BLOCK).astype(BF16)
        pl.when(ch >= 1)(lambda: flip(ch - 1))

        x_copy(ch).wait_recv()
        d_copy(ch).start()
        own_copy(ch).wait()
        s_copy(ch).wait_recv()
        d_copy(ch).wait_recv()

        first = pl.multiple_of(ch * chan_count * rows, rows)

        def each(i, turn):
            r, h = i // blocks, lax.rem(i, blocks)
            t0 = pl.multiple_of(h * BLOCK, BLOCK)
            total = jnp.zeros((BLOCK, LANE), F32)
            for b in range(chan_count):
                for j in range(tiles):
                    total = total + turn(raw[first + b * rows + r, pl.ds(t0, BLOCK), lanes(j)].astype(F32), h, r)
            part_s[h, r] = total

        def sum_rows(i, carry):
            each(i, lambda v, h, r: v)
            return carry

        lax.fori_loop(0, rows * blocks, sum_rows, 0)
        mean_s[...] = jnp.broadcast_to(jnp.sum(part_s[...], axis=-1, keepdims=True) * (1.0 / full), mean_s.shape)

        def square_rows(i, carry):
            r, h = i // blocks, lax.rem(i, blocks)
            m = mean_s[h, r]
            each(i, lambda v, h, r: (v - m) * (v - m))
            return carry

        lax.fori_loop(0, rows * blocks, square_rows, 0)
        var = jnp.sum(part_s[...], axis=-1, keepdims=True) * (1.0 / full)
        inv_s[...] = jnp.broadcast_to(lax.rsqrt(var + EPSILON), inv_s.shape)

        for h in range(blocks):
            mean_h = mean_s[h].reshape(part, LANE)
            inv_h = inv_s[h].reshape(part, LANE)

            def normalize(j, carry, h=h, mean_h=mean_h, inv_h=inv_h):
                cols = pl.ds(pl.multiple_of(j * LANE, LANE), LANE)
                where = pl.ds(first + (j // tiles) * rows, rows)
                inner = pl.ds(pl.multiple_of(lax.rem(j, tiles) * LANE, LANE), LANE)
                v = raw[where, h * BLOCK : (h + 1) * BLOCK, inner].astype(F32).reshape(part, LANE)
                v = (v - mean_h) * inv_h * gain[0:1, cols] + shift[0:1, cols]
                low[slot, h * part : (h + 1) * part, cols] = swapped(v, rows, BLOCK).astype(BF16)
                return carry

            lax.fori_loop(0, full // LANE, normalize, 0)
            at = pl.ds(pl.multiple_of(base + h * part, part), part)
            mean[at, :] = swapped(mean_h, rows, BLOCK)
            inv[at, :] = swapped(inv_h, rows, BLOCK)
            for j in range(tiles):
                v = raw[pl.ds(first + chan * rows, rows), h * BLOCK : (h + 1) * BLOCK, lanes(j)]
                own_tok[at, lanes(j)] = swapped(v.astype(F32).reshape(part, LANE), rows, BLOCK).astype(BF16)

        at = pl.ds(base, span)

        @pl.when(ch == 0)
        def _():
            for copy in w_copies:
                copy.wait()

        cand[at, :] = jnp.dot(low[slot], w_buf[0], preferred_element_type=F32)
        forget[at, :] = jnp.dot(low[slot], w_buf[1], preferred_element_type=F32)
        gate[at, :] = jnp.dot(low[slot], w_buf[2], preferred_element_type=F32)

        def gates(b, carry):
            a_list, b_list = list(carry[0]), list(carry[1])
            at = pl.ds(pl.multiple_of(base + b * part, part), part)
            mask = keep_mask[at, :]
            for j in range(tiles):
                cols = lanes(j)
                nrm = normed(at, j)
                f = sigmoid(forget[at, cols] + mix_f[0:1, cols] * nrm + bias_f[0:1, cols])
                o = sigmoid(gate[at, cols] + mix_r[0:1, cols] * nrm + bias_r[0:1, cols])
                forget[at, cols] = f
                gate[at, cols] = o
                inject = (1.0 - f) * cand[at, cols]
                keep = f * mask
                for t in range(BLOCK):
                    now = slice(t * rows, (t + 1) * rows)
                    a_list[j] = a_list[j] * keep[now]
                    b_list[j] = b_list[j] * keep[now] + inject[now]
            return tuple(a_list), tuple(b_list)

        return lax.fori_loop(0, blocks, gates, (a_run, b_run))

    ones = tuple(jnp.ones((rows, LANE), F32) for _ in range(tiles))
    zeros = tuple(jnp.zeros((rows, LANE), F32) for _ in range(tiles))
    a_run, b_run = lax.fori_loop(0, chunks, gather_step, (ones, zeros))

    for j in range(tiles):
        fore[tm, 0, :, lanes(j)] = a_run[j]
        fore[tm, 1, :, lanes(j)] = b_run[j]

    def fore_copy(source, target):
        return remote(fore.at[source], fore.at[source], fore_send.at[target], fore_recv.at[source], (target, chan))

    def back_copy(source, target):
        return remote(back.at[source], back.at[source], back_send.at[target], back_recv.at[source], (target, chan))

    def sum_copy(source, target):
        return remote(sum_rx.at[source], sum_rx.at[source], sum_send.at[target], sum_recv.at[source], (target, chan))

    def peers(act_on):
        def one(d, carry):
            act_on(lax.rem(tm + d, tm_count))
            return carry

        lax.fori_loop(1, tm_count, one, 0)

    peers(lambda p: fore_copy(tm, p).start())
    flip(chunks - 1)
    peers(lambda p: fore_copy(p, tm).wait_recv())

    def carry_on(d, carry):
        state, here = carry
        here = jnp.where(d == tm, state, here)
        return fore[d, 0] * state + fore[d, 1], here

    last, here = lax.fori_loop(0, tm_count, carry_on, (entry[...], entry[...]))
    final[...] = last
    tr_copy(chunks - 1).wait()
    low_copy(0).start()

    def forward(b, carry):
        states, runs, backs, mr, br = [list(v) for v in carry]
        ch, h = b // blocks, lax.rem(b, blocks)
        slot = lax.rem(ch, 2)

        @pl.when(both(h == 0, ch >= 2))
        def _():
            act_copy(ch - 2).wait()

        at = pl.ds(pl.multiple_of(b * part, part), part)
        t0 = pl.multiple_of(h * BLOCK, BLOCK)
        mask = keep_mask[at, :]
        for j in range(tiles):
            cols = lanes(j)
            f = forget[at, cols]
            inject = (1.0 - f) * cand[at, cols]
            before, after = [], []
            c = states[j]
            for t in range(BLOCK):
                now = slice(t * rows, (t + 1) * rows)
                c = c * mask[now]
                before.append(c)
                c = f[now] * c + inject[now]
                after.append(c)
            states[j] = c
            masked[at, cols] = jnp.concatenate(before, axis=0)
            th = jnp.tanh(jnp.concatenate(after, axis=0))
            o = gate[at, cols]
            x = own_tok[at, cols].astype(F32)
            ct = cot[at, cols].astype(F32)
            rest = 1.0 - o
            out = swapped(o * th + rest * x, BLOCK, rows).astype(BF16)
            act_buf[slot, :, pl.ds(t0, BLOCK), cols] = out.reshape(rows, BLOCK, LANE)
            reset_pre = ct * (th - x) * o * rest
            direct = ct * o * (1.0 - th * th)
            side[at, cols] = (ct * rest).astype(BF16)
            grad_buf[2, at, cols] = reset_pre.astype(BF16)
            gate[at, cols] = direct
            weighted = reset_pre * normed(at, j)
            keep = f * mask
            for t in range(BLOCK):
                now = slice(t * rows, (t + 1) * rows)
                runs[j] = runs[j] * keep[now]
                backs[j] = backs[j] + runs[j] * direct[now]
                mr[j] = mr[j] + weighted[now]
                br[j] = br[j] + reset_pre[now]

        @pl.when(h == blocks - 1)
        def _():
            act_copy(ch).start()

        return tuple(states), tuple(runs), tuple(backs), tuple(mr), tuple(br)

    state = tuple(here[:, lanes(j)] for j in range(tiles))
    _, _, backs, mr, br = lax.fori_loop(0, steps // BLOCK, forward, (state, ones, zeros, zeros, zeros))
    for j in range(tiles):
        back[tm, :, lanes(j)] = backs[j]
    peers(lambda p: back_copy(tm, p).start())

    def sent_on(ch, carry):
        d_copy(ch).wait_send()
        return carry

    lax.fori_loop(0, chunks, sent_on, 0)
    for target in (sibling, across):
        pl.semaphore_signal(ready_sem, inc=1, device_id=(tm, target), device_id_type=MESH)
    for j in range(tiles):
        sum_rx[tm, 1:2, lanes(j)] = jnp.sum(mr[j], axis=0, keepdims=True)
        sum_rx[tm, 3:4, lanes(j)] = jnp.sum(br[j], axis=0, keepdims=True)
    sum_rx[tm, 6:8, :] = jnp.zeros((2, width), F32)
    more[...] = jnp.zeros_like(more)

    n = tm_count // 2
    o, y = tm // 2, lax.rem(tm, 2)
    hops = n // 2
    partner = (o * 2 + 1 - y, chan)
    left = ((o - 1) * 2 + y, chan)
    right = ((o + 1) * 2 + y, chan)
    depth = LAG * (2 * hops + 2)
    ring = ring_of(tm_count)
    space = -(-depth // ring)
    lines = [(y, n // 2 - 1 + y, 1), (2, n // 2 - 1, 0), (3, n // 2, 0)]

    def stage(s, number):
        v = s - LAG * number
        if space == 1:
            return v, both(v >= 0, v < units)
        return v // space, both(v >= 0, lax.rem(v, space) == 0, v // space < units)

    def gate_of(u):
        return lax.rem(u // per_gate + 2, 3)

    def fin_at(u, p):
        return fin.at[gate_of(u) * per_gate + lax.rem(u, per_gate), p]

    def wg_rows(u, p):
        return pl.ds((u * 4 + p) * pieces, pieces)

    def wg_at(u, p):
        return raw.at[wg_rows(u, p)]

    def rx_rows(u, place):
        return pl.ds((lax.rem(u, ring) * SLICE + place) * pieces, pieces)

    def rx_at(u, place):
        return rx.at[rx_rows(u, place)]

    def arrival(l, column, way):
        if l == 0:
            return 1 + way
        other = 6 if l == 1 else jnp.where(column == lines[1][1], 6, 3)
        return jnp.where(column == lines[l][1], 3 + way, other)

    def pair_copy(u):
        return remote(wg_at(u, 1 - y), rx_at(u, 0), pair_send.at[u], pair_recv.at[u], partner)

    def red_copy(l, u, to_right):
        way, column = (0, o + 1) if to_right else (1, o - 1)
        return remote(
            wg_at(u, lines[l][0]), rx_at(u, arrival(l, column, way)), red_send.at[l, u], red_recv.at[l, u, way],
            right if to_right else left,
        )

    def red_wait(l, u, way):
        place = arrival(l, o, way)
        remote(rx_at(u, place), rx_at(u, place), red_send.at[l, u], red_recv.at[l, u, way], partner).wait_recv()
        return rx[rx_rows(u, place)].astype(F32)

    def bc_copy(l, u, to_right, src):
        return remote(
            src, fin_at(u, lines[l][0]), bc_send.at[l, u, 1 if to_right else 0], bc_recv.at[l, u],
            right if to_right else left,
        )

    def swap_copy(l, u):
        return remote(wg_at(u, lines[l][0]), rx_at(u, 5), swap_send.at[l - 1, u], swap_recv.at[l - 1, u], partner)

    def give_copy(u, src):
        return remote(src, fin_at(u, y), give_send.at[u], give_recv.at[u], partner)

    def local_copy(l, u):
        return pltpu.make_async_copy(wg_at(u, lines[l][0]), fin_at(u, lines[l][0]), loc_sem.at[l, u])

    def add_to(l, u, *others):
        at = wg_rows(u, lines[l][0])
        total = raw[at].astype(F32)
        for v in others:
            total = total + v
        raw[at] = total.astype(BF16)

    def red_start(l, u):
        c = lines[l][1]
        pl.when(o < c)(lambda: red_copy(l, u, True).start())
        pl.when(o > c)(lambda: red_copy(l, u, False).start())

    def publish(l, u):
        src = wg_at(u, lines[l][0])
        local_copy(l, u).start()
        pl.when(o > 0)(lambda: bc_copy(l, u, False, src).start())
        pl.when(o < n - 1)(lambda: bc_copy(l, u, True, src).start())
        if l == 0:
            give_copy(u, src).start()

    def block_cols(c):
        return pl.ds(pl.multiple_of(c * width, width), width)

    def sib_rows(ch, q):
        return pl.ds(units * 4 * pieces + (lax.rem(ch, 4) * 2 + q) * rows, rows)

    def sib_copy(ch, q):
        slot = lax.rem(ch, 2)
        cols = sibling if q == 0 else lax.rem(sibling + 2, 4)
        return remote(
            terms.at[slot, cols], raw.at[sib_rows(ch, q)], sib_send.at[ch, q], sib_recv.at[ch, q], (tm, sibling)
        )

    def acr_copy(ch):
        return remote(
            terms.at[lax.rem(ch, 2), across], cot_view(ch), acr_send.at[ch], acr_recv.at[ch], (tm, across)
        )

    def cot_view(ch):
        return cot.at[rows_of(ch)].reshape(rows, CHUNK, width)

    def row_copy(ch, source, d):
        return remote(
            row_rx.at[ch, source], row_rx.at[ch, source], row_send.at[ch, d - 1], row_recv.at[ch, source],
            (tm, lax.rem(chan + d, 4)),
        )

    def out_copy(ch):
        at = pl.ds(pl.multiple_of(ch * CHUNK, CHUNK), CHUNK)
        return pltpu.make_async_copy(out_buf.at[lax.rem(ch, 2)], in_grad.at[:, at, :], out_sem.at[lax.rem(ch, 2)])

    def project(ch):
        at = rows_of(ch)
        slot = lax.rem(ch, 2)

        @pl.when(ch == 0)
        def _():
            pl.semaphore_wait(ready_sem, 2)

        @pl.when(ch >= 2)
        def _():
            acr_copy(ch - 2).wait_send()

        for b in range(chan_count):
            total = jnp.zeros((span, width), F32)
            for k in range(3):
                total = total + lax.dot_general(
                    grad_buf[k, at, :], w_buf[k, b * width : (b + 1) * width, :], (((1,), (1,)), ((), ())),
                    preferred_element_type=F32,
                )
            terms[slot, b] = total.astype(BF16).reshape(rows, CHUNK, width)
        sib_copy(ch, 0).start()
        sib_copy(ch, 1).start()

    def chip_sum(ch):
        slot = lax.rem(ch, 2)
        for q in range(2):
            sib_copy(ch, q).wait_recv()
        there = terms[slot, across].astype(F32) + raw[sib_rows(ch, 1)].astype(F32)
        terms[slot, across] = there.astype(BF16)
        acr_copy(ch).start()
        here = terms[slot, chan].astype(F32) + raw[sib_rows(ch, 0)].astype(F32)
        cand[rows_of(ch), :] = here.reshape(span, width)
        for q in range(2):
            sib_copy(ch, q).wait_send()

    def full_sum(ch):
        acr_copy(ch).wait_recv()
        at = rows_of(ch)
        total = jnp.zeros((8, span), F32)
        pick = lax.broadcasted_iota(jnp.int32, (8, LANE), 0)
        for j in range(tiles):
            cols = lanes(j)
            own = grad_buf[1, at, cols].astype(F32) * mix_f[0:1, cols] + grad_buf[2, at, cols].astype(F32) * mix_r[0:1, cols]
            g = cand[at, cols] + cot[at, cols].astype(F32) + own
            cand[at, cols] = g
            weighted = g * hat(at, j)
            for i, v in enumerate((weighted, g)):
                more[i, :, cols] = more[i, :, cols] + jnp.sum(v.reshape(CHUNK, rows, LANE), axis=0)
            for i, v in enumerate((g * mine(gain, j), weighted * mine(gain, j))):
                lead = jnp.where(pick == i, 1.0, 0.0).astype(BF16)
                high = v.astype(BF16)
                low_part = (v - high.astype(F32)).astype(BF16)
                for p in (high, low_part):
                    total = total + lax.dot_general(lead, p, (((1,), (1,)), ((), ())), preferred_element_type=F32)
        row_rx[ch, chan] = total
        for d in range(1, 4):
            row_copy(ch, chan, d).start()

    def finish(ch):
        for d in range(1, 4):
            row_copy(ch, lax.rem(chan + d, 4), d).wait_recv()

        @pl.when(ch >= 2)
        def _():
            out_copy(ch - 2).wait()

        at = rows_of(ch)
        total = (row_rx[ch, 0] + row_rx[ch, 1] + row_rx[ch, 2] + row_rx[ch, 3]) * (1.0 / full)
        columns = jnp.transpose(total)
        first = jnp.broadcast_to(columns[:, 0:1], (span, LANE))
        second = jnp.broadcast_to(columns[:, 1:2], (span, LANE))
        for j in range(tiles):
            cols = lanes(j)
            g = cand[at, cols] * mine(gain, j)
            v = inv[at, :] * (g - first - hat(at, j) * second) + side[at, cols].astype(F32)
            out_buf[lax.rem(ch, 2), :, :, cols] = swapped(v, CHUNK, rows).reshape(rows, CHUNK, LANE)
        out_copy(ch).start()

    def share_sums():
        for i in range(2):
            sum_rx[tm, 2 * i : 2 * i + 1, :] = jnp.sum(flow[1 + i], axis=0, keepdims=True)
            sum_rx[tm, 4 + i : 5 + i, :] = jnp.sum(more[i], axis=0, keepdims=True)
        peers(lambda p: sum_copy(tm, p).start())

    share = steps // BLOCK // (FIRST - 1)

    def start_backward():
        peers(lambda p: back_copy(p, tm).wait_recv())

        def carry_back(i, v):
            d = tm_count - 1 - i
            return jnp.where(d > tm, fore[d, 0] * v + back[d], v)

        flow[0] = lax.fori_loop(0, tm_count, carry_back, jnp.zeros((rows, width), F32))
        flow[1] = jnp.zeros((rows, width), F32)
        flow[2] = jnp.zeros((rows, width), F32)

    def backward(i, carry):
        b = steps // BLOCK - 1 - i
        at = pl.ds(pl.multiple_of(b * part, part), part)
        mask = keep_mask[at, :]
        for j in range(tiles):
            cols = lanes(j)
            f = forget[at, cols]
            keep = f * mask
            direct = gate[at, cols]
            g = flow[0, :, cols]
            adjoint = [None] * BLOCK
            for t in reversed(range(BLOCK)):
                now = slice(t * rows, (t + 1) * rows)
                adjoint[t] = direct[now] + g
                g = keep[now] * adjoint[t]
            flow[0, :, cols] = g
            cand_grad = jnp.concatenate(adjoint, axis=0) * (1.0 - f)
            forget_pre = cand_grad * (masked[at, cols] - cand[at, cols]) * f
            grad_buf[0, at, cols] = cand_grad.astype(BF16)
            grad_buf[1, at, cols] = forget_pre.astype(BF16)
            for i, v in enumerate((forget_pre * normed(at, j), forget_pre)):
                flow[1 + i, :, cols] = flow[1 + i, :, cols] + jnp.sum(v.reshape(BLOCK, rows, LANE), axis=0)
        return carry

    def slot_step(s, carry):
        u, go = stage(s, 2 * hops + 2)
        pl.when(go)(lambda: give_copy(u, wg_at(u, 0)).wait_recv())

        for l in range(3):
            p, c, first = lines[l]
            late = first + hops + (0 if l == 0 else 1)
            u, go = stage(s, late + jnp.abs(o - c))

            @pl.when(both(o != c, go))
            def _(l=l, c=c, u=u):
                here = fin_at(u, lines[l][0])
                bc_copy(l, u, True, here).wait_recv()
                pl.when(both(o < c, o > 0))(lambda: bc_copy(l, u, False, here).start())
                pl.when(both(o > c, o < n - 1))(lambda: bc_copy(l, u, True, here).start())
                if l == 0:
                    give_copy(u, here).start()

            if l > 0:
                u, go = stage(s, late)

                @pl.when(both(o == c, go))
                def _(l=l, u=u):
                    swap_copy(l, u).wait()
                    add_to(l, u, rx[rx_rows(u, 5)].astype(F32))
                    publish(l, u)

            u, go = stage(s, first + hops)

            @pl.when(both(o == c, go))
            def _(l=l, u=u):
                if n > 2:
                    add_to(l, u, red_wait(l, u, 0), red_wait(l, u, 1))
                else:
                    pl.when(o > 0)(lambda: add_to(l, u, red_wait(l, u, 0)))
                    pl.when(o < n - 1)(lambda: add_to(l, u, red_wait(l, u, 1)))
                if l == 0:
                    publish(l, u)
                else:
                    swap_copy(l, u).start()

            hop = jnp.where(o < c, o, n - 1 - o)
            u, go = stage(s, first + hop)

            @pl.when(both(o < c, o > 0, go))
            def _(l=l, u=u):
                add_to(l, u, red_wait(l, u, 0))
                red_copy(l, u, True).start()

            @pl.when(both(o > c, o < n - 1, go))
            def _(l=l, u=u):
                add_to(l, u, red_wait(l, u, 1))
                red_copy(l, u, False).start()

        u, go = stage(s, 1)

        @pl.when(go)
        def _():
            pair_copy(u).wait_recv()
            add_to(0, u, rx[rx_rows(u, 0)].astype(F32))
            pl.when(jnp.logical_or(o == 0, o == n - 1))(lambda: red_start(0, u))

        u0, go0 = stage(s, 0)

        @pl.when(go0)
        def _():
            pl.when(u0 + 1 < units)(lambda: low_copy(u0 + 1).start())
            low_copy(u0).wait()
            g = jnp.dot(low[lax.rem(u0, 2)], grad_buf[gate_of(u0)], preferred_element_type=F32).astype(BF16)
            raw[pl.ds(u0 * 4 * pieces, 4 * pieces)] = g.reshape(4 * pieces, CHUNK, width)
            pair_copy(u0).start()

            @pl.when(jnp.logical_or(o == 0, o == n - 1))
            def _():
                red_start(1, u0)
                red_start(2, u0)

        pl.when(s == 1)(start_backward)

        @pl.when(both(s >= 1, s < FIRST))
        def _():
            lax.fori_loop((s - 1) * share, s * share, backward, 0)

        for job, offset in ((finish, 5), (full_sum, 3), (chip_sum, 1), (project, 0)):
            at = s - FIRST - offset
            pl.when(both(at >= 0, lax.rem(at, 2) == 0, at // 2 < chunks))(lambda job=job, at=at: job(at // 2))
        pl.when(s == FIRST + 2 * chunks + 2)(share_sums)
        return carry

    slots = max((units - 1) * space + depth + 1, FIRST + 2 * chunks + 4)
    lax.fori_loop(0, slots, slot_step, 0)

    def close_unit(u, carry):
        give_copy(u, wg_at(u, 0)).wait_send()
        pair_copy(u).wait_send()
        for l in range(3):
            c = lines[l][1]
            src = wg_at(u, 0)
            pl.when(o != c)(lambda l=l: red_copy(l, u, True).wait_send())
            pl.when(o == c)(lambda l=l: local_copy(l, u).wait())
            pl.when(both(o <= c, o > 0))(lambda l=l: bc_copy(l, u, False, src).wait_send())
            pl.when(both(o >= c, o < n - 1))(lambda l=l: bc_copy(l, u, True, src).wait_send())
        return carry

    lax.fori_loop(0, units, close_unit, 0)

    def close_chunk(ch, carry):
        x_copy(ch).wait_send()
        s_copy(ch).wait_send()
        for d in range(1, 4):
            row_copy(ch, chan, d).wait_send()
        return carry

    lax.fori_loop(0, chunks, close_chunk, 0)
    for ch in (chunks - 2, chunks - 1):
        out_copy(ch).wait()
        act_copy(ch).wait()
        acr_copy(ch).wait_send()
    peers(lambda p: fore_copy(tm, p).wait_send())
    peers(lambda p: back_copy(tm, p).wait_send())
    peers(lambda p: sum_copy(p, tm).wait_recv())
    peers(lambda p: sum_copy(tm, p).wait_send())
    totals[...] = lax.fori_loop(0, tm_count, lambda d, v: v + sum_rx[d], jnp.zeros(totals.shape, F32))


def layer(tokens, weights, cotangent, gain, shift, mix_f, mix_r, bias_f, bias_r, bank, selector, resets):
    rows, steps, width = tokens.shape
    full = gain.shape[-1]
    tm_count, chan_count = lax.axis_size("tm"), lax.axis_size("chan")
    chunks = steps // CHUNK
    span = CHUNK * rows
    count = steps * rows
    units = 3 * full // UNIT
    pieces = UNIT // 4 // CHUNK
    hbm = pl.BlockSpec(memory_space=pl.ANY)
    vmem = pl.BlockSpec(memory_space=pltpu.VMEM)
    smem = pl.BlockSpec(memory_space=pltpu.SMEM)
    dma = pltpu.SemaphoreType.DMA
    stat = pltpu.VMEM((CHUNK // BLOCK, rows, BLOCK, LANE), F32)
    wide = pltpu.VMEM((count, width), F32)
    narrow = pltpu.VMEM((count, LANE), F32)
    short = pltpu.VMEM((count, width), BF16)
    return pl.pallas_call(
        layer_kernel,
        out_shape=(
            jax.ShapeDtypeStruct((units, 4, pieces, CHUNK, width), BF16),
            jax.ShapeDtypeStruct(tokens.shape, F32),
            jax.ShapeDtypeStruct(tokens.shape, BF16),
            jax.ShapeDtypeStruct((full, count), BF16),
            jax.ShapeDtypeStruct((rows, width), F32),
            jax.ShapeDtypeStruct((8, width), F32),
        ),
        in_specs=[hbm, hbm, hbm] + [vmem] * 7 + [smem, vmem],
        out_specs=(hbm, hbm, hbm, hbm, vmem, vmem),
        scratch_shapes=[
            pltpu.VMEM((chunks * chan_count * rows, CHUNK, width), BF16),
            pltpu.VMEM((ring_of(tm_count) * SLICE * pieces, CHUNK, width), BF16),
            pltpu.VMEM((2, span, full), BF16),
            pltpu.VMEM((full, span), BF16),
            pltpu.VMEM((3, full, width), BF16),
            wide, wide, wide, wide,
            short,
            pltpu.VMEM((2, rows, CHUNK, width), BF16),
            short,
            narrow, narrow, narrow,
            pltpu.VMEM((3, count, width), BF16),
            pltpu.VMEM((2, rows, CHUNK, width), BF16),
            short,
            pltpu.VMEM((2, chan_count, rows, CHUNK, width), BF16),
            pltpu.VMEM((2, rows, CHUNK, width), F32),
            pltpu.VMEM((chunks, 4, 8, span), F32),
            pltpu.VMEM((2, rows, width), F32),
            pltpu.VMEM((tm_count, 8, width), F32),
            stat, stat, stat,
            pltpu.VMEM((rows, width), F32),
            pltpu.VMEM((tm_count, 2, rows, width), F32),
            pltpu.VMEM((tm_count, rows, width), F32),
            pltpu.VMEM((3, rows, width), F32),
            pltpu.VMEM((resets.shape[1], rows, LANE), jnp.int32),
            dma((chunks,)), dma((chunks,)), dma((chunks,)), dma((chunks,)), dma((chunks,)), dma((chunks,)), dma((chunks,)),
            dma((3,)), dma((2,)), dma((2,)), dma(()), dma((2,)),
            dma((tm_count,)), dma((tm_count,)), dma((tm_count,)), dma((tm_count,)),
            pltpu.SemaphoreType.REGULAR,
            dma((2,)), dma((3, units)), dma((units,)), dma((units,)),
            dma((3, units)), dma((3, units, 2)), dma((3, units, 2)), dma((3, units)), dma((2, units)), dma((2, units)),
            dma((units,)), dma((units,)), dma((chunks, 2)), dma((chunks, 2)), dma((chunks,)), dma((chunks,)),
            dma((chunks, 3)), dma((chunks, 4)), dma((tm_count,)), dma((tm_count,)),
        ],
        compiler_params=pltpu.CompilerParams(collective_id=0, has_side_effects=True, vmem_limit_bytes=VMEM_BYTES),
        name="whole",
    )(tokens, weights, cotangent, gain, shift, mix_f, mix_r, bias_f, bias_r, bank, selector, resets)


def widen_kernel(narrow, wide):
    wide[...] = narrow[...].astype(F32)


def widen(fin, shape):
    flat = fin.reshape(-1, shape[-1])
    block = pl.BlockSpec((WIDEN, shape[-1]), lambda i: (i, 0))
    out = pl.pallas_call(
        widen_kernel,
        out_shape=jax.ShapeDtypeStruct(flat.shape, F32),
        grid=(flat.shape[0] // WIDEN,),
        in_specs=[block],
        out_specs=block,
        name="tail",
    )(flat)
    return out.reshape(shape)


def body(
    tokens, ln_gain, ln_bias, weights, mix_forget, mix_reset, bias_forget, bias_reset, state_bank, selector, resets, cotangent
):
    fin, in_grad, act, _, final, totals = layer(
        tokens, weights, cotangent, ln_gain[None], ln_bias[None], mix_forget[None], mix_reset[None], bias_forget[None],
        bias_reset[None], state_bank, selector, resets,
    )
    weight_grad = widen(fin, weights.shape)
    return act, final, in_grad, weight_grad, totals[4], totals[5], totals[0], totals[1], totals[2], totals[3]


def solution(mesh):
    placed = (
        P(None, "tm", "chan"), P(), P(), P(None, None, "chan"), P("chan"), P("chan"), P("chan"), P("chan"),
        P(None, "chan"), P(), P(), P(None, "tm", "chan"),
    )
    return jax.shard_map(
        body,
        mesh=mesh,
        in_specs=placed,
        out_specs=(
            P(None, "tm", "chan"), P(None, "chan"), P(None, "tm", "chan"), P(None, None, "chan"),
            P("chan"), P("chan"), P("chan"), P("chan"), P("chan"), P("chan"),
        ),
        check_vma=False,
    )
```

```python
import jax
import jax.numpy as jnp
from jax import lax
from jax.experimental import pallas as pl
from jax.experimental.pallas import tpu as pltpu
from jax.sharding import PartitionSpec as P

EPSILON = 1e-05
CHUNK = 32
BLOCK = 16
LANE = 128
UNIT = 256
LAG = 2
SLICE = 7
VMEM_BYTES = 63 << 20
TAIL = 12
LATER = 4
FIRST = 8
MESH = pl.DeviceIdType.MESH
F32 = jnp.float32
BF16 = jnp.bfloat16


def sigmoid(v):
    return 1.0 / (1.0 + jnp.exp(-v))


def swapped(v, outer, inner):
    return jnp.swapaxes(v.reshape(outer, inner, v.shape[-1]), 0, 1).reshape(outer * inner, v.shape[-1])


def both(*conditions):
    out = conditions[0]
    for c in conditions[1:]:
        out = jnp.logical_and(out, c)
    return out


def ring_of(tm_count):
    return 12 if tm_count <= 8 else 3


def layer_kernel(
    tokens, weights, cotangent, gain, shift, mix_f, mix_r, bias_f, bias_r, bank, selector, resets,
    fin, in_grad, act, low_t, final, totals,
    raw, rx, low, low_t_buf, w_buf, cand, forget, gate, masked, own_tok, cot_raw, cot, mean, inv, keep_mask, grad_buf,
    act_buf, side, terms, out_buf, row_rx, more, sum_rx, mean_s, inv_s, part_s, entry, fore, back, flow, reset_rows,
    x_send, x_recv, s_send, s_recv, d_send, d_recv, own_sem, w_sem, cot_sem, act_sem, tr_sem, low_sem,
    fore_send, fore_recv, back_send, back_recv, ready_sem, out_sem, loc_sem, pair_send, pair_recv, red_send, red_recv,
    bc_send, bc_recv, swap_send, swap_recv, give_send, give_recv, sib_send, sib_recv, acr_send, acr_recv, row_send,
    row_recv, sum_send, sum_recv,
):
    rows, steps, width = tokens.shape
    full = gain.shape[-1]
    tm_count, tm = lax.axis_size("tm"), lax.axis_index("tm")
    chan_count, chan = lax.axis_size("chan"), lax.axis_index("chan")
    sibling = chan + 1 - 2 * lax.rem(chan, 2)
    across = lax.rem(chan + 2, 4)
    chunks = steps // CHUNK
    span = CHUNK * rows
    part = BLOCK * rows
    tiles = width // LANE
    blocks = CHUNK // BLOCK
    units = 3 * full // UNIT
    per_gate = full // UNIT
    pieces = UNIT // 4 // CHUNK

    def remote(src, dst, send, recv, target):
        return pltpu.make_async_remote_copy(src, dst, send, recv, device_id=target, device_id_type=MESH)

    def lanes(j):
        return slice(j * LANE, (j + 1) * LANE)

    def mine(ref, j):
        return ref[0:1, pl.ds(pl.multiple_of(chan * width + j * LANE, LANE), LANE)]

    def hat(at, j):
        return (own_tok[at, lanes(j)].astype(F32) - mean[at, :]) * inv[at, :]

    def normed(at, j):
        return hat(at, j) * mine(gain, j) + mine(shift, j)

    def rows_of(ch):
        return pl.ds(pl.multiple_of(ch * span, span), span)

    def piece(ch):
        return tokens.at[:, pl.ds(pl.multiple_of(ch * CHUNK, CHUNK), CHUNK), :]

    def raw_at(ch, block):
        return raw.at[pl.ds(pl.multiple_of((ch * chan_count + block) * rows, rows), rows)]

    def own_copy(ch):
        return pltpu.make_async_copy(piece(ch), raw_at(ch, chan), own_sem.at[ch])

    def x_copy(ch):
        return remote(piece(ch), raw_at(ch, chan), x_send.at[ch], x_recv.at[ch], (tm, across))

    def s_copy(ch):
        return remote(piece(ch), raw_at(ch, chan), s_send.at[ch], s_recv.at[ch], (tm, sibling))

    def d_copy(ch):
        return remote(raw_at(ch, across), raw_at(ch, across), d_send.at[ch], d_recv.at[ch], (tm, sibling))

    def cot_copy(ch):
        at = pl.ds(pl.multiple_of(ch * CHUNK, CHUNK), CHUNK)
        return pltpu.make_async_copy(cotangent.at[:, at, :], cot_raw.at[lax.rem(ch, 2)], cot_sem.at[lax.rem(ch, 2)])

    def act_copy(ch):
        at = pl.ds(pl.multiple_of(ch * CHUNK, CHUNK), CHUNK)
        return pltpu.make_async_copy(act_buf.at[lax.rem(ch, 2)], act.at[:, at, :], act_sem.at[lax.rem(ch, 2)])

    def tr_copy(ch):
        return pltpu.make_async_copy(low_t_buf, low_t.at[:, rows_of(ch)], tr_sem)

    def low_copy(u):
        at = pl.ds(pl.multiple_of(lax.rem(u, per_gate) * UNIT, UNIT), UNIT)
        return pltpu.make_async_copy(low_t.at[at], low.at[lax.rem(u, 2)], low_sem.at[lax.rem(u, 2)])

    w_copies = [pltpu.make_async_copy(weights.at[k], w_buf.at[k], w_sem.at[k]) for k in range(3)]

    barrier = pltpu.get_barrier_semaphore()
    for d in range(1, 4):
        pl.semaphore_signal(barrier, inc=1, device_id=(tm, lax.rem(chan + d, 4)), device_id_type=MESH)

    def greet(d, carry):
        pl.semaphore_signal(barrier, inc=1, device_id=(lax.rem(tm + d, tm_count), chan), device_id_type=MESH)
        return carry

    lax.fori_loop(1, tm_count, greet, 0)
    own_copy(0).start()
    own_copy(1).start()
    cot_copy(0).start()
    for copy in w_copies:
        copy.start()
    pl.semaphore_wait(barrier, tm_count + 2)
    for ch in range(2):
        x_copy(ch).start()
        s_copy(ch).start()

    count = resets.shape[1]
    for j in range(count):
        reset_rows[j] = jnp.broadcast_to(resets[:, j : j + 1], (rows, LANE))

    def mark(t, carry):
        at = tm * steps + t

        def compare(j, hit):
            return jnp.maximum(hit, jnp.where(reset_rows[j] == at, 1.0, 0.0))

        hit = lax.fori_loop(0, count, compare, jnp.zeros((rows, LANE), F32), unroll=16)
        keep_mask[pl.ds(pl.multiple_of(t * rows, rows), rows), :] = 1.0 - hit
        return carry

    lax.fori_loop(0, steps, mark, 0)
    for r in range(rows):
        entry[r : r + 1, :] = bank[pl.ds(selector[r], 1), :]

    def flip(ch):
        @pl.when(ch >= 1)
        def _():
            tr_copy(ch - 1).wait()

        def one(j, carry):
            cols = pl.ds(pl.multiple_of(j * 256, 256), 256)
            low_t_buf[cols, :] = jnp.transpose(low[lax.rem(ch, 2), :, cols])
            return carry

        lax.fori_loop(0, full // 256, one, 0)
        tr_copy(ch).start()

    def gather_step(ch, carry):
        a_run, b_run = carry

        @pl.when(ch + 2 < chunks)
        def _():
            own_copy(ch + 2).start()
            x_copy(ch + 2).start()
            s_copy(ch + 2).start()

        @pl.when(ch + 1 < chunks)
        def _():
            cot_copy(ch + 1).start()

        base = pl.multiple_of(ch * span, span)
        slot = lax.rem(ch, 2)

        cot_copy(ch).wait()
        for h in range(blocks):
            for j in range(tiles):
                v = cot_raw[slot, :, h * BLOCK : (h + 1) * BLOCK, lanes(j)].astype(F32).reshape(part, LANE)
                cot[pl.ds(pl.multiple_of(base + h * part, part), part), lanes(j)] = swapped(v, rows, BLOCK).astype(BF16)
        pl.when(ch >= 1)(lambda: flip(ch - 1))

        x_copy(ch).wait_recv()
        d_copy(ch).start()
        own_copy(ch).wait()
        s_copy(ch).wait_recv()
        d_copy(ch).wait_recv()

        first = pl.multiple_of(ch * chan_count * rows, rows)

        def each(i, turn):
            r, h = i // blocks, lax.rem(i, blocks)
            t0 = pl.multiple_of(h * BLOCK, BLOCK)
            total = jnp.zeros((BLOCK, LANE), F32)
            for b in range(chan_count):
                for j in range(tiles):
                    total = total + turn(raw[first + b * rows + r, pl.ds(t0, BLOCK), lanes(j)].astype(F32), h, r)
            part_s[h, r] = total

        def sum_rows(i, carry):
            each(i, lambda v, h, r: v)
            return carry

        lax.fori_loop(0, rows * blocks, sum_rows, 0)
        mean_s[...] = jnp.broadcast_to(jnp.sum(part_s[...], axis=-1, keepdims=True) * (1.0 / full), mean_s.shape)

        def square_rows(i, carry):
            r, h = i // blocks, lax.rem(i, blocks)
            m = mean_s[h, r]
            each(i, lambda v, h, r: (v - m) * (v - m))
            return carry

        lax.fori_loop(0, rows * blocks, square_rows, 0)
        var = jnp.sum(part_s[...], axis=-1, keepdims=True) * (1.0 / full)
        inv_s[...] = jnp.broadcast_to(lax.rsqrt(var + EPSILON), inv_s.shape)

        for h in range(blocks):
            mean_h = mean_s[h].reshape(part, LANE)
            inv_h = inv_s[h].reshape(part, LANE)

            def normalize(j, carry, h=h, mean_h=mean_h, inv_h=inv_h):
                cols = pl.ds(pl.multiple_of(j * LANE, LANE), LANE)
                where = pl.ds(first + (j // tiles) * rows, rows)
                inner = pl.ds(pl.multiple_of(lax.rem(j, tiles) * LANE, LANE), LANE)
                v = raw[where, h * BLOCK : (h + 1) * BLOCK, inner].astype(F32).reshape(part, LANE)
                v = (v - mean_h) * inv_h * gain[0:1, cols] + shift[0:1, cols]
                low[slot, h * part : (h + 1) * part, cols] = swapped(v, rows, BLOCK).astype(BF16)
                return carry

            lax.fori_loop(0, full // LANE, normalize, 0)
            at = pl.ds(pl.multiple_of(base + h * part, part), part)
            mean[at, :] = swapped(mean_h, rows, BLOCK)
            inv[at, :] = swapped(inv_h, rows, BLOCK)
            for j in range(tiles):
                v = raw[pl.ds(first + chan * rows, rows), h * BLOCK : (h + 1) * BLOCK, lanes(j)]
                own_tok[at, lanes(j)] = swapped(v.astype(F32).reshape(part, LANE), rows, BLOCK).astype(BF16)

        at = pl.ds(base, span)

        @pl.when(ch == 0)
        def _():
            for copy in w_copies:
                copy.wait()

        cand[at, :] = jnp.dot(low[slot], w_buf[0], preferred_element_type=F32)
        forget[at, :] = jnp.dot(low[slot], w_buf[1], preferred_element_type=F32)
        gate[at, :] = jnp.dot(low[slot], w_buf[2], preferred_element_type=F32)

        def gates(b, carry):
            a_list, b_list = list(carry[0]), list(carry[1])
            at = pl.ds(pl.multiple_of(base + b * part, part), part)
            mask = keep_mask[at, :]
            for j in range(tiles):
                cols = lanes(j)
                nrm = normed(at, j)
                f = sigmoid(forget[at, cols] + mix_f[0:1, cols] * nrm + bias_f[0:1, cols])
                o = sigmoid(gate[at, cols] + mix_r[0:1, cols] * nrm + bias_r[0:1, cols])
                forget[at, cols] = f
                gate[at, cols] = o
                inject = (1.0 - f) * cand[at, cols]
                keep = f * mask
                for t in range(BLOCK):
                    now = slice(t * rows, (t + 1) * rows)
                    a_list[j] = a_list[j] * keep[now]
                    b_list[j] = b_list[j] * keep[now] + inject[now]
            return tuple(a_list), tuple(b_list)

        return lax.fori_loop(0, blocks, gates, (a_run, b_run))

    ones = tuple(jnp.ones((rows, LANE), F32) for _ in range(tiles))
    zeros = tuple(jnp.zeros((rows, LANE), F32) for _ in range(tiles))
    a_run, b_run = lax.fori_loop(0, chunks, gather_step, (ones, zeros))

    for j in range(tiles):
        fore[tm, 0, :, lanes(j)] = a_run[j]
        fore[tm, 1, :, lanes(j)] = b_run[j]

    def fore_copy(source, target):
        return remote(fore.at[source], fore.at[source], fore_send.at[target], fore_recv.at[source], (target, chan))

    def back_copy(source, target):
        return remote(back.at[source], back.at[source], back_send.at[target], back_recv.at[source], (target, chan))

    def sum_copy(source, target):
        return remote(sum_rx.at[source], sum_rx.at[source], sum_send.at[target], sum_recv.at[source], (target, chan))

    def peers(act_on):
        def one(d, carry):
            act_on(lax.rem(tm + d, tm_count))
            return carry

        lax.fori_loop(1, tm_count, one, 0)

    peers(lambda p: fore_copy(tm, p).start())
    flip(chunks - 1)
    peers(lambda p: fore_copy(p, tm).wait_recv())

    def carry_on(d, carry):
        state, here = carry
        here = jnp.where(d == tm, state, here)
        return fore[d, 0] * state + fore[d, 1], here

    last, here = lax.fori_loop(0, tm_count, carry_on, (entry[...], entry[...]))
    final[...] = last
    tr_copy(chunks - 1).wait()
    low_copy(0).start()

    def forward(b, states):
        states = list(states)
        at = pl.ds(pl.multiple_of(b * part, part), part)
        mask = keep_mask[at, :]
        for j in range(tiles):
            cols = lanes(j)
            f = forget[at, cols]
            inject = (1.0 - f) * cand[at, cols]
            before, after = [], []
            c = states[j]
            for t in range(BLOCK):
                now = slice(t * rows, (t + 1) * rows)
                c = c * mask[now]
                before.append(c)
                c = f[now] * c + inject[now]
                after.append(c)
            states[j] = c
            masked[at, cols] = jnp.concatenate(before, axis=0)
            th = jnp.tanh(jnp.concatenate(after, axis=0))
            o = gate[at, cols]
            gate_grad = cot[at, cols].astype(F32) * (th - own_tok[at, cols].astype(F32))
            grad_buf[2, at, cols] = (gate_grad * o * (1.0 - o)).astype(BF16)
        return tuple(states)

    lax.fori_loop(0, steps // BLOCK, forward, tuple(here[:, lanes(j)] for j in range(tiles)))

    def start_later():
        flow[0] = jnp.ones((rows, width), F32)
        for i in range(1, 4):
            flow[i] = jnp.zeros((rows, width), F32)

    def later(b, carry):
        ch, h = b // blocks, lax.rem(b, blocks)
        slot = lax.rem(ch, 2)

        @pl.when(both(h == 0, ch >= 2))
        def _():
            act_copy(ch - 2).wait()

        at = pl.ds(pl.multiple_of(b * part, part), part)
        t0 = pl.multiple_of(h * BLOCK, BLOCK)
        mask = keep_mask[at, :]
        for j in range(tiles):
            cols = lanes(j)
            f = forget[at, cols]
            th = jnp.tanh(f * masked[at, cols] + (1.0 - f) * cand[at, cols])
            o = gate[at, cols]
            x = own_tok[at, cols].astype(F32)
            ct = cot[at, cols].astype(F32)
            rest = 1.0 - o
            out = swapped(o * th + rest * x, BLOCK, rows).astype(BF16)
            act_buf[slot, :, pl.ds(t0, BLOCK), cols] = out.reshape(rows, BLOCK, LANE)
            reset_pre = ct * (th - x) * o * rest
            direct = ct * o * (1.0 - th * th)
            side[at, cols] = (ct * rest).astype(BF16)
            gate[at, cols] = direct
            keep = f * mask
            run, total = flow[0, :, cols], flow[1, :, cols]
            for t in range(BLOCK):
                now = slice(t * rows, (t + 1) * rows)
                run = run * keep[now]
                total = total + run * direct[now]
            flow[0, :, cols], flow[1, :, cols] = run, total
            for i, v in enumerate((reset_pre * normed(at, j), reset_pre)):
                flow[2 + i, :, cols] = flow[2 + i, :, cols] + jnp.sum(v.reshape(BLOCK, rows, LANE), axis=0)

        @pl.when(h == blocks - 1)
        def _():
            act_copy(ch).start()

        return carry

    def end_later():
        back[tm] = flow[1]
        peers(lambda p: back_copy(tm, p).start())
        for target in (sibling, across):
            pl.semaphore_signal(ready_sem, inc=1, device_id=(tm, target), device_id_type=MESH)
        for i in range(2):
            sum_rx[tm, 2 * i + 1 : 2 * i + 2, :] = jnp.sum(flow[2 + i], axis=0, keepdims=True)
        sum_rx[tm, 6:8, :] = jnp.zeros((2, width), F32)
        more[...] = jnp.zeros_like(more)

    def sent_on(ch, carry):
        d_copy(ch).wait_send()
        return carry

    lax.fori_loop(0, chunks, sent_on, 0)

    n = tm_count // 2
    o, y = tm // 2, lax.rem(tm, 2)
    hops = n // 2
    partner = (o * 2 + 1 - y, chan)
    left = ((o - 1) * 2 + y, chan)
    right = ((o + 1) * 2 + y, chan)
    depth = LAG * (2 * hops + 2)
    ring = ring_of(tm_count)
    space = -(-depth // ring)
    lines = [(y, n // 2 - 1 + y, 1), (2, n // 2 - 1, 0), (3, n // 2, 0)]

    def stage(s, number):
        v = s - LAG * number
        if space == 1:
            return v, both(v >= 0, v < units)
        return v // space, both(v >= 0, lax.rem(v, space) == 0, v // space < units)

    def gate_of(u):
        return lax.rem(u // per_gate + 2, 3)

    def fin_at(u, p):
        return fin.at[gate_of(u) * per_gate + lax.rem(u, per_gate), p]

    def wg_rows(u, p):
        return pl.ds((u * 4 + p) * pieces, pieces)

    def wg_at(u, p):
        return raw.at[wg_rows(u, p)]

    def rx_rows(u, place):
        return pl.ds((lax.rem(u, ring) * SLICE + place) * pieces, pieces)

    def rx_at(u, place):
        return rx.at[rx_rows(u, place)]

    def arrival(l, column, way):
        if l == 0:
            return 1 + way
        other = 6 if l == 1 else jnp.where(column == lines[1][1], 6, 3)
        return jnp.where(column == lines[l][1], 3 + way, other)

    def pair_copy(u):
        return remote(wg_at(u, 1 - y), rx_at(u, 0), pair_send.at[u], pair_recv.at[u], partner)

    def red_copy(l, u, to_right):
        way, column = (0, o + 1) if to_right else (1, o - 1)
        return remote(
            wg_at(u, lines[l][0]), rx_at(u, arrival(l, column, way)), red_send.at[l, u], red_recv.at[l, u, way],
            right if to_right else left,
        )

    def red_wait(l, u, way):
        place = arrival(l, o, way)
        remote(rx_at(u, place), rx_at(u, place), red_send.at[l, u], red_recv.at[l, u, way], partner).wait_recv()
        return rx[rx_rows(u, place)].astype(F32)

    def bc_copy(l, u, to_right, src):
        return remote(
            src, fin_at(u, lines[l][0]), bc_send.at[l, u, 1 if to_right else 0], bc_recv.at[l, u],
            right if to_right else left,
        )

    def swap_copy(l, u):
        return remote(wg_at(u, lines[l][0]), rx_at(u, 5), swap_send.at[l - 1, u], swap_recv.at[l - 1, u], partner)

    def give_copy(u, src):
        return remote(src, fin_at(u, y), give_send.at[u], give_recv.at[u], partner)

    def local_copy(l, u):
        return pltpu.make_async_copy(wg_at(u, lines[l][0]), fin_at(u, lines[l][0]), loc_sem.at[l, u])

    def add_to(l, u, *others):
        at = wg_rows(u, lines[l][0])
        total = raw[at].astype(F32)
        for v in others:
            total = total + v
        raw[at] = total.astype(BF16)

    def red_start(l, u):
        c = lines[l][1]
        pl.when(o < c)(lambda: red_copy(l, u, True).start())
        pl.when(o > c)(lambda: red_copy(l, u, False).start())

    def publish(l, u):
        src = wg_at(u, lines[l][0])
        local_copy(l, u).start()
        pl.when(o > 0)(lambda: bc_copy(l, u, False, src).start())
        pl.when(o < n - 1)(lambda: bc_copy(l, u, True, src).start())
        if l == 0:
            give_copy(u, src).start()

    def block_cols(c):
        return pl.ds(pl.multiple_of(c * width, width), width)

    def sib_rows(ch, q):
        return pl.ds(units * 4 * pieces + (lax.rem(ch, 4) * 2 + q) * rows, rows)

    def sib_copy(ch, q):
        slot = lax.rem(ch, 2)
        cols = sibling if q == 0 else lax.rem(sibling + 2, 4)
        return remote(
            terms.at[slot, cols], raw.at[sib_rows(ch, q)], sib_send.at[ch, q], sib_recv.at[ch, q], (tm, sibling)
        )

    def acr_copy(ch):
        return remote(
            terms.at[lax.rem(ch, 2), across], cot_view(ch), acr_send.at[ch], acr_recv.at[ch], (tm, across)
        )

    def cot_view(ch):
        return cot.at[rows_of(ch)].reshape(rows, CHUNK, width)

    def row_copy(ch, source, d):
        return remote(
            row_rx.at[ch, source], row_rx.at[ch, source], row_send.at[ch, d - 1], row_recv.at[ch, source],
            (tm, lax.rem(chan + d, 4)),
        )

    def out_copy(ch):
        at = pl.ds(pl.multiple_of(ch * CHUNK, CHUNK), CHUNK)
        return pltpu.make_async_copy(out_buf.at[lax.rem(ch, 2)], in_grad.at[:, at, :], out_sem.at[lax.rem(ch, 2)])

    def project(ch):
        at = rows_of(ch)
        slot = lax.rem(ch, 2)

        @pl.when(ch == 0)
        def _():
            pl.semaphore_wait(ready_sem, 2)

        @pl.when(ch >= 2)
        def _():
            acr_copy(ch - 2).wait_send()

        for b in range(chan_count):
            total = jnp.zeros((span, width), F32)
            for k in range(3):
                total = total + lax.dot_general(
                    grad_buf[k, at, :], w_buf[k, b * width : (b + 1) * width, :], (((1,), (1,)), ((), ())),
                    preferred_element_type=F32,
                )
            terms[slot, b] = total.astype(BF16).reshape(rows, CHUNK, width)
        sib_copy(ch, 0).start()
        sib_copy(ch, 1).start()

    def chip_sum(ch):
        slot = lax.rem(ch, 2)
        for q in range(2):
            sib_copy(ch, q).wait_recv()
        there = terms[slot, across].astype(F32) + raw[sib_rows(ch, 1)].astype(F32)
        terms[slot, across] = there.astype(BF16)
        acr_copy(ch).start()
        here = terms[slot, chan].astype(F32) + raw[sib_rows(ch, 0)].astype(F32)
        cand[rows_of(ch), :] = here.reshape(span, width)
        for q in range(2):
            sib_copy(ch, q).wait_send()

    def full_sum(ch):
        acr_copy(ch).wait_recv()
        at = rows_of(ch)
        total = jnp.zeros((8, span), F32)
        pick = lax.broadcasted_iota(jnp.int32, (8, LANE), 0)
        for j in range(tiles):
            cols = lanes(j)
            own = grad_buf[1, at, cols].astype(F32) * mix_f[0:1, cols] + grad_buf[2, at, cols].astype(F32) * mix_r[0:1, cols]
            g = cand[at, cols] + cot[at, cols].astype(F32) + own
            cand[at, cols] = g
            weighted = g * hat(at, j)
            for i, v in enumerate((weighted, g)):
                more[i, :, cols] = more[i, :, cols] + jnp.sum(v.reshape(CHUNK, rows, LANE), axis=0)
            for i, v in enumerate((g * mine(gain, j), weighted * mine(gain, j))):
                lead = jnp.where(pick == i, 1.0, 0.0).astype(BF16)
                high = v.astype(BF16)
                low_part = (v - high.astype(F32)).astype(BF16)
                for p in (high, low_part):
                    total = total + lax.dot_general(lead, p, (((1,), (1,)), ((), ())), preferred_element_type=F32)
        row_rx[ch, chan] = total
        for d in range(1, 4):
            row_copy(ch, chan, d).start()

    def finish(ch):
        for d in range(1, 4):
            row_copy(ch, lax.rem(chan + d, 4), d).wait_recv()

        @pl.when(ch >= 2)
        def _():
            out_copy(ch - 2).wait()

        at = rows_of(ch)
        total = (row_rx[ch, 0] + row_rx[ch, 1] + row_rx[ch, 2] + row_rx[ch, 3]) * (1.0 / full)
        columns = jnp.transpose(total)
        first = jnp.broadcast_to(columns[:, 0:1], (span, LANE))
        second = jnp.broadcast_to(columns[:, 1:2], (span, LANE))
        for j in range(tiles):
            cols = lanes(j)
            g = cand[at, cols] * mine(gain, j)
            v = inv[at, :] * (g - first - hat(at, j) * second) + side[at, cols].astype(F32)
            out_buf[lax.rem(ch, 2), :, :, cols] = swapped(v, CHUNK, rows).reshape(rows, CHUNK, LANE)
        out_copy(ch).start()

    def share_sums():
        for i in range(2):
            sum_rx[tm, 2 * i : 2 * i + 1, :] = jnp.sum(flow[1 + i], axis=0, keepdims=True)
            sum_rx[tm, 4 + i : 5 + i, :] = jnp.sum(more[i], axis=0, keepdims=True)
        peers(lambda p: sum_copy(tm, p).start())

    def start_backward():
        peers(lambda p: back_copy(p, tm).wait_recv())

        def carry_back(i, v):
            d = tm_count - 1 - i
            return jnp.where(d > tm, fore[d, 0] * v + back[d], v)

        flow[0] = lax.fori_loop(0, tm_count, carry_back, jnp.zeros((rows, width), F32))
        flow[1] = jnp.zeros((rows, width), F32)
        flow[2] = jnp.zeros((rows, width), F32)

    def backward(i, carry):
        b = steps // BLOCK - 1 - i
        at = pl.ds(pl.multiple_of(b * part, part), part)
        mask = keep_mask[at, :]
        for j in range(tiles):
            cols = lanes(j)
            f = forget[at, cols]
            keep = f * mask
            direct = gate[at, cols]
            g = flow[0, :, cols]
            adjoint = [None] * BLOCK
            for t in reversed(range(BLOCK)):
                now = slice(t * rows, (t + 1) * rows)
                adjoint[t] = direct[now] + g
                g = keep[now] * adjoint[t]
            flow[0, :, cols] = g
            cand_grad = jnp.concatenate(adjoint, axis=0) * (1.0 - f)
            forget_pre = cand_grad * (masked[at, cols] - cand[at, cols]) * f
            grad_buf[0, at, cols] = cand_grad.astype(BF16)
            grad_buf[1, at, cols] = forget_pre.astype(BF16)
            for i, v in enumerate((forget_pre * normed(at, j), forget_pre)):
                flow[1 + i, :, cols] = flow[1 + i, :, cols] + jnp.sum(v.reshape(BLOCK, rows, LANE), axis=0)
        return carry

    def slot_step(s, carry):
        u, go = stage(s, 2 * hops + 2)
        pl.when(go)(lambda: give_copy(u, wg_at(u, 0)).wait_recv())

        for l in range(3):
            p, c, first = lines[l]
            late = first + hops + (0 if l == 0 else 1)
            u, go = stage(s, late + jnp.abs(o - c))

            @pl.when(both(o != c, go))
            def _(l=l, c=c, u=u):
                here = fin_at(u, lines[l][0])
                bc_copy(l, u, True, here).wait_recv()
                pl.when(both(o < c, o > 0))(lambda: bc_copy(l, u, False, here).start())
                pl.when(both(o > c, o < n - 1))(lambda: bc_copy(l, u, True, here).start())
                if l == 0:
                    give_copy(u, here).start()

            if l > 0:
                u, go = stage(s, late)

                @pl.when(both(o == c, go))
                def _(l=l, u=u):
                    swap_copy(l, u).wait()
                    add_to(l, u, rx[rx_rows(u, 5)].astype(F32))
                    publish(l, u)

            u, go = stage(s, first + hops)

            @pl.when(both(o == c, go))
            def _(l=l, u=u):
                if n > 2:
                    add_to(l, u, red_wait(l, u, 0), red_wait(l, u, 1))
                else:
                    pl.when(o > 0)(lambda: add_to(l, u, red_wait(l, u, 0)))
                    pl.when(o < n - 1)(lambda: add_to(l, u, red_wait(l, u, 1)))
                if l == 0:
                    publish(l, u)
                else:
                    swap_copy(l, u).start()

            hop = jnp.where(o < c, o, n - 1 - o)
            u, go = stage(s, first + hop)

            @pl.when(both(o < c, o > 0, go))
            def _(l=l, u=u):
                add_to(l, u, red_wait(l, u, 0))
                red_copy(l, u, True).start()

            @pl.when(both(o > c, o < n - 1, go))
            def _(l=l, u=u):
                add_to(l, u, red_wait(l, u, 1))
                red_copy(l, u, False).start()

        u, go = stage(s, 1)

        @pl.when(go)
        def _():
            pair_copy(u).wait_recv()
            add_to(0, u, rx[rx_rows(u, 0)].astype(F32))
            pl.when(jnp.logical_or(o == 0, o == n - 1))(lambda: red_start(0, u))

        u0, go0 = stage(s, 0)

        @pl.when(go0)
        def _():
            pl.when(u0 + 1 < units)(lambda: low_copy(u0 + 1).start())
            low_copy(u0).wait()
            g = jnp.dot(low[lax.rem(u0, 2)], grad_buf[gate_of(u0)], preferred_element_type=F32).astype(BF16)
            raw[pl.ds(u0 * 4 * pieces, 4 * pieces)] = g.reshape(4 * pieces, CHUNK, width)
            pair_copy(u0).start()

            @pl.when(jnp.logical_or(o == 0, o == n - 1))
            def _():
                red_start(1, u0)
                red_start(2, u0)

        count = steps // BLOCK
        pl.when(s == 0)(start_later)
        share = -(-count // LATER)
        at = s * share

        @pl.when(s < LATER)
        def _():
            lax.fori_loop(at, jnp.minimum(at + share, count), later, 0)

        pl.when(s == LATER - 1)(end_later)
        pl.when(s == LATER + 1)(start_backward)
        share = -(-count // (FIRST - LATER - 1))
        at2 = (s - LATER - 1) * share

        @pl.when(both(s > LATER, s < FIRST))
        def _():
            lax.fori_loop(at2, jnp.minimum(at2 + share, count), backward, 0)

        for job, offset in ((finish, 5), (full_sum, 3), (chip_sum, 1), (project, 0)):
            at = s - FIRST - offset
            pl.when(both(at >= 0, lax.rem(at, 2) == 0, at // 2 < chunks))(lambda job=job, at=at: job(at // 2))
        pl.when(s == FIRST + 2 * chunks + 2)(share_sums)
        return carry

    slots = max((units - 1) * space + depth + 1, FIRST + 2 * chunks + 4)
    lax.fori_loop(0, slots, slot_step, 0)

    def close_unit(u, carry):
        give_copy(u, wg_at(u, 0)).wait_send()
        pair_copy(u).wait_send()
        for l in range(3):
            c = lines[l][1]
            src = wg_at(u, 0)
            pl.when(o != c)(lambda l=l: red_copy(l, u, True).wait_send())
            pl.when(o == c)(lambda l=l: local_copy(l, u).wait())
            pl.when(both(o <= c, o > 0))(lambda l=l: bc_copy(l, u, False, src).wait_send())
            pl.when(both(o >= c, o < n - 1))(lambda l=l: bc_copy(l, u, True, src).wait_send())
        return carry

    lax.fori_loop(0, units, close_unit, 0)

    def close_chunk(ch, carry):
        x_copy(ch).wait_send()
        s_copy(ch).wait_send()
        for d in range(1, 4):
            row_copy(ch, chan, d).wait_send()
        return carry

    lax.fori_loop(0, chunks, close_chunk, 0)
    for ch in (chunks - 2, chunks - 1):
        out_copy(ch).wait()
        act_copy(ch).wait()
        acr_copy(ch).wait_send()
    peers(lambda p: fore_copy(tm, p).wait_send())
    peers(lambda p: back_copy(tm, p).wait_send())
    peers(lambda p: sum_copy(p, tm).wait_recv())
    peers(lambda p: sum_copy(tm, p).wait_send())
    totals[...] = lax.fori_loop(0, tm_count, lambda d, v: v + sum_rx[d], jnp.zeros(totals.shape, F32))


def layer(tokens, weights, cotangent, gain, shift, mix_f, mix_r, bias_f, bias_r, bank, selector, resets):
    rows, steps, width = tokens.shape
    full = gain.shape[-1]
    tm_count, chan_count = lax.axis_size("tm"), lax.axis_size("chan")
    chunks = steps // CHUNK
    span = CHUNK * rows
    count = steps * rows
    units = 3 * full // UNIT
    pieces = UNIT // 4 // CHUNK
    hbm = pl.BlockSpec(memory_space=pl.ANY)
    vmem = pl.BlockSpec(memory_space=pltpu.VMEM)
    smem = pl.BlockSpec(memory_space=pltpu.SMEM)
    dma = pltpu.SemaphoreType.DMA
    stat = pltpu.VMEM((CHUNK // BLOCK, rows, BLOCK, LANE), F32)
    wide = pltpu.VMEM((count, width), F32)
    narrow = pltpu.VMEM((count, LANE), F32)
    short = pltpu.VMEM((count, width), BF16)
    return pl.pallas_call(
        layer_kernel,
        out_shape=(
            jax.ShapeDtypeStruct((units, 4, pieces, CHUNK, width), BF16),
            jax.ShapeDtypeStruct(tokens.shape, F32),
            jax.ShapeDtypeStruct(tokens.shape, BF16),
            jax.ShapeDtypeStruct((full, count), BF16),
            jax.ShapeDtypeStruct((rows, width), F32),
            jax.ShapeDtypeStruct((8, width), F32),
        ),
        in_specs=[hbm, hbm, hbm] + [vmem] * 7 + [smem, vmem],
        out_specs=(hbm, hbm, hbm, hbm, vmem, vmem),
        scratch_shapes=[
            pltpu.VMEM((chunks * chan_count * rows, CHUNK, width), BF16),
            pltpu.VMEM((ring_of(tm_count) * SLICE * pieces, CHUNK, width), BF16),
            pltpu.VMEM((2, span, full), BF16),
            pltpu.VMEM((full, span), BF16),
            pltpu.VMEM((3, full, width), BF16),
            wide, wide, wide, wide,
            short,
            pltpu.VMEM((2, rows, CHUNK, width), BF16),
            short,
            narrow, narrow, narrow,
            pltpu.VMEM((3, count, width), BF16),
            pltpu.VMEM((2, rows, CHUNK, width), BF16),
            short,
            pltpu.VMEM((2, chan_count, rows, CHUNK, width), BF16),
            pltpu.VMEM((2, rows, CHUNK, width), F32),
            pltpu.VMEM((chunks, 4, 8, span), F32),
            pltpu.VMEM((2, rows, width), F32),
            pltpu.VMEM((tm_count, 8, width), F32),
            stat, stat, stat,
            pltpu.VMEM((rows, width), F32),
            pltpu.VMEM((tm_count, 2, rows, width), F32),
            pltpu.VMEM((tm_count, rows, width), F32),
            pltpu.VMEM((4, rows, width), F32),
            pltpu.VMEM((resets.shape[1], rows, LANE), jnp.int32),
            dma((chunks,)), dma((chunks,)), dma((chunks,)), dma((chunks,)), dma((chunks,)), dma((chunks,)), dma((chunks,)),
            dma((3,)), dma((2,)), dma((2,)), dma(()), dma((2,)),
            dma((tm_count,)), dma((tm_count,)), dma((tm_count,)), dma((tm_count,)),
            pltpu.SemaphoreType.REGULAR,
            dma((2,)), dma((3, units)), dma((units,)), dma((units,)),
            dma((3, units)), dma((3, units, 2)), dma((3, units, 2)), dma((3, units)), dma((2, units)), dma((2, units)),
            dma((units,)), dma((units,)), dma((chunks, 2)), dma((chunks, 2)), dma((chunks,)), dma((chunks,)),
            dma((chunks, 3)), dma((chunks, 4)), dma((tm_count,)), dma((tm_count,)),
        ],
        compiler_params=pltpu.CompilerParams(collective_id=0, has_side_effects=True, vmem_limit_bytes=VMEM_BYTES),
        name="whole",
    )(tokens, weights, cotangent, gain, shift, mix_f, mix_r, bias_f, bias_r, bank, selector, resets)


def tail_kernel(
    fin, in_grad, act, final, totals, wide_out, in_out, act_out, final_out, s0, s1, s2, s3, s4, s5,
    fin_buf, wide_buf, in_buf, act_buf, fin_sem, wide_sem, in_sem, act_sem,
):
    parts = fin_sem.shape[0]
    size = fin.shape[0] // parts
    rows = in_sem.shape[1]

    def move(src, dst, sem, i, n):
        at = pl.ds(i * n, n)
        return pltpu.make_async_copy(src.at[at], dst.at[at], sem)

    loads = [move(fin, fin_buf, fin_sem.at[i], i, size) for i in range(parts)]
    stores = [move(wide_buf, wide_out, wide_sem.at[i], i, size) for i in range(parts)]
    pairs = []
    for src, buf, dst, sem in ((in_grad, in_buf, in_out, in_sem), (act, act_buf, act_out, act_sem)):
        for r in range(rows):
            pairs.append((move(src, buf, sem.at[0, r], r, 1), move(buf, dst, sem.at[1, r], r, 1)))
    for copy in loads:
        copy.start()
    for copy, _ in pairs:
        copy.start()
    final_out[...] = final[...]
    for i, ref in enumerate((s0, s1, s2, s3, s4, s5)):
        ref[...] = totals[i : i + 1, :]
    for i in range(parts):
        loads[i].wait()

        def cast(j, carry, i=i):
            at = pl.ds(pl.multiple_of(i * size + j * 64, 64), 64)
            wide_buf[at] = fin_buf[at].astype(F32)
            return carry

        lax.fori_loop(0, size // 64, cast, 0)
        stores[i].start()
    for copy, onward in pairs:
        copy.wait()
        onward.start()
    for copy in stores:
        copy.wait()
    for _, onward in pairs:
        onward.wait()


def tail(fin, in_grad, act, final, totals):
    width = fin.shape[-1]
    flat = fin.reshape(-1, width)
    rows = in_grad.shape[0]
    hbm = pl.BlockSpec(memory_space=pl.ANY)
    vmem = pl.BlockSpec(memory_space=pltpu.VMEM)
    dma = pltpu.SemaphoreType.DMA
    line = jax.ShapeDtypeStruct((1, width), F32)
    return pl.pallas_call(
        tail_kernel,
        out_shape=(
            jax.ShapeDtypeStruct(flat.shape, F32),
            jax.ShapeDtypeStruct(in_grad.shape, F32),
            jax.ShapeDtypeStruct(act.shape, BF16),
            jax.ShapeDtypeStruct(final.shape, F32),
        ) + (line,) * 6,
        in_specs=[hbm] * 3 + [vmem] * 2,
        out_specs=(hbm,) * 3 + (vmem,) * 7,
        scratch_shapes=[
            pltpu.VMEM(flat.shape, BF16), pltpu.VMEM(flat.shape, F32),
            pltpu.VMEM(in_grad.shape, F32), pltpu.VMEM(act.shape, BF16),
            dma((TAIL,)), dma((TAIL,)), dma((2, rows)), dma((2, rows)),
        ],
        compiler_params=pltpu.CompilerParams(vmem_limit_bytes=40 << 20),
        name="tail",
    )(flat, in_grad, act, final, totals)


def body(
    tokens, ln_gain, ln_bias, weights, mix_forget, mix_reset, bias_forget, bias_reset, state_bank, selector, resets, cotangent
):
    fin, in_grad, act, _, final, totals = layer(
        tokens, weights, cotangent, ln_gain[None], ln_bias[None], mix_forget[None], mix_reset[None], bias_forget[None],
        bias_reset[None], state_bank, selector, resets,
    )
    wide, in_grad, act, final, *sums = tail(fin, in_grad, act, final, totals)
    sums = [v[0] for v in sums]
    return act, final, in_grad, wide.reshape(weights.shape), sums[4], sums[5], sums[0], sums[1], sums[2], sums[3]


def solution(mesh):
    placed = (
        P(None, "tm", "chan"), P(), P(), P(None, None, "chan"), P("chan"), P("chan"), P("chan"), P("chan"),
        P(None, "chan"), P(), P(), P(None, "tm", "chan"),
    )
    return jax.shard_map(
        body,
        mesh=mesh,
        in_specs=placed,
        out_specs=(
            P(None, "tm", "chan"), P(None, "chan"), P(None, "tm", "chan"), P(None, None, "chan"),
            P("chan"), P("chan"), P("chan"), P("chan"), P("chan"), P("chan"),
        ),
        check_vma=False,
    )
```

```python
import jax
import jax.numpy as jnp
from jax import lax
from jax.experimental import pallas as pl
from jax.experimental.pallas import tpu as pltpu
from jax.sharding import PartitionSpec as P

EPSILON = 1e-05
CHUNK = 32
BLOCK = 16
LANE = 128
UNIT = 256
LAG = 2
PAIR = 80
LINE = 48
SENDS = 4
VMEM_BYTES = 63 << 20
TAIL = 12
LATER = 4
FIRST = 8
MESH = pl.DeviceIdType.MESH
F32 = jnp.float32
BF16 = jnp.bfloat16


def sigmoid(v):
    return 1.0 / (1.0 + jnp.exp(-v))


def swapped(v, outer, inner):
    return jnp.swapaxes(v.reshape(outer, inner, v.shape[-1]), 0, 1).reshape(outer * inner, v.shape[-1])


def both(*conditions):
    out = conditions[0]
    for c in conditions[1:]:
        out = jnp.logical_and(out, c)
    return out


def ring_of(tm_count):
    return 14 if tm_count <= 8 else 3


def layer_kernel(
    tokens, weights, cotangent, gain, shift, mix_f, mix_r, bias_f, bias_r, bank, selector, resets,
    fin, in_grad, act, low_t, final, totals,
    raw, rx, low, low_t_buf, w_buf, cand, forget, gate, masked, own_tok, cot_raw, cot, mean, inv, keep_mask, grad_buf,
    act_buf, side, terms, out_buf, row_rx, more, sum_rx, mean_s, inv_s, part_s, entry, near, far, flow, reset_rows,
    x_send, x_recv, s_send, s_recv, d_send, d_recv, own_sem, w_sem, cot_sem, act_sem, tr_sem, low_sem,
    near_send, near_recv, far_send, far_recv, last_send, last_recv, ready_sem, out_sem, loc_sem, pair_send, red_send,
    bc_send, bc_recv, swap_send, give_send, give_recv, rx_recv, sib_send, sib_recv, acr_send, acr_recv, row_send,
    row_recv, sum_send, sum_recv,
):
    rows, steps, width = tokens.shape
    full = gain.shape[-1]
    tm_count, tm = lax.axis_size("tm"), lax.axis_index("tm")
    chan_count, chan = lax.axis_size("chan"), lax.axis_index("chan")
    sibling = chan + 1 - 2 * lax.rem(chan, 2)
    across = lax.rem(chan + 2, 4)
    chunks = steps // CHUNK
    span = CHUNK * rows
    part = BLOCK * rows
    tiles = width // LANE
    blocks = CHUNK // BLOCK
    units = 3 * full // UNIT
    per_gate = full // UNIT

    def remote(src, dst, send, recv, target):
        return pltpu.make_async_remote_copy(src, dst, send, recv, device_id=target, device_id_type=MESH)

    def lanes(j):
        return slice(j * LANE, (j + 1) * LANE)

    def mine(ref, j):
        return ref[0:1, pl.ds(pl.multiple_of(chan * width + j * LANE, LANE), LANE)]

    def hat(at, j):
        return (own_tok[at, lanes(j)].astype(F32) - mean[at, :]) * inv[at, :]

    def normed(at, j):
        return hat(at, j) * mine(gain, j) + mine(shift, j)

    def rows_of(ch):
        return pl.ds(pl.multiple_of(ch * span, span), span)

    def piece(ch):
        return tokens.at[:, pl.ds(pl.multiple_of(ch * CHUNK, CHUNK), CHUNK), :]

    def raw_at(ch, block):
        return raw.at[pl.ds(pl.multiple_of((ch * chan_count + block) * span, span), span)].reshape(rows, CHUNK, width)

    def own_copy(ch):
        return pltpu.make_async_copy(piece(ch), raw_at(ch, chan), own_sem.at[ch])

    def x_copy(ch):
        return remote(piece(ch), raw_at(ch, chan), x_send.at[ch], x_recv.at[ch], (tm, across))

    def s_copy(ch):
        return remote(piece(ch), raw_at(ch, chan), s_send.at[ch], s_recv.at[ch], (tm, sibling))

    def d_copy(ch):
        return remote(raw_at(ch, across), raw_at(ch, across), d_send.at[ch], d_recv.at[ch], (tm, sibling))

    def cot_copy(ch):
        at = pl.ds(pl.multiple_of(ch * CHUNK, CHUNK), CHUNK)
        return pltpu.make_async_copy(cotangent.at[:, at, :], cot_raw.at[lax.rem(ch, 2)], cot_sem.at[lax.rem(ch, 2)])

    def act_copy(ch):
        at = pl.ds(pl.multiple_of(ch * CHUNK, CHUNK), CHUNK)
        return pltpu.make_async_copy(act_buf.at[lax.rem(ch, 2)], act.at[:, at, :], act_sem.at[lax.rem(ch, 2)])

    def tr_copy(ch):
        return pltpu.make_async_copy(low_t_buf, low_t.at[:, rows_of(ch)], tr_sem)

    def low_copy(u):
        at = pl.ds(pl.multiple_of(lax.rem(u, per_gate) * UNIT, UNIT), UNIT)
        return pltpu.make_async_copy(low_t.at[at], low.at[lax.rem(u, 2)], low_sem.at[lax.rem(u, 2)])

    w_copies = [pltpu.make_async_copy(weights.at[k], w_buf.at[k], w_sem.at[k]) for k in range(3)]

    barrier = pltpu.get_barrier_semaphore()
    for d in range(1, 4):
        pl.semaphore_signal(barrier, inc=1, device_id=(tm, lax.rem(chan + d, 4)), device_id_type=MESH)

    def greet(d, carry):
        pl.semaphore_signal(barrier, inc=1, device_id=(lax.rem(tm + d, tm_count), chan), device_id_type=MESH)
        return carry

    lax.fori_loop(1, tm_count, greet, 0)
    own_copy(0).start()
    own_copy(1).start()
    cot_copy(0).start()
    for copy in w_copies:
        copy.start()
    pl.semaphore_wait(barrier, tm_count + 2)
    for ch in range(2):
        x_copy(ch).start()
        s_copy(ch).start()

    count = resets.shape[1]
    for j in range(count):
        reset_rows[j] = jnp.broadcast_to(resets[:, j : j + 1], (rows, LANE))

    def mark(t, carry):
        at = tm * steps + t

        def compare(j, hit):
            return jnp.maximum(hit, jnp.where(reset_rows[j] == at, 1.0, 0.0))

        hit = lax.fori_loop(0, count, compare, jnp.zeros((rows, LANE), F32), unroll=16)
        keep_mask[pl.ds(pl.multiple_of(t * rows, rows), rows), :] = 1.0 - hit
        return carry

    lax.fori_loop(0, steps, mark, 0)
    for r in range(rows):
        entry[r : r + 1, :] = bank[pl.ds(selector[r], 1), :]

    def flip(ch):
        @pl.when(ch >= 1)
        def _():
            tr_copy(ch - 1).wait()

        def one(j, carry):
            cols = pl.ds(pl.multiple_of(j * 256, 256), 256)
            low_t_buf[cols, :] = jnp.transpose(low[lax.rem(ch, 2), :, cols])
            return carry

        lax.fori_loop(0, full // 256, one, 0)
        tr_copy(ch).start()

    def gather_step(ch, carry):
        a_run, b_run = carry

        @pl.when(ch + 2 < chunks)
        def _():
            own_copy(ch + 2).start()
            x_copy(ch + 2).start()
            s_copy(ch + 2).start()

        @pl.when(ch + 1 < chunks)
        def _():
            cot_copy(ch + 1).start()

        base = pl.multiple_of(ch * span, span)
        slot = lax.rem(ch, 2)

        cot_copy(ch).wait()
        for h in range(blocks):
            for j in range(tiles):
                v = cot_raw[slot, :, h * BLOCK : (h + 1) * BLOCK, lanes(j)].astype(F32).reshape(part, LANE)
                cot[pl.ds(pl.multiple_of(base + h * part, part), part), lanes(j)] = swapped(v, rows, BLOCK).astype(BF16)
        pl.when(ch >= 1)(lambda: flip(ch - 1))

        x_copy(ch).wait_recv()
        d_copy(ch).start()
        own_copy(ch).wait()
        s_copy(ch).wait_recv()
        d_copy(ch).wait_recv()

        first = pl.multiple_of(ch * chan_count * span, span)

        def tokens_at(block, r, t0, cols):
            at = pl.multiple_of(first + block * span + r * CHUNK + t0, BLOCK)
            return raw[pl.ds(at, BLOCK), cols].astype(F32)

        def each(i, turn):
            r, h = i // blocks, lax.rem(i, blocks)
            totals = [jnp.zeros((BLOCK, LANE), F32) for _ in range(chan_count)]
            for j in range(tiles):
                for b in range(chan_count):
                    totals[b] = totals[b] + turn(tokens_at(b, r, h * BLOCK, lanes(j)))
            while len(totals) > 1:
                totals = [a + b for a, b in zip(totals[::2], totals[1::2])]
            part_s[h, r] = totals[0]

        def sum_rows(i, carry):
            each(i, lambda v: v)
            return carry

        lax.fori_loop(0, rows * blocks, sum_rows, 0)
        mean_s[...] = jnp.broadcast_to(jnp.sum(part_s[...], axis=-1, keepdims=True) * (1.0 / full), mean_s.shape)

        def square_rows(i, carry):
            r, h = i // blocks, lax.rem(i, blocks)
            m = mean_s[h, r]
            each(i, lambda v: (v - m) * (v - m))
            return carry

        lax.fori_loop(0, rows * blocks, square_rows, 0)
        var = jnp.sum(part_s[...], axis=-1, keepdims=True) * (1.0 / full)
        inv_s[...] = jnp.broadcast_to(lax.rsqrt(var + EPSILON), inv_s.shape)

        for h in range(blocks):
            mean_h = mean_s[h].reshape(part, LANE)
            inv_h = inv_s[h].reshape(part, LANE)

            def normalize(j, carry, h=h, mean_h=mean_h, inv_h=inv_h):
                cols = pl.ds(pl.multiple_of(j * LANE, LANE), LANE)
                inner = pl.ds(pl.multiple_of(lax.rem(j, tiles) * LANE, LANE), LANE)
                v = jnp.concatenate([tokens_at(j // tiles, r, h * BLOCK, inner) for r in range(rows)], axis=0)
                v = (v - mean_h) * inv_h * gain[0:1, cols] + shift[0:1, cols]
                low[slot, h * part : (h + 1) * part, cols] = swapped(v, rows, BLOCK).astype(BF16)
                return carry

            lax.fori_loop(0, full // LANE, normalize, 0)
            at = pl.ds(pl.multiple_of(base + h * part, part), part)
            mean[at, :] = swapped(mean_h, rows, BLOCK)
            inv[at, :] = swapped(inv_h, rows, BLOCK)
            for j in range(tiles):
                v = jnp.concatenate([tokens_at(chan, r, h * BLOCK, lanes(j)) for r in range(rows)], axis=0)
                own_tok[at, lanes(j)] = swapped(v, rows, BLOCK).astype(BF16)

        at = pl.ds(base, span)

        @pl.when(ch == 0)
        def _():
            for copy in w_copies:
                copy.wait()

        cand[at, :] = jnp.dot(low[slot], w_buf[0], preferred_element_type=F32)
        forget[at, :] = jnp.dot(low[slot], w_buf[1], preferred_element_type=F32)
        gate[at, :] = jnp.dot(low[slot], w_buf[2], preferred_element_type=F32)

        def gates(b, carry):
            a_list, b_list = list(carry[0]), list(carry[1])
            at = pl.ds(pl.multiple_of(base + b * part, part), part)
            mask = keep_mask[at, :]
            for j in range(tiles):
                cols = lanes(j)
                nrm = normed(at, j)
                f = sigmoid(forget[at, cols] + mix_f[0:1, cols] * nrm + bias_f[0:1, cols])
                o = sigmoid(gate[at, cols] + mix_r[0:1, cols] * nrm + bias_r[0:1, cols])
                forget[at, cols] = f
                gate[at, cols] = o
                inject = (1.0 - f) * cand[at, cols]
                keep = f * mask
                for t in range(BLOCK):
                    now = slice(t * rows, (t + 1) * rows)
                    a_list[j] = a_list[j] * keep[now]
                    b_list[j] = b_list[j] * keep[now] + inject[now]
            return tuple(a_list), tuple(b_list)

        return lax.fori_loop(0, blocks, gates, (a_run, b_run))

    ones = tuple(jnp.ones((rows, LANE), F32) for _ in range(tiles))
    zeros = tuple(jnp.zeros((rows, LANE), F32) for _ in range(tiles))
    a_run, b_run = lax.fori_loop(0, chunks, gather_step, (ones, zeros))

    spans = jnp.where(reset_rows[0] >= tm_count * steps, 1.0, 0.0)
    last_tm = tm_count - 1

    def spanning(v):
        return jnp.sum(v * spans, axis=0, keepdims=True)

    def near_copy(way, target):
        return remote(near.at[way, 0], near.at[way, 1], near_send.at[way], near_recv.at[way], (target, chan))

    def far_copy(way, source, target):
        return remote(
            far.at[way, source], far.at[way, source], far_send.at[way, target], far_recv.at[way, source], (target, chan)
        )

    def last_copy(target):
        return remote(near.at[0, 0], near.at[0, 2], last_send.at[target], last_recv, (target, chan))

    def sum_copy(source, target):
        return remote(sum_rx.at[source], sum_rx.at[source], sum_send.at[target], sum_recv.at[source], (target, chan))

    def peers(act_on):
        def one(d, carry):
            act_on(lax.rem(tm + d, tm_count))
            return carry

        lax.fori_loop(1, tm_count, one, 0)

    for j in range(tiles):
        near[0, 0, :, lanes(j)] = b_run[j]
        far[0, tm, j : j + 1, :] = spanning(a_run[j])
        far[0, tm, tiles + j : tiles + j + 1, :] = spanning(b_run[j])
    pl.when(tm < last_tm)(lambda: near_copy(0, tm + 1).start())
    peers(lambda p: far_copy(0, tm, p).start())
    pl.when(tm == last_tm)(lambda: peers(lambda p: last_copy(p).start()))
    flip(chunks - 1)
    peers(lambda p: far_copy(0, p, tm).wait_recv())
    pl.when(tm > 0)(lambda: near_copy(0, tm).wait_recv())

    def carry_on(d, carry):
        state, here = carry
        here = jnp.where(d == tm, state, here)
        return far[0, d, 0:tiles, :] * state + far[0, d, tiles : 2 * tiles, :], here

    lead = jnp.concatenate([spanning(entry[:, lanes(j)]) for j in range(tiles)], axis=0)
    last, here = lax.fori_loop(0, tm_count, carry_on, (lead, lead))
    states = []
    for j in range(tiles):
        row = jnp.broadcast_to(here[j : j + 1], (rows, LANE))
        others = jnp.where(tm == 0, entry[:, lanes(j)], near[0, 1, :, lanes(j)])
        states.append(jnp.where(spans > 0, row, others))
    tr_copy(chunks - 1).wait()
    low_copy(0).start()

    def forward(b, states):
        states = list(states)
        at = pl.ds(pl.multiple_of(b * part, part), part)
        mask = keep_mask[at, :]
        for j in range(tiles):
            cols = lanes(j)
            f = forget[at, cols]
            inject = (1.0 - f) * cand[at, cols]
            before, after = [], []
            c = states[j]
            for t in range(BLOCK):
                now = slice(t * rows, (t + 1) * rows)
                c = c * mask[now]
                before.append(c)
                c = f[now] * c + inject[now]
                after.append(c)
            states[j] = c
            masked[at, cols] = jnp.concatenate(before, axis=0)
            th = jnp.tanh(jnp.concatenate(after, axis=0))
            o = gate[at, cols]
            gate_grad = cot[at, cols].astype(F32) * (th - own_tok[at, cols].astype(F32))
            grad_buf[2, at, cols] = (gate_grad * o * (1.0 - o)).astype(BF16)
        return tuple(states)

    lax.fori_loop(0, steps // BLOCK, forward, tuple(states))

    def start_later():
        flow[0] = jnp.ones((rows, width), F32)
        for i in range(1, 4):
            flow[i] = jnp.zeros((rows, width), F32)

    def later(b, carry):
        ch, h = b // blocks, lax.rem(b, blocks)
        slot = lax.rem(ch, 2)

        @pl.when(both(h == 0, ch >= 2))
        def _():
            act_copy(ch - 2).wait()

        at = pl.ds(pl.multiple_of(b * part, part), part)
        t0 = pl.multiple_of(h * BLOCK, BLOCK)
        mask = keep_mask[at, :]
        for j in range(tiles):
            cols = lanes(j)
            f = forget[at, cols]
            th = jnp.tanh(f * masked[at, cols] + (1.0 - f) * cand[at, cols])
            o = gate[at, cols]
            x = own_tok[at, cols].astype(F32)
            ct = cot[at, cols].astype(F32)
            rest = 1.0 - o
            out = swapped(o * th + rest * x, BLOCK, rows).astype(BF16)
            act_buf[slot, :, pl.ds(t0, BLOCK), cols] = out.reshape(rows, BLOCK, LANE)
            reset_pre = ct * (th - x) * o * rest
            direct = ct * o * (1.0 - th * th)
            side[at, cols] = (ct * rest).astype(BF16)
            gate[at, cols] = direct
            keep = f * mask
            run, total = flow[0, :, cols], flow[1, :, cols]
            for t in range(BLOCK):
                now = slice(t * rows, (t + 1) * rows)
                run = run * keep[now]
                total = total + run * direct[now]
            flow[0, :, cols], flow[1, :, cols] = run, total
            for i, v in enumerate((reset_pre * normed(at, j), reset_pre)):
                flow[2 + i, :, cols] = flow[2 + i, :, cols] + jnp.sum(v.reshape(BLOCK, rows, LANE), axis=0)

        @pl.when(h == blocks - 1)
        def _():
            act_copy(ch).start()

        return carry

    def end_later():
        near[1, 0] = flow[1]
        for j in range(tiles):
            far[1, tm, j : j + 1, :] = spanning(flow[1, :, lanes(j)])
        pl.when(tm > 0)(lambda: near_copy(1, tm - 1).start())
        peers(lambda p: far_copy(1, tm, p).start())
        for target in (sibling, across):
            pl.semaphore_signal(ready_sem, inc=1, device_id=(tm, target), device_id_type=MESH)
        for i in range(2):
            sum_rx[tm, 2 * i + 1 : 2 * i + 2, :] = jnp.sum(flow[2 + i], axis=0, keepdims=True)
        sum_rx[tm, 6:8, :] = jnp.zeros((2, width), F32)
        more[...] = jnp.zeros_like(more)

    def sent_on(ch, carry):
        d_copy(ch).wait_send()
        return carry

    lax.fori_loop(0, chunks, sent_on, 0)

    n = tm_count // 2
    o, y = tm // 2, lax.rem(tm, 2)
    partner = (o * 2 + 1 - y, chan)
    left = ((o - 1) * 2 + y, chan)
    right = ((o + 1) * 2 + y, chan)
    ring = ring_of(tm_count)
    ends, middle = (0, n - 1), (n // 2 - 1, n // 2)
    lines = [(0, middle[0] + y, n // 2, 1, None)]
    for l in (1, 2):
        if n == 4:
            lines += [(l, ends[l - 1], n - 1, 0, 0), (l, middle[l - 1], n // 2, 0, 1)]
        else:
            lines += [(l, middle[l - 1], n // 2, 0, None)]
    give_stage = 2 * (n // 2) + 2
    depth = LAG * max([give_stage] + [first + reach + (l > 0) + reach for l, c, reach, first, parity in lines])
    space = -(-depth // ring)

    def stage(s, number, parity=None):
        v = s - LAG * number
        u = v if space == 1 else v // space
        go = both(v >= 0, u < units)
        if space > 1:
            go = both(go, lax.rem(v, space) == 0)
        return u, go if parity is None else both(go, lax.rem(u, 2) == parity)

    def gate_of(u):
        return lax.rem(u // per_gate + 2, 3)

    def piece_of(l, mate=False):
        if l == 0:
            return (1 - y if mate else y) * PAIR, PAIR
        return 2 * PAIR + (l - 1) * LINE, LINE

    def wg_rows(l, u, mate=False):
        start, size = piece_of(l, mate)
        return pl.ds(pl.multiple_of(u * UNIT + start, 16), size)

    def fin_at(l, u):
        start, size = piece_of(l)
        return fin.at[pl.ds(pl.multiple_of((gate_of(u) * per_gate + lax.rem(u, per_gate)) * UNIT + start, 16), size)]

    def rx_rows(u, place, l):
        start = place * PAIR if l == 0 else 3 * PAIR + (place - 3) * LINE
        size = PAIR if l == 0 else LINE
        return pl.ds(pl.multiple_of(lax.rem(u, ring) * (3 * PAIR + 4 * LINE) + start, 16), size)

    def arrival(l, c, column, way, u):
        if l == 0:
            return 1 + way
        if l == 1:
            other = 6
        elif n == 4:
            other = jnp.where(column == jnp.where(lax.rem(u, 2) == 0, ends[0], middle[0]), 6, 3)
        else:
            other = jnp.where(column == middle[0], 6, 3)
        return jnp.where(column == c, 3 + way, other)

    def launch(make, u):
        @pl.when(u >= SENDS)
        def _():
            make(u - SENDS).wait_send()

        make(u).start()

    def to_rx(src, u, place, l, sem, target):
        return remote(src, rx.at[rx_rows(u, place, l)], sem, rx_recv.at[lax.rem(u, ring), place], target)

    def pair_copy(u):
        return to_rx(raw.at[wg_rows(0, u, True)], u, 0, 0, pair_send.at[lax.rem(u, SENDS)], partner)

    def red_copy(l, c, u, to_right):
        way, column = (0, o + 1) if to_right else (1, o - 1)
        return to_rx(
            raw.at[wg_rows(l, u)], u, arrival(l, c, column, way, u), l, red_send.at[l, lax.rem(u, SENDS)],
            right if to_right else left,
        )

    def red_wait(l, c, u, way):
        place = arrival(l, c, o, way, u)
        at = rx_rows(u, place, l)
        to_rx(rx.at[at], u, place, l, red_send.at[l, 0], partner).wait_recv()
        return rx[at].astype(F32)

    def bc_copy(l, u, to_right, src):
        return remote(
            src, fin_at(l, u), bc_send.at[l, lax.rem(u, SENDS), 1 if to_right else 0], bc_recv.at[l, lax.rem(u, ring)],
            right if to_right else left,
        )

    def swap_copy(l, u):
        return to_rx(raw.at[wg_rows(l, u)], u, 5, l, swap_send.at[lax.rem(u, SENDS)], partner)

    def give_copy(u, src):
        return remote(src, fin_at(0, u), give_send.at[lax.rem(u, SENDS)], give_recv.at[lax.rem(u, ring)], partner)

    def local_copy(l, u):
        return pltpu.make_async_copy(raw.at[wg_rows(l, u)], fin_at(l, u), loc_sem.at[l, lax.rem(u, SENDS)])

    def add_to(l, u, *others):
        at = wg_rows(l, u)
        total = raw[at].astype(F32)
        for v in others:
            total = total + v
        raw[at] = total.astype(BF16)

    def red_start(l, c, u):
        pl.when(o < c)(lambda: launch(lambda v: red_copy(l, c, v, True), u))
        pl.when(o > c)(lambda: launch(lambda v: red_copy(l, c, v, False), u))

    def publish(l, u):
        @pl.when(u >= SENDS)
        def _():
            local_copy(l, u - SENDS).wait()

        local_copy(l, u).start()
        pl.when(o > 0)(lambda: launch(lambda v: bc_copy(l, v, False, raw.at[wg_rows(l, v)]), u))
        pl.when(o < n - 1)(lambda: launch(lambda v: bc_copy(l, v, True, raw.at[wg_rows(l, v)]), u))
        if l == 0:
            launch(lambda v: give_copy(v, raw.at[wg_rows(0, v)]), u)

    def block_cols(c):
        return pl.ds(pl.multiple_of(c * width, width), width)

    def sib_rows(ch, q):
        return pl.ds(pl.multiple_of(units * UNIT + (lax.rem(ch, 4) * 2 + q) * span, span), span)

    def sib_copy(ch, q):
        slot = lax.rem(ch, 2)
        cols = sibling if q == 0 else lax.rem(sibling + 2, 4)
        return remote(
            terms.at[slot, cols], raw.at[sib_rows(ch, q)], sib_send.at[q], sib_recv.at[lax.rem(ch, 4), q], (tm, sibling)
        )

    def acr_copy(ch):
        return remote(
            terms.at[lax.rem(ch, 2), across], cot.at[rows_of(ch)], acr_send.at[lax.rem(ch, 2)], acr_recv.at[ch], (tm, across)
        )

    def row_copy(ch, source, d):
        return remote(
            row_rx.at[ch, source], row_rx.at[ch, source], row_send.at[lax.rem(ch, 4), d - 1],
            row_recv.at[lax.rem(ch, 4), source], (tm, lax.rem(chan + d, 4)),
        )

    def out_copy(ch):
        at = pl.ds(pl.multiple_of(ch * CHUNK, CHUNK), CHUNK)
        return pltpu.make_async_copy(out_buf.at[lax.rem(ch, 2)], in_grad.at[:, at, :], out_sem.at[lax.rem(ch, 2)])

    def project(ch):
        at = rows_of(ch)
        slot = lax.rem(ch, 2)

        @pl.when(ch == 0)
        def _():
            pl.semaphore_wait(ready_sem, 2)

        @pl.when(ch >= 2)
        def _():
            acr_copy(ch - 2).wait_send()

        for b in range(chan_count):
            total = jnp.zeros((span, width), F32)
            for k in range(3):
                total = total + lax.dot_general(
                    grad_buf[k, at, :], w_buf[k, b * width : (b + 1) * width, :], (((1,), (1,)), ((), ())),
                    preferred_element_type=F32,
                )
            terms[slot, b] = total.astype(BF16)
        sib_copy(ch, 0).start()
        sib_copy(ch, 1).start()

    def chip_sum(ch):
        slot = lax.rem(ch, 2)
        for q in range(2):
            sib_copy(ch, q).wait_recv()
        there = terms[slot, across].astype(F32) + raw[sib_rows(ch, 1)].astype(F32)
        terms[slot, across] = there.astype(BF16)
        acr_copy(ch).start()
        here = terms[slot, chan].astype(F32) + raw[sib_rows(ch, 0)].astype(F32)
        cand[rows_of(ch), :] = here
        for q in range(2):
            sib_copy(ch, q).wait_send()

    def full_sum(ch):
        acr_copy(ch).wait_recv()
        at = rows_of(ch)
        total = jnp.zeros((8, span), F32)
        pick = lax.broadcasted_iota(jnp.int32, (8, LANE), 0)
        for j in range(tiles):
            cols = lanes(j)
            own = grad_buf[1, at, cols].astype(F32) * mix_f[0:1, cols] + grad_buf[2, at, cols].astype(F32) * mix_r[0:1, cols]
            g = cand[at, cols] + cot[at, cols].astype(F32) + own
            cand[at, cols] = g
            weighted = g * hat(at, j)
            for i, v in enumerate((weighted, g)):
                more[i, :, cols] = more[i, :, cols] + jnp.sum(v.reshape(CHUNK, rows, LANE), axis=0)
            for i, v in enumerate((g * mine(gain, j), weighted * mine(gain, j))):
                lead = jnp.where(pick == i, 1.0, 0.0).astype(BF16)
                high = v.astype(BF16)
                low_part = (v - high.astype(F32)).astype(BF16)
                for p in (high, low_part):
                    total = total + lax.dot_general(lead, p, (((1,), (1,)), ((), ())), preferred_element_type=F32)
        row_rx[ch, chan] = total
        for d in range(1, 4):
            pl.when(ch >= 4)(lambda d=d: row_copy(ch - 4, chan, d).wait_send())
            row_copy(ch, chan, d).start()

    def finish(ch):
        for d in range(1, 4):
            row_copy(ch, lax.rem(chan + d, 4), d).wait_recv()

        @pl.when(ch >= 2)
        def _():
            out_copy(ch - 2).wait()

        at = rows_of(ch)
        total = (row_rx[ch, 0] + row_rx[ch, 1] + row_rx[ch, 2] + row_rx[ch, 3]) * (1.0 / full)
        columns = jnp.transpose(total)
        first = jnp.broadcast_to(columns[:, 0:1], (span, LANE))
        second = jnp.broadcast_to(columns[:, 1:2], (span, LANE))
        for j in range(tiles):
            cols = lanes(j)
            g = cand[at, cols] * mine(gain, j)
            v = inv[at, :] * (g - first - hat(at, j) * second) + side[at, cols].astype(F32)
            out_buf[lax.rem(ch, 2), :, :, cols] = swapped(v, CHUNK, rows).reshape(rows, CHUNK, LANE)
        out_copy(ch).start()

    def share_sums():
        for i in range(2):
            sum_rx[tm, 2 * i : 2 * i + 1, :] = jnp.sum(flow[1 + i], axis=0, keepdims=True)
            sum_rx[tm, 4 + i : 5 + i, :] = jnp.sum(more[i], axis=0, keepdims=True)
        peers(lambda p: sum_copy(tm, p).start())

    def start_backward():
        peers(lambda p: far_copy(1, p, tm).wait_recv())
        pl.when(tm < last_tm)(lambda: near_copy(1, tm).wait_recv())

        def carry_back(i, v):
            d = tm_count - 1 - i
            return jnp.where(d > tm, far[0, d, 0:tiles, :] * v + far[1, d, 0:tiles, :], v)

        inflow = lax.fori_loop(0, tm_count, carry_back, jnp.zeros((tiles, LANE), F32))
        for j in range(tiles):
            row = jnp.broadcast_to(inflow[j : j + 1], (rows, LANE))
            others = jnp.where(tm == last_tm, 0.0, near[1, 1, :, lanes(j)])
            flow[0, :, lanes(j)] = jnp.where(spans > 0, row, others)
        flow[1] = jnp.zeros((rows, width), F32)
        flow[2] = jnp.zeros((rows, width), F32)

    def backward(i, carry):
        b = steps // BLOCK - 1 - i
        at = pl.ds(pl.multiple_of(b * part, part), part)
        mask = keep_mask[at, :]
        for j in range(tiles):
            cols = lanes(j)
            f = forget[at, cols]
            keep = f * mask
            direct = gate[at, cols]
            g = flow[0, :, cols]
            adjoint = [None] * BLOCK
            for t in reversed(range(BLOCK)):
                now = slice(t * rows, (t + 1) * rows)
                adjoint[t] = direct[now] + g
                g = keep[now] * adjoint[t]
            flow[0, :, cols] = g
            cand_grad = jnp.concatenate(adjoint, axis=0) * (1.0 - f)
            forget_pre = cand_grad * (masked[at, cols] - cand[at, cols]) * f
            grad_buf[0, at, cols] = cand_grad.astype(BF16)
            grad_buf[1, at, cols] = forget_pre.astype(BF16)
            for i, v in enumerate((forget_pre * normed(at, j), forget_pre)):
                flow[1 + i, :, cols] = flow[1 + i, :, cols] + jnp.sum(v.reshape(BLOCK, rows, LANE), axis=0)
        return carry

    def slot_step(s, carry):
        u, go = stage(s, give_stage)
        pl.when(go)(lambda: give_copy(u, raw.at[wg_rows(0, u)]).wait_recv())

        for l, c, reach, first, parity in lines:
            late = first + reach + (1 if l else 0)
            u, go = stage(s, late + jnp.abs(o - c), parity)

            @pl.when(both(o != c, go))
            def _(l=l, c=c, u=u):
                bc_copy(l, u, True, fin_at(l, u)).wait_recv()
                pl.when(both(o < c, o > 0))(lambda: launch(lambda v: bc_copy(l, v, False, fin_at(l, v)), u))
                pl.when(both(o > c, o < n - 1))(lambda: launch(lambda v: bc_copy(l, v, True, fin_at(l, v)), u))
                if l == 0:
                    launch(lambda v: give_copy(v, fin_at(0, v)), u)

        for l, c, reach, first, parity in lines[1:]:
            u, go = stage(s, reach + 1, parity)

            @pl.when(both(o == c, go))
            def _(l=l, u=u):
                swap_copy(l, u).wait()
                add_to(l, u, rx[rx_rows(u, 5, l)].astype(F32))
                publish(l, u)

        for l, c, reach, first, parity in lines:
            u, go = stage(s, first + reach, parity)

            @pl.when(both(o == c, go))
            def _(l=l, c=c, u=u):
                if l == 0 and n > 2:
                    add_to(l, u, red_wait(l, c, u, 0), red_wait(l, c, u, 1))
                elif l > 0 and 0 < c < n - 1:
                    add_to(l, u, red_wait(l, c, u, 0), red_wait(l, c, u, 1))
                else:
                    pl.when(o > 0)(lambda: add_to(l, u, red_wait(l, c, u, 0)))
                    pl.when(o < n - 1)(lambda: add_to(l, u, red_wait(l, c, u, 1)))
                if l == 0:
                    publish(l, u)
                else:
                    swap_copy(l, u).start()

        for l, c, reach, first, parity in lines:
            u, go = stage(s, first + jnp.where(o < c, o, n - 1 - o), parity)

            @pl.when(both(o < c, o > 0, go))
            def _(l=l, c=c, u=u):
                add_to(l, u, red_wait(l, c, u, 0))
                launch(lambda v: red_copy(l, c, v, True), u)

            @pl.when(both(o > c, o < n - 1, go))
            def _(l=l, c=c, u=u):
                add_to(l, u, red_wait(l, c, u, 1))
                launch(lambda v: red_copy(l, c, v, False), u)

        u, go = stage(s, 1)

        @pl.when(go)
        def _():
            pair_copy(u).wait_recv()
            add_to(0, u, rx[rx_rows(u, 0, 0)].astype(F32))
            pl.when(jnp.logical_or(o == 0, o == n - 1))(lambda: red_start(0, lines[0][1], u))

        u0, go0 = stage(s, 0)

        @pl.when(go0)
        def _():
            pl.when(u0 + 1 < units)(lambda: low_copy(u0 + 1).start())
            low_copy(u0).wait()
            g = jnp.dot(low[lax.rem(u0, 2)], grad_buf[gate_of(u0)], preferred_element_type=F32)
            raw[pl.ds(pl.multiple_of(u0 * UNIT, UNIT), UNIT)] = g.astype(BF16)
            launch(pair_copy, u0)
            for l, c, reach, first, parity in lines[1:]:
                mine_now = jnp.logical_or(o == 0, o == n - 1)
                if parity is not None:
                    mine_now = both(mine_now, lax.rem(u0, 2) == parity)
                pl.when(mine_now)(lambda l=l, c=c: red_start(l, c, u0))

        count = steps // BLOCK
        pl.when(s == 0)(start_later)
        share = -(-count // LATER)
        at = s * share

        @pl.when(s < LATER)
        def _():
            lax.fori_loop(at, jnp.minimum(at + share, count), later, 0)

        pl.when(s == LATER - 1)(end_later)
        pl.when(s == LATER + 1)(start_backward)
        share = -(-count // (FIRST - LATER - 1))
        at2 = (s - LATER - 1) * share

        @pl.when(both(s > LATER, s < FIRST))
        def _():
            lax.fori_loop(at2, jnp.minimum(at2 + share, count), backward, 0)

        for job, offset in ((finish, 5), (full_sum, 3), (chip_sum, 1), (project, 0)):
            at = s - FIRST - offset
            pl.when(both(at >= 0, lax.rem(at, 2) == 0, at // 2 < chunks))(lambda job=job, at=at: job(at // 2))
        pl.when(s == FIRST + 2 * chunks + 2)(share_sums)
        return carry

    slots = max((units - 1) * space + depth + 1, FIRST + 2 * chunks + 4)
    lax.fori_loop(0, slots, slot_step, 0)

    def close_unit(u, carry):
        give_copy(u, raw.at[wg_rows(0, u)]).wait_send()
        pair_copy(u).wait_send()
        for l, c, reach, first, parity in lines:

            @pl.when(True if parity is None else lax.rem(u, 2) == parity)
            def _(l=l, c=c):
                src = raw.at[wg_rows(l, u)]
                pl.when(o != c)(lambda: red_copy(l, c, u, True).wait_send())
                pl.when(o == c)(lambda: local_copy(l, u).wait())
                pl.when(both(o <= c, o > 0))(lambda: bc_copy(l, u, False, src).wait_send())
                pl.when(both(o >= c, o < n - 1))(lambda: bc_copy(l, u, True, src).wait_send())

        return carry

    lax.fori_loop(units - SENDS, units, close_unit, 0)

    def close_chunk(ch, carry):
        x_copy(ch).wait_send()
        s_copy(ch).wait_send()

        @pl.when(ch >= chunks - 4)
        def _():
            for d in range(1, 4):
                row_copy(ch, chan, d).wait_send()

        return carry

    lax.fori_loop(0, chunks, close_chunk, 0)
    for ch in (chunks - 2, chunks - 1):
        out_copy(ch).wait()
        act_copy(ch).wait()
        acr_copy(ch).wait_send()
    for way in range(2):
        peers(lambda p, way=way: far_copy(way, tm, p).wait_send())
    pl.when(tm < last_tm)(lambda: near_copy(0, tm).wait_send())
    pl.when(tm > 0)(lambda: near_copy(1, tm).wait_send())
    pl.when(tm == last_tm)(lambda: peers(lambda p: last_copy(p).wait_send()))
    pl.when(tm != last_tm)(lambda: last_copy(tm).wait_recv())
    for j in range(tiles):
        row = jnp.broadcast_to(last[j : j + 1], (rows, LANE))
        others = jnp.where(tm == last_tm, near[0, 0, :, lanes(j)], near[0, 2, :, lanes(j)])
        final[:, lanes(j)] = jnp.where(spans > 0, row, others)
    peers(lambda p: sum_copy(p, tm).wait_recv())
    peers(lambda p: sum_copy(tm, p).wait_send())
    totals[...] = lax.fori_loop(0, tm_count, lambda d, v: v + sum_rx[d], jnp.zeros(totals.shape, F32))


def layer(tokens, weights, cotangent, gain, shift, mix_f, mix_r, bias_f, bias_r, bank, selector, resets):
    rows, steps, width = tokens.shape
    full = gain.shape[-1]
    tm_count, chan_count = lax.axis_size("tm"), lax.axis_size("chan")
    chunks = steps // CHUNK
    span = CHUNK * rows
    count = steps * rows
    units = 3 * full // UNIT
    ring = ring_of(tm_count)
    hbm = pl.BlockSpec(memory_space=pl.ANY)
    vmem = pl.BlockSpec(memory_space=pltpu.VMEM)
    smem = pl.BlockSpec(memory_space=pltpu.SMEM)
    dma = pltpu.SemaphoreType.DMA
    stat = pltpu.VMEM((CHUNK // BLOCK, rows, BLOCK, LANE), F32)
    wide = pltpu.VMEM((count, width), F32)
    narrow = pltpu.VMEM((count, LANE), F32)
    short = pltpu.VMEM((count, width), BF16)
    return pl.pallas_call(
        layer_kernel,
        out_shape=(
            jax.ShapeDtypeStruct((units * UNIT, width), BF16),
            jax.ShapeDtypeStruct(tokens.shape, F32),
            jax.ShapeDtypeStruct(tokens.shape, BF16),
            jax.ShapeDtypeStruct((full, count), BF16),
            jax.ShapeDtypeStruct((rows, width), F32),
            jax.ShapeDtypeStruct((8, width), F32),
        ),
        in_specs=[hbm, hbm, hbm] + [vmem] * 7 + [smem, vmem],
        out_specs=(hbm, hbm, hbm, hbm, vmem, vmem),
        scratch_shapes=[
            pltpu.VMEM((chunks * chan_count * span, width), BF16),
            pltpu.VMEM((ring * (3 * PAIR + 4 * LINE), width), BF16),
            pltpu.VMEM((2, span, full), BF16),
            pltpu.VMEM((full, span), BF16),
            pltpu.VMEM((3, full, width), BF16),
            wide, wide, wide, wide,
            short,
            pltpu.VMEM((2, rows, CHUNK, width), BF16),
            short,
            narrow, narrow, narrow,
            pltpu.VMEM((3, count, width), BF16),
            pltpu.VMEM((2, rows, CHUNK, width), BF16),
            short,
            pltpu.VMEM((2, chan_count, span, width), BF16),
            pltpu.VMEM((2, rows, CHUNK, width), F32),
            pltpu.VMEM((chunks, 4, 8, span), F32),
            pltpu.VMEM((2, rows, width), F32),
            pltpu.VMEM((tm_count, 8, width), F32),
            stat, stat, stat,
            pltpu.VMEM((rows, width), F32),
            pltpu.VMEM((2, 3, rows, width), F32),
            pltpu.VMEM((2, tm_count, 8, LANE), F32),
            pltpu.VMEM((4, rows, width), F32),
            pltpu.VMEM((resets.shape[1], rows, LANE), jnp.int32),
            dma((chunks,)), dma((chunks,)), dma((chunks,)), dma((chunks,)), dma((chunks,)), dma((chunks,)), dma((chunks,)),
            dma((3,)), dma((2,)), dma((2,)), dma(()), dma((2,)),
            dma((2,)), dma((2,)), dma((2, tm_count)), dma((2, tm_count)), dma((tm_count,)), dma(()),
            pltpu.SemaphoreType.REGULAR,
            dma((2,)), dma((3, SENDS)), dma((SENDS,)), dma((3, SENDS)), dma((3, SENDS, 2)), dma((3, ring)), dma((SENDS,)),
            dma((SENDS,)), dma((ring,)), dma((ring, 7)), dma((2,)), dma((4, 2)), dma((2,)), dma((chunks,)),
            dma((4, 3)), dma((4, 4)), dma((tm_count,)), dma((tm_count,)),
        ],
        compiler_params=pltpu.CompilerParams(collective_id=0, has_side_effects=True, vmem_limit_bytes=VMEM_BYTES),
        name="whole",
    )(tokens, weights, cotangent, gain, shift, mix_f, mix_r, bias_f, bias_r, bank, selector, resets)


def tail_kernel(
    fin, in_grad, act, final, totals, wide_out, in_out, act_out, final_out, s0, s1, s2, s3, s4, s5,
    fin_buf, wide_buf, in_buf, act_buf, fin_sem, wide_sem, in_sem, act_sem,
):
    parts = fin_sem.shape[0]
    size = fin.shape[0] // parts
    rows = in_sem.shape[1]

    def move(src, dst, sem, i, n):
        at = pl.ds(i * n, n)
        return pltpu.make_async_copy(src.at[at], dst.at[at], sem)

    loads = [move(fin, fin_buf, fin_sem.at[i], i, size) for i in range(parts)]
    stores = [move(wide_buf, wide_out, wide_sem.at[i], i, size) for i in range(parts)]
    pairs = []
    for src, buf, dst, sem in ((in_grad, in_buf, in_out, in_sem), (act, act_buf, act_out, act_sem)):
        for r in range(rows):
            pairs.append((move(src, buf, sem.at[0, r], r, 1), move(buf, dst, sem.at[1, r], r, 1)))
    for copy in loads:
        copy.start()
    for copy, _ in pairs:
        copy.start()
    final_out[...] = final[...]
    for i, ref in enumerate((s0, s1, s2, s3, s4, s5)):
        ref[...] = totals[i : i + 1, :]
    for i in range(parts):
        loads[i].wait()

        def cast(j, carry, i=i):
            at = pl.ds(pl.multiple_of(i * size + j * 64, 64), 64)
            wide_buf[at] = fin_buf[at].astype(F32)
            return carry

        lax.fori_loop(0, size // 64, cast, 0)
        stores[i].start()
    for copy, onward in pairs:
        copy.wait()
        onward.start()
    for copy in stores:
        copy.wait()
    for _, onward in pairs:
        onward.wait()


def tail(fin, in_grad, act, final, totals):
    width = fin.shape[-1]
    flat = fin.reshape(-1, width)
    rows = in_grad.shape[0]
    hbm = pl.BlockSpec(memory_space=pl.ANY)
    vmem = pl.BlockSpec(memory_space=pltpu.VMEM)
    dma = pltpu.SemaphoreType.DMA
    line = jax.ShapeDtypeStruct((1, width), F32)
    return pl.pallas_call(
        tail_kernel,
        out_shape=(
            jax.ShapeDtypeStruct(flat.shape, F32),
            jax.ShapeDtypeStruct(in_grad.shape, F32),
            jax.ShapeDtypeStruct(act.shape, BF16),
            jax.ShapeDtypeStruct(final.shape, F32),
        ) + (line,) * 6,
        in_specs=[hbm] * 3 + [vmem] * 2,
        out_specs=(hbm,) * 3 + (vmem,) * 7,
        scratch_shapes=[
            pltpu.VMEM(flat.shape, BF16), pltpu.VMEM(flat.shape, F32),
            pltpu.VMEM(in_grad.shape, F32), pltpu.VMEM(act.shape, BF16),
            dma((TAIL,)), dma((TAIL,)), dma((2, rows)), dma((2, rows)),
        ],
        compiler_params=pltpu.CompilerParams(vmem_limit_bytes=VMEM_BYTES),
        name="tail",
    )(flat, in_grad, act, final, totals)


def body(
    tokens, ln_gain, ln_bias, weights, mix_forget, mix_reset, bias_forget, bias_reset, state_bank, selector, resets, cotangent
):
    fin, in_grad, act, _, final, totals = layer(
        tokens, weights, cotangent, ln_gain[None], ln_bias[None], mix_forget[None], mix_reset[None], bias_forget[None],
        bias_reset[None], state_bank, selector, resets,
    )
    wide, in_grad, act, final, *sums = tail(fin, in_grad, act, final, totals)
    sums = [v[0] for v in sums]
    return act, final, in_grad, wide.reshape(weights.shape), sums[4], sums[5], sums[0], sums[1], sums[2], sums[3]


def solution(mesh):
    placed = (
        P(None, "tm", "chan"), P(), P(), P(None, None, "chan"), P("chan"), P("chan"), P("chan"), P("chan"),
        P(None, "chan"), P(), P(), P(None, "tm", "chan"),
    )
    return jax.shard_map(
        body,
        mesh=mesh,
        in_specs=placed,
        out_specs=(
            P(None, "tm", "chan"), P(None, "chan"), P(None, "tm", "chan"), P(None, None, "chan"),
            P("chan"), P("chan"), P("chan"), P("chan"), P("chan"), P("chan"),
        ),
        check_vma=False,
    )
```

```python
import jax
import jax.numpy as jnp
from jax import lax
from jax.experimental import pallas as pl
from jax.experimental.pallas import tpu as pltpu
from jax.sharding import PartitionSpec as P

EPSILON = 1e-05
CHUNK = 32
BLOCK = 16
LANE = 128
UNIT = 256
LAG = 2
PAIR = 80
LINE = 48
SENDS = 4
VMEM_BYTES = 63 << 20
TAIL = 4
LATER = 4
FIRST = 8
MESH = pl.DeviceIdType.MESH
F32 = jnp.float32
BF16 = jnp.bfloat16


def sigmoid(v):
    return 1.0 / (1.0 + jnp.exp(-v))


def swapped(v, outer, inner):
    return jnp.swapaxes(v.reshape(outer, inner, v.shape[-1]), 0, 1).reshape(outer * inner, v.shape[-1])


def both(*conditions):
    out = conditions[0]
    for c in conditions[1:]:
        out = jnp.logical_and(out, c)
    return out


def ring_of(tm_count):
    return 14 if tm_count <= 8 else 3


def layer_kernel(
    tokens, weights, cotangent, gain, shift, mix_f, mix_r, bias_f, bias_r, bank, selector, resets,
    fin, in_grad, act, low_t, final, totals,
    raw, rx, low, low_t_buf, w_buf, cand, forget, gate, masked, own_tok, cot_raw, cot, mean, inv, keep_mask, grad_buf,
    act_buf, side, terms, out_buf, row_rx, more, sum_rx, mean_s, inv_s, part_s, entry, near, far, flow, reset_rows,
    x_send, x_recv, s_send, s_recv, d_send, d_recv, own_sem, w_sem, cot_sem, act_sem, tr_sem, low_sem,
    near_send, near_recv, far_send, far_recv, last_send, last_recv, ready_sem, out_sem, loc_sem, pair_send, red_send,
    bc_send, bc_recv, swap_send, give_send, give_recv, rx_recv, sib_send, sib_recv, acr_send, acr_recv, row_send,
    row_recv, sum_send, sum_recv,
):
    rows, steps, width = tokens.shape
    full = gain.shape[-1]
    tm_count, tm = lax.axis_size("tm"), lax.axis_index("tm")
    chan_count, chan = lax.axis_size("chan"), lax.axis_index("chan")
    sibling = chan + 1 - 2 * lax.rem(chan, 2)
    across = lax.rem(chan + 2, 4)
    chunks = steps // CHUNK
    span = CHUNK * rows
    part = BLOCK * rows
    tiles = width // LANE
    blocks = CHUNK // BLOCK
    units = 3 * full // UNIT
    per_gate = full // UNIT

    def remote(src, dst, send, recv, target):
        return pltpu.make_async_remote_copy(src, dst, send, recv, device_id=target, device_id_type=MESH)

    def lanes(j):
        return slice(j * LANE, (j + 1) * LANE)

    def mine(ref, j):
        return ref[0:1, pl.ds(pl.multiple_of(chan * width + j * LANE, LANE), LANE)]

    def hat(at, j):
        return (own_tok[at, lanes(j)].astype(F32) - mean[at, :]) * inv[at, :]

    def normed(at, j):
        return hat(at, j) * mine(gain, j) + mine(shift, j)

    def rows_of(ch):
        return pl.ds(pl.multiple_of(ch * span, span), span)

    def piece(ch):
        return tokens.at[:, pl.ds(pl.multiple_of(ch * CHUNK, CHUNK), CHUNK), :]

    def raw_at(ch, block):
        return raw.at[pl.ds(pl.multiple_of((ch * chan_count + block) * span, span), span)].reshape(rows, CHUNK, width)

    def own_copy(ch):
        return pltpu.make_async_copy(piece(ch), raw_at(ch, chan), own_sem.at[ch])

    def x_copy(ch):
        return remote(piece(ch), raw_at(ch, chan), x_send.at[ch], x_recv.at[ch], (tm, across))

    def s_copy(ch):
        return remote(piece(ch), raw_at(ch, chan), s_send.at[ch], s_recv.at[ch], (tm, sibling))

    def d_copy(ch):
        return remote(raw_at(ch, across), raw_at(ch, across), d_send.at[ch], d_recv.at[ch], (tm, sibling))

    def cot_copy(ch):
        at = pl.ds(pl.multiple_of(ch * CHUNK, CHUNK), CHUNK)
        return pltpu.make_async_copy(cotangent.at[:, at, :], cot_raw.at[lax.rem(ch, 2)], cot_sem.at[lax.rem(ch, 2)])

    def act_copy(ch):
        at = pl.ds(pl.multiple_of(ch * CHUNK, CHUNK), CHUNK)
        return pltpu.make_async_copy(act_buf.at[lax.rem(ch, 2)], act.at[:, at, :], act_sem.at[lax.rem(ch, 2)])

    def tr_copy(ch):
        return pltpu.make_async_copy(low_t_buf, low_t.at[:, rows_of(ch)], tr_sem)

    def low_copy(u):
        at = pl.ds(pl.multiple_of(lax.rem(u, per_gate) * UNIT, UNIT), UNIT)
        return pltpu.make_async_copy(low_t.at[at], low.at[lax.rem(u, 2)], low_sem.at[lax.rem(u, 2)])

    w_copies = [pltpu.make_async_copy(weights.at[k], w_buf.at[k], w_sem.at[k]) for k in range(3)]

    barrier = pltpu.get_barrier_semaphore()
    for d in range(1, 4):
        pl.semaphore_signal(barrier, inc=1, device_id=(tm, lax.rem(chan + d, 4)), device_id_type=MESH)

    def greet(d, carry):
        pl.semaphore_signal(barrier, inc=1, device_id=(lax.rem(tm + d, tm_count), chan), device_id_type=MESH)
        return carry

    lax.fori_loop(1, tm_count, greet, 0)
    own_copy(0).start()
    own_copy(1).start()
    cot_copy(0).start()
    for copy in w_copies:
        copy.start()
    pl.semaphore_wait(barrier, tm_count + 2)
    for ch in range(2):
        x_copy(ch).start()
        s_copy(ch).start()

    count = resets.shape[1]
    for j in range(count):
        reset_rows[j] = jnp.broadcast_to(resets[:, j : j + 1], (rows, LANE))

    def mark(t, carry):
        at = tm * steps + t

        def compare(j, hit):
            return jnp.maximum(hit, jnp.where(reset_rows[j] == at, 1.0, 0.0))

        hit = lax.fori_loop(0, count, compare, jnp.zeros((rows, LANE), F32), unroll=16)
        keep_mask[pl.ds(pl.multiple_of(t * rows, rows), rows), :] = 1.0 - hit
        return carry

    lax.fori_loop(0, steps, mark, 0)
    for r in range(rows):
        entry[r : r + 1, :] = bank[pl.ds(selector[r], 1), :]

    def flip(ch):
        @pl.when(ch >= 1)
        def _():
            tr_copy(ch - 1).wait()

        def one(j, carry):
            cols = pl.ds(pl.multiple_of(j * 256, 256), 256)
            low_t_buf[cols, :] = jnp.transpose(low[lax.rem(ch, 2), :, cols])
            return carry

        lax.fori_loop(0, full // 256, one, 0, unroll=2)
        tr_copy(ch).start()

    def gather_step(ch, carry):
        a_run, b_run = carry

        @pl.when(ch + 2 < chunks)
        def _():
            own_copy(ch + 2).start()
            x_copy(ch + 2).start()
            s_copy(ch + 2).start()

        @pl.when(ch + 1 < chunks)
        def _():
            cot_copy(ch + 1).start()

        base = pl.multiple_of(ch * span, span)
        slot = lax.rem(ch, 2)

        x_copy(ch).wait_recv()
        d_copy(ch).start()
        cot_copy(ch).wait()
        for h in range(blocks):
            for j in range(tiles):
                v = cot_raw[slot, :, h * BLOCK : (h + 1) * BLOCK, lanes(j)].astype(F32).reshape(part, LANE)
                cot[pl.ds(pl.multiple_of(base + h * part, part), part), lanes(j)] = swapped(v, rows, BLOCK).astype(BF16)
        pl.when(ch >= 1)(lambda: flip(ch - 1))
        own_copy(ch).wait()
        s_copy(ch).wait_recv()
        d_copy(ch).wait_recv()

        first = pl.multiple_of(ch * chan_count * span, span)

        def tokens_at(block, r, t0, cols):
            at = pl.multiple_of(first + block * span + r * CHUNK + t0, BLOCK)
            return raw[pl.ds(at, BLOCK), cols].astype(F32)

        def each(i, turn):
            r, h = i // blocks, lax.rem(i, blocks)
            totals = [jnp.zeros((BLOCK, LANE), F32) for _ in range(chan_count)]
            for j in range(tiles):
                for b in range(chan_count):
                    totals[b] = totals[b] + turn(tokens_at(b, r, h * BLOCK, lanes(j)))
            while len(totals) > 1:
                totals = [a + b for a, b in zip(totals[::2], totals[1::2])]
            part_s[h, r] = totals[0]

        def sum_rows(i, carry):
            each(i, lambda v: v)
            return carry

        lax.fori_loop(0, rows * blocks, sum_rows, 0, unroll=2)
        mean_s[...] = jnp.broadcast_to(jnp.sum(part_s[...], axis=-1, keepdims=True) * (1.0 / full), mean_s.shape)

        def square_rows(i, carry):
            r, h = i // blocks, lax.rem(i, blocks)
            m = mean_s[h, r]
            each(i, lambda v: (v - m) * (v - m))
            return carry

        lax.fori_loop(0, rows * blocks, square_rows, 0, unroll=2)
        var = jnp.sum(part_s[...], axis=-1, keepdims=True) * (1.0 / full)
        inv_s[...] = jnp.broadcast_to(lax.rsqrt(var + EPSILON), inv_s.shape)

        for h in range(blocks):
            mean_h = mean_s[h].reshape(part, LANE)
            inv_h = inv_s[h].reshape(part, LANE)

            def normalize(j, carry, h=h, mean_h=mean_h, inv_h=inv_h):
                cols = pl.ds(pl.multiple_of(j * LANE, LANE), LANE)
                inner = pl.ds(pl.multiple_of(lax.rem(j, tiles) * LANE, LANE), LANE)
                v = jnp.concatenate([tokens_at(j // tiles, r, h * BLOCK, inner) for r in range(rows)], axis=0)
                v = (v - mean_h) * inv_h * gain[0:1, cols] + shift[0:1, cols]
                low[slot, h * part : (h + 1) * part, cols] = swapped(v, rows, BLOCK).astype(BF16)
                return carry

            lax.fori_loop(0, full // LANE, normalize, 0, unroll=2)
            at = pl.ds(pl.multiple_of(base + h * part, part), part)
            mean[at, :] = swapped(mean_h, rows, BLOCK)
            inv[at, :] = swapped(inv_h, rows, BLOCK)
            for j in range(tiles):
                v = jnp.concatenate([tokens_at(chan, r, h * BLOCK, lanes(j)) for r in range(rows)], axis=0)
                own_tok[at, lanes(j)] = swapped(v, rows, BLOCK).astype(BF16)

        at = pl.ds(base, span)

        @pl.when(ch == 0)
        def _():
            for copy in w_copies:
                copy.wait()

        cand[at, :] = jnp.dot(low[slot], w_buf[0], preferred_element_type=F32)
        forget[at, :] = jnp.dot(low[slot], w_buf[1], preferred_element_type=F32)
        gate[at, :] = jnp.dot(low[slot], w_buf[2], preferred_element_type=F32)

        def gates(b, carry):
            a_list, b_list = list(carry[0]), list(carry[1])
            at = pl.ds(pl.multiple_of(base + b * part, part), part)
            mask = keep_mask[at, :]
            for j in range(tiles):
                cols = lanes(j)
                nrm = normed(at, j)
                f = sigmoid(forget[at, cols] + mix_f[0:1, cols] * nrm + bias_f[0:1, cols])
                o = sigmoid(gate[at, cols] + mix_r[0:1, cols] * nrm + bias_r[0:1, cols])
                forget[at, cols] = f
                gate[at, cols] = o
                inject = (1.0 - f) * cand[at, cols]
                keep = f * mask
                for t in range(BLOCK):
                    now = slice(t * rows, (t + 1) * rows)
                    a_list[j] = a_list[j] * keep[now]
                    b_list[j] = b_list[j] * keep[now] + inject[now]
            return tuple(a_list), tuple(b_list)

        return lax.fori_loop(0, blocks, gates, (a_run, b_run))

    ones = tuple(jnp.ones((rows, LANE), F32) for _ in range(tiles))
    zeros = tuple(jnp.zeros((rows, LANE), F32) for _ in range(tiles))
    a_run, b_run = lax.fori_loop(0, chunks, gather_step, (ones, zeros))

    spans = jnp.where(reset_rows[0] >= tm_count * steps, 1.0, 0.0)
    last_tm = tm_count - 1

    def spanning(v):
        return jnp.sum(v * spans, axis=0, keepdims=True)

    def near_copy(way, target):
        return remote(near.at[way, 0], near.at[way, 1], near_send.at[way], near_recv.at[way], (target, chan))

    def far_copy(way, source, target):
        return remote(
            far.at[way, source], far.at[way, source], far_send.at[way, target], far_recv.at[way, source], (target, chan)
        )

    def last_copy(target):
        return remote(near.at[0, 0], near.at[0, 2], last_send.at[target], last_recv, (target, chan))

    def sum_copy(source, target):
        return remote(sum_rx.at[source], sum_rx.at[source], sum_send.at[target], sum_recv.at[source], (target, chan))

    def peers(act_on):
        def one(d, carry):
            act_on(lax.rem(tm + d, tm_count))
            return carry

        lax.fori_loop(1, tm_count, one, 0)

    for j in range(tiles):
        near[0, 0, :, lanes(j)] = b_run[j]
        far[0, tm, j : j + 1, :] = spanning(a_run[j])
        far[0, tm, tiles + j : tiles + j + 1, :] = spanning(b_run[j])
    pl.when(tm < last_tm)(lambda: near_copy(0, tm + 1).start())
    peers(lambda p: far_copy(0, tm, p).start())
    pl.when(tm == last_tm)(lambda: peers(lambda p: last_copy(p).start()))
    flip(chunks - 1)
    peers(lambda p: far_copy(0, p, tm).wait_recv())
    pl.when(tm > 0)(lambda: near_copy(0, tm).wait_recv())

    def carry_on(d, carry):
        state, here = carry
        here = jnp.where(d == tm, state, here)
        return far[0, d, 0:tiles, :] * state + far[0, d, tiles : 2 * tiles, :], here

    lead = jnp.concatenate([spanning(entry[:, lanes(j)]) for j in range(tiles)], axis=0)
    last, here = lax.fori_loop(0, tm_count, carry_on, (lead, lead))
    states = []
    for j in range(tiles):
        row = jnp.broadcast_to(here[j : j + 1], (rows, LANE))
        others = jnp.where(tm == 0, entry[:, lanes(j)], near[0, 1, :, lanes(j)])
        states.append(jnp.where(spans > 0, row, others))
    tr_copy(chunks - 1).wait()
    low_copy(0).start()

    def forward(b, states):
        states = list(states)
        at = pl.ds(pl.multiple_of(b * part, part), part)
        mask = keep_mask[at, :]
        for j in range(tiles):
            cols = lanes(j)
            f = forget[at, cols]
            inject = (1.0 - f) * cand[at, cols]
            before, after = [], []
            c = states[j]
            for t in range(BLOCK):
                now = slice(t * rows, (t + 1) * rows)
                c = c * mask[now]
                before.append(c)
                c = f[now] * c + inject[now]
                after.append(c)
            states[j] = c
            masked[at, cols] = jnp.concatenate(before, axis=0)
            th = jnp.tanh(jnp.concatenate(after, axis=0))
            o = gate[at, cols]
            gate_grad = cot[at, cols].astype(F32) * (th - own_tok[at, cols].astype(F32))
            grad_buf[2, at, cols] = (gate_grad * o * (1.0 - o)).astype(BF16)
        return tuple(states)

    lax.fori_loop(0, steps // BLOCK, forward, tuple(states))

    def start_later():
        flow[0] = jnp.ones((rows, width), F32)
        for i in range(1, 4):
            flow[i] = jnp.zeros((rows, width), F32)

    def later(b, carry):
        ch, h = b // blocks, lax.rem(b, blocks)
        slot = lax.rem(ch, 2)

        @pl.when(both(h == 0, ch >= 2))
        def _():
            act_copy(ch - 2).wait()

        at = pl.ds(pl.multiple_of(b * part, part), part)
        t0 = pl.multiple_of(h * BLOCK, BLOCK)
        mask = keep_mask[at, :]
        for j in range(tiles):
            cols = lanes(j)
            f = forget[at, cols]
            th = jnp.tanh(f * masked[at, cols] + (1.0 - f) * cand[at, cols])
            o = gate[at, cols]
            x = own_tok[at, cols].astype(F32)
            ct = cot[at, cols].astype(F32)
            rest = 1.0 - o
            out = swapped(o * th + rest * x, BLOCK, rows).astype(BF16)
            act_buf[slot, :, pl.ds(t0, BLOCK), cols] = out.reshape(rows, BLOCK, LANE)
            reset_pre = ct * (th - x) * o * rest
            direct = ct * o * (1.0 - th * th)
            side[at, cols] = (ct * rest).astype(BF16)
            gate[at, cols] = direct
            keep = f * mask
            run, total = flow[0, :, cols], flow[1, :, cols]
            for t in range(BLOCK):
                now = slice(t * rows, (t + 1) * rows)
                run = run * keep[now]
                total = total + run * direct[now]
            flow[0, :, cols], flow[1, :, cols] = run, total
            for i, v in enumerate((reset_pre * normed(at, j), reset_pre)):
                flow[2 + i, :, cols] = flow[2 + i, :, cols] + jnp.sum(v.reshape(BLOCK, rows, LANE), axis=0)

        @pl.when(h == blocks - 1)
        def _():
            act_copy(ch).start()

        return carry

    def end_later():
        near[1, 0] = flow[1]
        for j in range(tiles):
            far[1, tm, j : j + 1, :] = spanning(flow[1, :, lanes(j)])
        pl.when(tm > 0)(lambda: near_copy(1, tm - 1).start())
        peers(lambda p: far_copy(1, tm, p).start())
        for target in (sibling, across):
            pl.semaphore_signal(ready_sem, inc=1, device_id=(tm, target), device_id_type=MESH)
        for i in range(2):
            sum_rx[tm, 2 * i + 1 : 2 * i + 2, :] = jnp.sum(flow[2 + i], axis=0, keepdims=True)
        sum_rx[tm, 6:8, :] = jnp.zeros((2, width), F32)
        more[...] = jnp.zeros_like(more)

    def sent_on(ch, carry):
        d_copy(ch).wait_send()
        return carry

    lax.fori_loop(0, chunks, sent_on, 0)

    n = tm_count // 2
    o, y = tm // 2, lax.rem(tm, 2)
    partner = (o * 2 + 1 - y, chan)
    left = ((o - 1) * 2 + y, chan)
    right = ((o + 1) * 2 + y, chan)
    ring = ring_of(tm_count)
    ends, middle = (0, n - 1), (n // 2 - 1, n // 2)
    lines = [(0, middle[0] + y, n // 2, 1, None)]
    for l in (1, 2):
        if n == 4:
            lines += [(l, ends[l - 1], n - 1, 0, 0), (l, middle[l - 1], n // 2, 0, 1)]
        else:
            lines += [(l, middle[l - 1], n // 2, 0, None)]
    give_stage = 2 * (n // 2) + 2
    depth = LAG * max([give_stage] + [first + reach + (l > 0) + reach for l, c, reach, first, parity in lines])
    space = -(-depth // ring)

    def stage(s, number, parity=None):
        v = s - LAG * number
        u = v if space == 1 else v // space
        go = both(v >= 0, u < units)
        if space > 1:
            go = both(go, lax.rem(v, space) == 0)
        return u, go if parity is None else both(go, lax.rem(u, 2) == parity)

    def gate_of(u):
        return lax.rem(u // per_gate + 2, 3)

    def piece_of(l, mate=False):
        if l == 0:
            return (1 - y if mate else y) * PAIR, PAIR
        return 2 * PAIR + (l - 1) * LINE, LINE

    def wg_rows(l, u, mate=False):
        start, size = piece_of(l, mate)
        return pl.ds(pl.multiple_of(u * UNIT + start, 16), size)

    def fin_at(l, u):
        start, size = piece_of(l)
        return fin.at[pl.ds(pl.multiple_of((gate_of(u) * per_gate + lax.rem(u, per_gate)) * UNIT + start, 16), size)]

    def rx_rows(u, place, l):
        start = place * PAIR if l == 0 else 3 * PAIR + (place - 3) * LINE
        size = PAIR if l == 0 else LINE
        return pl.ds(pl.multiple_of(lax.rem(u, ring) * (3 * PAIR + 4 * LINE) + start, 16), size)

    def arrival(l, c, column, way, u):
        if l == 0:
            return 1 + way
        if l == 1:
            other = 6
        elif n == 4:
            other = jnp.where(column == jnp.where(lax.rem(u, 2) == 0, ends[0], middle[0]), 6, 3)
        else:
            other = jnp.where(column == middle[0], 6, 3)
        return jnp.where(column == c, 3 + way, other)

    def launch(make, u):
        @pl.when(u >= SENDS)
        def _():
            make(u - SENDS).wait_send()

        make(u).start()

    def to_rx(src, u, place, l, sem, target):
        return remote(src, rx.at[rx_rows(u, place, l)], sem, rx_recv.at[lax.rem(u, ring), place], target)

    def pair_copy(u):
        return to_rx(raw.at[wg_rows(0, u, True)], u, 0, 0, pair_send.at[lax.rem(u, SENDS)], partner)

    def red_copy(l, c, u, to_right):
        way, column = (0, o + 1) if to_right else (1, o - 1)
        return to_rx(
            raw.at[wg_rows(l, u)], u, arrival(l, c, column, way, u), l, red_send.at[l, lax.rem(u, SENDS)],
            right if to_right else left,
        )

    def red_wait(l, c, u, way):
        place = arrival(l, c, o, way, u)
        at = rx_rows(u, place, l)
        to_rx(rx.at[at], u, place, l, red_send.at[l, 0], partner).wait_recv()
        return rx[at].astype(F32)

    def bc_copy(l, u, to_right, src):
        return remote(
            src, fin_at(l, u), bc_send.at[l, lax.rem(u, SENDS), 1 if to_right else 0], bc_recv.at[l, lax.rem(u, ring)],
            right if to_right else left,
        )

    def swap_copy(l, u):
        return to_rx(raw.at[wg_rows(l, u)], u, 5, l, swap_send.at[lax.rem(u, SENDS)], partner)

    def give_copy(u, src):
        return remote(src, fin_at(0, u), give_send.at[lax.rem(u, SENDS)], give_recv.at[lax.rem(u, ring)], partner)

    def local_copy(l, u):
        return pltpu.make_async_copy(raw.at[wg_rows(l, u)], fin_at(l, u), loc_sem.at[l, lax.rem(u, SENDS)])

    def add_to(l, u, *others):
        at = wg_rows(l, u)
        total = raw[at].astype(F32)
        for v in others:
            total = total + v
        raw[at] = total.astype(BF16)

    def red_start(l, c, u):
        pl.when(o < c)(lambda: launch(lambda v: red_copy(l, c, v, True), u))
        pl.when(o > c)(lambda: launch(lambda v: red_copy(l, c, v, False), u))

    def publish(l, u):
        @pl.when(u >= SENDS)
        def _():
            local_copy(l, u - SENDS).wait()

        local_copy(l, u).start()
        pl.when(o > 0)(lambda: launch(lambda v: bc_copy(l, v, False, raw.at[wg_rows(l, v)]), u))
        pl.when(o < n - 1)(lambda: launch(lambda v: bc_copy(l, v, True, raw.at[wg_rows(l, v)]), u))
        if l == 0:
            launch(lambda v: give_copy(v, raw.at[wg_rows(0, v)]), u)

    def block_cols(c):
        return pl.ds(pl.multiple_of(c * width, width), width)

    def sib_rows(ch, q):
        return pl.ds(pl.multiple_of(units * UNIT + (lax.rem(ch, 4) * 2 + q) * span, span), span)

    def sib_copy(ch, q):
        slot = lax.rem(ch, 2)
        cols = sibling if q == 0 else lax.rem(sibling + 2, 4)
        return remote(
            terms.at[slot, cols], raw.at[sib_rows(ch, q)], sib_send.at[q], sib_recv.at[lax.rem(ch, 4), q], (tm, sibling)
        )

    def acr_copy(ch):
        return remote(
            terms.at[lax.rem(ch, 2), across], cot.at[rows_of(ch)], acr_send.at[lax.rem(ch, 2)], acr_recv.at[ch], (tm, across)
        )

    def row_copy(ch, source, d):
        return remote(
            row_rx.at[ch, source], row_rx.at[ch, source], row_send.at[lax.rem(ch, 4), d - 1],
            row_recv.at[lax.rem(ch, 4), source], (tm, lax.rem(chan + d, 4)),
        )

    def out_copy(ch):
        at = pl.ds(pl.multiple_of(ch * CHUNK, CHUNK), CHUNK)
        return pltpu.make_async_copy(out_buf.at[lax.rem(ch, 2)], in_grad.at[:, at, :], out_sem.at[lax.rem(ch, 2)])

    def project(ch):
        at = rows_of(ch)
        slot = lax.rem(ch, 2)

        @pl.when(ch == 0)
        def _():
            pl.semaphore_wait(ready_sem, 2)

        @pl.when(ch >= 2)
        def _():
            acr_copy(ch - 2).wait_send()

        for b in range(chan_count):
            total = jnp.zeros((span, width), F32)
            for k in range(3):
                total = total + lax.dot_general(
                    grad_buf[k, at, :], w_buf[k, b * width : (b + 1) * width, :], (((1,), (1,)), ((), ())),
                    preferred_element_type=F32,
                )
            terms[slot, b] = total.astype(BF16)
        sib_copy(ch, 0).start()
        sib_copy(ch, 1).start()

    def chip_sum(ch):
        slot = lax.rem(ch, 2)
        for q in range(2):
            sib_copy(ch, q).wait_recv()
        there = terms[slot, across].astype(F32) + raw[sib_rows(ch, 1)].astype(F32)
        terms[slot, across] = there.astype(BF16)
        acr_copy(ch).start()
        here = terms[slot, chan].astype(F32) + raw[sib_rows(ch, 0)].astype(F32)
        cand[rows_of(ch), :] = here
        for q in range(2):
            sib_copy(ch, q).wait_send()

    def full_sum(ch):
        acr_copy(ch).wait_recv()
        at = rows_of(ch)
        total = jnp.zeros((8, span), F32)
        pick = lax.broadcasted_iota(jnp.int32, (8, LANE), 0)
        for j in range(tiles):
            cols = lanes(j)
            own = grad_buf[1, at, cols].astype(F32) * mix_f[0:1, cols] + grad_buf[2, at, cols].astype(F32) * mix_r[0:1, cols]
            g = cand[at, cols] + cot[at, cols].astype(F32) + own
            cand[at, cols] = g
            weighted = g * hat(at, j)
            for i, v in enumerate((weighted, g)):
                more[i, :, cols] = more[i, :, cols] + jnp.sum(v.reshape(CHUNK, rows, LANE), axis=0)
            for i, v in enumerate((g * mine(gain, j), weighted * mine(gain, j))):
                lead = jnp.where(pick == i, 1.0, 0.0).astype(BF16)
                high = v.astype(BF16)
                low_part = (v - high.astype(F32)).astype(BF16)
                for p in (high, low_part):
                    total = total + lax.dot_general(lead, p, (((1,), (1,)), ((), ())), preferred_element_type=F32)
        row_rx[ch, chan] = total
        for d in range(1, 4):
            pl.when(ch >= 4)(lambda d=d: row_copy(ch - 4, chan, d).wait_send())
            row_copy(ch, chan, d).start()

    def finish(ch):
        for d in range(1, 4):
            row_copy(ch, lax.rem(chan + d, 4), d).wait_recv()

        @pl.when(ch >= 2)
        def _():
            out_copy(ch - 2).wait()

        at = rows_of(ch)
        total = (row_rx[ch, 0] + row_rx[ch, 1] + row_rx[ch, 2] + row_rx[ch, 3]) * (1.0 / full)
        columns = jnp.transpose(total)
        first = jnp.broadcast_to(columns[:, 0:1], (span, LANE))
        second = jnp.broadcast_to(columns[:, 1:2], (span, LANE))
        for j in range(tiles):
            cols = lanes(j)
            g = cand[at, cols] * mine(gain, j)
            v = inv[at, :] * (g - first - hat(at, j) * second) + side[at, cols].astype(F32)
            out_buf[lax.rem(ch, 2), :, :, cols] = swapped(v, CHUNK, rows).reshape(rows, CHUNK, LANE)
        out_copy(ch).start()

    def share_sums():
        for i in range(2):
            sum_rx[tm, 2 * i : 2 * i + 1, :] = jnp.sum(flow[1 + i], axis=0, keepdims=True)
            sum_rx[tm, 4 + i : 5 + i, :] = jnp.sum(more[i], axis=0, keepdims=True)
        peers(lambda p: sum_copy(tm, p).start())

    def start_backward():
        peers(lambda p: far_copy(1, p, tm).wait_recv())
        pl.when(tm < last_tm)(lambda: near_copy(1, tm).wait_recv())

        def carry_back(i, v):
            d = tm_count - 1 - i
            return jnp.where(d > tm, far[0, d, 0:tiles, :] * v + far[1, d, 0:tiles, :], v)

        inflow = lax.fori_loop(0, tm_count, carry_back, jnp.zeros((tiles, LANE), F32))
        for j in range(tiles):
            row = jnp.broadcast_to(inflow[j : j + 1], (rows, LANE))
            others = jnp.where(tm == last_tm, 0.0, near[1, 1, :, lanes(j)])
            flow[0, :, lanes(j)] = jnp.where(spans > 0, row, others)
        flow[1] = jnp.zeros((rows, width), F32)
        flow[2] = jnp.zeros((rows, width), F32)

    def backward(i, carry):
        b = steps // BLOCK - 1 - i
        at = pl.ds(pl.multiple_of(b * part, part), part)
        mask = keep_mask[at, :]
        for j in range(tiles):
            cols = lanes(j)
            f = forget[at, cols]
            keep = f * mask
            direct = gate[at, cols]
            g = flow[0, :, cols]
            adjoint = [None] * BLOCK
            for t in reversed(range(BLOCK)):
                now = slice(t * rows, (t + 1) * rows)
                adjoint[t] = direct[now] + g
                g = keep[now] * adjoint[t]
            flow[0, :, cols] = g
            cand_grad = jnp.concatenate(adjoint, axis=0) * (1.0 - f)
            forget_pre = cand_grad * (masked[at, cols] - cand[at, cols]) * f
            grad_buf[0, at, cols] = cand_grad.astype(BF16)
            grad_buf[1, at, cols] = forget_pre.astype(BF16)
            for i, v in enumerate((forget_pre * normed(at, j), forget_pre)):
                flow[1 + i, :, cols] = flow[1 + i, :, cols] + jnp.sum(v.reshape(BLOCK, rows, LANE), axis=0)
        return carry

    def slot_step(s, carry):
        u, go = stage(s, give_stage)
        pl.when(go)(lambda: give_copy(u, raw.at[wg_rows(0, u)]).wait_recv())

        for l, c, reach, first, parity in lines:
            late = first + reach + (1 if l else 0)
            u, go = stage(s, late + jnp.abs(o - c), parity)

            @pl.when(both(o != c, go))
            def _(l=l, c=c, u=u):
                bc_copy(l, u, True, fin_at(l, u)).wait_recv()
                pl.when(both(o < c, o > 0))(lambda: launch(lambda v: bc_copy(l, v, False, fin_at(l, v)), u))
                pl.when(both(o > c, o < n - 1))(lambda: launch(lambda v: bc_copy(l, v, True, fin_at(l, v)), u))
                if l == 0:
                    launch(lambda v: give_copy(v, fin_at(0, v)), u)

        for l, c, reach, first, parity in lines[1:]:
            u, go = stage(s, reach + 1, parity)

            @pl.when(both(o == c, go))
            def _(l=l, u=u):
                swap_copy(l, u).wait()
                add_to(l, u, rx[rx_rows(u, 5, l)].astype(F32))
                publish(l, u)

        for l, c, reach, first, parity in lines:
            u, go = stage(s, first + reach, parity)

            @pl.when(both(o == c, go))
            def _(l=l, c=c, u=u):
                if l == 0 and n > 2:
                    add_to(l, u, red_wait(l, c, u, 0), red_wait(l, c, u, 1))
                elif l > 0 and 0 < c < n - 1:
                    add_to(l, u, red_wait(l, c, u, 0), red_wait(l, c, u, 1))
                else:
                    pl.when(o > 0)(lambda: add_to(l, u, red_wait(l, c, u, 0)))
                    pl.when(o < n - 1)(lambda: add_to(l, u, red_wait(l, c, u, 1)))
                if l == 0:
                    publish(l, u)
                else:
                    swap_copy(l, u).start()

        u0, go0 = stage(s, 0)

        @pl.when(go0)
        def _():
            pl.when(u0 + 1 < units)(lambda: low_copy(u0 + 1).start())
            low_copy(u0).wait()
            g = jnp.dot(low[lax.rem(u0, 2)], grad_buf[gate_of(u0)], preferred_element_type=F32)
            raw[pl.ds(pl.multiple_of(u0 * UNIT, UNIT), UNIT)] = g.astype(BF16)
            launch(pair_copy, u0)
            for l, c, reach, first, parity in lines[1:]:
                mine_now = jnp.logical_or(o == 0, o == n - 1)
                if parity is not None:
                    mine_now = both(mine_now, lax.rem(u0, 2) == parity)
                pl.when(mine_now)(lambda l=l, c=c: red_start(l, c, u0))

        for l, c, reach, first, parity in lines:
            u, go = stage(s, first + jnp.where(o < c, o, n - 1 - o), parity)

            @pl.when(both(o < c, o > 0, go))
            def _(l=l, c=c, u=u):
                add_to(l, u, red_wait(l, c, u, 0))
                launch(lambda v: red_copy(l, c, v, True), u)

            @pl.when(both(o > c, o < n - 1, go))
            def _(l=l, c=c, u=u):
                add_to(l, u, red_wait(l, c, u, 1))
                launch(lambda v: red_copy(l, c, v, False), u)

        u, go = stage(s, 1)

        @pl.when(go)
        def _():
            pair_copy(u).wait_recv()
            add_to(0, u, rx[rx_rows(u, 0, 0)].astype(F32))
            pl.when(jnp.logical_or(o == 0, o == n - 1))(lambda: red_start(0, lines[0][1], u))

        count = steps // BLOCK
        pl.when(s == 0)(start_later)
        share = -(-count // LATER)
        at = s * share

        @pl.when(s < LATER)
        def _():
            lax.fori_loop(at, jnp.minimum(at + share, count), later, 0)

        pl.when(s == LATER - 1)(end_later)
        pl.when(s == LATER + 1)(start_backward)
        share = -(-count // (FIRST - LATER - 1))
        at2 = (s - LATER - 1) * share

        @pl.when(both(s > LATER, s < FIRST))
        def _():
            lax.fori_loop(at2, jnp.minimum(at2 + share, count), backward, 0)

        for job, offset in ((finish, 5), (full_sum, 3), (chip_sum, 1), (project, 0)):
            at = s - FIRST - offset
            pl.when(both(at >= 0, lax.rem(at, 2) == 0, at // 2 < chunks))(lambda job=job, at=at: job(at // 2))
        pl.when(s == FIRST + 2 * chunks + 2)(share_sums)
        return carry

    slots = max((units - 1) * space + depth + 1, FIRST + 2 * chunks + 4)
    lax.fori_loop(0, slots, slot_step, 0)

    def close_unit(u, carry):
        give_copy(u, raw.at[wg_rows(0, u)]).wait_send()
        pair_copy(u).wait_send()
        for l, c, reach, first, parity in lines:

            @pl.when(True if parity is None else lax.rem(u, 2) == parity)
            def _(l=l, c=c):
                src = raw.at[wg_rows(l, u)]
                pl.when(o != c)(lambda: red_copy(l, c, u, True).wait_send())
                pl.when(o == c)(lambda: local_copy(l, u).wait())
                pl.when(both(o <= c, o > 0))(lambda: bc_copy(l, u, False, src).wait_send())
                pl.when(both(o >= c, o < n - 1))(lambda: bc_copy(l, u, True, src).wait_send())

        return carry

    lax.fori_loop(units - SENDS, units, close_unit, 0)

    def close_chunk(ch, carry):
        x_copy(ch).wait_send()
        s_copy(ch).wait_send()

        @pl.when(ch >= chunks - 4)
        def _():
            for d in range(1, 4):
                row_copy(ch, chan, d).wait_send()

        return carry

    lax.fori_loop(0, chunks, close_chunk, 0)
    for ch in (chunks - 2, chunks - 1):
        out_copy(ch).wait()
        act_copy(ch).wait()
        acr_copy(ch).wait_send()
    for way in range(2):
        peers(lambda p, way=way: far_copy(way, tm, p).wait_send())
    pl.when(tm < last_tm)(lambda: near_copy(0, tm).wait_send())
    pl.when(tm > 0)(lambda: near_copy(1, tm).wait_send())
    pl.when(tm == last_tm)(lambda: peers(lambda p: last_copy(p).wait_send()))
    pl.when(tm != last_tm)(lambda: last_copy(tm).wait_recv())
    for j in range(tiles):
        row = jnp.broadcast_to(last[j : j + 1], (rows, LANE))
        others = jnp.where(tm == last_tm, near[0, 0, :, lanes(j)], near[0, 2, :, lanes(j)])
        final[:, lanes(j)] = jnp.where(spans > 0, row, others)
    peers(lambda p: sum_copy(p, tm).wait_recv())
    peers(lambda p: sum_copy(tm, p).wait_send())
    totals[...] = lax.fori_loop(0, tm_count, lambda d, v: v + sum_rx[d], jnp.zeros(totals.shape, F32))


def layer(tokens, weights, cotangent, gain, shift, mix_f, mix_r, bias_f, bias_r, bank, selector, resets):
    rows, steps, width = tokens.shape
    full = gain.shape[-1]
    tm_count, chan_count = lax.axis_size("tm"), lax.axis_size("chan")
    chunks = steps // CHUNK
    span = CHUNK * rows
    count = steps * rows
    units = 3 * full // UNIT
    ring = ring_of(tm_count)
    hbm = pl.BlockSpec(memory_space=pl.ANY)
    vmem = pl.BlockSpec(memory_space=pltpu.VMEM)
    smem = pl.BlockSpec(memory_space=pltpu.SMEM)
    dma = pltpu.SemaphoreType.DMA
    stat = pltpu.VMEM((CHUNK // BLOCK, rows, BLOCK, LANE), F32)
    wide = pltpu.VMEM((count, width), F32)
    narrow = pltpu.VMEM((count, LANE), F32)
    short = pltpu.VMEM((count, width), BF16)
    return pl.pallas_call(
        layer_kernel,
        out_shape=(
            jax.ShapeDtypeStruct((units * UNIT, width), BF16),
            jax.ShapeDtypeStruct(tokens.shape, F32),
            jax.ShapeDtypeStruct(tokens.shape, BF16),
            jax.ShapeDtypeStruct((full, count), BF16),
            jax.ShapeDtypeStruct((rows, width), F32),
            jax.ShapeDtypeStruct((8, width), F32),
        ),
        in_specs=[hbm, hbm, hbm] + [vmem] * 7 + [smem, vmem],
        out_specs=(hbm, hbm, hbm, hbm, vmem, vmem),
        scratch_shapes=[
            pltpu.VMEM((chunks * chan_count * span, width), BF16),
            pltpu.VMEM((ring * (3 * PAIR + 4 * LINE), width), BF16),
            pltpu.VMEM((2, span, full), BF16),
            pltpu.VMEM((full, span), BF16),
            pltpu.VMEM((3, full, width), BF16),
            wide, wide, wide, wide,
            short,
            pltpu.VMEM((2, rows, CHUNK, width), BF16),
            short,
            narrow, narrow, narrow,
            pltpu.VMEM((3, count, width), BF16),
            pltpu.VMEM((2, rows, CHUNK, width), BF16),
            short,
            pltpu.VMEM((2, chan_count, span, width), BF16),
            pltpu.VMEM((2, rows, CHUNK, width), F32),
            pltpu.VMEM((chunks, 4, 8, span), F32),
            pltpu.VMEM((2, rows, width), F32),
            pltpu.VMEM((tm_count, 8, width), F32),
            stat, stat, stat,
            pltpu.VMEM((rows, width), F32),
            pltpu.VMEM((2, 3, rows, width), F32),
            pltpu.VMEM((2, tm_count, 8, LANE), F32),
            pltpu.VMEM((4, rows, width), F32),
            pltpu.VMEM((resets.shape[1], rows, LANE), jnp.int32),
            dma((chunks,)), dma((chunks,)), dma((chunks,)), dma((chunks,)), dma((chunks,)), dma((chunks,)), dma((chunks,)),
            dma((3,)), dma((2,)), dma((2,)), dma(()), dma((2,)),
            dma((2,)), dma((2,)), dma((2, tm_count)), dma((2, tm_count)), dma((tm_count,)), dma(()),
            pltpu.SemaphoreType.REGULAR,
            dma((2,)), dma((3, SENDS)), dma((SENDS,)), dma((3, SENDS)), dma((3, SENDS, 2)), dma((3, ring)), dma((SENDS,)),
            dma((SENDS,)), dma((ring,)), dma((ring, 7)), dma((2,)), dma((4, 2)), dma((2,)), dma((chunks,)),
            dma((4, 3)), dma((4, 4)), dma((tm_count,)), dma((tm_count,)),
        ],
        compiler_params=pltpu.CompilerParams(collective_id=0, has_side_effects=True, vmem_limit_bytes=VMEM_BYTES),
        name="whole",
    )(tokens, weights, cotangent, gain, shift, mix_f, mix_r, bias_f, bias_r, bank, selector, resets)


def tail_kernel(
    fin, in_grad, act, final, totals, wide_out, in_out, act_out, final_out, s0, s1, s2, s3, s4, s5,
    fin_buf, wide_buf, in_buf, act_buf, fin_sem, wide_sem, in_sem, act_sem,
):
    parts = fin_sem.shape[0]
    size = fin.shape[0] // parts

    def move(src, dst, sem, i, n):
        at = pl.ds(i * n, n)
        return pltpu.make_async_copy(src.at[at], dst.at[at], sem)

    loads = [move(fin, fin_buf, fin_sem.at[i], i, size) for i in range(parts)]
    stores = [move(wide_buf, wide_out, wide_sem.at[i], i, size) for i in range(parts)]
    pairs = []
    for src, buf, dst, sem in ((in_grad, in_buf, in_out, in_sem), (act, act_buf, act_out, act_sem)):
        n = sem.shape[1]
        some = src.shape[0] // n
        pairs += [(move(src, buf, sem.at[0, i], i, some), move(buf, dst, sem.at[1, i], i, some)) for i in range(n)]
    for i in range(max(parts, len(pairs))):
        if i < parts:
            loads[i].start()
        if i < len(pairs):
            pairs[i][0].start()
    final_out[...] = final[...]
    for i, ref in enumerate((s0, s1, s2, s3, s4, s5)):
        ref[...] = totals[i : i + 1, :]
    for i in range(max(parts, len(pairs))):
        if i < parts:
            loads[i].wait()

            def cast(j, carry, i=i):
                at = pl.ds(pl.multiple_of(i * size + j * 64, 64), 64)
                wide_buf[at] = fin_buf[at].astype(F32)
                return carry

            lax.fori_loop(0, size // 64, cast, 0, unroll=2)
            stores[i].start()
        if i < len(pairs):
            pairs[i][0].wait()
            pairs[i][1].start()
    for copy in stores:
        copy.wait()
    for _, onward in pairs:
        onward.wait()


def tail(fin, in_grad, act, final, totals):
    width = fin.shape[-1]
    flat = fin.reshape(-1, width)
    hbm = pl.BlockSpec(memory_space=pl.ANY)
    vmem = pl.BlockSpec(memory_space=pltpu.VMEM)
    dma = pltpu.SemaphoreType.DMA
    line = jax.ShapeDtypeStruct((1, width), F32)
    return pl.pallas_call(
        tail_kernel,
        out_shape=(
            jax.ShapeDtypeStruct(flat.shape, F32),
            jax.ShapeDtypeStruct(in_grad.shape, F32),
            jax.ShapeDtypeStruct(act.shape, BF16),
            jax.ShapeDtypeStruct(final.shape, F32),
        ) + (line,) * 6,
        in_specs=[hbm] * 3 + [vmem] * 2,
        out_specs=(hbm,) * 3 + (vmem,) * 7,
        scratch_shapes=[
            pltpu.VMEM(flat.shape, BF16), pltpu.VMEM(flat.shape, F32),
            pltpu.VMEM(in_grad.shape, F32), pltpu.VMEM(act.shape, BF16),
            dma((TAIL,)), dma((TAIL,)), dma((2, 4)), dma((2, 2)),
        ],
        compiler_params=pltpu.CompilerParams(vmem_limit_bytes=VMEM_BYTES),
        name="tail",
    )(flat, in_grad, act, final, totals)


def body(
    tokens, ln_gain, ln_bias, weights, mix_forget, mix_reset, bias_forget, bias_reset, state_bank, selector, resets, cotangent
):
    fin, in_grad, act, _, final, totals = layer(
        tokens, weights, cotangent, ln_gain[None], ln_bias[None], mix_forget[None], mix_reset[None], bias_forget[None],
        bias_reset[None], state_bank, selector, resets,
    )
    wide, in_grad, act, final, *sums = tail(fin, in_grad, act, final, totals)
    sums = [v[0] for v in sums]
    return act, final, in_grad, wide.reshape(weights.shape), sums[4], sums[5], sums[0], sums[1], sums[2], sums[3]


def solution(mesh):
    placed = (
        P(None, "tm", "chan"), P(), P(), P(None, None, "chan"), P("chan"), P("chan"), P("chan"), P("chan"),
        P(None, "chan"), P(), P(), P(None, "tm", "chan"),
    )
    return jax.shard_map(
        body,
        mesh=mesh,
        in_specs=placed,
        out_specs=(
            P(None, "tm", "chan"), P(None, "chan"), P(None, "tm", "chan"), P(None, None, "chan"),
            P("chan"), P("chan"), P("chan"), P("chan"), P("chan"), P("chan"),
        ),
        check_vma=False,
    )
```

```python
import jax
import jax.numpy as jnp
from jax import lax
from jax.experimental import pallas as pl
from jax.experimental.pallas import tpu as pltpu
from jax.sharding import PartitionSpec as P

EPSILON = 1e-05
CHUNK = 32
BLOCK = 16
LANE = 128
UNIT = 256
LAG = 2
PAIR = 80
LINE = 48
SENDS = 4
VMEM_BYTES = 63 << 20
TAIL = 4
LATER = 4
FIRST = 8
MESH = pl.DeviceIdType.MESH
F32 = jnp.float32
BF16 = jnp.bfloat16


def sigmoid(v):
    return 1.0 / (1.0 + jnp.exp(-v))


def swapped(v, outer, inner):
    return jnp.swapaxes(v.reshape(outer, inner, v.shape[-1]), 0, 1).reshape(outer * inner, v.shape[-1])


def both(*conditions):
    out = conditions[0]
    for c in conditions[1:]:
        out = jnp.logical_and(out, c)
    return out


def ring_of(tm_count):
    return 14 if tm_count <= 8 else 3


def layer_kernel(
    tokens, weights, cotangent, gain, shift, mix_f, mix_r, bias_f, bias_r, bank, selector, resets,
    fin, in_grad, act, low_all, final, totals,
    raw, rx, low, left_buf, w_buf, cand, forget, gate, masked, own_tok, cot_raw, cot, mean, inv, keep_mask, grad_buf,
    act_buf, side, terms, out_buf, row_rx, more, sum_rx, mean_s, inv_s, part_s, entry, near, far, flow, reset_rows,
    x_send, x_recv, s_send, s_recv, d_send, d_recv, own_sem, w_sem, cot_sem, act_sem, keep_sem, low_sem,
    near_send, near_recv, far_send, far_recv, last_send, last_recv, ready_sem, out_sem, loc_sem, pair_send, red_send,
    bc_send, bc_recv, swap_send, give_send, give_recv, rx_recv, sib_send, sib_recv, acr_send, acr_recv, row_send,
    row_recv, sum_send, sum_recv,
):
    rows, steps, width = tokens.shape
    full = gain.shape[-1]
    tm_count, tm = lax.axis_size("tm"), lax.axis_index("tm")
    chan_count, chan = lax.axis_size("chan"), lax.axis_index("chan")
    sibling = chan + 1 - 2 * lax.rem(chan, 2)
    across = lax.rem(chan + 2, 4)
    chunks = steps // CHUNK
    span = CHUNK * rows
    part = BLOCK * rows
    tiles = width // LANE
    blocks = CHUNK // BLOCK
    units = 3 * full // UNIT
    per_gate = full // UNIT

    def remote(src, dst, send, recv, target):
        return pltpu.make_async_remote_copy(src, dst, send, recv, device_id=target, device_id_type=MESH)

    def lanes(j):
        return slice(j * LANE, (j + 1) * LANE)

    def mine(ref, j):
        return ref[0:1, pl.ds(pl.multiple_of(chan * width + j * LANE, LANE), LANE)]

    def hat(at, j):
        return (own_tok[at, lanes(j)].astype(F32) - mean[at, :]) * inv[at, :]

    def normed(at, j):
        return hat(at, j) * mine(gain, j) + mine(shift, j)

    def rows_of(ch):
        return pl.ds(pl.multiple_of(ch * span, span), span)

    def raw_rows(ch, block, h0, h1):
        return pl.ds(pl.multiple_of((ch * chan_count + block) * span + h0 * part, part), (h1 - h0) * part)

    def token_copies(ch, h0, h1, copy):
        at = [pl.ds(pl.multiple_of(ch * CHUNK + h * BLOCK, BLOCK), BLOCK) for h in range(h0, h1)]
        return [
            copy(tokens.at[:, t, :], raw.at[raw_rows(ch, chan, h, h + 1)].reshape(rows, BLOCK, width), ch + h0)
            for h, t in zip(range(h0, h1), at)
        ]

    def own_move(src, dst, sem):
        return pltpu.make_async_copy(src, dst, own_sem.at[sem])

    def x_move(src, dst, sem):
        return remote(src, dst, x_send.at[sem], x_recv.at[sem], (tm, across))

    def s_move(src, dst, sem):
        return remote(src, dst, s_send.at[sem], s_recv.at[sem], (tm, sibling))

    def arrived(ch, block, h0, h1, copy):
        here = raw.at[raw_rows(ch, block, h0, h1)]
        return copy(here, here, ch + h0)

    def send_tokens(ch, h0, h1):
        for copy in (own_move, x_move, s_move):
            for c in token_copies(ch, h0, h1, copy):
                c.start()

    def d_copy(ch, h0, h1):
        view = raw.at[raw_rows(ch, across, h0, h1)]
        return remote(view, view, d_send.at[ch + h0], d_recv.at[ch + h0], (tm, sibling))

    def cot_copy(ch):
        at = pl.ds(pl.multiple_of(ch * CHUNK, CHUNK), CHUNK)
        return pltpu.make_async_copy(cotangent.at[:, at, :], cot_raw.at[lax.rem(ch, 2)], cot_sem.at[lax.rem(ch, 2)])

    def act_copy(ch):
        at = pl.ds(pl.multiple_of(ch * CHUNK, CHUNK), CHUNK)
        return pltpu.make_async_copy(act_buf.at[lax.rem(ch, 2)], act.at[:, at, :], act_sem.at[lax.rem(ch, 2)])

    def keep_copy(ch):
        return pltpu.make_async_copy(low.at[lax.rem(ch, 2)], low_all.at[rows_of(ch)], keep_sem.at[lax.rem(ch, 2)])

    def low_copy(u):
        at = pl.ds(pl.multiple_of(lax.rem(u, per_gate) * UNIT, UNIT), UNIT)
        return pltpu.make_async_copy(low_all.at[:, at], left_buf.at[lax.rem(u, 2)], low_sem.at[lax.rem(u, 2)])

    w_copies = [pltpu.make_async_copy(weights.at[k], w_buf.at[k], w_sem.at[k]) for k in range(3)]

    barrier = pltpu.get_barrier_semaphore()
    for d in range(1, 4):
        pl.semaphore_signal(barrier, inc=1, device_id=(tm, lax.rem(chan + d, 4)), device_id_type=MESH)

    def greet(d, carry):
        pl.semaphore_signal(barrier, inc=1, device_id=(lax.rem(tm + d, tm_count), chan), device_id_type=MESH)
        return carry

    lax.fori_loop(1, tm_count, greet, 0)
    for ch in range(2):
        for copy in token_copies(ch, 0, blocks, own_move):
            copy.start()
    cot_copy(0).start()
    for copy in w_copies:
        copy.start()
    pl.semaphore_wait(barrier, tm_count + 2)
    for ch in range(2):
        for copy in token_copies(ch, 0, blocks, x_move) + token_copies(ch, 0, blocks, s_move):
            copy.start()

    count = resets.shape[1]
    for j in range(count):
        reset_rows[j] = jnp.broadcast_to(resets[:, j : j + 1], (rows, LANE))

    def mark(t, carry):
        at = tm * steps + t

        def compare(j, hit):
            return jnp.maximum(hit, jnp.where(reset_rows[j] == at, 1.0, 0.0))

        hit = lax.fori_loop(0, count, compare, jnp.zeros((rows, LANE), F32), unroll=16)
        keep_mask[pl.ds(pl.multiple_of(t * rows, rows), rows), :] = 1.0 - hit
        return carry

    lax.fori_loop(0, steps, mark, 0)
    for r in range(rows):
        entry[r : r + 1, :] = bank[pl.ds(selector[r], 1), :]

    def send_last():
        for h in range(blocks):
            send_tokens(chunks - 1, h, h + 1)

    def gates(b, carry):
        a_list, b_list = list(carry[0]), list(carry[1])
        at = pl.ds(pl.multiple_of(b * part, part), part)
        mask = keep_mask[at, :]
        for j in range(tiles):
            cols = lanes(j)
            nrm = normed(at, j)
            f = sigmoid(forget[at, cols] + mix_f[0:1, cols] * nrm + bias_f[0:1, cols])
            o = sigmoid(gate[at, cols] + mix_r[0:1, cols] * nrm + bias_r[0:1, cols])
            forget[at, cols] = f
            gate[at, cols] = o
            inject = (1.0 - f) * cand[at, cols]
            keep = f * mask
            for t in range(BLOCK):
                now = slice(t * rows, (t + 1) * rows)
                a_list[j] = a_list[j] * keep[now]
                b_list[j] = b_list[j] * keep[now] + inject[now]
        return tuple(a_list), tuple(b_list)

    def gather_step(ch, runs, h0=0, h1=blocks):
        entire = h1 - h0 == blocks
        if entire:
            pl.when(ch + 2 < chunks - 1)(lambda: send_tokens(ch + 2, 0, blocks))
            pl.when(ch + 2 == chunks - 1)(send_last)
            cot_copy(ch + 1).start()

        base = pl.multiple_of(ch * span, span)
        slot = lax.rem(ch, 2)

        arrived(ch, across, h0, h1, x_move).wait_recv()
        d_copy(ch, h0, h1).start()

        if h0 == 0:
            runs = lax.fori_loop(jnp.maximum(ch - 1, 0) * blocks, ch * blocks, gates, runs)
        else:
            runs = lax.fori_loop(ch * blocks, ch * blocks + h0, gates, runs)

        if h0 == 0:
            cot_copy(ch).wait()
            for h in range(blocks):
                for j in range(tiles):
                    v = cot_raw[slot, :, h * BLOCK : (h + 1) * BLOCK, lanes(j)].astype(F32).reshape(part, LANE)
                    at = pl.ds(pl.multiple_of(base + h * part, part), part)
                    cot[at, lanes(j)] = swapped(v, rows, BLOCK).astype(BF16)
            pl.when(ch >= 2)(lambda: keep_copy(ch - 2).wait())
        arrived(ch, chan, h0, h1, own_move).wait()
        arrived(ch, sibling, h0, h1, s_move).wait_recv()
        d_copy(ch, h0, h1).wait_recv()

        first = pl.multiple_of(ch * chan_count * span, span)

        def tokens_at(block, r, h, cols):
            at = pl.multiple_of(first + block * span + h * part + r * BLOCK, BLOCK)
            return raw[pl.ds(at, BLOCK), cols].astype(F32)

        def each(i, turn):
            r, h = lax.rem(i, rows), h0 + i // rows
            totals = [jnp.zeros((BLOCK, LANE), F32) for _ in range(chan_count)]
            for j in range(tiles):
                for b in range(chan_count):
                    totals[b] = totals[b] + turn(tokens_at(b, r, h, lanes(j)))
            while len(totals) > 1:
                totals = [a + b for a, b in zip(totals[::2], totals[1::2])]
            part_s[h, r] = totals[0]

        def sum_rows(i, carry):
            each(i, lambda v: v)
            return carry

        count = (h1 - h0) * rows
        stat = (h1 - h0,) + mean_s.shape[1:]
        lax.fori_loop(0, count, sum_rows, 0, unroll=2)
        total = jnp.sum(part_s[h0:h1], axis=-1, keepdims=True)
        mean_s[h0:h1] = jnp.broadcast_to(total * (1.0 / full), stat)

        def square_rows(i, carry):
            m = mean_s[h0 + i // rows, lax.rem(i, rows)]
            each(i, lambda v: (v - m) * (v - m))
            return carry

        lax.fori_loop(0, count, square_rows, 0, unroll=2)
        var = jnp.sum(part_s[h0:h1], axis=-1, keepdims=True) * (1.0 / full)
        inv_s[h0:h1] = jnp.broadcast_to(lax.rsqrt(var + EPSILON), stat)

        for h in range(h0, h1):
            mean_h = mean_s[h].reshape(part, LANE)
            inv_h = inv_s[h].reshape(part, LANE)

            def normalize(j, carry, h=h, mean_h=mean_h, inv_h=inv_h):
                cols = pl.ds(pl.multiple_of(j * LANE, LANE), LANE)
                inner = pl.ds(pl.multiple_of(lax.rem(j, tiles) * LANE, LANE), LANE)
                v = jnp.concatenate([tokens_at(j // tiles, r, h, inner) for r in range(rows)], axis=0)
                v = (v - mean_h) * inv_h * gain[0:1, cols] + shift[0:1, cols]
                low[slot, h * part : (h + 1) * part, cols] = swapped(v, rows, BLOCK).astype(BF16)
                return carry

            lax.fori_loop(0, full // LANE, normalize, 0, unroll=2)
            at = pl.ds(pl.multiple_of(base + h * part, part), part)
            mean[at, :] = swapped(mean_h, rows, BLOCK)
            inv[at, :] = swapped(inv_h, rows, BLOCK)
            for j in range(tiles):
                v = jnp.concatenate([tokens_at(chan, r, h, lanes(j)) for r in range(rows)], axis=0)
                own_tok[at, lanes(j)] = swapped(v, rows, BLOCK).astype(BF16)

        if entire:

            @pl.when(ch == 0)
            def _():
                for copy in w_copies:
                    copy.wait()

        at = pl.ds(pl.multiple_of(base + h0 * part, part), (h1 - h0) * part)
        for k, ref in enumerate((cand, forget, gate)):
            ref[at, :] = jnp.dot(low[slot, h0 * part : h1 * part], w_buf[k], preferred_element_type=F32)

        if h1 == blocks:
            keep_copy(ch).start()

        return runs

    ones = tuple(jnp.ones((rows, LANE), F32) for _ in range(tiles))
    zeros = tuple(jnp.zeros((rows, LANE), F32) for _ in range(tiles))
    runs = lax.fori_loop(0, chunks - 1, gather_step, (ones, zeros))
    for h in range(blocks):
        runs = gather_step(chunks - 1, runs, h, h + 1)
    a_run, b_run = lax.fori_loop(chunks * blocks - 1, chunks * blocks, gates, runs)

    spans = jnp.where(reset_rows[0] >= tm_count * steps, 1.0, 0.0)
    last_tm = tm_count - 1

    def spanning(v):
        return jnp.sum(v * spans, axis=0, keepdims=True)

    def near_copy(way, target):
        return remote(near.at[way, 0], near.at[way, 1], near_send.at[way], near_recv.at[way], (target, chan))

    def far_copy(way, source, target):
        return remote(
            far.at[way, source], far.at[way, source], far_send.at[way, target], far_recv.at[way, source], (target, chan)
        )

    def last_copy(target):
        return remote(near.at[0, 0], near.at[0, 2], last_send.at[target], last_recv, (target, chan))

    def sum_copy(source, target):
        return remote(sum_rx.at[source], sum_rx.at[source], sum_send.at[target], sum_recv.at[source], (target, chan))

    def peers(act_on):
        def one(d, carry):
            act_on(lax.rem(tm + d, tm_count))
            return carry

        lax.fori_loop(1, tm_count, one, 0)

    for j in range(tiles):
        near[0, 0, :, lanes(j)] = b_run[j]
        far[0, tm, j : j + 1, :] = spanning(a_run[j])
        far[0, tm, tiles + j : tiles + j + 1, :] = spanning(b_run[j])
    pl.when(tm < last_tm)(lambda: near_copy(0, tm + 1).start())
    peers(lambda p: far_copy(0, tm, p).start())
    pl.when(tm == last_tm)(lambda: peers(lambda p: last_copy(p).start()))
    peers(lambda p: far_copy(0, p, tm).wait_recv())
    pl.when(tm > 0)(lambda: near_copy(0, tm).wait_recv())

    def carry_on(d, carry):
        state, here = carry
        here = jnp.where(d == tm, state, here)
        return far[0, d, 0:tiles, :] * state + far[0, d, tiles : 2 * tiles, :], here

    lead = jnp.concatenate([spanning(entry[:, lanes(j)]) for j in range(tiles)], axis=0)
    last, here = lax.fori_loop(0, tm_count, carry_on, (lead, lead))
    states = []
    for j in range(tiles):
        row = jnp.broadcast_to(here[j : j + 1], (rows, LANE))
        others = jnp.where(tm == 0, entry[:, lanes(j)], near[0, 1, :, lanes(j)])
        states.append(jnp.where(spans > 0, row, others))
    keep_copy(chunks - 2).wait()
    keep_copy(chunks - 1).wait()
    low_copy(0).start()

    def forward(b, states):
        states = list(states)
        at = pl.ds(pl.multiple_of(b * part, part), part)
        mask = keep_mask[at, :]
        for j in range(tiles):
            cols = lanes(j)
            f = forget[at, cols]
            inject = (1.0 - f) * cand[at, cols]
            before, after = [], []
            c = states[j]
            for t in range(BLOCK):
                now = slice(t * rows, (t + 1) * rows)
                c = c * mask[now]
                before.append(c)
                c = f[now] * c + inject[now]
                after.append(c)
            states[j] = c
            masked[at, cols] = jnp.concatenate(before, axis=0)
            th = jnp.tanh(jnp.concatenate(after, axis=0))
            o = gate[at, cols]
            gate_grad = cot[at, cols].astype(F32) * (th - own_tok[at, cols].astype(F32))
            grad_buf[2, at, cols] = (gate_grad * o * (1.0 - o)).astype(BF16)
        return tuple(states)

    lax.fori_loop(0, steps // BLOCK, forward, tuple(states))

    def start_later():
        flow[0] = jnp.ones((rows, width), F32)
        flow[1] = jnp.zeros((rows, width), F32)

    def later(b, carry):
        ch, h = b // blocks, lax.rem(b, blocks)
        slot = lax.rem(ch, 2)

        @pl.when(both(h == 0, ch >= 2))
        def _():
            act_copy(ch - 2).wait()

        at = pl.ds(pl.multiple_of(b * part, part), part)
        t0 = pl.multiple_of(h * BLOCK, BLOCK)
        mask = keep_mask[at, :]
        for j in range(tiles):
            cols = lanes(j)
            f = forget[at, cols]
            th = jnp.tanh(f * masked[at, cols] + (1.0 - f) * cand[at, cols])
            o = gate[at, cols]
            x = own_tok[at, cols].astype(F32)
            ct = cot[at, cols].astype(F32)
            rest = 1.0 - o
            out = swapped(o * th + rest * x, BLOCK, rows).astype(BF16)
            act_buf[slot, :, pl.ds(t0, BLOCK), cols] = out.reshape(rows, BLOCK, LANE)
            direct = ct * o * (1.0 - th * th)
            side[at, cols] = (ct * rest).astype(BF16)
            gate[at, cols] = direct
            keep = f * mask
            run, total = flow[0, :, cols], flow[1, :, cols]
            for t in range(BLOCK):
                now = slice(t * rows, (t + 1) * rows)
                run = run * keep[now]
                total = total + run * direct[now]
            flow[0, :, cols], flow[1, :, cols] = run, total

        @pl.when(h == blocks - 1)
        def _():
            act_copy(ch).start()

        return carry

    def end_later():
        near[1, 0] = flow[1]
        for j in range(tiles):
            far[1, tm, j : j + 1, :] = spanning(flow[1, :, lanes(j)])
        pl.when(tm > 0)(lambda: near_copy(1, tm - 1).start())
        peers(lambda p: far_copy(1, tm, p).start())
        for target in (sibling, across):
            pl.semaphore_signal(ready_sem, inc=1, device_id=(tm, target), device_id_type=MESH)
        more[...] = jnp.zeros_like(more)

    def sent_on(ch, carry):
        d_copy(ch, 0, blocks).wait_send()
        return carry

    lax.fori_loop(0, chunks - 1, sent_on, 0)
    for h in range(blocks):
        d_copy(chunks - 1, h, h + 1).wait_send()

    n = tm_count // 2
    o, y = tm // 2, lax.rem(tm, 2)
    partner = (o * 2 + 1 - y, chan)
    left = ((o - 1) * 2 + y, chan)
    right = ((o + 1) * 2 + y, chan)
    ring = ring_of(tm_count)
    ends, middle = (0, n - 1), (n // 2 - 1, n // 2)
    lines = [(0, middle[0] + y, n // 2, 1, None)]
    for l in (1, 2):
        if n == 4:
            lines += [(l, ends[l - 1], n - 1, 0, 0), (l, middle[l - 1], n // 2, 0, 1)]
        else:
            lines += [(l, middle[l - 1], n // 2, 0, None)]
    give_stage = 2 * (n // 2) + 2
    depth = LAG * max([give_stage] + [first + reach + (l > 0) + reach for l, c, reach, first, parity in lines])
    space = -(-depth // ring)

    def stage(s, number, parity=None):
        v = s - LAG * number
        u = v if space == 1 else v // space
        go = both(v >= 0, u < units)
        if space > 1:
            go = both(go, lax.rem(v, space) == 0)
        return u, go if parity is None else both(go, lax.rem(u, 2) == parity)

    def gate_of(u):
        return lax.rem(u // per_gate + 2, 3)

    def piece_of(l, mate=False):
        if l == 0:
            return (1 - y if mate else y) * PAIR, PAIR
        return 2 * PAIR + (l - 1) * LINE, LINE

    def wg_rows(l, u, mate=False):
        start, size = piece_of(l, mate)
        return pl.ds(pl.multiple_of(u * UNIT + start, 16), size)

    def fin_at(l, u):
        start, size = piece_of(l)
        return fin.at[pl.ds(pl.multiple_of((gate_of(u) * per_gate + lax.rem(u, per_gate)) * UNIT + start, 16), size)]

    def rx_rows(u, place, l):
        start = place * PAIR if l == 0 else 3 * PAIR + (place - 3) * LINE
        size = PAIR if l == 0 else LINE
        return pl.ds(pl.multiple_of(lax.rem(u, ring) * (3 * PAIR + 4 * LINE) + start, 16), size)

    def arrival(l, c, column, way, u):
        if l == 0:
            return 1 + way
        if l == 1:
            other = 6
        elif n == 4:
            other = jnp.where(column == jnp.where(lax.rem(u, 2) == 0, ends[0], middle[0]), 6, 3)
        else:
            other = jnp.where(column == middle[0], 6, 3)
        return jnp.where(column == c, 3 + way, other)

    def launch(make, u):
        @pl.when(u >= SENDS)
        def _():
            make(u - SENDS).wait_send()

        make(u).start()

    def to_rx(src, u, place, l, sem, target):
        return remote(src, rx.at[rx_rows(u, place, l)], sem, rx_recv.at[lax.rem(u, ring), place], target)

    def pair_copy(u):
        return to_rx(raw.at[wg_rows(0, u, True)], u, 0, 0, pair_send.at[lax.rem(u, SENDS)], partner)

    def red_copy(l, c, u, to_right):
        way, column = (0, o + 1) if to_right else (1, o - 1)
        return to_rx(
            raw.at[wg_rows(l, u)], u, arrival(l, c, column, way, u), l, red_send.at[l, lax.rem(u, SENDS)],
            right if to_right else left,
        )

    def red_wait(l, c, u, way):
        place = arrival(l, c, o, way, u)
        at = rx_rows(u, place, l)
        to_rx(rx.at[at], u, place, l, red_send.at[l, 0], partner).wait_recv()
        return rx[at].astype(F32)

    def bc_copy(l, u, to_right, src):
        return remote(
            src, fin_at(l, u), bc_send.at[l, lax.rem(u, SENDS), 1 if to_right else 0], bc_recv.at[l, lax.rem(u, ring)],
            right if to_right else left,
        )

    def swap_copy(l, u):
        return to_rx(raw.at[wg_rows(l, u)], u, 5, l, swap_send.at[lax.rem(u, SENDS)], partner)

    def give_copy(u, src):
        return remote(src, fin_at(0, u), give_send.at[lax.rem(u, SENDS)], give_recv.at[lax.rem(u, ring)], partner)

    def local_copy(l, u):
        return pltpu.make_async_copy(raw.at[wg_rows(l, u)], fin_at(l, u), loc_sem.at[l, lax.rem(u, SENDS)])

    def add_to(l, u, *others):
        at = wg_rows(l, u)
        total = raw[at].astype(F32)
        for v in others:
            total = total + v
        raw[at] = total.astype(BF16)

    def red_start(l, c, u):
        pl.when(o < c)(lambda: launch(lambda v: red_copy(l, c, v, True), u))
        pl.when(o > c)(lambda: launch(lambda v: red_copy(l, c, v, False), u))

    def publish(l, u):
        @pl.when(u >= SENDS)
        def _():
            local_copy(l, u - SENDS).wait()

        local_copy(l, u).start()
        pl.when(o > 0)(lambda: launch(lambda v: bc_copy(l, v, False, raw.at[wg_rows(l, v)]), u))
        pl.when(o < n - 1)(lambda: launch(lambda v: bc_copy(l, v, True, raw.at[wg_rows(l, v)]), u))
        if l == 0:
            launch(lambda v: give_copy(v, raw.at[wg_rows(0, v)]), u)

    def block_cols(c):
        return pl.ds(pl.multiple_of(c * width, width), width)

    def sib_rows(ch, q):
        return pl.ds(pl.multiple_of(units * UNIT + (lax.rem(ch, 4) * 2 + q) * span, span), span)

    def sib_copy(ch, q):
        slot = lax.rem(ch, 2)
        cols = sibling if q == 0 else lax.rem(sibling + 2, 4)
        return remote(
            terms.at[slot, cols], raw.at[sib_rows(ch, q)], sib_send.at[q], sib_recv.at[lax.rem(ch, 4), q], (tm, sibling)
        )

    def acr_copy(ch):
        return remote(
            terms.at[lax.rem(ch, 2), across], cot.at[rows_of(ch)], acr_send.at[lax.rem(ch, 2)], acr_recv.at[ch], (tm, across)
        )

    def row_copy(ch, source, d):
        return remote(
            row_rx.at[ch, source], row_rx.at[ch, source], row_send.at[lax.rem(ch, 4), d - 1],
            row_recv.at[lax.rem(ch, 4), source], (tm, lax.rem(chan + d, 4)),
        )

    def out_copy(ch):
        at = pl.ds(pl.multiple_of(ch * CHUNK, CHUNK), CHUNK)
        return pltpu.make_async_copy(out_buf.at[lax.rem(ch, 2)], in_grad.at[:, at, :], out_sem.at[lax.rem(ch, 2)])

    def project(ch):
        at = rows_of(ch)
        slot = lax.rem(ch, 2)

        @pl.when(ch == 0)
        def _():
            pl.semaphore_wait(ready_sem, 2)

        @pl.when(ch >= 2)
        def _():
            acr_copy(ch - 2).wait_send()

        for b in range(chan_count):
            total = jnp.zeros((span, width), F32)
            for k in range(3):
                total = total + lax.dot_general(
                    grad_buf[k, at, :], w_buf[k, b * width : (b + 1) * width, :], (((1,), (1,)), ((), ())),
                    preferred_element_type=F32,
                )
            terms[slot, b] = total.astype(BF16)
        sib_copy(ch, 0).start()
        sib_copy(ch, 1).start()

    def chip_sum(ch):
        slot = lax.rem(ch, 2)
        for q in range(2):
            sib_copy(ch, q).wait_recv()
        there = terms[slot, across].astype(F32) + raw[sib_rows(ch, 1)].astype(F32)
        terms[slot, across] = there.astype(BF16)
        acr_copy(ch).start()
        here = terms[slot, chan].astype(F32) + raw[sib_rows(ch, 0)].astype(F32)
        cand[rows_of(ch), :] = here
        for q in range(2):
            sib_copy(ch, q).wait_send()

    def full_sum(ch):
        acr_copy(ch).wait_recv()
        at = rows_of(ch)
        total = jnp.zeros((8, span), F32)
        pick = lax.broadcasted_iota(jnp.int32, (8, LANE), 0)
        for j in range(tiles):
            cols = lanes(j)
            fp, rp = grad_buf[1, at, cols].astype(F32), grad_buf[2, at, cols].astype(F32)
            g = cand[at, cols] + cot[at, cols].astype(F32) + fp * mix_f[0:1, cols] + rp * mix_r[0:1, cols]
            cand[at, cols] = g
            h = hat(at, j)
            nrm = h * mine(gain, j) + mine(shift, j)
            weighted = g * h
            for i, v in enumerate((fp * nrm, rp * nrm, fp, rp, weighted, g)):
                more[i, :, cols] = more[i, :, cols] + jnp.sum(v.reshape(CHUNK, rows, LANE), axis=0)
            for i, v in enumerate((g * mine(gain, j), weighted * mine(gain, j))):
                lead = jnp.where(pick == i, 1.0, 0.0).astype(BF16)
                high = v.astype(BF16)
                low_part = (v - high.astype(F32)).astype(BF16)
                for p in (high, low_part):
                    total = total + lax.dot_general(lead, p, (((1,), (1,)), ((), ())), preferred_element_type=F32)
        row_rx[ch, chan] = total
        for d in range(1, 4):
            pl.when(ch >= 4)(lambda d=d: row_copy(ch - 4, chan, d).wait_send())
            row_copy(ch, chan, d).start()

    def finish(ch):
        for d in range(1, 4):
            row_copy(ch, lax.rem(chan + d, 4), d).wait_recv()

        @pl.when(ch >= 2)
        def _():
            out_copy(ch - 2).wait()

        at = rows_of(ch)
        total = (row_rx[ch, 0] + row_rx[ch, 1] + row_rx[ch, 2] + row_rx[ch, 3]) * (1.0 / full)
        columns = jnp.transpose(total)
        first = jnp.broadcast_to(columns[:, 0:1], (span, LANE))
        second = jnp.broadcast_to(columns[:, 1:2], (span, LANE))
        for j in range(tiles):
            cols = lanes(j)
            g = cand[at, cols] * mine(gain, j)
            v = inv[at, :] * (g - first - hat(at, j) * second) + side[at, cols].astype(F32)
            out_buf[lax.rem(ch, 2), :, :, cols] = swapped(v, CHUNK, rows).reshape(rows, CHUNK, LANE)
        out_copy(ch).start()

    def share_sums():
        for i in range(6):
            sum_rx[tm, i : i + 1, :] = jnp.sum(more[i], axis=0, keepdims=True)
        sum_rx[tm, 6:8, :] = jnp.zeros((2, width), F32)
        peers(lambda p: sum_copy(tm, p).start())

    def start_backward():
        peers(lambda p: far_copy(1, p, tm).wait_recv())
        pl.when(tm < last_tm)(lambda: near_copy(1, tm).wait_recv())

        def carry_back(i, v):
            d = tm_count - 1 - i
            return jnp.where(d > tm, far[0, d, 0:tiles, :] * v + far[1, d, 0:tiles, :], v)

        inflow = lax.fori_loop(0, tm_count, carry_back, jnp.zeros((tiles, LANE), F32))
        for j in range(tiles):
            row = jnp.broadcast_to(inflow[j : j + 1], (rows, LANE))
            others = jnp.where(tm == last_tm, 0.0, near[1, 1, :, lanes(j)])
            flow[0, :, lanes(j)] = jnp.where(spans > 0, row, others)

    def backward(i, carry):
        b = steps // BLOCK - 1 - i
        at = pl.ds(pl.multiple_of(b * part, part), part)
        mask = keep_mask[at, :]
        for j in range(tiles):
            cols = lanes(j)
            f = forget[at, cols]
            keep = f * mask
            direct = gate[at, cols]
            g = flow[0, :, cols]
            adjoint = [None] * BLOCK
            for t in reversed(range(BLOCK)):
                now = slice(t * rows, (t + 1) * rows)
                adjoint[t] = direct[now] + g
                g = keep[now] * adjoint[t]
            flow[0, :, cols] = g
            cand_grad = jnp.concatenate(adjoint, axis=0) * (1.0 - f)
            forget_pre = cand_grad * (masked[at, cols] - cand[at, cols]) * f
            grad_buf[0, at, cols] = cand_grad.astype(BF16)
            grad_buf[1, at, cols] = forget_pre.astype(BF16)
        return carry

    def close_tokens(ch, carry, h0=0, h1=blocks):
        arrived(ch, chan, h0, h1, x_move).wait_send()
        arrived(ch, chan, h0, h1, s_move).wait_send()
        return carry

    def close_first():
        lax.fori_loop(0, chunks - 1, close_tokens, 0)
        for h in range(blocks):
            close_tokens(chunks - 1, 0, h, h + 1)
        for way in range(2):
            peers(lambda p, way=way: far_copy(way, tm, p).wait_send())
        pl.when(tm < last_tm)(lambda: near_copy(0, tm).wait_send())
        pl.when(tm > 0)(lambda: near_copy(1, tm).wait_send())
        pl.when(tm == last_tm)(lambda: peers(lambda p: last_copy(p).wait_send()))
        pl.when(tm != last_tm)(lambda: last_copy(tm).wait_recv())
        for ch in (chunks - 2, chunks - 1):
            act_copy(ch).wait()
        for j in range(tiles):
            row = jnp.broadcast_to(last[j : j + 1], (rows, LANE))
            others = jnp.where(tm == last_tm, near[0, 0, :, lanes(j)], near[0, 2, :, lanes(j)])
            final[:, lanes(j)] = jnp.where(spans > 0, row, others)

    def close_second():
        for ch in range(chunks - 4, chunks):
            for d in range(1, 4):
                row_copy(ch, chan, d).wait_send()
        for ch in (chunks - 2, chunks - 1):
            out_copy(ch).wait()
            acr_copy(ch).wait_send()
        peers(lambda p: sum_copy(p, tm).wait_recv())
        peers(lambda p: sum_copy(tm, p).wait_send())
        totals[...] = lax.fori_loop(0, tm_count, lambda d, v: v + sum_rx[d], jnp.zeros(totals.shape, F32))

    def slot_step(s, carry):
        u, go = stage(s, give_stage)
        pl.when(go)(lambda: give_copy(u, raw.at[wg_rows(0, u)]).wait_recv())

        for l, c, reach, first, parity in lines:
            late = first + reach + (1 if l else 0)
            u, go = stage(s, late + jnp.abs(o - c), parity)

            @pl.when(both(o != c, go))
            def _(l=l, c=c, u=u):
                bc_copy(l, u, True, fin_at(l, u)).wait_recv()
                pl.when(both(o < c, o > 0))(lambda: launch(lambda v: bc_copy(l, v, False, fin_at(l, v)), u))
                pl.when(both(o > c, o < n - 1))(lambda: launch(lambda v: bc_copy(l, v, True, fin_at(l, v)), u))
                if l == 0:
                    launch(lambda v: give_copy(v, fin_at(0, v)), u)

        for l, c, reach, first, parity in lines[1:]:
            u, go = stage(s, reach + 1, parity)

            @pl.when(both(o == c, go))
            def _(l=l, u=u):
                swap_copy(l, u).wait()
                add_to(l, u, rx[rx_rows(u, 5, l)].astype(F32))
                publish(l, u)

        for l, c, reach, first, parity in lines:
            u, go = stage(s, first + reach, parity)

            @pl.when(both(o == c, go))
            def _(l=l, c=c, u=u):
                if l == 0 and n > 2:
                    add_to(l, u, red_wait(l, c, u, 0), red_wait(l, c, u, 1))
                elif l > 0 and 0 < c < n - 1:
                    add_to(l, u, red_wait(l, c, u, 0), red_wait(l, c, u, 1))
                else:
                    pl.when(o > 0)(lambda: add_to(l, u, red_wait(l, c, u, 0)))
                    pl.when(o < n - 1)(lambda: add_to(l, u, red_wait(l, c, u, 1)))
                if l == 0:
                    publish(l, u)
                else:
                    swap_copy(l, u).start()

        u0, go0 = stage(s, 0)

        @pl.when(go0)
        def _():
            pl.when(u0 + 1 < units)(lambda: low_copy(u0 + 1).start())
            low_copy(u0).wait()
            g = lax.dot_general(
                left_buf[lax.rem(u0, 2)], grad_buf[gate_of(u0)], (((0,), (0,)), ((), ())), preferred_element_type=F32
            )
            raw[pl.ds(pl.multiple_of(u0 * UNIT, UNIT), UNIT)] = g.astype(BF16)
            launch(pair_copy, u0)
            for l, c, reach, first, parity in lines[1:]:
                mine_now = jnp.logical_or(o == 0, o == n - 1)
                if parity is not None:
                    mine_now = both(mine_now, lax.rem(u0, 2) == parity)
                pl.when(mine_now)(lambda l=l, c=c: red_start(l, c, u0))

        for l, c, reach, first, parity in lines:
            u, go = stage(s, first + jnp.where(o < c, o, n - 1 - o), parity)

            @pl.when(both(o < c, o > 0, go))
            def _(l=l, c=c, u=u):
                add_to(l, u, red_wait(l, c, u, 0))
                launch(lambda v: red_copy(l, c, v, True), u)

            @pl.when(both(o > c, o < n - 1, go))
            def _(l=l, c=c, u=u):
                add_to(l, u, red_wait(l, c, u, 1))
                launch(lambda v: red_copy(l, c, v, False), u)

        u, go = stage(s, 1)

        @pl.when(go)
        def _():
            pair_copy(u).wait_recv()
            add_to(0, u, rx[rx_rows(u, 0, 0)].astype(F32))
            pl.when(jnp.logical_or(o == 0, o == n - 1))(lambda: red_start(0, lines[0][1], u))

        count = steps // BLOCK
        pl.when(s == 0)(start_later)
        share = -(-count // LATER)
        at = s * share

        @pl.when(s < LATER)
        def _():
            lax.fori_loop(at, jnp.minimum(at + share, count), later, 0)

        pl.when(s == LATER - 1)(end_later)
        pl.when(s == LATER + 1)(start_backward)
        share = -(-count // (FIRST - LATER - 1))
        at2 = (s - LATER - 1) * share

        @pl.when(both(s > LATER, s < FIRST))
        def _():
            lax.fori_loop(at2, jnp.minimum(at2 + share, count), backward, 0)

        for job, offset in ((finish, 5), (full_sum, 3), (chip_sum, 1), (project, 0)):
            at = s - FIRST - offset
            pl.when(both(at >= 0, lax.rem(at, 2) == 0, at // 2 < chunks))(lambda job=job, at=at: job(at // 2))
        pl.when(s == FIRST + 3)(close_first)
        pl.when(s == FIRST + 2 * chunks + 2)(share_sums)
        pl.when(s == FIRST + 2 * chunks + 6)(close_second)
        return carry

    slots = max((units - 1) * space + depth + 1, FIRST + 2 * chunks + 7)
    lax.fori_loop(0, slots, slot_step, 0)

    def close_unit(u, carry):
        give_copy(u, raw.at[wg_rows(0, u)]).wait_send()
        pair_copy(u).wait_send()
        for l, c, reach, first, parity in lines:

            @pl.when(True if parity is None else lax.rem(u, 2) == parity)
            def _(l=l, c=c):
                src = raw.at[wg_rows(l, u)]
                pl.when(o != c)(lambda: red_copy(l, c, u, True).wait_send())
                pl.when(o == c)(lambda: local_copy(l, u).wait())
                pl.when(both(o <= c, o > 0))(lambda: bc_copy(l, u, False, src).wait_send())
                pl.when(both(o >= c, o < n - 1))(lambda: bc_copy(l, u, True, src).wait_send())

        return carry

    lax.fori_loop(units - SENDS, units, close_unit, 0)


def layer(tokens, weights, cotangent, gain, shift, mix_f, mix_r, bias_f, bias_r, bank, selector, resets):
    rows, steps, width = tokens.shape
    full = gain.shape[-1]
    tm_count, chan_count = lax.axis_size("tm"), lax.axis_size("chan")
    chunks = steps // CHUNK
    span = CHUNK * rows
    pieces = chunks - 1 + CHUNK // BLOCK
    count = steps * rows
    units = 3 * full // UNIT
    ring = ring_of(tm_count)
    hbm = pl.BlockSpec(memory_space=pl.ANY)
    vmem = pl.BlockSpec(memory_space=pltpu.VMEM)
    smem = pl.BlockSpec(memory_space=pltpu.SMEM)
    dma = pltpu.SemaphoreType.DMA
    stat = pltpu.VMEM((CHUNK // BLOCK, rows, BLOCK, LANE), F32)
    wide = pltpu.VMEM((count, width), F32)
    narrow = pltpu.VMEM((count, LANE), F32)
    short = pltpu.VMEM((count, width), BF16)
    return pl.pallas_call(
        layer_kernel,
        out_shape=(
            jax.ShapeDtypeStruct((units * UNIT, width), BF16),
            jax.ShapeDtypeStruct(tokens.shape, F32),
            jax.ShapeDtypeStruct(tokens.shape, BF16),
            jax.ShapeDtypeStruct((count, full), BF16),
            jax.ShapeDtypeStruct((rows, width), F32),
            jax.ShapeDtypeStruct((8, width), F32),
        ),
        in_specs=[hbm, hbm, hbm] + [vmem] * 7 + [smem, vmem],
        out_specs=(hbm, hbm, hbm, hbm, vmem, vmem),
        scratch_shapes=[
            pltpu.VMEM((chunks * chan_count * span, width), BF16),
            pltpu.VMEM((ring * (3 * PAIR + 4 * LINE), width), BF16),
            pltpu.VMEM((2, span, full), BF16),
            pltpu.VMEM((2, count, UNIT), BF16),
            pltpu.VMEM((3, full, width), BF16),
            wide, wide, wide, wide,
            short,
            pltpu.VMEM((2, rows, CHUNK, width), BF16),
            short,
            narrow, narrow, narrow,
            pltpu.VMEM((3, count, width), BF16),
            pltpu.VMEM((2, rows, CHUNK, width), BF16),
            short,
            pltpu.VMEM((2, chan_count, span, width), BF16),
            pltpu.VMEM((2, rows, CHUNK, width), F32),
            pltpu.VMEM((chunks, 4, 8, span), F32),
            pltpu.VMEM((6, rows, width), F32),
            pltpu.VMEM((tm_count, 8, width), F32),
            stat, stat, stat,
            pltpu.VMEM((rows, width), F32),
            pltpu.VMEM((2, 3, rows, width), F32),
            pltpu.VMEM((2, tm_count, 8, LANE), F32),
            pltpu.VMEM((2, rows, width), F32),
            pltpu.VMEM((resets.shape[1], rows, LANE), jnp.int32),
            dma((pieces,)), dma((pieces,)), dma((pieces,)), dma((pieces,)), dma((pieces,)), dma((pieces,)), dma((pieces,)),
            dma((3,)), dma((2,)), dma((2,)), dma((2,)), dma((2,)),
            dma((2,)), dma((2,)), dma((2, tm_count)), dma((2, tm_count)), dma((tm_count,)), dma(()),
            pltpu.SemaphoreType.REGULAR,
            dma((2,)), dma((3, SENDS)), dma((SENDS,)), dma((3, SENDS)), dma((3, SENDS, 2)), dma((3, ring)), dma((SENDS,)),
            dma((SENDS,)), dma((ring,)), dma((ring, 7)), dma((2,)), dma((4, 2)), dma((2,)), dma((chunks,)),
            dma((4, 3)), dma((4, 4)), dma((tm_count,)), dma((tm_count,)),
        ],
        compiler_params=pltpu.CompilerParams(collective_id=0, has_side_effects=True, vmem_limit_bytes=VMEM_BYTES),
        name="whole",
    )(tokens, weights, cotangent, gain, shift, mix_f, mix_r, bias_f, bias_r, bank, selector, resets)


def tail_kernel(
    fin, in_grad, act, final, totals, wide_out, in_out, act_out, final_out, s0, s1, s2, s3, s4, s5,
    fin_buf, wide_buf, in_buf, act_buf, fin_sem, wide_sem, in_sem, act_sem,
):
    parts = fin_sem.shape[0]
    size = fin.shape[0] // parts

    def move(src, dst, sem, i, n):
        at = pl.ds(i * n, n)
        return pltpu.make_async_copy(src.at[at], dst.at[at], sem)

    loads = [move(fin, fin_buf, fin_sem.at[i], i, size) for i in range(parts)]
    stores = [move(wide_buf, wide_out, wide_sem.at[i], i, size) for i in range(parts)]
    pairs = []
    for src, buf, dst, sem in ((in_grad, in_buf, in_out, in_sem), (act, act_buf, act_out, act_sem)):
        n = sem.shape[1]
        some = src.shape[0] // n
        pairs += [(move(src, buf, sem.at[0, i], i, some), move(buf, dst, sem.at[1, i], i, some)) for i in range(n)]
    for i in range(max(parts, len(pairs))):
        if i < parts:
            loads[i].start()
        if i < len(pairs):
            pairs[i][0].start()
    final_out[...] = final[...]
    for i, ref in enumerate((s0, s1, s2, s3, s4, s5)):
        ref[...] = totals[i : i + 1, :]
    for i in range(max(parts, len(pairs))):
        if i < parts:
            loads[i].wait()

            def cast(j, carry, i=i):
                at = pl.ds(pl.multiple_of(i * size + j * 64, 64), 64)
                wide_buf[at] = fin_buf[at].astype(F32)
                return carry

            lax.fori_loop(0, size // 64, cast, 0, unroll=2)
            stores[i].start()
        if i < len(pairs):
            pairs[i][0].wait()
            pairs[i][1].start()
    for copy in stores:
        copy.wait()
    for _, onward in pairs:
        onward.wait()


def tail(fin, in_grad, act, final, totals):
    width = fin.shape[-1]
    flat = fin.reshape(-1, width)
    hbm = pl.BlockSpec(memory_space=pl.ANY)
    vmem = pl.BlockSpec(memory_space=pltpu.VMEM)
    dma = pltpu.SemaphoreType.DMA
    line = jax.ShapeDtypeStruct((1, width), F32)
    return pl.pallas_call(
        tail_kernel,
        out_shape=(
            jax.ShapeDtypeStruct(flat.shape, F32),
            jax.ShapeDtypeStruct(in_grad.shape, F32),
            jax.ShapeDtypeStruct(act.shape, BF16),
            jax.ShapeDtypeStruct(final.shape, F32),
        ) + (line,) * 6,
        in_specs=[hbm] * 3 + [vmem] * 2,
        out_specs=(hbm,) * 3 + (vmem,) * 7,
        scratch_shapes=[
            pltpu.VMEM(flat.shape, BF16), pltpu.VMEM(flat.shape, F32),
            pltpu.VMEM(in_grad.shape, F32), pltpu.VMEM(act.shape, BF16),
            dma((TAIL,)), dma((TAIL,)), dma((2, 4)), dma((2, 2)),
        ],
        compiler_params=pltpu.CompilerParams(vmem_limit_bytes=VMEM_BYTES),
        name="tail",
    )(flat, in_grad, act, final, totals)


def body(
    tokens, ln_gain, ln_bias, weights, mix_forget, mix_reset, bias_forget, bias_reset, state_bank, selector, resets, cotangent
):
    fin, in_grad, act, _, final, totals = layer(
        tokens, weights, cotangent, ln_gain[None], ln_bias[None], mix_forget[None], mix_reset[None], bias_forget[None],
        bias_reset[None], state_bank, selector, resets,
    )
    wide, in_grad, act, final, *sums = tail(fin, in_grad, act, final, totals)
    sums = [v[0] for v in sums]
    return act, final, in_grad, wide.reshape(weights.shape), sums[4], sums[5], sums[0], sums[1], sums[2], sums[3]


def solution(mesh):
    placed = (
        P(None, "tm", "chan"), P(), P(), P(None, None, "chan"), P("chan"), P("chan"), P("chan"), P("chan"),
        P(None, "chan"), P(), P(), P(None, "tm", "chan"),
    )
    return jax.shard_map(
        body,
        mesh=mesh,
        in_specs=placed,
        out_specs=(
            P(None, "tm", "chan"), P(None, "chan"), P(None, "tm", "chan"), P(None, None, "chan"),
            P("chan"), P("chan"), P("chan"), P("chan"), P("chan"), P("chan"),
        ),
        check_vma=False,
    )
```

```python
import jax
import jax.numpy as jnp
from jax import lax
from jax.experimental import pallas as pl
from jax.experimental.pallas import tpu as pltpu
from jax.sharding import PartitionSpec as P

EPSILON = 1e-05
CHUNK = 32
BLOCK = 16
LANE = 128
UNIT = 256
LAG = 2
PAIR = 80
LINE = 48
SENDS = 2
VMEM_BYTES = 63 << 20
TAIL = 4
LATER = 4
OUTPUT = 8
FIRST = 12
MESH = pl.DeviceIdType.MESH
F32 = jnp.float32
BF16 = jnp.bfloat16


def sigmoid(v):
    return 1.0 / (1.0 + jnp.exp(-v))


def swapped(v, outer, inner):
    return jnp.swapaxes(v.reshape(outer, inner, v.shape[-1]), 0, 1).reshape(outer * inner, v.shape[-1])


def both(*conditions):
    out = conditions[0]
    for c in conditions[1:]:
        out = jnp.logical_and(out, c)
    return out


def ring_of(tm_count):
    return 14 if tm_count <= 8 else 3


def layer_kernel(
    tokens, weights, cotangent, gain, shift, mix_f, mix_r, bias_f, bias_r, bank, selector, resets,
    fin, in_grad, act, low_t, final, totals,
    raw, rx, low, low_t_buf, w_buf, cand, forget, gate, masked, own_tok, cot_raw, cot, mean, inv, keep_mask, grad_buf,
    act_buf, side, terms, out_buf, row_rx, more, sum_rx, mean_s, inv_s, part_s, entry, near, far, flow, reset_rows,
    x_send, x_recv, s_send, s_recv, d_send, d_recv, own_sem, w_sem, cot_sem, act_sem, tr_sem, low_sem,
    near_send, near_recv, far_send, far_recv, last_send, last_recv, ready_sem, out_sem, loc_sem, pair_send, red_send,
    bc_send, bc_recv, swap_send, give_send, give_recv, rx_recv, sib_send, sib_recv, acr_send, acr_recv, row_send,
    row_recv, sum_send, sum_recv,
):
    rows, steps, width = tokens.shape
    full = gain.shape[-1]
    tm_count, tm = lax.axis_size("tm"), lax.axis_index("tm")
    chan_count, chan = lax.axis_size("chan"), lax.axis_index("chan")
    sibling = chan + 1 - 2 * lax.rem(chan, 2)
    across = lax.rem(chan + 2, 4)
    chunks = steps // CHUNK
    span = CHUNK * rows
    part = BLOCK * rows
    tiles = width // LANE
    blocks = CHUNK // BLOCK
    units = 3 * full // UNIT
    per_gate = full // UNIT

    def remote(src, dst, send, recv, target):
        return pltpu.make_async_remote_copy(src, dst, send, recv, device_id=target, device_id_type=MESH)

    def lanes(j):
        return slice(j * LANE, (j + 1) * LANE)

    def mine(ref, j):
        return ref[0:1, pl.ds(pl.multiple_of(chan * width + j * LANE, LANE), LANE)]

    def hat(at, j):
        return (own_tok[at, lanes(j)].astype(F32) - mean[at, :]) * inv[at, :]

    def normed(at, j):
        return hat(at, j) * mine(gain, j) + mine(shift, j)

    def rows_of(ch):
        return pl.ds(pl.multiple_of(ch * span, span), span)

    def raw_rows(ch, block, h0, h1):
        return pl.ds(pl.multiple_of((ch * chan_count + block) * span + h0 * part, part), (h1 - h0) * part)

    def token_copies(ch, h0, h1, copy):
        at = [pl.ds(pl.multiple_of(ch * CHUNK + h * BLOCK, BLOCK), BLOCK) for h in range(h0, h1)]
        return [
            copy(tokens.at[:, t, :], raw.at[raw_rows(ch, chan, h, h + 1)].reshape(rows, BLOCK, width), ch + h0)
            for h, t in zip(range(h0, h1), at)
        ]

    def own_move(src, dst, sem):
        return pltpu.make_async_copy(src, dst, own_sem)

    def x_move(src, dst, sem):
        return remote(src, dst, x_send, x_recv.at[sem], (tm, across))

    def s_move(src, dst, sem):
        return remote(src, dst, s_send, s_recv, (tm, sibling))

    def arrived(ch, block, h0, h1, copy):
        here = raw.at[raw_rows(ch, block, h0, h1)]
        return copy(here, here, ch + h0)

    def d_copy(ch, h0, h1):
        view = raw.at[raw_rows(ch, across, h0, h1)]
        return remote(view, view, d_send, d_recv.at[ch + h0], (tm, sibling))

    all_tokens = raw.at[pl.ds(0, steps * rows)]

    def cot_copy(ch):
        at = pl.ds(pl.multiple_of(ch * CHUNK, CHUNK), CHUNK)
        return pltpu.make_async_copy(cotangent.at[:, at, :], cot_raw.at[lax.rem(ch, 2)], cot_sem.at[lax.rem(ch, 2)])

    def act_copy(ch):
        at = pl.ds(pl.multiple_of(ch * CHUNK, CHUNK), CHUNK)
        return pltpu.make_async_copy(act_buf.at[lax.rem(ch, 2)], act.at[:, at, :], act_sem.at[lax.rem(ch, 2)])

    def tr_copy(ch):
        return pltpu.make_async_copy(low_t_buf, low_t.at[:, rows_of(ch)], tr_sem)

    def low_copy(u):
        at = pl.ds(pl.multiple_of(lax.rem(u, per_gate) * UNIT, UNIT), UNIT)
        return pltpu.make_async_copy(low_t.at[at], low.at[lax.rem(u, 2)], low_sem.at[lax.rem(u, 2)])

    w_copies = [pltpu.make_async_copy(weights.at[k], w_buf.at[k], w_sem.at[k]) for k in range(3)]

    barrier = pltpu.get_barrier_semaphore()
    for d in range(1, 4):
        pl.semaphore_signal(barrier, inc=1, device_id=(tm, lax.rem(chan + d, 4)), device_id_type=MESH)

    def greet(d, carry):
        pl.semaphore_signal(barrier, inc=1, device_id=(lax.rem(tm + d, tm_count), chan), device_id_type=MESH)
        return carry

    lax.fori_loop(1, tm_count, greet, 0)
    def start_own(ch, carry):
        for copy in token_copies(ch, 0, blocks, own_move):
            copy.start()
        return carry

    def start_sibling(ch, carry):
        for copy in token_copies(ch, 0, blocks, s_move):
            copy.start()
        return carry

    lax.fori_loop(0, chunks, start_own, 0)
    cot_copy(0).start()
    for copy in w_copies:
        copy.start()
    pl.semaphore_wait(barrier, tm_count + 2)
    for ch in range(2):
        for copy in token_copies(ch, 0, blocks, x_move):
            copy.start()
    lax.fori_loop(0, chunks, start_sibling, 0)

    count = resets.shape[1]
    for j in range(count):
        reset_rows[j] = jnp.broadcast_to(resets[:, j : j + 1], (rows, LANE))

    def mark(t, carry):
        at = tm * steps + t

        def compare(j, hit):
            return jnp.maximum(hit, jnp.where(reset_rows[j] == at, 1.0, 0.0))

        hit = lax.fori_loop(0, count, compare, jnp.zeros((rows, LANE), F32), unroll=16)
        keep_mask[pl.ds(pl.multiple_of(t * rows, rows), rows), :] = 1.0 - hit
        return carry

    lax.fori_loop(0, steps, mark, 0)
    for r in range(rows):
        entry[r : r + 1, :] = bank[pl.ds(selector[r], 1), :]

    def flip(ch):
        @pl.when(ch >= 1)
        def _():
            tr_copy(ch - 1).wait()

        def one(j, carry):
            cols = pl.ds(pl.multiple_of(j * 256, 256), 256)
            low_t_buf[cols, :] = jnp.transpose(low[lax.rem(ch, 2), :, cols])
            return carry

        lax.fori_loop(0, full // 256, one, 0, unroll=2)
        tr_copy(ch).start()

    def project_one(ch, k, h0, h1):
        at = pl.ds(pl.multiple_of(ch * span + h0 * part, part), (h1 - h0) * part)
        ref = (cand, forget, gate)[k]
        ref[at, :] = jnp.dot(low[lax.rem(ch, 2), h0 * part : h1 * part], w_buf[k], preferred_element_type=F32)

    def send_across(ch):
        for copy in token_copies(ch, 0, blocks, x_move):
            copy.start()

    def send_last():
        for h in range(blocks):
            for copy in token_copies(chunks - 1, h, h + 1, x_move):
                copy.start()

    def gates(b, carry):
        a_list, b_list = list(carry[0]), list(carry[1])
        at = pl.ds(pl.multiple_of(b * part, part), part)
        mask = keep_mask[at, :]
        for j in range(tiles):
            cols = lanes(j)
            nrm = normed(at, j)
            f = sigmoid(forget[at, cols] + mix_f[0:1, cols] * nrm + bias_f[0:1, cols])
            o = sigmoid(gate[at, cols] + mix_r[0:1, cols] * nrm + bias_r[0:1, cols])
            forget[at, cols] = f
            gate[at, cols] = o
            inject = (1.0 - f) * cand[at, cols]
            keep = f * mask
            for t in range(BLOCK):
                now = slice(t * rows, (t + 1) * rows)
                a_list[j] = a_list[j] * keep[now]
                b_list[j] = b_list[j] * keep[now] + inject[now]
        return tuple(a_list), tuple(b_list)

    def gather_step(ch, runs, h0=0, h1=blocks):
        entire = h1 - h0 == blocks
        if entire:
            pl.when(ch + 2 < chunks - 1)(lambda: send_across(ch + 2))
            pl.when(ch + 2 == chunks - 1)(send_last)
            cot_copy(ch + 1).start()

        base = pl.multiple_of(ch * span, span)
        slot = lax.rem(ch, 2)

        arrived(ch, across, h0, h1, x_move).wait_recv()
        d_copy(ch, h0, h1).start()

        if entire:
            pl.when(ch >= 1)(lambda: project_one(ch - 1, 2, 0, blocks))
        elif h0 == 0:
            project_one(ch - 1, 2, 0, blocks)
        else:
            project_one(ch, 2, 0, h0)
        if h0 == 0:
            runs = lax.fori_loop(jnp.maximum(ch - 1, 0) * blocks, ch * blocks, gates, runs)
        else:
            runs = lax.fori_loop(ch * blocks, ch * blocks + h0, gates, runs)

        if h0 == 0:
            cot_copy(ch).wait()
            for h in range(blocks):
                for j in range(tiles):
                    v = cot_raw[slot, :, h * BLOCK : (h + 1) * BLOCK, lanes(j)].astype(F32).reshape(part, LANE)
                    at = pl.ds(pl.multiple_of(base + h * part, part), part)
                    cot[at, lanes(j)] = swapped(v, rows, BLOCK).astype(BF16)
        if entire:

            @pl.when(ch == 0)
            def _():
                own_move(all_tokens, all_tokens, 0).wait()
                s_move(all_tokens, all_tokens, 0).wait_recv()
                for copy in w_copies:
                    copy.wait()

        d_copy(ch, h0, h1).wait_recv()

        first = pl.multiple_of(ch * chan_count * span, span)

        def tokens_at(block, r, h, cols):
            at = pl.multiple_of(first + block * span + h * part + r * BLOCK, BLOCK)
            return raw[pl.ds(at, BLOCK), cols].astype(F32)

        def each(i, turn):
            r, h = lax.rem(i, rows), h0 + i // rows
            totals = [jnp.zeros((BLOCK, LANE), F32) for _ in range(chan_count)]
            for j in range(tiles):
                for b in range(chan_count):
                    totals[b] = totals[b] + turn(tokens_at(b, r, h, lanes(j)))
            while len(totals) > 1:
                totals = [a + b for a, b in zip(totals[::2], totals[1::2])]
            part_s[h, r] = totals[0]

        def sum_rows(i, carry):
            each(i, lambda v: v)
            return carry

        count = (h1 - h0) * rows
        stat = (h1 - h0,) + mean_s.shape[1:]
        lax.fori_loop(0, count, sum_rows, 0, unroll=2)
        total = jnp.sum(part_s[h0:h1], axis=-1, keepdims=True)
        mean_s[h0:h1] = jnp.broadcast_to(total * (1.0 / full), stat)

        def square_rows(i, carry):
            m = mean_s[h0 + i // rows, lax.rem(i, rows)]
            each(i, lambda v: (v - m) * (v - m))
            return carry

        lax.fori_loop(0, count, square_rows, 0, unroll=2)
        var = jnp.sum(part_s[h0:h1], axis=-1, keepdims=True) * (1.0 / full)
        inv_s[h0:h1] = jnp.broadcast_to(lax.rsqrt(var + EPSILON), stat)

        for h in range(h0, h1):
            mean_h = mean_s[h].reshape(part, LANE)
            inv_h = inv_s[h].reshape(part, LANE)

            def normalize(j, carry, h=h, mean_h=mean_h, inv_h=inv_h):
                cols = pl.ds(pl.multiple_of(j * LANE, LANE), LANE)
                inner = pl.ds(pl.multiple_of(lax.rem(j, tiles) * LANE, LANE), LANE)
                v = jnp.concatenate([tokens_at(j // tiles, r, h, inner) for r in range(rows)], axis=0)
                v = (v - mean_h) * inv_h * gain[0:1, cols] + shift[0:1, cols]
                low[slot, h * part : (h + 1) * part, cols] = swapped(v, rows, BLOCK).astype(BF16)
                return carry

            lax.fori_loop(0, full // LANE, normalize, 0, unroll=2)
            at = pl.ds(pl.multiple_of(base + h * part, part), part)
            mean[at, :] = swapped(mean_h, rows, BLOCK)
            inv[at, :] = swapped(inv_h, rows, BLOCK)
            for j in range(tiles):
                v = jnp.concatenate([tokens_at(chan, r, h, lanes(j)) for r in range(rows)], axis=0)
                own_tok[at, lanes(j)] = swapped(v, rows, BLOCK).astype(BF16)

        project_one(ch, 0, h0, h1)
        project_one(ch, 1, h0, h1)
        if entire:
            flip(ch)
        return runs

    ones = tuple(jnp.ones((rows, LANE), F32) for _ in range(tiles))
    zeros = tuple(jnp.zeros((rows, LANE), F32) for _ in range(tiles))
    runs = lax.fori_loop(0, chunks - 1, gather_step, (ones, zeros))
    for h in range(blocks):
        runs = gather_step(chunks - 1, runs, h, h + 1)
    project_one(chunks - 1, 2, blocks - 1, blocks)
    a_run, b_run = lax.fori_loop(chunks * blocks - 1, chunks * blocks, gates, runs)

    spans = jnp.where(reset_rows[0] >= tm_count * steps, 1.0, 0.0)
    last_tm = tm_count - 1

    def spanning(v):
        return jnp.sum(v * spans, axis=0, keepdims=True)

    def near_copy(way, target):
        return remote(near.at[way, 0], near.at[way, 1], near_send.at[way], near_recv.at[way], (target, chan))

    def far_copy(way, source, target):
        return remote(
            far.at[way, source], far.at[way, source], far_send.at[way], far_recv.at[way], (target, chan)
        )

    def far_all(way):
        maps = far.at[way, pl.ds(0, tm_count - 1)]
        return remote(maps, maps, far_send.at[way], far_recv.at[way], (tm, sibling))

    def last_copy(target):
        return remote(near.at[0, 0], near.at[0, 2], last_send, last_recv, (target, chan))

    def last_all():
        sent = sum_rx.at[pl.ds(0, tm_count - 1)]
        remote(sent, sent, last_send, last_recv, (tm, sibling)).wait_send()

    def sum_copy(source, target):
        return remote(sum_rx.at[source], sum_rx.at[source], sum_send, sum_recv, (target, chan))

    def peers(act_on):
        def one(d, carry):
            act_on(lax.rem(tm + d, tm_count))
            return carry

        lax.fori_loop(1, tm_count, one, 0)

    for j in range(tiles):
        near[0, 0, :, lanes(j)] = b_run[j]
        far[0, tm, j : j + 1, :] = spanning(a_run[j])
        far[0, tm, tiles + j : tiles + j + 1, :] = spanning(b_run[j])
    pl.when(tm < last_tm)(lambda: near_copy(0, tm + 1).start())
    peers(lambda p: far_copy(0, tm, p).start())
    pl.when(tm == last_tm)(lambda: peers(lambda p: last_copy(p).start()))
    flip(chunks - 1)
    far_all(0).wait_recv()
    pl.when(tm > 0)(lambda: near_copy(0, tm).wait_recv())

    def carry_on(d, carry):
        state, here = carry
        here = jnp.where(d == tm, state, here)
        return far[0, d, 0:tiles, :] * state + far[0, d, tiles : 2 * tiles, :], here

    lead = jnp.concatenate([spanning(entry[:, lanes(j)]) for j in range(tiles)], axis=0)
    last, here = lax.fori_loop(0, tm_count, carry_on, (lead, lead))
    states = []
    for j in range(tiles):
        row = jnp.broadcast_to(here[j : j + 1], (rows, LANE))
        others = jnp.where(tm == 0, entry[:, lanes(j)], near[0, 1, :, lanes(j)])
        states.append(jnp.where(spans > 0, row, others))
    tr_copy(chunks - 1).wait()
    low_copy(0).start()

    def forward(b, states):
        states = list(states)
        at = pl.ds(pl.multiple_of(b * part, part), part)
        mask = keep_mask[at, :]
        for j in range(tiles):
            cols = lanes(j)
            f = forget[at, cols]
            inject = (1.0 - f) * cand[at, cols]
            before, after = [], []
            c = states[j]
            for t in range(BLOCK):
                now = slice(t * rows, (t + 1) * rows)
                c = c * mask[now]
                before.append(c)
                c = f[now] * c + inject[now]
                after.append(c)
            states[j] = c
            masked[at, cols] = jnp.concatenate(before, axis=0)
            th = jnp.tanh(jnp.concatenate(after, axis=0))
            o = gate[at, cols]
            gate_grad = cot[at, cols].astype(F32) * (th - own_tok[at, cols].astype(F32))
            grad_buf[2, at, cols] = (gate_grad * o * (1.0 - o)).astype(BF16)
        return tuple(states)

    lax.fori_loop(0, steps // BLOCK, forward, tuple(states))

    def start_later():
        flow[0] = jnp.ones((rows, width), F32)
        flow[1] = jnp.zeros((rows, width), F32)

    def later(b, carry):
        at = pl.ds(pl.multiple_of(b * part, part), part)
        mask = keep_mask[at, :]
        for j in range(tiles):
            cols = lanes(j)
            f = forget[at, cols]
            th = jnp.tanh(f * masked[at, cols] + (1.0 - f) * cand[at, cols])
            o = gate[at, cols]
            direct = cot[at, cols].astype(F32) * o * (1.0 - th * th)
            side[at, cols] = o.astype(BF16)
            gate[at, cols] = direct
            keep = f * mask
            run, total = flow[0, :, cols], flow[1, :, cols]
            for t in range(BLOCK):
                now = slice(t * rows, (t + 1) * rows)
                run = run * keep[now]
                total = total + run * direct[now]
            flow[0, :, cols], flow[1, :, cols] = run, total
        return carry

    def output(b, carry):
        ch, h = b // blocks, lax.rem(b, blocks)
        slot = lax.rem(ch, 2)

        @pl.when(both(h == 0, ch >= 2))
        def _():
            act_copy(ch - 2).wait()

        at = pl.ds(pl.multiple_of(b * part, part), part)
        t0 = pl.multiple_of(h * BLOCK, BLOCK)
        for j in range(tiles):
            cols = lanes(j)
            f = forget[at, cols]
            th = jnp.tanh(f * masked[at, cols] + (1.0 - f) * cand[at, cols])
            o = side[at, cols].astype(F32)
            rest = 1.0 - o
            out = swapped(o * th + rest * own_tok[at, cols].astype(F32), BLOCK, rows).astype(BF16)
            act_buf[slot, :, pl.ds(t0, BLOCK), cols] = out.reshape(rows, BLOCK, LANE)
            side[at, cols] = (cot[at, cols].astype(F32) * rest).astype(BF16)

        @pl.when(h == blocks - 1)
        def _():
            act_copy(ch).start()

        return carry

    def end_output():
        for target in (sibling, across):
            pl.semaphore_signal(ready_sem, inc=1, device_id=(tm, target), device_id_type=MESH)

    def end_later():
        near[1, 0] = flow[1]
        for j in range(tiles):
            far[1, tm, j : j + 1, :] = spanning(flow[1, :, lanes(j)])
        pl.when(tm > 0)(lambda: near_copy(1, tm - 1).start())
        peers(lambda p: far_copy(1, tm, p).start())
        more[...] = jnp.zeros_like(more)

    remote(all_tokens, all_tokens, d_send, d_recv.at[0], (tm, sibling)).wait_send()

    n = tm_count // 2
    o, y = tm // 2, lax.rem(tm, 2)
    partner = (o * 2 + 1 - y, chan)
    left = ((o - 1) * 2 + y, chan)
    right = ((o + 1) * 2 + y, chan)
    ring = ring_of(tm_count)
    ends, middle = (0, n - 1), (n // 2 - 1, n // 2)
    lines = [(0, middle[0] + y, n // 2, 1, None)]
    for l in (1, 2):
        if n == 4:
            lines += [(l, ends[l - 1], n - 1, 0, 0), (l, middle[l - 1], n // 2, 0, 1)]
        else:
            lines += [(l, middle[l - 1], n // 2, 0, None)]
    give_stage = 2 * (n // 2) + 2
    depth = LAG * max([give_stage] + [first + reach + (l > 0) + reach for l, c, reach, first, parity in lines])
    space = -(-depth // ring)

    def stage(s, number, parity=None):
        v = s - LAG * number
        u = v if space == 1 else v // space
        go = both(v >= 0, u < units)
        if space > 1:
            go = both(go, lax.rem(v, space) == 0)
        return u, go if parity is None else both(go, lax.rem(u, 2) == parity)

    def gate_of(u):
        return lax.rem(u // per_gate + 2, 3)

    def piece_of(l, mate=False):
        if l == 0:
            return (1 - y if mate else y) * PAIR, PAIR
        return 2 * PAIR + (l - 1) * LINE, LINE

    def wg_rows(l, u, mate=False):
        start, size = piece_of(l, mate)
        return pl.ds(pl.multiple_of(u * UNIT + start, 16), size)

    def fin_at(l, u):
        start, size = piece_of(l)
        return fin.at[pl.ds(pl.multiple_of((gate_of(u) * per_gate + lax.rem(u, per_gate)) * UNIT + start, 16), size)]

    def rx_rows(u, place, l):
        start = place * PAIR if l == 0 else 3 * PAIR + (place - 3) * LINE
        size = PAIR if l == 0 else LINE
        return pl.ds(pl.multiple_of(lax.rem(u, ring) * (3 * PAIR + 4 * LINE) + start, 16), size)

    def arrival(l, c, column, way, u):
        if l == 0:
            return 1 + way
        if l == 1:
            other = 6
        elif n == 4:
            other = jnp.where(column == jnp.where(lax.rem(u, 2) == 0, ends[0], middle[0]), 6, 3)
        else:
            other = jnp.where(column == middle[0], 6, 3)
        return jnp.where(column == c, 3 + way, other)

    def launch(make, u):
        @pl.when(u >= SENDS)
        def _():
            make(u - SENDS).wait_send()

        make(u).start()

    def to_rx(src, u, place, l, sem, target):
        return remote(src, rx.at[rx_rows(u, place, l)], sem, rx_recv.at[lax.rem(u, ring), place], target)

    def pair_copy(u):
        return to_rx(raw.at[wg_rows(0, u, True)], u, 0, 0, pair_send.at[lax.rem(u, SENDS)], partner)

    def red_copy(l, c, u, to_right):
        way, column = (0, o + 1) if to_right else (1, o - 1)
        return to_rx(
            raw.at[wg_rows(l, u)], u, arrival(l, c, column, way, u), l, red_send.at[l, lax.rem(u, SENDS)],
            right if to_right else left,
        )

    def red_wait(l, c, u, way):
        place = arrival(l, c, o, way, u)
        at = rx_rows(u, place, l)
        to_rx(rx.at[at], u, place, l, red_send.at[l, 0], partner).wait_recv()
        return rx[at].astype(F32)

    def bc_copy(l, u, to_right, src):
        return remote(
            src, fin_at(l, u), bc_send.at[l, lax.rem(u, SENDS), 1 if to_right else 0], bc_recv.at[l, lax.rem(u, ring)],
            right if to_right else left,
        )

    def swap_copy(l, u):
        return to_rx(raw.at[wg_rows(l, u)], u, 5, l, swap_send.at[lax.rem(u, SENDS)], partner)

    def give_copy(u, src):
        return remote(src, fin_at(0, u), give_send.at[lax.rem(u, SENDS)], give_recv.at[lax.rem(u, ring)], partner)

    def local_copy(l, u):
        return pltpu.make_async_copy(raw.at[wg_rows(l, u)], fin_at(l, u), loc_sem.at[l, lax.rem(u, SENDS)])

    def add_to(l, u, *others):
        at = wg_rows(l, u)
        total = raw[at].astype(F32)
        for v in others:
            total = total + v
        raw[at] = total.astype(BF16)

    def red_start(l, c, u):
        pl.when(o < c)(lambda: launch(lambda v: red_copy(l, c, v, True), u))
        pl.when(o > c)(lambda: launch(lambda v: red_copy(l, c, v, False), u))

    def publish(l, u):
        @pl.when(u >= SENDS)
        def _():
            local_copy(l, u - SENDS).wait()

        local_copy(l, u).start()
        pl.when(o > 0)(lambda: launch(lambda v: bc_copy(l, v, False, raw.at[wg_rows(l, v)]), u))
        pl.when(o < n - 1)(lambda: launch(lambda v: bc_copy(l, v, True, raw.at[wg_rows(l, v)]), u))
        if l == 0:
            launch(lambda v: give_copy(v, raw.at[wg_rows(0, v)]), u)

    def block_cols(c):
        return pl.ds(pl.multiple_of(c * width, width), width)

    def sib_rows(ch, q):
        return pl.ds(pl.multiple_of(units * UNIT + (lax.rem(ch, 4) * 2 + q) * span, span), span)

    def sib_copy(ch, q):
        slot = lax.rem(ch, 2)
        cols = sibling if q == 0 else lax.rem(sibling + 2, 4)
        return remote(
            terms.at[slot, cols], raw.at[sib_rows(ch, q)], sib_send.at[q], sib_recv.at[lax.rem(ch, 4), q], (tm, sibling)
        )

    def acr_copy(ch):
        return remote(
            terms.at[lax.rem(ch, 2), across], cot.at[rows_of(ch)], acr_send.at[lax.rem(ch, 2)], acr_recv.at[ch], (tm, across)
        )

    def row_copy(ch, source, d):
        return remote(
            row_rx.at[ch, source], row_rx.at[ch, source], row_send.at[lax.rem(ch, 4)], row_recv.at[lax.rem(ch, 4)],
            (tm, lax.rem(chan + d, 4)),
        )

    def row_all(ch):
        sums = row_rx.at[ch, pl.ds(0, chan_count - 1)]
        return remote(sums, sums, row_send.at[lax.rem(ch, 4)], row_recv.at[lax.rem(ch, 4)], (tm, sibling))

    def out_copy(ch):
        at = pl.ds(pl.multiple_of(ch * CHUNK, CHUNK), CHUNK)
        return pltpu.make_async_copy(out_buf.at[lax.rem(ch, 2)], in_grad.at[:, at, :], out_sem.at[lax.rem(ch, 2)])

    def project(ch):
        at = rows_of(ch)
        slot = lax.rem(ch, 2)

        @pl.when(ch == 0)
        def _():
            pl.semaphore_wait(ready_sem, 2)

        @pl.when(ch >= 2)
        def _():
            acr_copy(ch - 2).wait_send()

        for b in range(chan_count):
            total = jnp.zeros((span, width), F32)
            for k in range(3):
                total = total + lax.dot_general(
                    grad_buf[k, at, :], w_buf[k, b * width : (b + 1) * width, :], (((1,), (1,)), ((), ())),
                    preferred_element_type=F32,
                )
            terms[slot, b] = total.astype(BF16)
        sib_copy(ch, 0).start()
        sib_copy(ch, 1).start()

    def chip_sum(ch):
        slot = lax.rem(ch, 2)
        for q in range(2):
            sib_copy(ch, q).wait_recv()
        there = terms[slot, across].astype(F32) + raw[sib_rows(ch, 1)].astype(F32)
        terms[slot, across] = there.astype(BF16)
        acr_copy(ch).start()
        here = terms[slot, chan].astype(F32) + raw[sib_rows(ch, 0)].astype(F32)
        cand[rows_of(ch), :] = here
        for q in range(2):
            sib_copy(ch, q).wait_send()

    def full_sum(ch):
        acr_copy(ch).wait_recv()
        at = rows_of(ch)
        total = jnp.zeros((8, span), F32)
        pick = lax.broadcasted_iota(jnp.int32, (8, LANE), 0)
        for j in range(tiles):
            cols = lanes(j)
            fp, rp = grad_buf[1, at, cols].astype(F32), grad_buf[2, at, cols].astype(F32)
            g = cand[at, cols] + cot[at, cols].astype(F32) + fp * mix_f[0:1, cols] + rp * mix_r[0:1, cols]
            cand[at, cols] = g
            h = hat(at, j)
            nrm = h * mine(gain, j) + mine(shift, j)
            weighted = g * h
            for i, v in enumerate((fp * nrm, rp * nrm, fp, rp, weighted, g)):
                more[i, :, cols] = more[i, :, cols] + jnp.sum(v.reshape(CHUNK, rows, LANE), axis=0)
            for i, v in enumerate((g * mine(gain, j), weighted * mine(gain, j))):
                lead = jnp.where(pick == i, 1.0, 0.0).astype(BF16)
                high = v.astype(BF16)
                low_part = (v - high.astype(F32)).astype(BF16)
                for p in (high, low_part):
                    total = total + lax.dot_general(lead, p, (((1,), (1,)), ((), ())), preferred_element_type=F32)
        row_rx[ch, chan] = total
        pl.when(ch >= 4)(lambda: row_all(ch - 4).wait_send())
        for d in range(1, 4):
            row_copy(ch, chan, d).start()

    def finish(ch):
        row_all(ch).wait_recv()

        @pl.when(ch >= 2)
        def _():
            out_copy(ch - 2).wait()

        at = rows_of(ch)
        total = (row_rx[ch, 0] + row_rx[ch, 1] + row_rx[ch, 2] + row_rx[ch, 3]) * (1.0 / full)
        columns = jnp.transpose(total)
        first = jnp.broadcast_to(columns[:, 0:1], (span, LANE))
        second = jnp.broadcast_to(columns[:, 1:2], (span, LANE))
        for j in range(tiles):
            cols = lanes(j)
            g = cand[at, cols] * mine(gain, j)
            v = inv[at, :] * (g - first - hat(at, j) * second) + side[at, cols].astype(F32)
            out_buf[lax.rem(ch, 2), :, :, cols] = swapped(v, CHUNK, rows).astype(BF16).reshape(rows, CHUNK, LANE)
        out_copy(ch).start()

    def share_sums():
        for i in range(6):
            sum_rx[tm, i : i + 1, :] = jnp.sum(more[i], axis=0, keepdims=True)
        sum_rx[tm, 6:8, :] = jnp.zeros((2, width), F32)
        peers(lambda p: sum_copy(tm, p).start())

    def start_backward():
        far_all(1).wait_recv()
        pl.when(tm < last_tm)(lambda: near_copy(1, tm).wait_recv())

        def carry_back(i, v):
            d = tm_count - 1 - i
            return jnp.where(d > tm, far[0, d, 0:tiles, :] * v + far[1, d, 0:tiles, :], v)

        inflow = lax.fori_loop(0, tm_count, carry_back, jnp.zeros((tiles, LANE), F32))
        for j in range(tiles):
            row = jnp.broadcast_to(inflow[j : j + 1], (rows, LANE))
            others = jnp.where(tm == last_tm, 0.0, near[1, 1, :, lanes(j)])
            flow[0, :, lanes(j)] = jnp.where(spans > 0, row, others)

    def backward(i, carry):
        b = steps // BLOCK - 1 - i
        at = pl.ds(pl.multiple_of(b * part, part), part)
        mask = keep_mask[at, :]
        for j in range(tiles):
            cols = lanes(j)
            f = forget[at, cols]
            keep = f * mask
            direct = gate[at, cols]
            g = flow[0, :, cols]
            adjoint = [None] * BLOCK
            for t in reversed(range(BLOCK)):
                now = slice(t * rows, (t + 1) * rows)
                adjoint[t] = direct[now] + g
                g = keep[now] * adjoint[t]
            flow[0, :, cols] = g
            cand_grad = jnp.concatenate(adjoint, axis=0) * (1.0 - f)
            forget_pre = cand_grad * (masked[at, cols] - cand[at, cols]) * f
            grad_buf[0, at, cols] = cand_grad.astype(BF16)
            grad_buf[1, at, cols] = forget_pre.astype(BF16)
        return carry

    def close_first():
        x_move(all_tokens, all_tokens, 0).wait_send()
        s_move(all_tokens, all_tokens, 0).wait_send()
        for way in range(2):
            far_all(way).wait_send()
        pl.when(tm < last_tm)(lambda: near_copy(0, tm).wait_send())
        pl.when(tm > 0)(lambda: near_copy(1, tm).wait_send())
        pl.when(tm == last_tm)(last_all)
        pl.when(tm != last_tm)(lambda: last_copy(tm).wait_recv())
        for ch in (chunks - 2, chunks - 1):
            act_copy(ch).wait()
        for j in range(tiles):
            row = jnp.broadcast_to(last[j : j + 1], (rows, LANE))
            others = jnp.where(tm == last_tm, near[0, 0, :, lanes(j)], near[0, 2, :, lanes(j)])
            final[:, lanes(j)] = jnp.where(spans > 0, row, others)

    def close_second():
        for ch in range(chunks - 4, chunks):
            row_all(ch).wait_send()
        for ch in (chunks - 2, chunks - 1):
            out_copy(ch).wait()
            acr_copy(ch).wait_send()
        sums = sum_rx.at[pl.ds(0, tm_count - 1)]
        remote(sums, sums, sum_send, sum_recv, (tm, sibling)).wait()
        totals[...] = lax.fori_loop(0, tm_count, lambda d, v: v + sum_rx[d], jnp.zeros(totals.shape, F32))

    def slot_step(s, carry):
        u, go = stage(s, give_stage)
        pl.when(go)(lambda: give_copy(u, raw.at[wg_rows(0, u)]).wait_recv())

        for l, c, reach, first, parity in lines:
            late = first + reach + (1 if l else 0)
            u, go = stage(s, late + jnp.abs(o - c), parity)

            @pl.when(both(o != c, go))
            def _(l=l, c=c, u=u):
                bc_copy(l, u, True, fin_at(l, u)).wait_recv()
                pl.when(both(o < c, o > 0))(lambda: launch(lambda v: bc_copy(l, v, False, fin_at(l, v)), u))
                pl.when(both(o > c, o < n - 1))(lambda: launch(lambda v: bc_copy(l, v, True, fin_at(l, v)), u))
                if l == 0:
                    launch(lambda v: give_copy(v, fin_at(0, v)), u)

        for l, c, reach, first, parity in lines[1:]:
            u, go = stage(s, reach + 1, parity)

            @pl.when(both(o == c, go))
            def _(l=l, u=u):
                swap_copy(l, u).wait()
                add_to(l, u, rx[rx_rows(u, 5, l)].astype(F32))
                publish(l, u)

        for l, c, reach, first, parity in lines:
            u, go = stage(s, first + reach, parity)

            @pl.when(both(o == c, go))
            def _(l=l, c=c, u=u):
                if l == 0 and n > 2:
                    add_to(l, u, red_wait(l, c, u, 0), red_wait(l, c, u, 1))
                elif l > 0 and 0 < c < n - 1:
                    add_to(l, u, red_wait(l, c, u, 0), red_wait(l, c, u, 1))
                else:
                    pl.when(o > 0)(lambda: add_to(l, u, red_wait(l, c, u, 0)))
                    pl.when(o < n - 1)(lambda: add_to(l, u, red_wait(l, c, u, 1)))
                if l == 0:
                    publish(l, u)
                else:
                    swap_copy(l, u).start()

        u0, go0 = stage(s, 0)

        @pl.when(go0)
        def _():
            pl.when(u0 + 1 < units)(lambda: low_copy(u0 + 1).start())
            low_copy(u0).wait()
            g = jnp.dot(low[lax.rem(u0, 2)], grad_buf[gate_of(u0)], preferred_element_type=F32)
            raw[pl.ds(pl.multiple_of(u0 * UNIT, UNIT), UNIT)] = g.astype(BF16)
            launch(pair_copy, u0)
            for l, c, reach, first, parity in lines[1:]:
                mine_now = jnp.logical_or(o == 0, o == n - 1)
                if parity is not None:
                    mine_now = both(mine_now, lax.rem(u0, 2) == parity)
                pl.when(mine_now)(lambda l=l, c=c: red_start(l, c, u0))

        for l, c, reach, first, parity in lines:
            u, go = stage(s, first + jnp.where(o < c, o, n - 1 - o), parity)

            @pl.when(both(o < c, o > 0, go))
            def _(l=l, c=c, u=u):
                add_to(l, u, red_wait(l, c, u, 0))
                launch(lambda v: red_copy(l, c, v, True), u)

            @pl.when(both(o > c, o < n - 1, go))
            def _(l=l, c=c, u=u):
                add_to(l, u, red_wait(l, c, u, 1))
                launch(lambda v: red_copy(l, c, v, False), u)

        u, go = stage(s, 1)

        @pl.when(go)
        def _():
            pair_copy(u).wait_recv()
            add_to(0, u, rx[rx_rows(u, 0, 0)].astype(F32))
            pl.when(jnp.logical_or(o == 0, o == n - 1))(lambda: red_start(0, lines[0][1], u))

        count = steps // BLOCK
        pl.when(s == 0)(start_later)
        share = -(-count // LATER)
        at = s * share

        @pl.when(s < LATER)
        def _():
            lax.fori_loop(at, jnp.minimum(at + share, count), later, 0)

        pl.when(s == LATER - 1)(end_later)
        pl.when(s == LATER + 1)(start_backward)
        share = -(-count // (OUTPUT - LATER - 1))
        at2 = (s - LATER - 1) * share

        @pl.when(both(s > LATER, s < OUTPUT))
        def _():
            lax.fori_loop(at2, jnp.minimum(at2 + share, count), backward, 0)

        share = -(-count // (FIRST - OUTPUT))
        at3 = (s - OUTPUT) * share

        @pl.when(both(s >= OUTPUT, s < FIRST))
        def _():
            lax.fori_loop(at3, jnp.minimum(at3 + share, count), output, 0)

        pl.when(s == FIRST - 1)(end_output)

        for job, offset in ((finish, 5), (full_sum, 3), (chip_sum, 1), (project, 0)):
            at = s - FIRST - offset
            pl.when(both(at >= 0, lax.rem(at, 2) == 0, at // 2 < chunks))(lambda job=job, at=at: job(at // 2))
        pl.when(s == FIRST + 3)(close_first)
        pl.when(s == FIRST + 2 * chunks + 2)(share_sums)
        pl.when(s == FIRST + 2 * chunks + 6)(close_second)
        return carry

    slots = max((units - 1) * space + depth + 1, FIRST + 2 * chunks + 7)
    lax.fori_loop(0, slots, slot_step, 0)

    def close_unit(u, carry):
        give_copy(u, raw.at[wg_rows(0, u)]).wait_send()
        pair_copy(u).wait_send()
        for l, c, reach, first, parity in lines:

            @pl.when(True if parity is None else lax.rem(u, 2) == parity)
            def _(l=l, c=c):
                src = raw.at[wg_rows(l, u)]
                pl.when(o != c)(lambda: red_copy(l, c, u, True).wait_send())
                pl.when(o == c)(lambda: local_copy(l, u).wait())
                pl.when(both(o <= c, o > 0))(lambda: bc_copy(l, u, False, src).wait_send())
                pl.when(both(o >= c, o < n - 1))(lambda: bc_copy(l, u, True, src).wait_send())

        return carry

    lax.fori_loop(units - SENDS, units, close_unit, 0)


def layer(tokens, weights, cotangent, gain, shift, mix_f, mix_r, bias_f, bias_r, bank, selector, resets):
    rows, steps, width = tokens.shape
    full = gain.shape[-1]
    tm_count, chan_count = lax.axis_size("tm"), lax.axis_size("chan")
    chunks = steps // CHUNK
    span = CHUNK * rows
    pieces = chunks - 1 + CHUNK // BLOCK
    count = steps * rows
    units = 3 * full // UNIT
    ring = ring_of(tm_count)
    hbm = pl.BlockSpec(memory_space=pl.ANY)
    vmem = pl.BlockSpec(memory_space=pltpu.VMEM)
    smem = pl.BlockSpec(memory_space=pltpu.SMEM)
    dma = pltpu.SemaphoreType.DMA
    stat = pltpu.VMEM((CHUNK // BLOCK, rows, BLOCK, LANE), F32)
    wide = pltpu.VMEM((count, width), F32)
    narrow = pltpu.VMEM((count, LANE), F32)
    short = pltpu.VMEM((count, width), BF16)
    return pl.pallas_call(
        layer_kernel,
        out_shape=(
            jax.ShapeDtypeStruct((units * UNIT, width), BF16),
            jax.ShapeDtypeStruct(tokens.shape, BF16),
            jax.ShapeDtypeStruct(tokens.shape, BF16),
            jax.ShapeDtypeStruct((full, count), BF16),
            jax.ShapeDtypeStruct((rows, width), F32),
            jax.ShapeDtypeStruct((8, width), F32),
        ),
        in_specs=[hbm, hbm, hbm] + [vmem] * 7 + [smem, vmem],
        out_specs=(hbm, hbm, hbm, hbm, vmem, vmem),
        scratch_shapes=[
            pltpu.VMEM((chunks * chan_count * span, width), BF16),
            pltpu.VMEM((ring * (3 * PAIR + 4 * LINE), width), BF16),
            pltpu.VMEM((2, span, full), BF16),
            pltpu.VMEM((full, span), BF16),
            pltpu.VMEM((3, full, width), BF16),
            wide, wide, wide, wide,
            short,
            pltpu.VMEM((2, rows, CHUNK, width), BF16),
            short,
            narrow, narrow, narrow,
            pltpu.VMEM((3, count, width), BF16),
            pltpu.VMEM((2, rows, CHUNK, width), BF16),
            short,
            pltpu.VMEM((2, chan_count, span, width), BF16),
            pltpu.VMEM((2, rows, CHUNK, width), BF16),
            pltpu.VMEM((chunks, 4, 8, span), F32),
            pltpu.VMEM((6, rows, width), F32),
            pltpu.VMEM((tm_count, 8, width), F32),
            stat, stat, stat,
            pltpu.VMEM((rows, width), F32),
            pltpu.VMEM((2, 3, rows, width), F32),
            pltpu.VMEM((2, tm_count, 8, LANE), F32),
            pltpu.VMEM((2, rows, width), F32),
            pltpu.VMEM((resets.shape[1], rows, LANE), jnp.int32),
            dma(()), dma((pieces,)), dma(()), dma(()), dma(()), dma((pieces,)), dma(()),
            dma((3,)), dma((2,)), dma((2,)), dma(()), dma((2,)),
            dma((2,)), dma((2,)), dma((2,)), dma((2,)), dma(()), dma(()),
            pltpu.SemaphoreType.REGULAR,
            dma((2,)), dma((3, SENDS)), dma((SENDS,)), dma((3, SENDS)), dma((3, SENDS, 2)), dma((3, ring)), dma((SENDS,)),
            dma((SENDS,)), dma((ring,)), dma((ring, 7)), dma((2,)), dma((4, 2)), dma((2,)), dma((chunks,)),
            dma((4,)), dma((4,)), dma(()), dma(()),
        ],
        compiler_params=pltpu.CompilerParams(collective_id=0, has_side_effects=True, vmem_limit_bytes=VMEM_BYTES),
        name="whole",
    )(tokens, weights, cotangent, gain, shift, mix_f, mix_r, bias_f, bias_r, bank, selector, resets)


def tail_kernel(
    fin, in_grad, act, final, totals, wide_out, in_out, act_out, final_out, s0, s1, s2, s3, s4, s5,
    fin_buf, wide_buf, in_buf, in_wide, act_buf, load_sem, store_sem,
):
    def move(src, dst, sem, i, n):
        at = pl.ds(i * n, n)
        return pltpu.make_async_copy(src.at[at], dst.at[at], sem)

    jobs = []

    def job(src, buf, wide, dst, parts):
        n = src.shape[0] // parts
        for i in range(parts):
            k = len(jobs)
            jobs.append((move(src, buf, load_sem.at[k], i, n), buf, wide, i * n, n, move(wide, dst, store_sem.at[k], i, n)))

    job(fin, fin_buf, wide_buf, wide_out, TAIL)
    job(in_grad, in_buf, in_wide, in_out, 2)
    job(act, act_buf, act_buf, act_out, 2)
    order = [0, 4, 1, 6, 2, 5, 3, 7] if TAIL == 4 else list(range(len(jobs)))
    for k in order:
        jobs[k][0].start()
    final_out[...] = final[...]
    for i, ref in enumerate((s0, s1, s2, s3, s4, s5)):
        ref[...] = totals[i : i + 1, :]
    for k in order:
        load, buf, wide, start, n, store = jobs[k]
        load.wait()
        if buf is not wide:
            step = 64 if len(buf.shape) == 2 else 1

            def cast(j, carry, buf=buf, wide=wide, start=start, step=step):
                at = pl.ds(start + j * step, step)
                wide[at] = buf[at].astype(F32)
                return carry

            lax.fori_loop(0, n // step, cast, 0, unroll=2)
        store.start()
    for k in order:
        jobs[k][-1].wait()


def tail(fin, in_grad, act, final, totals):
    width = fin.shape[-1]
    hbm = pl.BlockSpec(memory_space=pl.ANY)
    vmem = pl.BlockSpec(memory_space=pltpu.VMEM)
    dma = pltpu.SemaphoreType.DMA
    line = jax.ShapeDtypeStruct((1, width), F32)
    return pl.pallas_call(
        tail_kernel,
        out_shape=(
            jax.ShapeDtypeStruct(fin.shape, F32),
            jax.ShapeDtypeStruct(in_grad.shape, F32),
            jax.ShapeDtypeStruct(act.shape, BF16),
            jax.ShapeDtypeStruct(final.shape, F32),
        ) + (line,) * 6,
        in_specs=[hbm] * 3 + [vmem] * 2,
        out_specs=(hbm,) * 3 + (vmem,) * 7,
        scratch_shapes=[
            pltpu.VMEM(fin.shape, BF16), pltpu.VMEM(fin.shape, F32),
            pltpu.VMEM(in_grad.shape, BF16), pltpu.VMEM(in_grad.shape, F32), pltpu.VMEM(act.shape, BF16),
            dma((TAIL + 4,)), dma((TAIL + 4,)),
        ],
        compiler_params=pltpu.CompilerParams(vmem_limit_bytes=VMEM_BYTES),
        name="tail",
    )(fin, in_grad, act, final, totals)


def body(
    tokens, ln_gain, ln_bias, weights, mix_forget, mix_reset, bias_forget, bias_reset, state_bank, selector, resets, cotangent
):
    fin, in_grad, act, _, final, totals = layer(
        tokens, weights, cotangent, ln_gain[None], ln_bias[None], mix_forget[None], mix_reset[None], bias_forget[None],
        bias_reset[None], state_bank, selector, resets,
    )
    wide, in_grad, act, final, *sums = tail(fin, in_grad, act, final, totals)
    sums = [v[0] for v in sums]
    return act, final, in_grad, wide.reshape(weights.shape), sums[4], sums[5], sums[0], sums[1], sums[2], sums[3]


def solution(mesh):
    placed = (
        P(None, "tm", "chan"), P(), P(), P(None, None, "chan"), P("chan"), P("chan"), P("chan"), P("chan"),
        P(None, "chan"), P(), P(), P(None, "tm", "chan"),
    )
    return jax.shard_map(
        body,
        mesh=mesh,
        in_specs=placed,
        out_specs=(
            P(None, "tm", "chan"), P(None, "chan"), P(None, "tm", "chan"), P(None, None, "chan"),
            P("chan"), P("chan"), P("chan"), P("chan"), P("chan"), P("chan"),
        ),
        check_vma=False,
    )
```

```python
import jax
import jax.numpy as jnp
from jax import lax
from jax.experimental import pallas as pl
from jax.experimental.pallas import tpu as pltpu
from jax.sharding import PartitionSpec as P

EPSILON = 1e-05
CHUNK = 32
BLOCK = 16
LANE = 128
AHEAD = 4
UNIT = 256
LAG = 2
PAIR = 80
LINE = 48
SENDS = 2
VMEM_BYTES = 63 << 20
TAIL = 4
LATER = 4
OUTPUT = 8
FIRST = 12
MESH = pl.DeviceIdType.MESH
F32 = jnp.float32
BF16 = jnp.bfloat16


def sigmoid(v):
    return 1.0 / (1.0 + jnp.exp(-v))


def swapped(v, outer, inner):
    return jnp.swapaxes(v.reshape(outer, inner, v.shape[-1]), 0, 1).reshape(outer * inner, v.shape[-1])


def both(*conditions):
    out = conditions[0]
    for c in conditions[1:]:
        out = jnp.logical_and(out, c)
    return out


def ring_of(tm_count):
    return 14 if tm_count <= 8 else 3


def layer_kernel(
    tokens, weights, cotangent, gain, shift, mix_f, mix_r, bias_f, bias_r, bank, selector, resets,
    fin, in_grad, act, low_t, final, totals,
    raw, rx, low, low_t_buf, w_buf, cand, forget, gate, masked, own_tok, cot_raw, cot, mean, inv, keep_mask, grad_buf,
    act_buf, side, terms, out_buf, row_rx, more, sum_rx, mean_s, inv_s, part_s, entry, near, far, flow, reset_rows,
    x_send, x_recv, s_send, s_recv, d_send, d_recv, own_sem, w_sem, cot_sem, act_sem, tr_sem, low_sem,
    near_send, near_recv, far_send, far_recv, last_send, last_recv, ready_sem, out_sem, loc_sem, pair_send, red_send,
    bc_send, bc_recv, swap_send, give_send, give_recv, rx_recv, sib_send, sib_recv, acr_send, acr_recv, row_send,
    row_recv, sum_send, sum_recv,
):
    rows, steps, width = tokens.shape
    full = gain.shape[-1]
    tm_count, tm = lax.axis_size("tm"), lax.axis_index("tm")
    chan_count, chan = lax.axis_size("chan"), lax.axis_index("chan")
    sibling = chan + 1 - 2 * lax.rem(chan, 2)
    across = lax.rem(chan + 2, 4)
    chunks = steps // CHUNK
    span = CHUNK * rows
    part = BLOCK * rows
    tiles = width // LANE
    blocks = CHUNK // BLOCK
    units = 3 * full // UNIT
    per_gate = full // UNIT

    def remote(src, dst, send, recv, target):
        return pltpu.make_async_remote_copy(src, dst, send, recv, device_id=target, device_id_type=MESH)

    def lanes(j):
        return slice(j * LANE, (j + 1) * LANE)

    def mine(ref, j):
        return ref[0:1, pl.ds(pl.multiple_of(chan * width + j * LANE, LANE), LANE)]

    def hat(at, j):
        return (own_tok[at, lanes(j)].astype(F32) - mean[at, :]) * inv[at, :]

    def normed(at, j):
        return hat(at, j) * mine(gain, j) + mine(shift, j)

    def rows_of(ch):
        return pl.ds(pl.multiple_of(ch * span, span), span)

    def raw_rows(ch, block, h0, h1):
        return pl.ds(pl.multiple_of((ch * chan_count + block) * span + h0 * part, part), (h1 - h0) * part)

    def token_copies(ch, h0, h1, copy):
        at = [pl.ds(pl.multiple_of(ch * CHUNK + h * BLOCK, BLOCK), BLOCK) for h in range(h0, h1)]
        return [
            copy(tokens.at[:, t, :], raw.at[raw_rows(ch, chan, h, h + 1)].reshape(rows, BLOCK, width), ch + h0)
            for h, t in zip(range(h0, h1), at)
        ]

    def own_move(src, dst, sem):
        return pltpu.make_async_copy(src, dst, own_sem)

    def x_move(src, dst, sem):
        return remote(src, dst, x_send, x_recv.at[sem], (tm, across))

    def s_move(src, dst, sem):
        return remote(src, dst, s_send, s_recv, (tm, sibling))

    def arrived(ch, block, h0, h1, copy):
        here = raw.at[raw_rows(ch, block, h0, h1)]
        return copy(here, here, ch + h0)

    def d_copy(ch, h0, h1):
        view = raw.at[raw_rows(ch, across, h0, h1)]
        return remote(view, view, d_send, d_recv.at[ch + h0], (tm, sibling))

    all_tokens = raw.at[pl.ds(0, steps * rows)]

    def cot_copy(ch):
        at = pl.ds(pl.multiple_of(ch * CHUNK, CHUNK), CHUNK)
        return pltpu.make_async_copy(cotangent.at[:, at, :], cot_raw.at[lax.rem(ch, 2)], cot_sem.at[lax.rem(ch, 2)])

    def act_copy(ch):
        at = pl.ds(pl.multiple_of(ch * CHUNK, CHUNK), CHUNK)
        return pltpu.make_async_copy(act_buf.at[lax.rem(ch, 2)], act.at[:, at, :], act_sem.at[lax.rem(ch, 2)])

    def tr_copy(ch):
        return pltpu.make_async_copy(low_t_buf, low_t.at[:, rows_of(ch)], tr_sem)

    def low_copy(u):
        at = pl.ds(pl.multiple_of(lax.rem(u, per_gate) * UNIT, UNIT), UNIT)
        return pltpu.make_async_copy(low_t.at[at], low.at[lax.rem(u, 2)], low_sem.at[lax.rem(u, 2)])

    w_copies = [pltpu.make_async_copy(weights.at[k], w_buf.at[k], w_sem.at[k]) for k in range(3)]

    barrier = pltpu.get_barrier_semaphore()
    for d in range(1, 4):
        pl.semaphore_signal(barrier, inc=1, device_id=(tm, lax.rem(chan + d, 4)), device_id_type=MESH)

    def greet(d, carry):
        pl.semaphore_signal(barrier, inc=1, device_id=(lax.rem(tm + d, tm_count), chan), device_id_type=MESH)
        return carry

    lax.fori_loop(1, tm_count, greet, 0)
    def start_own(ch, carry):
        for copy in token_copies(ch, 0, blocks, own_move):
            copy.start()
        return carry

    def start_sibling(ch, carry):
        for copy in token_copies(ch, 0, blocks, s_move):
            copy.start()
        return carry

    lax.fori_loop(0, chunks, start_own, 0)
    cot_copy(0).start()
    for copy in w_copies:
        copy.start()
    pl.semaphore_wait(barrier, tm_count + 2)
    for ch in range(AHEAD):
        for copy in token_copies(ch, 0, blocks, x_move):
            copy.start()
    lax.fori_loop(0, chunks, start_sibling, 0)

    count = resets.shape[1]
    for j in range(count):
        reset_rows[j] = jnp.broadcast_to(resets[:, j : j + 1], (rows, LANE))

    def mark(t, carry):
        at = tm * steps + t

        def compare(j, hit):
            return jnp.maximum(hit, jnp.where(reset_rows[j] == at, 1.0, 0.0))

        hit = lax.fori_loop(0, count, compare, jnp.zeros((rows, LANE), F32), unroll=16)
        keep_mask[pl.ds(pl.multiple_of(t * rows, rows), rows), :] = 1.0 - hit
        return carry

    lax.fori_loop(0, steps, mark, 0)
    for r in range(rows):
        entry[r : r + 1, :] = bank[pl.ds(selector[r], 1), :]

    def flip(ch):
        @pl.when(ch >= 1)
        def _():
            tr_copy(ch - 1).wait()

        def one(j, carry):
            cols = pl.ds(pl.multiple_of(j * 256, 256), 256)
            low_t_buf[cols, :] = jnp.transpose(low[lax.rem(ch, 2), :, cols])
            return carry

        lax.fori_loop(0, full // 256, one, 0, unroll=2)
        tr_copy(ch).start()

    def project_one(ch, k, h0, h1):
        at = pl.ds(pl.multiple_of(ch * span + h0 * part, part), (h1 - h0) * part)
        ref = (cand, forget, gate)[k]
        ref[at, :] = jnp.dot(low[lax.rem(ch, 2), h0 * part : h1 * part], w_buf[k], preferred_element_type=F32)

    def send_across(ch):
        for copy in token_copies(ch, 0, blocks, x_move):
            copy.start()

    def send_last():
        for h in range(blocks):
            for copy in token_copies(chunks - 1, h, h + 1, x_move):
                copy.start()

    def gates(b, carry):
        a_list, b_list = list(carry[0]), list(carry[1])
        at = pl.ds(pl.multiple_of(b * part, part), part)
        mask = keep_mask[at, :]
        for j in range(tiles):
            cols = lanes(j)
            nrm = normed(at, j)
            f = sigmoid(forget[at, cols] + mix_f[0:1, cols] * nrm + bias_f[0:1, cols])
            o = sigmoid(gate[at, cols] + mix_r[0:1, cols] * nrm + bias_r[0:1, cols])
            forget[at, cols] = f
            gate[at, cols] = o
            inject = (1.0 - f) * cand[at, cols]
            keep = f * mask
            for t in range(BLOCK):
                now = slice(t * rows, (t + 1) * rows)
                a_list[j] = a_list[j] * keep[now]
                b_list[j] = b_list[j] * keep[now] + inject[now]
        return tuple(a_list), tuple(b_list)

    def gather_step(ch, runs, h0=0, h1=blocks):
        entire = h1 - h0 == blocks
        if entire:
            pl.when(ch + AHEAD < chunks - 1)(lambda: send_across(ch + AHEAD))
            pl.when(ch + AHEAD == chunks - 1)(send_last)
            cot_copy(ch + 1).start()

        base = pl.multiple_of(ch * span, span)
        slot = lax.rem(ch, 2)

        arrived(ch, across, h0, h1, x_move).wait_recv()
        d_copy(ch, h0, h1).start()

        if entire:
            pl.when(ch >= 1)(lambda: project_one(ch - 1, 2, 0, blocks))
        elif h0 == 0:
            project_one(ch - 1, 2, 0, blocks)
        else:
            project_one(ch, 2, 0, h0)
        if h0 == 0:
            runs = lax.fori_loop(jnp.maximum(ch - 1, 0) * blocks, ch * blocks, gates, runs)
        else:
            runs = lax.fori_loop(ch * blocks, ch * blocks + h0, gates, runs)

        if h0 == 0:
            cot_copy(ch).wait()
            for h in range(blocks):
                for j in range(tiles):
                    v = cot_raw[slot, :, h * BLOCK : (h + 1) * BLOCK, lanes(j)].astype(F32).reshape(part, LANE)
                    at = pl.ds(pl.multiple_of(base + h * part, part), part)
                    cot[at, lanes(j)] = swapped(v, rows, BLOCK).astype(BF16)
        if entire:

            @pl.when(ch == 0)
            def _():
                own_move(all_tokens, all_tokens, 0).wait()
                s_move(all_tokens, all_tokens, 0).wait_recv()
                for copy in w_copies:
                    copy.wait()

        d_copy(ch, h0, h1).wait_recv()

        first = pl.multiple_of(ch * chan_count * span, span)

        def tokens_at(block, r, h, cols):
            at = pl.multiple_of(first + block * span + h * part + r * BLOCK, BLOCK)
            return raw[pl.ds(at, BLOCK), cols].astype(F32)

        def each(i, turn):
            r, h = lax.rem(i, rows), h0 + i // rows
            totals = [jnp.zeros((BLOCK, LANE), F32) for _ in range(chan_count)]
            for j in range(tiles):
                for b in range(chan_count):
                    totals[b] = totals[b] + turn(tokens_at(b, r, h, lanes(j)))
            while len(totals) > 1:
                totals = [a + b for a, b in zip(totals[::2], totals[1::2])]
            part_s[h, r] = totals[0]

        def sum_rows(i, carry):
            each(i, lambda v: v)
            return carry

        count = (h1 - h0) * rows
        stat = (h1 - h0,) + mean_s.shape[1:]
        lax.fori_loop(0, count, sum_rows, 0, unroll=2)
        total = jnp.sum(part_s[h0:h1], axis=-1, keepdims=True)
        mean_s[h0:h1] = jnp.broadcast_to(total * (1.0 / full), stat)

        def square_rows(i, carry):
            m = mean_s[h0 + i // rows, lax.rem(i, rows)]
            each(i, lambda v: (v - m) * (v - m))
            return carry

        lax.fori_loop(0, count, square_rows, 0, unroll=2)
        var = jnp.sum(part_s[h0:h1], axis=-1, keepdims=True) * (1.0 / full)
        inv_s[h0:h1] = jnp.broadcast_to(lax.rsqrt(var + EPSILON), stat)

        for h in range(h0, h1):
            mean_h = mean_s[h].reshape(part, LANE)
            inv_h = inv_s[h].reshape(part, LANE)

            def normalize(j, carry, h=h, mean_h=mean_h, inv_h=inv_h):
                cols = pl.ds(pl.multiple_of(j * LANE, LANE), LANE)
                inner = pl.ds(pl.multiple_of(lax.rem(j, tiles) * LANE, LANE), LANE)
                v = jnp.concatenate([tokens_at(j // tiles, r, h, inner) for r in range(rows)], axis=0)
                v = (v - mean_h) * inv_h * gain[0:1, cols] + shift[0:1, cols]
                low[slot, h * part : (h + 1) * part, cols] = swapped(v, rows, BLOCK).astype(BF16)
                return carry

            lax.fori_loop(0, full // LANE, normalize, 0, unroll=2)
            at = pl.ds(pl.multiple_of(base + h * part, part), part)
            mean[at, :] = swapped(mean_h, rows, BLOCK)
            inv[at, :] = swapped(inv_h, rows, BLOCK)
            for j in range(tiles):
                v = jnp.concatenate([tokens_at(chan, r, h, lanes(j)) for r in range(rows)], axis=0)
                own_tok[at, lanes(j)] = swapped(v, rows, BLOCK).astype(BF16)

        project_one(ch, 0, h0, h1)
        project_one(ch, 1, h0, h1)
        if entire:
            flip(ch)
        return runs

    ones = tuple(jnp.ones((rows, LANE), F32) for _ in range(tiles))
    zeros = tuple(jnp.zeros((rows, LANE), F32) for _ in range(tiles))
    runs = lax.fori_loop(0, chunks - 1, gather_step, (ones, zeros))
    for h in range(blocks):
        runs = gather_step(chunks - 1, runs, h, h + 1)
    project_one(chunks - 1, 2, blocks - 1, blocks)
    a_run, b_run = lax.fori_loop(chunks * blocks - 1, chunks * blocks, gates, runs)

    spans = jnp.where(reset_rows[0] >= tm_count * steps, 1.0, 0.0)
    last_tm = tm_count - 1

    def spanning(v):
        return jnp.sum(v * spans, axis=0, keepdims=True)

    def near_copy(way, target):
        return remote(near.at[way, 0], near.at[way, 1], near_send.at[way], near_recv.at[way], (target, chan))

    def far_copy(way, source, target):
        return remote(
            far.at[way, source], far.at[way, source], far_send.at[way], far_recv.at[way], (target, chan)
        )

    def far_all(way):
        maps = far.at[way, pl.ds(0, tm_count - 1)]
        return remote(maps, maps, far_send.at[way], far_recv.at[way], (tm, sibling))

    def last_copy(target):
        return remote(near.at[0, 0], near.at[0, 2], last_send, last_recv, (target, chan))

    def last_all():
        sent = sum_rx.at[pl.ds(0, tm_count - 1)]
        remote(sent, sent, last_send, last_recv, (tm, sibling)).wait_send()

    def sum_copy(source, target):
        return remote(sum_rx.at[source], sum_rx.at[source], sum_send, sum_recv, (target, chan))

    def peers(act_on):
        def one(d, carry):
            act_on(lax.rem(tm + d, tm_count))
            return carry

        lax.fori_loop(1, tm_count, one, 0)

    for j in range(tiles):
        near[0, 0, :, lanes(j)] = b_run[j]
        far[0, tm, j : j + 1, :] = spanning(a_run[j])
        far[0, tm, tiles + j : tiles + j + 1, :] = spanning(b_run[j])
    pl.when(tm < last_tm)(lambda: near_copy(0, tm + 1).start())
    peers(lambda p: far_copy(0, tm, p).start())
    pl.when(tm == last_tm)(lambda: peers(lambda p: last_copy(p).start()))
    flip(chunks - 1)
    far_all(0).wait_recv()
    pl.when(tm > 0)(lambda: near_copy(0, tm).wait_recv())

    def carry_on(d, carry):
        state, here = carry
        here = jnp.where(d == tm, state, here)
        return far[0, d, 0:tiles, :] * state + far[0, d, tiles : 2 * tiles, :], here

    lead = jnp.concatenate([spanning(entry[:, lanes(j)]) for j in range(tiles)], axis=0)
    last, here = lax.fori_loop(0, tm_count, carry_on, (lead, lead))
    states = []
    for j in range(tiles):
        row = jnp.broadcast_to(here[j : j + 1], (rows, LANE))
        others = jnp.where(tm == 0, entry[:, lanes(j)], near[0, 1, :, lanes(j)])
        states.append(jnp.where(spans > 0, row, others))
    tr_copy(chunks - 1).wait()
    low_copy(0).start()

    def forward(b, states):
        states = list(states)
        at = pl.ds(pl.multiple_of(b * part, part), part)
        mask = keep_mask[at, :]
        for j in range(tiles):
            cols = lanes(j)
            f = forget[at, cols]
            inject = (1.0 - f) * cand[at, cols]
            before, after = [], []
            c = states[j]
            for t in range(BLOCK):
                now = slice(t * rows, (t + 1) * rows)
                c = c * mask[now]
                before.append(c)
                c = f[now] * c + inject[now]
                after.append(c)
            states[j] = c
            masked[at, cols] = jnp.concatenate(before, axis=0)
            th = jnp.tanh(jnp.concatenate(after, axis=0))
            o = gate[at, cols]
            gate_grad = cot[at, cols].astype(F32) * (th - own_tok[at, cols].astype(F32))
            grad_buf[2, at, cols] = (gate_grad * o * (1.0 - o)).astype(BF16)
        return tuple(states)

    lax.fori_loop(0, steps // BLOCK, forward, tuple(states))

    def start_later():
        flow[0] = jnp.ones((rows, width), F32)
        flow[1] = jnp.zeros((rows, width), F32)

    def later(b, carry):
        at = pl.ds(pl.multiple_of(b * part, part), part)
        mask = keep_mask[at, :]
        for j in range(tiles):
            cols = lanes(j)
            f = forget[at, cols]
            th = jnp.tanh(f * masked[at, cols] + (1.0 - f) * cand[at, cols])
            o = gate[at, cols]
            direct = cot[at, cols].astype(F32) * o * (1.0 - th * th)
            side[at, cols] = jnp.where(o > 0.5, jnp.minimum(o - 1.0, -1e-30), o).astype(BF16)
            gate[at, cols] = direct
            keep = f * mask
            run, total = flow[0, :, cols], flow[1, :, cols]
            for t in range(BLOCK):
                now = slice(t * rows, (t + 1) * rows)
                run = run * keep[now]
                total = total + run * direct[now]
            flow[0, :, cols], flow[1, :, cols] = run, total
        return carry

    def output(b, carry):
        ch, h = b // blocks, lax.rem(b, blocks)
        slot = lax.rem(ch, 2)

        @pl.when(both(h == 0, ch >= 2))
        def _():
            act_copy(ch - 2).wait()

        at = pl.ds(pl.multiple_of(b * part, part), part)
        t0 = pl.multiple_of(h * BLOCK, BLOCK)
        for j in range(tiles):
            cols = lanes(j)
            f = forget[at, cols]
            th = jnp.tanh(f * masked[at, cols] + (1.0 - f) * cand[at, cols])
            q = side[at, cols].astype(F32)
            o = jnp.where(q < 0.0, 1.0 + q, q)
            rest = jnp.where(q < 0.0, -q, 1.0 - q)
            out = swapped(o * th + rest * own_tok[at, cols].astype(F32), BLOCK, rows).astype(BF16)
            act_buf[slot, :, pl.ds(t0, BLOCK), cols] = out.reshape(rows, BLOCK, LANE)
            side[at, cols] = (cot[at, cols].astype(F32) * rest).astype(BF16)

        @pl.when(h == blocks - 1)
        def _():
            act_copy(ch).start()

        return carry

    def end_output():
        for target in (sibling, across):
            pl.semaphore_signal(ready_sem, inc=1, device_id=(tm, target), device_id_type=MESH)

    def end_later():
        near[1, 0] = flow[1]
        for j in range(tiles):
            far[1, tm, j : j + 1, :] = spanning(flow[1, :, lanes(j)])
        pl.when(tm > 0)(lambda: near_copy(1, tm - 1).start())
        peers(lambda p: far_copy(1, tm, p).start())
        more[...] = jnp.zeros_like(more)

    remote(all_tokens, all_tokens, d_send, d_recv.at[0], (tm, sibling)).wait_send()

    n = tm_count // 2
    o, y = tm // 2, lax.rem(tm, 2)
    partner = (o * 2 + 1 - y, chan)
    left = (lax.rem(o - 1 + n, n) * 2 + y, chan)
    right = (lax.rem(o + 1, n) * 2 + y, chan)
    ring = ring_of(tm_count)
    ends, middle = (0, n - 1), (n // 2 - 1, n // 2)
    lines = [(0, middle[0] + y, n // 2, 1, None)]
    for l in (1, 2):
        if n == 4:
            lines += [(l, ends[l - 1], n - 1, 0, 0), (l, middle[l - 1], n // 2, 0, 1)]
        else:
            lines += [(l, middle[l - 1], n // 2, 0, None)]
    give_stage = 2 * (n // 2) + 2
    depth = LAG * max([give_stage] + [first + reach + (l > 0) + reach for l, c, reach, first, parity in lines])
    space = -(-depth // ring)

    def stage(s, number, parity=None):
        v = s - LAG * number
        u = v if space == 1 else v // space
        go = both(v >= 0, u < units)
        if space > 1:
            go = both(go, lax.rem(v, space) == 0)
        return u, go if parity is None else both(go, lax.rem(u, 2) == parity)

    def gate_of(u):
        return lax.rem(u // per_gate + 2, 3)

    def piece_of(l, mate=False):
        if l == 0:
            return (1 - y if mate else y) * PAIR, PAIR
        return 2 * PAIR + (l - 1) * LINE, LINE

    def wg_rows(l, u, mate=False):
        start, size = piece_of(l, mate)
        return pl.ds(pl.multiple_of(u * UNIT + start, 16), size)

    def fin_at(l, u):
        start, size = piece_of(l)
        return fin.at[pl.ds(pl.multiple_of((gate_of(u) * per_gate + lax.rem(u, per_gate)) * UNIT + start, 16), size)]

    def rx_rows(u, place, l):
        start = place * PAIR if l == 0 else 3 * PAIR + (place - 3) * LINE
        size = PAIR if l == 0 else LINE
        return pl.ds(pl.multiple_of(lax.rem(u, ring) * (3 * PAIR + 4 * LINE) + start, 16), size)

    def arrival(l, c, column, way, u):
        if l == 0:
            return 1 + way
        if l == 1:
            other = 6
        elif n == 4:
            other = jnp.where(column == jnp.where(lax.rem(u, 2) == 0, ends[0], middle[0]), 6, 3)
        else:
            other = jnp.where(column == middle[0], 6, 3)
        return jnp.where(column == c, 3 + way, other)

    def launch(make, u):
        @pl.when(u >= SENDS)
        def _():
            make(u - SENDS).wait_send()

        make(u).start()

    def to_rx(src, u, place, l, sem, target):
        return remote(src, rx.at[rx_rows(u, place, l)], sem, rx_recv.at[lax.rem(u, ring), place], target)

    def pair_copy(u):
        return to_rx(raw.at[wg_rows(0, u, True)], u, 0, 0, pair_send.at[lax.rem(u, SENDS)], partner)

    def red_copy(l, c, u, to_right):
        way, column = (0, o + 1) if to_right else (1, o - 1)
        return to_rx(
            raw.at[wg_rows(l, u)], u, arrival(l, c, column, way, u), l, red_send.at[l, lax.rem(u, SENDS)],
            right if to_right else left,
        )

    def red_wait(l, c, u, way):
        place = arrival(l, c, o, way, u)
        at = rx_rows(u, place, l)
        to_rx(rx.at[at], u, place, l, red_send.at[l, 0], partner).wait_recv()
        return rx[at].astype(F32)

    def bc_copy(l, u, to_right, src):
        return remote(
            src, fin_at(l, u), bc_send.at[l, lax.rem(u, SENDS), 1 if to_right else 0], bc_recv.at[l, lax.rem(u, ring)],
            right if to_right else left,
        )

    def swap_copy(l, u):
        return to_rx(raw.at[wg_rows(l, u)], u, 5, l, swap_send.at[lax.rem(u, SENDS)], partner)

    def give_copy(u, src):
        return remote(src, fin_at(0, u), give_send.at[lax.rem(u, SENDS)], give_recv.at[lax.rem(u, ring)], partner)

    def local_copy(l, u):
        return pltpu.make_async_copy(raw.at[wg_rows(l, u)], fin_at(l, u), loc_sem.at[l, lax.rem(u, SENDS)])

    def add_to(l, u, *others):
        at = wg_rows(l, u)
        total = raw[at].astype(F32)
        for v in others:
            total = total + v
        raw[at] = total.astype(BF16)

    def red_start(l, c, u):
        pl.when(o < c)(lambda: launch(lambda v: red_copy(l, c, v, True), u))
        pl.when(o > c)(lambda: launch(lambda v: red_copy(l, c, v, False), u))

    def publish(l, u):
        @pl.when(u >= SENDS)
        def _():
            local_copy(l, u - SENDS).wait()

        local_copy(l, u).start()
        pl.when(o > 0)(lambda: launch(lambda v: bc_copy(l, v, False, raw.at[wg_rows(l, v)]), u))
        pl.when(o < n - 1)(lambda: launch(lambda v: bc_copy(l, v, True, raw.at[wg_rows(l, v)]), u))
        if l == 0:
            launch(lambda v: give_copy(v, raw.at[wg_rows(0, v)]), u)

    def block_cols(c):
        return pl.ds(pl.multiple_of(c * width, width), width)

    def sib_rows(ch, q):
        return pl.ds(pl.multiple_of(units * UNIT + (lax.rem(ch, 4) * 2 + q) * span, span), span)

    def sib_copy(ch, q):
        slot = lax.rem(ch, 2)
        cols = sibling if q == 0 else lax.rem(sibling + 2, 4)
        return remote(
            terms.at[slot, cols], raw.at[sib_rows(ch, q)], sib_send.at[q], sib_recv.at[lax.rem(ch, 4), q], (tm, sibling)
        )

    def acr_copy(ch):
        return remote(
            terms.at[lax.rem(ch, 2), across], cot.at[rows_of(ch)], acr_send.at[lax.rem(ch, 2)], acr_recv.at[ch], (tm, across)
        )

    def row_copy(ch, source, d):
        return remote(
            row_rx.at[ch, source], row_rx.at[ch, source], row_send.at[lax.rem(ch, 4)], row_recv.at[lax.rem(ch, 4)],
            (tm, lax.rem(chan + d, 4)),
        )

    def row_all(ch):
        sums = row_rx.at[ch, pl.ds(0, chan_count - 1)]
        return remote(sums, sums, row_send.at[lax.rem(ch, 4)], row_recv.at[lax.rem(ch, 4)], (tm, sibling))

    def out_copy(ch):
        at = pl.ds(pl.multiple_of(ch * CHUNK, CHUNK), CHUNK)
        return pltpu.make_async_copy(out_buf.at[lax.rem(ch, 2)], in_grad.at[:, at, :], out_sem.at[lax.rem(ch, 2)])

    def project(ch):
        at = rows_of(ch)
        slot = lax.rem(ch, 2)

        @pl.when(ch == 0)
        def _():
            pl.semaphore_wait(ready_sem, 2)

        @pl.when(ch >= 2)
        def _():
            acr_copy(ch - 2).wait_send()

        for b in range(chan_count):
            total = jnp.zeros((span, width), F32)
            for k in range(3):
                total = total + lax.dot_general(
                    grad_buf[k, at, :], w_buf[k, b * width : (b + 1) * width, :], (((1,), (1,)), ((), ())),
                    preferred_element_type=F32,
                )
            terms[slot, b] = total.astype(BF16)
        sib_copy(ch, 0).start()
        sib_copy(ch, 1).start()

    def chip_sum(ch):
        slot = lax.rem(ch, 2)
        for q in range(2):
            sib_copy(ch, q).wait_recv()
        there = terms[slot, across].astype(F32) + raw[sib_rows(ch, 1)].astype(F32)
        terms[slot, across] = there.astype(BF16)
        acr_copy(ch).start()
        here = terms[slot, chan].astype(F32) + raw[sib_rows(ch, 0)].astype(F32)
        cand[rows_of(ch), :] = here
        for q in range(2):
            sib_copy(ch, q).wait_send()

    def full_sum(ch):
        acr_copy(ch).wait_recv()
        at = rows_of(ch)
        total = jnp.zeros((8, span), F32)
        pick = lax.broadcasted_iota(jnp.int32, (8, LANE), 0)
        for j in range(tiles):
            cols = lanes(j)
            fp, rp = grad_buf[1, at, cols].astype(F32), grad_buf[2, at, cols].astype(F32)
            g = cand[at, cols] + cot[at, cols].astype(F32) + fp * mix_f[0:1, cols] + rp * mix_r[0:1, cols]
            cand[at, cols] = g
            h = hat(at, j)
            nrm = h * mine(gain, j) + mine(shift, j)
            weighted = g * h
            for i, v in enumerate((fp * nrm, rp * nrm, fp, rp, weighted, g)):
                more[i, :, cols] = more[i, :, cols] + jnp.sum(v.reshape(CHUNK, rows, LANE), axis=0)
            for i, v in enumerate((g * mine(gain, j), weighted * mine(gain, j))):
                lead = jnp.where(pick == i, 1.0, 0.0).astype(BF16)
                high = v.astype(BF16)
                low_part = (v - high.astype(F32)).astype(BF16)
                for p in (high, low_part):
                    total = total + lax.dot_general(lead, p, (((1,), (1,)), ((), ())), preferred_element_type=F32)
        row_rx[ch, chan] = total
        pl.when(ch >= 4)(lambda: row_all(ch - 4).wait_send())
        for d in range(1, 4):
            row_copy(ch, chan, d).start()

    def finish(ch):
        row_all(ch).wait_recv()

        @pl.when(ch >= 2)
        def _():
            out_copy(ch - 2).wait()

        at = rows_of(ch)
        total = (row_rx[ch, 0] + row_rx[ch, 1] + row_rx[ch, 2] + row_rx[ch, 3]) * (1.0 / full)
        columns = jnp.transpose(total)
        first = jnp.broadcast_to(columns[:, 0:1], (span, LANE))
        second = jnp.broadcast_to(columns[:, 1:2], (span, LANE))
        for j in range(tiles):
            cols = lanes(j)
            g = cand[at, cols] * mine(gain, j)
            v = inv[at, :] * (g - first - hat(at, j) * second) + side[at, cols].astype(F32)
            out_buf[lax.rem(ch, 2), :, :, cols] = swapped(v, CHUNK, rows).astype(BF16).reshape(rows, CHUNK, LANE)
        out_copy(ch).start()

    def share_sums():
        for i in range(6):
            sum_rx[tm, i : i + 1, :] = jnp.sum(more[i], axis=0, keepdims=True)
        sum_rx[tm, 6:8, :] = jnp.zeros((2, width), F32)
        peers(lambda p: sum_copy(tm, p).start())

    def start_backward():
        far_all(1).wait_recv()
        pl.when(tm < last_tm)(lambda: near_copy(1, tm).wait_recv())

        def carry_back(i, v):
            d = tm_count - 1 - i
            return jnp.where(d > tm, far[0, d, 0:tiles, :] * v + far[1, d, 0:tiles, :], v)

        inflow = lax.fori_loop(0, tm_count, carry_back, jnp.zeros((tiles, LANE), F32))
        for j in range(tiles):
            row = jnp.broadcast_to(inflow[j : j + 1], (rows, LANE))
            others = jnp.where(tm == last_tm, 0.0, near[1, 1, :, lanes(j)])
            flow[0, :, lanes(j)] = jnp.where(spans > 0, row, others)

    def backward(i, carry):
        b = steps // BLOCK - 1 - i
        at = pl.ds(pl.multiple_of(b * part, part), part)
        mask = keep_mask[at, :]
        for j in range(tiles):
            cols = lanes(j)
            f = forget[at, cols]
            keep = f * mask
            direct = gate[at, cols]
            g = flow[0, :, cols]
            adjoint = [None] * BLOCK
            for t in reversed(range(BLOCK)):
                now = slice(t * rows, (t + 1) * rows)
                adjoint[t] = direct[now] + g
                g = keep[now] * adjoint[t]
            flow[0, :, cols] = g
            cand_grad = jnp.concatenate(adjoint, axis=0) * (1.0 - f)
            forget_pre = cand_grad * (masked[at, cols] - cand[at, cols]) * f
            grad_buf[0, at, cols] = cand_grad.astype(BF16)
            grad_buf[1, at, cols] = forget_pre.astype(BF16)
        return carry

    def close_first():
        x_move(all_tokens, all_tokens, 0).wait_send()
        s_move(all_tokens, all_tokens, 0).wait_send()
        for way in range(2):
            far_all(way).wait_send()
        pl.when(tm < last_tm)(lambda: near_copy(0, tm).wait_send())
        pl.when(tm > 0)(lambda: near_copy(1, tm).wait_send())
        pl.when(tm == last_tm)(last_all)
        pl.when(tm != last_tm)(lambda: last_copy(tm).wait_recv())
        for ch in (chunks - 2, chunks - 1):
            act_copy(ch).wait()
        for j in range(tiles):
            row = jnp.broadcast_to(last[j : j + 1], (rows, LANE))
            others = jnp.where(tm == last_tm, near[0, 0, :, lanes(j)], near[0, 2, :, lanes(j)])
            final[:, lanes(j)] = jnp.where(spans > 0, row, others)

    def close_second():
        for ch in range(chunks - 4, chunks):
            row_all(ch).wait_send()
        for ch in (chunks - 2, chunks - 1):
            out_copy(ch).wait()
            acr_copy(ch).wait_send()
        sums = sum_rx.at[pl.ds(0, tm_count - 1)]
        remote(sums, sums, sum_send, sum_recv, (tm, sibling)).wait()
        totals[...] = lax.fori_loop(0, tm_count, lambda d, v: v + sum_rx[d], jnp.zeros(totals.shape, F32))

    def slot_step(s, carry):
        u, go = stage(s, give_stage)
        pl.when(go)(lambda: give_copy(u, raw.at[wg_rows(0, u)]).wait_recv())

        for l, c, reach, first, parity in lines:
            late = first + reach + (1 if l else 0)
            u, go = stage(s, late + jnp.abs(o - c), parity)

            @pl.when(both(o != c, go))
            def _(l=l, c=c, u=u):
                bc_copy(l, u, True, fin_at(l, u)).wait_recv()
                pl.when(both(o < c, o > 0))(lambda: launch(lambda v: bc_copy(l, v, False, fin_at(l, v)), u))
                pl.when(both(o > c, o < n - 1))(lambda: launch(lambda v: bc_copy(l, v, True, fin_at(l, v)), u))
                if l == 0:
                    launch(lambda v: give_copy(v, fin_at(0, v)), u)

        for l, c, reach, first, parity in lines[1:]:
            u, go = stage(s, reach + 1, parity)

            @pl.when(both(o == c, go))
            def _(l=l, u=u):
                swap_copy(l, u).wait()
                add_to(l, u, rx[rx_rows(u, 5, l)].astype(F32))
                publish(l, u)

        for l, c, reach, first, parity in lines:
            u, go = stage(s, first + reach, parity)

            @pl.when(both(o == c, go))
            def _(l=l, c=c, u=u):
                if l == 0 and n > 2:
                    add_to(l, u, red_wait(l, c, u, 0), red_wait(l, c, u, 1))
                elif l > 0 and 0 < c < n - 1:
                    add_to(l, u, red_wait(l, c, u, 0), red_wait(l, c, u, 1))
                else:
                    pl.when(o > 0)(lambda: add_to(l, u, red_wait(l, c, u, 0)))
                    pl.when(o < n - 1)(lambda: add_to(l, u, red_wait(l, c, u, 1)))
                if l == 0:
                    publish(l, u)
                else:
                    swap_copy(l, u).start()

        u0, go0 = stage(s, 0)

        @pl.when(go0)
        def _():
            pl.when(u0 + 1 < units)(lambda: low_copy(u0 + 1).start())
            low_copy(u0).wait()
            g = jnp.dot(low[lax.rem(u0, 2)], grad_buf[gate_of(u0)], preferred_element_type=F32)
            raw[pl.ds(pl.multiple_of(u0 * UNIT, UNIT), UNIT)] = g.astype(BF16)
            launch(pair_copy, u0)
            for l, c, reach, first, parity in lines[1:]:
                mine_now = jnp.logical_or(o == 0, o == n - 1)
                if parity is not None:
                    mine_now = both(mine_now, lax.rem(u0, 2) == parity)
                pl.when(mine_now)(lambda l=l, c=c: red_start(l, c, u0))

        for l, c, reach, first, parity in lines:
            u, go = stage(s, first + jnp.where(o < c, o, n - 1 - o), parity)

            @pl.when(both(o < c, o > 0, go))
            def _(l=l, c=c, u=u):
                add_to(l, u, red_wait(l, c, u, 0))
                launch(lambda v: red_copy(l, c, v, True), u)

            @pl.when(both(o > c, o < n - 1, go))
            def _(l=l, c=c, u=u):
                add_to(l, u, red_wait(l, c, u, 1))
                launch(lambda v: red_copy(l, c, v, False), u)

        u, go = stage(s, 1)

        @pl.when(go)
        def _():
            pair_copy(u).wait_recv()
            add_to(0, u, rx[rx_rows(u, 0, 0)].astype(F32))
            pl.when(jnp.logical_or(o == 0, o == n - 1))(lambda: red_start(0, lines[0][1], u))

        count = steps // BLOCK
        pl.when(s == 0)(start_later)
        share = -(-count // LATER)
        at = s * share

        @pl.when(s < LATER)
        def _():
            lax.fori_loop(at, jnp.minimum(at + share, count), later, 0)

        pl.when(s == LATER - 1)(end_later)
        pl.when(s == LATER + 1)(start_backward)
        share = -(-count // (OUTPUT - LATER - 1))
        at2 = (s - LATER - 1) * share

        @pl.when(both(s > LATER, s < OUTPUT))
        def _():
            lax.fori_loop(at2, jnp.minimum(at2 + share, count), backward, 0)

        share = -(-count // (FIRST - OUTPUT))
        at3 = (s - OUTPUT) * share

        @pl.when(both(s >= OUTPUT, s < FIRST))
        def _():
            lax.fori_loop(at3, jnp.minimum(at3 + share, count), output, 0)

        pl.when(s == FIRST - 1)(end_output)

        for job, offset in ((finish, 5), (full_sum, 3), (chip_sum, 1), (project, 0)):
            at = s - FIRST - offset
            pl.when(both(at >= 0, lax.rem(at, 2) == 0, at // 2 < chunks))(lambda job=job, at=at: job(at // 2))
        pl.when(s == FIRST + 3)(close_first)
        pl.when(s == FIRST + 2 * chunks + 2)(share_sums)
        pl.when(s == FIRST + 2 * chunks + 6)(close_second)
        return carry

    slots = max((units - 1) * space + depth + 1, FIRST + 2 * chunks + 7)
    lax.fori_loop(0, slots, slot_step, 0)

    def close_unit(u, carry):
        give_copy(u, raw.at[wg_rows(0, u)]).wait_send()
        pair_copy(u).wait_send()
        for l, c, reach, first, parity in lines:

            @pl.when(True if parity is None else lax.rem(u, 2) == parity)
            def _(l=l, c=c):
                src = raw.at[wg_rows(l, u)]
                pl.when(o != c)(lambda: red_copy(l, c, u, True).wait_send())
                pl.when(o == c)(lambda: local_copy(l, u).wait())
                pl.when(both(o <= c, o > 0))(lambda: bc_copy(l, u, False, src).wait_send())
                pl.when(both(o >= c, o < n - 1))(lambda: bc_copy(l, u, True, src).wait_send())

        return carry

    lax.fori_loop(units - SENDS, units, close_unit, 0)


def layer(tokens, weights, cotangent, gain, shift, mix_f, mix_r, bias_f, bias_r, bank, selector, resets):
    rows, steps, width = tokens.shape
    full = gain.shape[-1]
    tm_count, chan_count = lax.axis_size("tm"), lax.axis_size("chan")
    chunks = steps // CHUNK
    span = CHUNK * rows
    pieces = chunks - 1 + CHUNK // BLOCK
    count = steps * rows
    units = 3 * full // UNIT
    ring = ring_of(tm_count)
    hbm = pl.BlockSpec(memory_space=pl.ANY)
    vmem = pl.BlockSpec(memory_space=pltpu.VMEM)
    smem = pl.BlockSpec(memory_space=pltpu.SMEM)
    dma = pltpu.SemaphoreType.DMA
    stat = pltpu.VMEM((CHUNK // BLOCK, rows, BLOCK, LANE), F32)
    wide = pltpu.VMEM((count, width), F32)
    narrow = pltpu.VMEM((count, LANE), F32)
    short = pltpu.VMEM((count, width), BF16)
    return pl.pallas_call(
        layer_kernel,
        out_shape=(
            jax.ShapeDtypeStruct((units * UNIT, width), BF16),
            jax.ShapeDtypeStruct(tokens.shape, BF16),
            jax.ShapeDtypeStruct(tokens.shape, BF16),
            jax.ShapeDtypeStruct((full, count), BF16),
            jax.ShapeDtypeStruct((rows, width), F32),
            jax.ShapeDtypeStruct((8, width), F32),
        ),
        in_specs=[hbm, hbm, hbm] + [vmem] * 7 + [smem, vmem],
        out_specs=(hbm, hbm, hbm, hbm, vmem, vmem),
        scratch_shapes=[
            pltpu.VMEM((chunks * chan_count * span, width), BF16),
            pltpu.VMEM((ring * (3 * PAIR + 4 * LINE), width), BF16),
            pltpu.VMEM((2, span, full), BF16),
            pltpu.VMEM((full, span), BF16),
            pltpu.VMEM((3, full, width), BF16),
            wide, wide, wide, wide,
            short,
            pltpu.VMEM((2, rows, CHUNK, width), BF16),
            short,
            narrow, narrow, narrow,
            pltpu.VMEM((3, count, width), BF16),
            pltpu.VMEM((2, rows, CHUNK, width), BF16),
            short,
            pltpu.VMEM((2, chan_count, span, width), BF16),
            pltpu.VMEM((2, rows, CHUNK, width), BF16),
            pltpu.VMEM((chunks, 4, 8, span), F32),
            pltpu.VMEM((6, rows, width), F32),
            pltpu.VMEM((tm_count, 8, width), F32),
            stat, stat, stat,
            pltpu.VMEM((rows, width), F32),
            pltpu.VMEM((2, 3, rows, width), F32),
            pltpu.VMEM((2, tm_count, 8, LANE), F32),
            pltpu.VMEM((2, rows, width), F32),
            pltpu.VMEM((resets.shape[1], rows, LANE), jnp.int32),
            dma(()), dma((pieces,)), dma(()), dma(()), dma(()), dma((pieces,)), dma(()),
            dma((3,)), dma((2,)), dma((2,)), dma(()), dma((2,)),
            dma((2,)), dma((2,)), dma((2,)), dma((2,)), dma(()), dma(()),
            pltpu.SemaphoreType.REGULAR,
            dma((2,)), dma((3, SENDS)), dma((SENDS,)), dma((3, SENDS)), dma((3, SENDS, 2)), dma((3, ring)), dma((SENDS,)),
            dma((SENDS,)), dma((ring,)), dma((ring, 7)), dma((2,)), dma((4, 2)), dma((2,)), dma((chunks,)),
            dma((4,)), dma((4,)), dma(()), dma(()),
        ],
        compiler_params=pltpu.CompilerParams(collective_id=0, has_side_effects=True, vmem_limit_bytes=VMEM_BYTES),
        name="whole",
    )(tokens, weights, cotangent, gain, shift, mix_f, mix_r, bias_f, bias_r, bank, selector, resets)


def tail_kernel(
    fin, in_grad, act, final, totals, wide_out, in_out, act_out, final_out, s0, s1, s2, s3, s4, s5,
    fin_buf, wide_buf, in_buf, in_wide, act_buf, load_sem, store_sem,
):
    def move(src, dst, sem, i, n):
        at = pl.ds(i * n, n)
        return pltpu.make_async_copy(src.at[at], dst.at[at], sem)

    jobs = []

    def job(src, buf, wide, dst, parts):
        n = src.shape[0] // parts
        for i in range(parts):
            k = len(jobs)
            jobs.append((move(src, buf, load_sem.at[k], i, n), buf, wide, i * n, n, move(wide, dst, store_sem.at[k], i, n)))

    job(fin, fin_buf, wide_buf, wide_out, TAIL)
    job(in_grad, in_buf, in_wide, in_out, 2)
    job(act, act_buf, act_buf, act_out, 2)
    order = [0, 4, 1, 6, 2, 5, 3, 7] if TAIL == 4 else list(range(len(jobs)))
    for k in order:
        jobs[k][0].start()
    final_out[...] = final[...]
    for i, ref in enumerate((s0, s1, s2, s3, s4, s5)):
        ref[...] = totals[i : i + 1, :]
    for k in order:
        load, buf, wide, start, n, store = jobs[k]
        load.wait()
        if buf is not wide:
            step = 64 if len(buf.shape) == 2 else 1

            def cast(j, carry, buf=buf, wide=wide, start=start, step=step):
                at = pl.ds(start + j * step, step)
                wide[at] = buf[at].astype(F32)
                return carry

            lax.fori_loop(0, n // step, cast, 0, unroll=2)
        store.start()
    for k in order:
        jobs[k][-1].wait()


def tail(fin, in_grad, act, final, totals):
    width = fin.shape[-1]
    hbm = pl.BlockSpec(memory_space=pl.ANY)
    vmem = pl.BlockSpec(memory_space=pltpu.VMEM)
    dma = pltpu.SemaphoreType.DMA
    line = jax.ShapeDtypeStruct((1, width), F32)
    return pl.pallas_call(
        tail_kernel,
        out_shape=(
            jax.ShapeDtypeStruct(fin.shape, F32),
            jax.ShapeDtypeStruct(in_grad.shape, F32),
            jax.ShapeDtypeStruct(act.shape, BF16),
            jax.ShapeDtypeStruct(final.shape, F32),
        ) + (line,) * 6,
        in_specs=[hbm] * 3 + [vmem] * 2,
        out_specs=(hbm,) * 3 + (vmem,) * 7,
        scratch_shapes=[
            pltpu.VMEM(fin.shape, BF16), pltpu.VMEM(fin.shape, F32),
            pltpu.VMEM(in_grad.shape, BF16), pltpu.VMEM(in_grad.shape, F32), pltpu.VMEM(act.shape, BF16),
            dma((TAIL + 4,)), dma((TAIL + 4,)),
        ],
        compiler_params=pltpu.CompilerParams(vmem_limit_bytes=VMEM_BYTES),
        name="tail",
    )(fin, in_grad, act, final, totals)


def body(
    tokens, ln_gain, ln_bias, weights, mix_forget, mix_reset, bias_forget, bias_reset, state_bank, selector, resets, cotangent
):
    fin, in_grad, act, _, final, totals = layer(
        tokens, weights, cotangent, ln_gain[None], ln_bias[None], mix_forget[None], mix_reset[None], bias_forget[None],
        bias_reset[None], state_bank, selector, resets,
    )
    wide, in_grad, act, final, *sums = tail(fin, in_grad, act, final, totals)
    sums = [v[0] for v in sums]
    return act, final, in_grad, wide.reshape(weights.shape), sums[4], sums[5], sums[0], sums[1], sums[2], sums[3]


def solution(mesh):
    placed = (
        P(None, "tm", "chan"), P(), P(), P(None, None, "chan"), P("chan"), P("chan"), P("chan"), P("chan"),
        P(None, "chan"), P(), P(), P(None, "tm", "chan"),
    )
    return jax.shard_map(
        body,
        mesh=mesh,
        in_specs=placed,
        out_specs=(
            P(None, "tm", "chan"), P(None, "chan"), P(None, "tm", "chan"), P(None, None, "chan"),
            P("chan"), P("chan"), P("chan"), P("chan"), P("chan"), P("chan"),
        ),
        check_vma=False,
    )
```

```python
import jax
import jax.numpy as jnp
from jax import lax
from jax.experimental import pallas as pl
from jax.experimental.pallas import tpu as pltpu
from jax.sharding import PartitionSpec as P

EPSILON = 1e-05
CHUNK = 32
BLOCK = 16
LANE = 128
AHEAD = 4
UNIT = 256
LAG = 2
PAIR = 80
LINE = 48
SENDS = 2
VMEM_BYTES = 63 << 20
TAIL = 4
LATER = 4
ADJOINT = 6
OUTPUT = 8
FIRST = 12
MESH = pl.DeviceIdType.MESH
F32 = jnp.float32
BF16 = jnp.bfloat16


def sigmoid(v):
    return 1.0 / (1.0 + jnp.exp(-v))


def swapped(v, outer, inner):
    return jnp.swapaxes(v.reshape(outer, inner, v.shape[-1]), 0, 1).reshape(outer * inner, v.shape[-1])


def both(*conditions):
    out = conditions[0]
    for c in conditions[1:]:
        out = jnp.logical_and(out, c)
    return out


def ring_of(tm_count):
    return 14 if tm_count <= 8 else 3


def layer_kernel(
    tokens, weights, cotangent, gain, shift, mix_f, mix_r, bias_f, bias_r, bank, selector, resets,
    fin, in_grad, act, low_t, final, totals,
    raw, rx, low, low_t_buf, w_buf, cand, forget, gate, masked, own_tok, cot_raw, cot, mean, inv, keep_mask, grad_buf,
    act_buf, side, terms, out_buf, row_rx, more, sum_rx, mean_s, inv_s, part_s, entry, near, far, flow, reset_rows,
    x_send, x_recv, s_send, s_recv, d_send, d_recv, own_sem, w_sem, cot_sem, act_sem, tr_sem, low_sem,
    near_send, near_recv, far_send, far_recv, last_send, last_recv, ready_sem, out_sem, loc_sem, pair_send, red_send,
    bc_send, bc_recv, swap_send, give_send, give_recv, rx_recv, sib_send, sib_recv, acr_send, acr_recv, row_send,
    row_recv, sum_send, sum_recv,
):
    rows, steps, width = tokens.shape
    full = gain.shape[-1]
    tm_count, tm = lax.axis_size("tm"), lax.axis_index("tm")
    chan_count, chan = lax.axis_size("chan"), lax.axis_index("chan")
    sibling = chan + 1 - 2 * lax.rem(chan, 2)
    across = lax.rem(chan + 2, 4)
    chunks = steps // CHUNK
    span = CHUNK * rows
    part = BLOCK * rows
    tiles = width // LANE
    blocks = CHUNK // BLOCK
    units = 3 * full // UNIT
    per_gate = full // UNIT

    def remote(src, dst, send, recv, target):
        return pltpu.make_async_remote_copy(src, dst, send, recv, device_id=target, device_id_type=MESH)

    def lanes(j):
        return slice(j * LANE, (j + 1) * LANE)

    def mine(ref, j):
        return ref[0:1, pl.ds(pl.multiple_of(chan * width + j * LANE, LANE), LANE)]

    def hat(at, j):
        return (own_tok[at, lanes(j)].astype(F32) - mean[at, :]) * inv[at, :]

    def normed(at, j):
        return hat(at, j) * mine(gain, j) + mine(shift, j)

    def rows_of(ch):
        return pl.ds(pl.multiple_of(ch * span, span), span)

    def raw_rows(ch, block, h0, h1):
        return pl.ds(pl.multiple_of((ch * chan_count + block) * span + h0 * part, part), (h1 - h0) * part)

    def token_copies(ch, h0, h1, copy):
        at = [pl.ds(pl.multiple_of(ch * CHUNK + h * BLOCK, BLOCK), BLOCK) for h in range(h0, h1)]
        return [
            copy(tokens.at[:, t, :], raw.at[raw_rows(ch, chan, h, h + 1)].reshape(rows, BLOCK, width), ch + h0)
            for h, t in zip(range(h0, h1), at)
        ]

    def own_move(src, dst, sem):
        return pltpu.make_async_copy(src, dst, own_sem)

    def x_move(src, dst, sem):
        return remote(src, dst, x_send, x_recv.at[sem], (tm, across))

    def s_move(src, dst, sem):
        return remote(src, dst, s_send, s_recv, (tm, sibling))

    def arrived(ch, block, h0, h1, copy):
        here = raw.at[raw_rows(ch, block, h0, h1)]
        return copy(here, here, ch + h0)

    def d_copy(ch, h0, h1):
        view = raw.at[raw_rows(ch, across, h0, h1)]
        return remote(view, view, d_send, d_recv.at[ch + h0], (tm, sibling))

    all_tokens = raw.at[pl.ds(0, steps * rows)]

    def cot_copy(ch):
        at = pl.ds(pl.multiple_of(ch * CHUNK, CHUNK), CHUNK)
        return pltpu.make_async_copy(cotangent.at[:, at, :], cot_raw.at[lax.rem(ch, 2)], cot_sem.at[lax.rem(ch, 2)])

    def act_copy(ch):
        at = pl.ds(pl.multiple_of(ch * CHUNK, CHUNK), CHUNK)
        return pltpu.make_async_copy(act_buf.at[lax.rem(ch, 2)], act.at[:, at, :], act_sem.at[lax.rem(ch, 2)])

    def tr_copy(ch):
        return pltpu.make_async_copy(low_t_buf, low_t.at[:, rows_of(ch)], tr_sem)

    def low_copy(u):
        at = pl.ds(pl.multiple_of(lax.rem(u, per_gate) * UNIT, UNIT), UNIT)
        return pltpu.make_async_copy(low_t.at[at], low.at[lax.rem(u, 2)], low_sem.at[lax.rem(u, 2)])

    w_copies = [pltpu.make_async_copy(weights.at[k], w_buf.at[k], w_sem.at[k]) for k in range(3)]

    barrier = pltpu.get_barrier_semaphore()
    for d in range(1, 4):
        pl.semaphore_signal(barrier, inc=1, device_id=(tm, lax.rem(chan + d, 4)), device_id_type=MESH)

    def greet(d, carry):
        pl.semaphore_signal(barrier, inc=1, device_id=(lax.rem(tm + d, tm_count), chan), device_id_type=MESH)
        return carry

    lax.fori_loop(1, tm_count, greet, 0)
    def start_own(ch, carry):
        for copy in token_copies(ch, 0, blocks, own_move):
            copy.start()
        return carry

    def start_sibling(ch, carry):
        for copy in token_copies(ch, 0, blocks, s_move):
            copy.start()
        return carry

    lax.fori_loop(0, chunks, start_own, 0)
    cot_copy(0).start()
    for copy in w_copies:
        copy.start()
    pl.semaphore_wait(barrier, tm_count + 2)
    for ch in range(AHEAD):
        for copy in token_copies(ch, 0, blocks, x_move):
            copy.start()
    lax.fori_loop(0, chunks, start_sibling, 0)

    count = resets.shape[1]
    for j in range(count):
        reset_rows[j] = jnp.broadcast_to(resets[:, j : j + 1], (rows, LANE))

    def mark(t, carry):
        at = tm * steps + t

        def compare(j, hit):
            return jnp.maximum(hit, jnp.where(reset_rows[j] == at, 1.0, 0.0))

        hit = lax.fori_loop(0, count, compare, jnp.zeros((rows, LANE), F32), unroll=16)
        keep_mask[pl.ds(pl.multiple_of(t * rows, rows), rows), :] = 1.0 - hit
        return carry

    lax.fori_loop(0, steps, mark, 0)
    for r in range(rows):
        entry[r : r + 1, :] = bank[pl.ds(selector[r], 1), :]

    def flip(ch):
        @pl.when(ch >= 1)
        def _():
            tr_copy(ch - 1).wait()

        def one(j, carry):
            cols = pl.ds(pl.multiple_of(j * 256, 256), 256)
            low_t_buf[cols, :] = jnp.transpose(low[lax.rem(ch, 2), :, cols])
            return carry

        lax.fori_loop(0, full // 256, one, 0, unroll=2)
        tr_copy(ch).start()

    def project_one(ch, k, h0, h1):
        at = pl.ds(pl.multiple_of(ch * span + h0 * part, part), (h1 - h0) * part)
        ref = (cand, forget, gate)[k]
        ref[at, :] = jnp.dot(low[lax.rem(ch, 2), h0 * part : h1 * part], w_buf[k], preferred_element_type=F32)

    def send_across(ch):
        for copy in token_copies(ch, 0, blocks, x_move):
            copy.start()

    def send_last():
        for h in range(blocks):
            for copy in token_copies(chunks - 1, h, h + 1, x_move):
                copy.start()

    def gates(b, carry):
        a_list, b_list = list(carry[0]), list(carry[1])
        at = pl.ds(pl.multiple_of(b * part, part), part)
        mask = keep_mask[at, :]
        for j in range(tiles):
            cols = lanes(j)
            nrm = normed(at, j)
            f = sigmoid(forget[at, cols] + mix_f[0:1, cols] * nrm + bias_f[0:1, cols])
            o = sigmoid(gate[at, cols] + mix_r[0:1, cols] * nrm + bias_r[0:1, cols])
            forget[at, cols] = f
            gate[at, cols] = o
            inject = (1.0 - f) * cand[at, cols]
            keep = f * mask
            for t in range(BLOCK):
                now = slice(t * rows, (t + 1) * rows)
                a_list[j] = a_list[j] * keep[now]
                b_list[j] = b_list[j] * keep[now] + inject[now]
        return tuple(a_list), tuple(b_list)

    def gather_step(ch, runs, h0=0, h1=blocks):
        entire = h1 - h0 == blocks
        if entire:
            pl.when(ch + AHEAD < chunks - 1)(lambda: send_across(ch + AHEAD))
            pl.when(ch + AHEAD == chunks - 1)(send_last)
            cot_copy(ch + 1).start()

        base = pl.multiple_of(ch * span, span)
        slot = lax.rem(ch, 2)

        arrived(ch, across, h0, h1, x_move).wait_recv()
        d_copy(ch, h0, h1).start()

        if entire:
            pl.when(ch >= 1)(lambda: project_one(ch - 1, 2, 0, blocks))
        elif h0 == 0:
            project_one(ch - 1, 2, 0, blocks)
        else:
            project_one(ch, 2, 0, h0)
        if h0 == 0:
            runs = lax.fori_loop(jnp.maximum(ch - 1, 0) * blocks, ch * blocks, gates, runs)
        else:
            runs = lax.fori_loop(ch * blocks, ch * blocks + h0, gates, runs)

        if h0 == 0:
            cot_copy(ch).wait()
            for h in range(blocks):
                for j in range(tiles):
                    v = cot_raw[slot, :, h * BLOCK : (h + 1) * BLOCK, lanes(j)].astype(F32).reshape(part, LANE)
                    at = pl.ds(pl.multiple_of(base + h * part, part), part)
                    cot[at, lanes(j)] = swapped(v, rows, BLOCK).astype(BF16)
        if entire:

            @pl.when(ch == 0)
            def _():
                own_move(all_tokens, all_tokens, 0).wait()
                s_move(all_tokens, all_tokens, 0).wait_recv()
                for copy in w_copies:
                    copy.wait()

        d_copy(ch, h0, h1).wait_recv()

        first = pl.multiple_of(ch * chan_count * span, span)

        def tokens_at(block, r, h, cols):
            at = pl.multiple_of(first + block * span + h * part + r * BLOCK, BLOCK)
            return raw[pl.ds(at, BLOCK), cols].astype(F32)

        def each(i, turn):
            r, h = lax.rem(i, rows), h0 + i // rows
            totals = [jnp.zeros((BLOCK, LANE), F32) for _ in range(chan_count)]
            for j in range(tiles):
                for b in range(chan_count):
                    totals[b] = totals[b] + turn(tokens_at(b, r, h, lanes(j)))
            while len(totals) > 1:
                totals = [a + b for a, b in zip(totals[::2], totals[1::2])]
            part_s[h, r] = totals[0]

        def sum_rows(i, carry):
            each(i, lambda v: v)
            return carry

        count = (h1 - h0) * rows
        stat = (h1 - h0,) + mean_s.shape[1:]
        lax.fori_loop(0, count, sum_rows, 0, unroll=2)
        total = jnp.sum(part_s[h0:h1], axis=-1, keepdims=True)
        mean_s[h0:h1] = jnp.broadcast_to(total * (1.0 / full), stat)

        def square_rows(i, carry):
            m = mean_s[h0 + i // rows, lax.rem(i, rows)]
            each(i, lambda v: (v - m) * (v - m))
            return carry

        lax.fori_loop(0, count, square_rows, 0, unroll=2)
        var = jnp.sum(part_s[h0:h1], axis=-1, keepdims=True) * (1.0 / full)
        inv_s[h0:h1] = jnp.broadcast_to(lax.rsqrt(var + EPSILON), stat)

        for h in range(h0, h1):
            mean_h = mean_s[h].reshape(part, LANE)
            inv_h = inv_s[h].reshape(part, LANE)

            def normalize(j, carry, h=h, mean_h=mean_h, inv_h=inv_h):
                cols = pl.ds(pl.multiple_of(j * LANE, LANE), LANE)
                inner = pl.ds(pl.multiple_of(lax.rem(j, tiles) * LANE, LANE), LANE)
                v = jnp.concatenate([tokens_at(j // tiles, r, h, inner) for r in range(rows)], axis=0)
                v = (v - mean_h) * inv_h * gain[0:1, cols] + shift[0:1, cols]
                low[slot, h * part : (h + 1) * part, cols] = swapped(v, rows, BLOCK).astype(BF16)
                return carry

            lax.fori_loop(0, full // LANE, normalize, 0, unroll=2)
            at = pl.ds(pl.multiple_of(base + h * part, part), part)
            mean[at, :] = swapped(mean_h, rows, BLOCK)
            inv[at, :] = swapped(inv_h, rows, BLOCK)
            for j in range(tiles):
                v = jnp.concatenate([tokens_at(chan, r, h, lanes(j)) for r in range(rows)], axis=0)
                own_tok[at, lanes(j)] = swapped(v, rows, BLOCK).astype(BF16)

        project_one(ch, 0, h0, h1)
        project_one(ch, 1, h0, h1)
        if entire:
            flip(ch)
        return runs

    ones = tuple(jnp.ones((rows, LANE), F32) for _ in range(tiles))
    zeros = tuple(jnp.zeros((rows, LANE), F32) for _ in range(tiles))
    runs = lax.fori_loop(0, chunks - 1, gather_step, (ones, zeros))
    for h in range(blocks):
        runs = gather_step(chunks - 1, runs, h, h + 1)
    project_one(chunks - 1, 2, blocks - 1, blocks)
    a_run, b_run = lax.fori_loop(chunks * blocks - 1, chunks * blocks, gates, runs)

    spans = jnp.where(reset_rows[0] >= tm_count * steps, 1.0, 0.0)
    last_tm = tm_count - 1

    def spanning(v):
        return jnp.sum(v * spans, axis=0, keepdims=True)

    def near_copy(way, target):
        return remote(near.at[way, 0], near.at[way, 1], near_send.at[way], near_recv.at[way], (target, chan))

    def far_copy(way, source, target):
        return remote(
            far.at[way, source], far.at[way, source], far_send.at[way], far_recv.at[way], (target, chan)
        )

    def far_all(way):
        maps = far.at[way, pl.ds(0, tm_count - 1)]
        return remote(maps, maps, far_send.at[way], far_recv.at[way], (tm, sibling))

    def last_copy(target):
        return remote(near.at[0, 0], near.at[0, 2], last_send, last_recv, (target, chan))

    def last_all():
        sent = sum_rx.at[pl.ds(0, tm_count - 1)]
        remote(sent, sent, last_send, last_recv, (tm, sibling)).wait_send()

    def sum_copy(source, target):
        return remote(sum_rx.at[source], sum_rx.at[source], sum_send, sum_recv, (target, chan))

    def peers(act_on):
        def one(d, carry):
            act_on(lax.rem(tm + d, tm_count))
            return carry

        lax.fori_loop(1, tm_count, one, 0)

    for j in range(tiles):
        near[0, 0, :, lanes(j)] = b_run[j]
        far[0, tm, j : j + 1, :] = spanning(a_run[j])
        far[0, tm, tiles + j : tiles + j + 1, :] = spanning(b_run[j])
    pl.when(tm < last_tm)(lambda: near_copy(0, tm + 1).start())
    peers(lambda p: far_copy(0, tm, p).start())
    pl.when(tm == last_tm)(lambda: peers(lambda p: last_copy(p).start()))
    flip(chunks - 1)
    far_all(0).wait_recv()
    pl.when(tm > 0)(lambda: near_copy(0, tm).wait_recv())

    def carry_on(d, carry):
        state, here = carry
        here = jnp.where(d == tm, state, here)
        return far[0, d, 0:tiles, :] * state + far[0, d, tiles : 2 * tiles, :], here

    lead = jnp.concatenate([spanning(entry[:, lanes(j)]) for j in range(tiles)], axis=0)
    last, here = lax.fori_loop(0, tm_count, carry_on, (lead, lead))
    states = []
    for j in range(tiles):
        row = jnp.broadcast_to(here[j : j + 1], (rows, LANE))
        others = jnp.where(tm == 0, entry[:, lanes(j)], near[0, 1, :, lanes(j)])
        states.append(jnp.where(spans > 0, row, others))
    tr_copy(chunks - 1).wait()
    low_copy(0).start()

    def forward(b, states):
        states = list(states)
        at = pl.ds(pl.multiple_of(b * part, part), part)
        mask = keep_mask[at, :]
        for j in range(tiles):
            cols = lanes(j)
            f = forget[at, cols]
            inject = (1.0 - f) * cand[at, cols]
            before, after = [], []
            c = states[j]
            for t in range(BLOCK):
                now = slice(t * rows, (t + 1) * rows)
                c = c * mask[now]
                before.append(c)
                c = f[now] * c + inject[now]
                after.append(c)
            states[j] = c
            masked[at, cols] = jnp.concatenate(before, axis=0)
            th = jnp.tanh(jnp.concatenate(after, axis=0))
            o = gate[at, cols]
            gate_grad = cot[at, cols].astype(F32) * (th - own_tok[at, cols].astype(F32))
            grad_buf[2, at, cols] = (gate_grad * o * (1.0 - o)).astype(BF16)
        return tuple(states)

    lax.fori_loop(0, steps // BLOCK, forward, tuple(states))

    def start_later():
        flow[0] = jnp.ones((rows, width), F32)
        flow[1] = jnp.zeros((rows, width), F32)

    def later(b, carry):
        at = pl.ds(pl.multiple_of(b * part, part), part)
        mask = keep_mask[at, :]
        for j in range(tiles):
            cols = lanes(j)
            f = forget[at, cols]
            th = jnp.tanh(f * masked[at, cols] + (1.0 - f) * cand[at, cols])
            o = gate[at, cols]
            direct = cot[at, cols].astype(F32) * o * (1.0 - th * th)
            side[at, cols] = jnp.where(o > 0.5, jnp.minimum(o - 1.0, -1e-30), o).astype(BF16)
            gate[at, cols] = direct
            keep = f * mask
            run, total = flow[0, :, cols], flow[1, :, cols]
            for t in range(BLOCK):
                now = slice(t * rows, (t + 1) * rows)
                run = run * keep[now]
                total = total + run * direct[now]
            flow[0, :, cols], flow[1, :, cols] = run, total
        return carry

    def output(b, carry):
        ch, h = b // blocks, lax.rem(b, blocks)
        slot = lax.rem(ch, 2)

        @pl.when(both(h == 0, ch >= 2))
        def _():
            act_copy(ch - 2).wait()

        at = pl.ds(pl.multiple_of(b * part, part), part)
        t0 = pl.multiple_of(h * BLOCK, BLOCK)
        for j in range(tiles):
            cols = lanes(j)
            f = forget[at, cols]
            th = jnp.tanh(f * masked[at, cols] + (1.0 - f) * cand[at, cols])
            q = side[at, cols].astype(F32)
            o = jnp.where(q < 0.0, 1.0 + q, q)
            rest = jnp.where(q < 0.0, -q, 1.0 - q)
            out = swapped(o * th + rest * own_tok[at, cols].astype(F32), BLOCK, rows).astype(BF16)
            act_buf[slot, :, pl.ds(t0, BLOCK), cols] = out.reshape(rows, BLOCK, LANE)
            side[at, cols] = (cot[at, cols].astype(F32) * rest).astype(BF16)

        @pl.when(h == blocks - 1)
        def _():
            act_copy(ch).start()

        return carry

    def end_output():
        for target in (sibling, across):
            pl.semaphore_signal(ready_sem, inc=1, device_id=(tm, target), device_id_type=MESH)

    def end_later():
        near[1, 0] = flow[1]
        for j in range(tiles):
            far[1, tm, j : j + 1, :] = spanning(flow[1, :, lanes(j)])
        pl.when(tm > 0)(lambda: near_copy(1, tm - 1).start())
        peers(lambda p: far_copy(1, tm, p).start())
        more[...] = jnp.zeros_like(more)

    remote(all_tokens, all_tokens, d_send, d_recv.at[0], (tm, sibling)).wait_send()

    n = tm_count // 2
    o, y = tm // 2, lax.rem(tm, 2)
    partner = (o * 2 + 1 - y, chan)
    left = (lax.rem(o - 1 + n, n) * 2 + y, chan)
    right = (lax.rem(o + 1, n) * 2 + y, chan)
    ring = ring_of(tm_count)
    ends, middle = (0, n - 1), (n // 2 - 1, n // 2)
    lines = [(0, middle[0] + y, n // 2, 1, None)]
    for l in (1, 2):
        if n == 4:
            lines += [(l, ends[l - 1], n - 1, 0, 0), (l, middle[l - 1], n // 2, 0, 1)]
        else:
            lines += [(l, middle[l - 1], n // 2, 0, None)]
    give_stage = 2 * (n // 2) + 2
    depth = LAG * max([give_stage] + [first + reach + (l > 0) + reach for l, c, reach, first, parity in lines])
    space = -(-depth // ring)

    def stage(s, number, parity=None):
        v = s - LAG * number
        u = v if space == 1 else v // space
        go = both(v >= 0, u < units)
        if space > 1:
            go = both(go, lax.rem(v, space) == 0)
        return u, go if parity is None else both(go, lax.rem(u, 2) == parity)

    def gate_of(u):
        return lax.rem(u // per_gate + 2, 3)

    def piece_of(l, mate=False):
        if l == 0:
            return (1 - y if mate else y) * PAIR, PAIR
        return 2 * PAIR + (l - 1) * LINE, LINE

    def wg_rows(l, u, mate=False):
        start, size = piece_of(l, mate)
        return pl.ds(pl.multiple_of(u * UNIT + start, 16), size)

    def fin_at(l, u):
        start, size = piece_of(l)
        return fin.at[pl.ds(pl.multiple_of((gate_of(u) * per_gate + lax.rem(u, per_gate)) * UNIT + start, 16), size)]

    def rx_rows(u, place, l):
        start = place * PAIR if l == 0 else 3 * PAIR + (place - 3) * LINE
        size = PAIR if l == 0 else LINE
        return pl.ds(pl.multiple_of(lax.rem(u, ring) * (3 * PAIR + 4 * LINE) + start, 16), size)

    def arrival(l, c, column, way, u):
        if l == 0:
            return 1 + way
        if l == 1:
            other = 6
        elif n == 4:
            other = jnp.where(column == jnp.where(lax.rem(u, 2) == 0, ends[0], middle[0]), 6, 3)
        else:
            other = jnp.where(column == middle[0], 6, 3)
        return jnp.where(column == c, 3 + way, other)

    def launch(make, u):
        @pl.when(u >= SENDS)
        def _():
            make(u - SENDS).wait_send()

        make(u).start()

    def to_rx(src, u, place, l, sem, target):
        return remote(src, rx.at[rx_rows(u, place, l)], sem, rx_recv.at[lax.rem(u, ring), place], target)

    def pair_copy(u):
        return to_rx(raw.at[wg_rows(0, u, True)], u, 0, 0, pair_send.at[lax.rem(u, SENDS)], partner)

    def red_copy(l, c, u, to_right):
        way, column = (0, o + 1) if to_right else (1, o - 1)
        return to_rx(
            raw.at[wg_rows(l, u)], u, arrival(l, c, column, way, u), l, red_send.at[l, lax.rem(u, SENDS)],
            right if to_right else left,
        )

    def red_wait(l, c, u, way):
        place = arrival(l, c, o, way, u)
        at = rx_rows(u, place, l)
        to_rx(rx.at[at], u, place, l, red_send.at[l, 0], partner).wait_recv()
        return rx[at].astype(F32)

    def bc_copy(l, u, to_right, src):
        return remote(
            src, fin_at(l, u), bc_send.at[l, lax.rem(u, SENDS), 1 if to_right else 0], bc_recv.at[l, lax.rem(u, ring)],
            right if to_right else left,
        )

    def swap_copy(l, u):
        return to_rx(raw.at[wg_rows(l, u)], u, 5, l, swap_send.at[lax.rem(u, SENDS)], partner)

    def give_copy(u, src):
        return remote(src, fin_at(0, u), give_send.at[lax.rem(u, SENDS)], give_recv.at[lax.rem(u, ring)], partner)

    def local_copy(l, u):
        return pltpu.make_async_copy(raw.at[wg_rows(l, u)], fin_at(l, u), loc_sem.at[l, lax.rem(u, SENDS)])

    def add_to(l, u, *others):
        at = wg_rows(l, u)
        total = raw[at].astype(F32)
        for v in others:
            total = total + v
        raw[at] = total.astype(BF16)

    def red_start(l, c, u):
        pl.when(o < c)(lambda: launch(lambda v: red_copy(l, c, v, True), u))
        pl.when(o > c)(lambda: launch(lambda v: red_copy(l, c, v, False), u))

    def publish(l, u):
        @pl.when(u >= SENDS)
        def _():
            local_copy(l, u - SENDS).wait()

        local_copy(l, u).start()
        pl.when(o > 0)(lambda: launch(lambda v: bc_copy(l, v, False, raw.at[wg_rows(l, v)]), u))
        pl.when(o < n - 1)(lambda: launch(lambda v: bc_copy(l, v, True, raw.at[wg_rows(l, v)]), u))
        if l == 0:
            launch(lambda v: give_copy(v, raw.at[wg_rows(0, v)]), u)

    def block_cols(c):
        return pl.ds(pl.multiple_of(c * width, width), width)

    def sib_rows(ch, q):
        return pl.ds(pl.multiple_of(units * UNIT + (lax.rem(ch, 4) * 2 + q) * span, span), span)

    def sib_copy(ch, q):
        slot = lax.rem(ch, 2)
        cols = sibling if q == 0 else lax.rem(sibling + 2, 4)
        return remote(
            terms.at[slot, cols], raw.at[sib_rows(ch, q)], sib_send.at[q], sib_recv.at[lax.rem(ch, 4), q], (tm, sibling)
        )

    def acr_copy(ch):
        return remote(
            terms.at[lax.rem(ch, 2), across], cot.at[rows_of(ch)], acr_send.at[lax.rem(ch, 2)], acr_recv.at[ch], (tm, across)
        )

    def row_copy(ch, source, d):
        return remote(
            row_rx.at[ch, source], row_rx.at[ch, source], row_send.at[lax.rem(ch, 4)], row_recv.at[lax.rem(ch, 4)],
            (tm, lax.rem(chan + d, 4)),
        )

    def row_all(ch):
        sums = row_rx.at[ch, pl.ds(0, chan_count - 1)]
        return remote(sums, sums, row_send.at[lax.rem(ch, 4)], row_recv.at[lax.rem(ch, 4)], (tm, sibling))

    def out_copy(ch):
        at = pl.ds(pl.multiple_of(ch * CHUNK, CHUNK), CHUNK)
        return pltpu.make_async_copy(out_buf.at[lax.rem(ch, 2)], in_grad.at[:, at, :], out_sem.at[lax.rem(ch, 2)])

    def project(ch):
        at = rows_of(ch)
        slot = lax.rem(ch, 2)

        @pl.when(ch == 0)
        def _():
            pl.semaphore_wait(ready_sem, 2)

        @pl.when(ch >= 2)
        def _():
            acr_copy(ch - 2).wait_send()

        for b in range(chan_count):
            total = jnp.zeros((span, width), F32)
            for k in range(3):
                total = total + lax.dot_general(
                    grad_buf[k, at, :], w_buf[k, b * width : (b + 1) * width, :], (((1,), (1,)), ((), ())),
                    preferred_element_type=F32,
                )
            terms[slot, b] = total.astype(BF16)
        sib_copy(ch, 0).start()
        sib_copy(ch, 1).start()

    def chip_sum(ch):
        slot = lax.rem(ch, 2)
        for q in range(2):
            sib_copy(ch, q).wait_recv()
        there = terms[slot, across].astype(F32) + raw[sib_rows(ch, 1)].astype(F32)
        terms[slot, across] = there.astype(BF16)
        acr_copy(ch).start()
        here = terms[slot, chan].astype(F32) + raw[sib_rows(ch, 0)].astype(F32)
        cand[rows_of(ch), :] = here
        for q in range(2):
            sib_copy(ch, q).wait_send()

    def full_sum(ch):
        acr_copy(ch).wait_recv()
        at = rows_of(ch)
        total = jnp.zeros((8, span), F32)
        pick = lax.broadcasted_iota(jnp.int32, (8, LANE), 0)
        for j in range(tiles):
            cols = lanes(j)
            fp, rp = grad_buf[1, at, cols].astype(F32), grad_buf[2, at, cols].astype(F32)
            g = cand[at, cols] + cot[at, cols].astype(F32) + fp * mix_f[0:1, cols] + rp * mix_r[0:1, cols]
            cand[at, cols] = g
            h = hat(at, j)
            nrm = h * mine(gain, j) + mine(shift, j)
            weighted = g * h
            for i, v in enumerate((fp * nrm, rp * nrm, fp, rp, weighted, g)):
                more[i, :, cols] = more[i, :, cols] + jnp.sum(v.reshape(CHUNK, rows, LANE), axis=0)
            for i, v in enumerate((g * mine(gain, j), weighted * mine(gain, j))):
                lead = jnp.where(pick == i, 1.0, 0.0).astype(BF16)
                high = v.astype(BF16)
                low_part = (v - high.astype(F32)).astype(BF16)
                for p in (high, low_part):
                    total = total + lax.dot_general(lead, p, (((1,), (1,)), ((), ())), preferred_element_type=F32)
        row_rx[ch, chan] = total
        pl.when(ch >= 4)(lambda: row_all(ch - 4).wait_send())
        for d in range(1, 4):
            row_copy(ch, chan, d).start()

    def finish(ch):
        row_all(ch).wait_recv()

        @pl.when(ch >= 2)
        def _():
            out_copy(ch - 2).wait()

        at = rows_of(ch)
        total = (row_rx[ch, 0] + row_rx[ch, 1] + row_rx[ch, 2] + row_rx[ch, 3]) * (1.0 / full)
        columns = jnp.transpose(total)
        first = jnp.broadcast_to(columns[:, 0:1], (span, LANE))
        second = jnp.broadcast_to(columns[:, 1:2], (span, LANE))
        for j in range(tiles):
            cols = lanes(j)
            g = cand[at, cols] * mine(gain, j)
            v = inv[at, :] * (g - first - hat(at, j) * second) + side[at, cols].astype(F32)
            out_buf[lax.rem(ch, 2), :, :, cols] = swapped(v, CHUNK, rows).astype(BF16).reshape(rows, CHUNK, LANE)
        out_copy(ch).start()

    def share_sums():
        for i in range(6):
            sum_rx[tm, i : i + 1, :] = jnp.sum(more[i], axis=0, keepdims=True)
        sum_rx[tm, 6:8, :] = jnp.zeros((2, width), F32)
        peers(lambda p: sum_copy(tm, p).start())

    def start_backward():
        far_all(1).wait_recv()
        pl.when(tm < last_tm)(lambda: near_copy(1, tm).wait_recv())

        def carry_back(i, v):
            d = tm_count - 1 - i
            return jnp.where(d > tm, far[0, d, 0:tiles, :] * v + far[1, d, 0:tiles, :], v)

        inflow = lax.fori_loop(0, tm_count, carry_back, jnp.zeros((tiles, LANE), F32))
        for j in range(tiles):
            row = jnp.broadcast_to(inflow[j : j + 1], (rows, LANE))
            others = jnp.where(tm == last_tm, 0.0, near[1, 1, :, lanes(j)])
            flow[0, :, lanes(j)] = jnp.where(spans > 0, row, others)

    def backward(i, carry):
        b = steps // BLOCK - 1 - i
        at = pl.ds(pl.multiple_of(b * part, part), part)
        mask = keep_mask[at, :]
        for j in range(tiles):
            cols = lanes(j)
            f = forget[at, cols]
            keep = f * mask
            direct = gate[at, cols]
            g = flow[0, :, cols]
            adjoint = [None] * BLOCK
            for t in reversed(range(BLOCK)):
                now = slice(t * rows, (t + 1) * rows)
                adjoint[t] = direct[now] + g
                g = keep[now] * adjoint[t]
            flow[0, :, cols] = g
            cand_grad = jnp.concatenate(adjoint, axis=0) * (1.0 - f)
            forget_pre = cand_grad * (masked[at, cols] - cand[at, cols]) * f
            grad_buf[0, at, cols] = cand_grad.astype(BF16)
            grad_buf[1, at, cols] = forget_pre.astype(BF16)
        return carry

    def close_first():
        x_move(all_tokens, all_tokens, 0).wait_send()
        s_move(all_tokens, all_tokens, 0).wait_send()
        for way in range(2):
            far_all(way).wait_send()
        pl.when(tm < last_tm)(lambda: near_copy(0, tm).wait_send())
        pl.when(tm > 0)(lambda: near_copy(1, tm).wait_send())
        pl.when(tm == last_tm)(last_all)
        pl.when(tm != last_tm)(lambda: last_copy(tm).wait_recv())
        for ch in (chunks - 2, chunks - 1):
            act_copy(ch).wait()
        for j in range(tiles):
            row = jnp.broadcast_to(last[j : j + 1], (rows, LANE))
            others = jnp.where(tm == last_tm, near[0, 0, :, lanes(j)], near[0, 2, :, lanes(j)])
            final[:, lanes(j)] = jnp.where(spans > 0, row, others)

    def close_second():
        for ch in range(chunks - 4, chunks):
            row_all(ch).wait_send()
        for ch in (chunks - 2, chunks - 1):
            out_copy(ch).wait()
            acr_copy(ch).wait_send()
        sums = sum_rx.at[pl.ds(0, tm_count - 1)]
        remote(sums, sums, sum_send, sum_recv, (tm, sibling)).wait()
        totals[...] = lax.fori_loop(0, tm_count, lambda d, v: v + sum_rx[d], jnp.zeros(totals.shape, F32))

    def slot_step(s, carry):
        u, go = stage(s, give_stage)
        pl.when(go)(lambda: give_copy(u, raw.at[wg_rows(0, u)]).wait_recv())

        for l, c, reach, first, parity in lines:
            late = first + reach + (1 if l else 0)
            u, go = stage(s, late + jnp.abs(o - c), parity)

            @pl.when(both(o != c, go))
            def _(l=l, c=c, u=u):
                bc_copy(l, u, True, fin_at(l, u)).wait_recv()
                pl.when(both(o < c, o > 0))(lambda: launch(lambda v: bc_copy(l, v, False, fin_at(l, v)), u))
                pl.when(both(o > c, o < n - 1))(lambda: launch(lambda v: bc_copy(l, v, True, fin_at(l, v)), u))
                if l == 0:
                    launch(lambda v: give_copy(v, fin_at(0, v)), u)

        for l, c, reach, first, parity in lines[1:]:
            u, go = stage(s, reach + 1, parity)

            @pl.when(both(o == c, go))
            def _(l=l, u=u):
                swap_copy(l, u).wait()
                add_to(l, u, rx[rx_rows(u, 5, l)].astype(F32))
                publish(l, u)

        for l, c, reach, first, parity in lines:
            u, go = stage(s, first + reach, parity)

            @pl.when(both(o == c, go))
            def _(l=l, c=c, u=u):
                if l == 0 and n > 2:
                    add_to(l, u, red_wait(l, c, u, 0), red_wait(l, c, u, 1))
                elif l > 0 and 0 < c < n - 1:
                    add_to(l, u, red_wait(l, c, u, 0), red_wait(l, c, u, 1))
                else:
                    pl.when(o > 0)(lambda: add_to(l, u, red_wait(l, c, u, 0)))
                    pl.when(o < n - 1)(lambda: add_to(l, u, red_wait(l, c, u, 1)))
                if l == 0:
                    publish(l, u)
                else:
                    swap_copy(l, u).start()

        u0, go0 = stage(s, 0)

        @pl.when(go0)
        def _():
            pl.when(u0 + 1 < units)(lambda: low_copy(u0 + 1).start())
            low_copy(u0).wait()
            g = jnp.dot(low[lax.rem(u0, 2)], grad_buf[gate_of(u0)], preferred_element_type=F32)
            raw[pl.ds(pl.multiple_of(u0 * UNIT, UNIT), UNIT)] = g.astype(BF16)
            launch(pair_copy, u0)
            for l, c, reach, first, parity in lines[1:]:
                mine_now = jnp.logical_or(o == 0, o == n - 1)
                if parity is not None:
                    mine_now = both(mine_now, lax.rem(u0, 2) == parity)
                pl.when(mine_now)(lambda l=l, c=c: red_start(l, c, u0))

        for l, c, reach, first, parity in lines:
            u, go = stage(s, first + jnp.where(o < c, o, n - 1 - o), parity)

            @pl.when(both(o < c, o > 0, go))
            def _(l=l, c=c, u=u):
                add_to(l, u, red_wait(l, c, u, 0))
                launch(lambda v: red_copy(l, c, v, True), u)

            @pl.when(both(o > c, o < n - 1, go))
            def _(l=l, c=c, u=u):
                add_to(l, u, red_wait(l, c, u, 1))
                launch(lambda v: red_copy(l, c, v, False), u)

        u, go = stage(s, 1)

        @pl.when(go)
        def _():
            pair_copy(u).wait_recv()
            add_to(0, u, rx[rx_rows(u, 0, 0)].astype(F32))
            pl.when(jnp.logical_or(o == 0, o == n - 1))(lambda: red_start(0, lines[0][1], u))

        count = steps // BLOCK
        pl.when(s == 0)(start_later)
        share = -(-count // LATER)
        at = s * share

        @pl.when(s < LATER)
        def _():
            lax.fori_loop(at, jnp.minimum(at + share, count), later, 0)

        pl.when(s == LATER - 1)(end_later)
        pl.when(s == ADJOINT)(start_backward)
        share = -(-count // (OUTPUT - ADJOINT))
        at2 = (s - ADJOINT) * share

        @pl.when(both(s >= ADJOINT, s < OUTPUT))
        def _():
            lax.fori_loop(at2, jnp.minimum(at2 + share, count), backward, 0)

        share = -(-count // (FIRST - OUTPUT))
        at3 = (s - OUTPUT) * share

        @pl.when(both(s >= OUTPUT, s < FIRST))
        def _():
            lax.fori_loop(at3, jnp.minimum(at3 + share, count), output, 0)

        pl.when(s == FIRST - 1)(end_output)

        for job, offset in ((finish, 5), (full_sum, 3), (chip_sum, 1), (project, 0)):
            at = s - FIRST - offset
            pl.when(both(at >= 0, lax.rem(at, 2) == 0, at // 2 < chunks))(lambda job=job, at=at: job(at // 2))
        pl.when(s == FIRST + 3)(close_first)
        pl.when(s == FIRST + 2 * chunks + 2)(share_sums)
        pl.when(s == FIRST + 2 * chunks + 6)(close_second)
        return carry

    slots = max((units - 1) * space + depth + 1, FIRST + 2 * chunks + 7)
    lax.fori_loop(0, slots, slot_step, 0)

    def close_unit(u, carry):
        give_copy(u, raw.at[wg_rows(0, u)]).wait_send()
        pair_copy(u).wait_send()
        for l, c, reach, first, parity in lines:

            @pl.when(True if parity is None else lax.rem(u, 2) == parity)
            def _(l=l, c=c):
                src = raw.at[wg_rows(l, u)]
                pl.when(o != c)(lambda: red_copy(l, c, u, True).wait_send())
                pl.when(o == c)(lambda: local_copy(l, u).wait())
                pl.when(both(o <= c, o > 0))(lambda: bc_copy(l, u, False, src).wait_send())
                pl.when(both(o >= c, o < n - 1))(lambda: bc_copy(l, u, True, src).wait_send())

        return carry

    lax.fori_loop(units - SENDS, units, close_unit, 0)


def layer(tokens, weights, cotangent, gain, shift, mix_f, mix_r, bias_f, bias_r, bank, selector, resets):
    rows, steps, width = tokens.shape
    full = gain.shape[-1]
    tm_count, chan_count = lax.axis_size("tm"), lax.axis_size("chan")
    chunks = steps // CHUNK
    span = CHUNK * rows
    pieces = chunks - 1 + CHUNK // BLOCK
    count = steps * rows
    units = 3 * full // UNIT
    ring = ring_of(tm_count)
    hbm = pl.BlockSpec(memory_space=pl.ANY)
    vmem = pl.BlockSpec(memory_space=pltpu.VMEM)
    smem = pl.BlockSpec(memory_space=pltpu.SMEM)
    dma = pltpu.SemaphoreType.DMA
    stat = pltpu.VMEM((CHUNK // BLOCK, rows, BLOCK, LANE), F32)
    wide = pltpu.VMEM((count, width), F32)
    narrow = pltpu.VMEM((count, LANE), F32)
    short = pltpu.VMEM((count, width), BF16)
    return pl.pallas_call(
        layer_kernel,
        out_shape=(
            jax.ShapeDtypeStruct((units * UNIT, width), BF16),
            jax.ShapeDtypeStruct(tokens.shape, BF16),
            jax.ShapeDtypeStruct(tokens.shape, BF16),
            jax.ShapeDtypeStruct((full, count), BF16),
            jax.ShapeDtypeStruct((rows, width), F32),
            jax.ShapeDtypeStruct((8, width), F32),
        ),
        in_specs=[hbm, hbm, hbm] + [vmem] * 7 + [smem, vmem],
        out_specs=(hbm, hbm, hbm, hbm, vmem, vmem),
        scratch_shapes=[
            pltpu.VMEM((chunks * chan_count * span, width), BF16),
            pltpu.VMEM((ring * (3 * PAIR + 4 * LINE), width), BF16),
            pltpu.VMEM((2, span, full), BF16),
            pltpu.VMEM((full, span), BF16),
            pltpu.VMEM((3, full, width), BF16),
            wide, wide, wide, wide,
            short,
            pltpu.VMEM((2, rows, CHUNK, width), BF16),
            short,
            narrow, narrow, narrow,
            pltpu.VMEM((3, count, width), BF16),
            pltpu.VMEM((2, rows, CHUNK, width), BF16),
            short,
            pltpu.VMEM((2, chan_count, span, width), BF16),
            pltpu.VMEM((2, rows, CHUNK, width), BF16),
            pltpu.VMEM((chunks, 4, 8, span), F32),
            pltpu.VMEM((6, rows, width), F32),
            pltpu.VMEM((tm_count, 8, width), F32),
            stat, stat, stat,
            pltpu.VMEM((rows, width), F32),
            pltpu.VMEM((2, 3, rows, width), F32),
            pltpu.VMEM((2, tm_count, 8, LANE), F32),
            pltpu.VMEM((2, rows, width), F32),
            pltpu.VMEM((resets.shape[1], rows, LANE), jnp.int32),
            dma(()), dma((pieces,)), dma(()), dma(()), dma(()), dma((pieces,)), dma(()),
            dma((3,)), dma((2,)), dma((2,)), dma(()), dma((2,)),
            dma((2,)), dma((2,)), dma((2,)), dma((2,)), dma(()), dma(()),
            pltpu.SemaphoreType.REGULAR,
            dma((2,)), dma((3, SENDS)), dma((SENDS,)), dma((3, SENDS)), dma((3, SENDS, 2)), dma((3, ring)), dma((SENDS,)),
            dma((SENDS,)), dma((ring,)), dma((ring, 7)), dma((2,)), dma((4, 2)), dma((2,)), dma((chunks,)),
            dma((4,)), dma((4,)), dma(()), dma(()),
        ],
        compiler_params=pltpu.CompilerParams(collective_id=0, has_side_effects=True, vmem_limit_bytes=VMEM_BYTES),
        name="whole",
    )(tokens, weights, cotangent, gain, shift, mix_f, mix_r, bias_f, bias_r, bank, selector, resets)


def tail_kernel(
    fin, in_grad, act, final, totals, wide_out, in_out, act_out, final_out, s0, s1, s2, s3, s4, s5,
    fin_buf, wide_buf, in_buf, in_wide, act_buf, load_sem, store_sem,
):
    def move(src, dst, sem, i, n):
        at = pl.ds(i * n, n)
        return pltpu.make_async_copy(src.at[at], dst.at[at], sem)

    jobs = []

    def job(src, buf, wide, dst, parts):
        n = src.shape[0] // parts
        for i in range(parts):
            k = len(jobs)
            jobs.append((move(src, buf, load_sem.at[k], i, n), buf, wide, i * n, n, move(wide, dst, store_sem.at[k], i, n)))

    job(fin, fin_buf, wide_buf, wide_out, TAIL)
    job(in_grad, in_buf, in_wide, in_out, 2)
    job(act, act_buf, act_buf, act_out, 2)
    order = [0, 4, 1, 6, 2, 5, 3, 7] if TAIL == 4 else list(range(len(jobs)))
    for k in order:
        jobs[k][0].start()
    final_out[...] = final[...]
    for i, ref in enumerate((s0, s1, s2, s3, s4, s5)):
        ref[...] = totals[i : i + 1, :]
    for k in order:
        load, buf, wide, start, n, store = jobs[k]
        load.wait()
        if buf is not wide:
            step = 64 if len(buf.shape) == 2 else 1

            def cast(j, carry, buf=buf, wide=wide, start=start, step=step):
                at = pl.ds(start + j * step, step)
                wide[at] = buf[at].astype(F32)
                return carry

            lax.fori_loop(0, n // step, cast, 0, unroll=2)
        store.start()
    for k in order:
        jobs[k][-1].wait()


def tail(fin, in_grad, act, final, totals):
    width = fin.shape[-1]
    hbm = pl.BlockSpec(memory_space=pl.ANY)
    vmem = pl.BlockSpec(memory_space=pltpu.VMEM)
    dma = pltpu.SemaphoreType.DMA
    line = jax.ShapeDtypeStruct((1, width), F32)
    return pl.pallas_call(
        tail_kernel,
        out_shape=(
            jax.ShapeDtypeStruct(fin.shape, F32),
            jax.ShapeDtypeStruct(in_grad.shape, F32),
            jax.ShapeDtypeStruct(act.shape, BF16),
            jax.ShapeDtypeStruct(final.shape, F32),
        ) + (line,) * 6,
        in_specs=[hbm] * 3 + [vmem] * 2,
        out_specs=(hbm,) * 3 + (vmem,) * 7,
        scratch_shapes=[
            pltpu.VMEM(fin.shape, BF16), pltpu.VMEM(fin.shape, F32),
            pltpu.VMEM(in_grad.shape, BF16), pltpu.VMEM(in_grad.shape, F32), pltpu.VMEM(act.shape, BF16),
            dma((TAIL + 4,)), dma((TAIL + 4,)),
        ],
        compiler_params=pltpu.CompilerParams(vmem_limit_bytes=VMEM_BYTES),
        name="tail",
    )(fin, in_grad, act, final, totals)


def body(
    tokens, ln_gain, ln_bias, weights, mix_forget, mix_reset, bias_forget, bias_reset, state_bank, selector, resets, cotangent
):
    fin, in_grad, act, _, final, totals = layer(
        tokens, weights, cotangent, ln_gain[None], ln_bias[None], mix_forget[None], mix_reset[None], bias_forget[None],
        bias_reset[None], state_bank, selector, resets,
    )
    wide, in_grad, act, final, *sums = tail(fin, in_grad, act, final, totals)
    sums = [v[0] for v in sums]
    return act, final, in_grad, wide.reshape(weights.shape), sums[4], sums[5], sums[0], sums[1], sums[2], sums[3]


def solution(mesh):
    placed = (
        P(None, "tm", "chan"), P(), P(), P(None, None, "chan"), P("chan"), P("chan"), P("chan"), P("chan"),
        P(None, "chan"), P(), P(), P(None, "tm", "chan"),
    )
    return jax.shard_map(
        body,
        mesh=mesh,
        in_specs=placed,
        out_specs=(
            P(None, "tm", "chan"), P(None, "chan"), P(None, "tm", "chan"), P(None, None, "chan"),
            P("chan"), P("chan"), P("chan"), P("chan"), P("chan"), P("chan"),
        ),
        check_vma=False,
    )
```

```python
import jax
import jax.numpy as jnp
from jax import lax
from jax.experimental import pallas as pl
from jax.experimental.pallas import tpu as pltpu
from jax.sharding import PartitionSpec as P

EPSILON = 1e-05
CHUNK = 32
BLOCK = 16
LANE = 128
AHEAD = 4
UNIT = 256
LAG = 2
PAIR = 80
LINE = 48
SENDS = 2
VMEM_BYTES = 63 << 20
TAIL = 2
LATER = 4
ADJOINT = 6
OUTPUT = 8
FIRST = 12
MESH = pl.DeviceIdType.MESH
F32 = jnp.float32
BF16 = jnp.bfloat16


def sigmoid(v):
    return 1.0 / (1.0 + jnp.exp(-v))


def swapped(v, outer, inner):
    return jnp.swapaxes(v.reshape(outer, inner, v.shape[-1]), 0, 1).reshape(outer * inner, v.shape[-1])


def both(*conditions):
    out = conditions[0]
    for c in conditions[1:]:
        out = jnp.logical_and(out, c)
    return out


def ring_of(tm_count):
    return 14 if tm_count <= 8 else 3


def layer_kernel(
    tokens, weights, cotangent, gain, shift, mix_f, mix_r, bias_f, bias_r, bank, selector, resets,
    fin, in_grad, act, low_t, final, totals,
    raw, rx, low, low_t_buf, w_buf, cand, forget, gate, masked, own_tok, cot_raw, cot, mean, inv, keep_mask, grad_buf,
    act_buf, side, terms, out_buf, row_rx, more, sum_rx, mean_s, inv_s, part_s, entry, near, far, flow, reset_rows,
    x_send, x_recv, s_send, s_recv, d_send, d_recv, own_sem, w_sem, cot_sem, act_sem, tr_sem, low_sem,
    near_send, near_recv, far_send, far_recv, last_send, last_recv, ready_sem, out_sem, loc_sem, pair_send, red_send,
    bc_send, bc_recv, swap_send, give_send, give_recv, rx_recv, sib_send, sib_recv, acr_send, acr_recv, row_send,
    row_recv, sum_send, sum_recv,
):
    rows, steps, width = tokens.shape
    full = gain.shape[-1]
    tm_count, tm = lax.axis_size("tm"), lax.axis_index("tm")
    chan_count, chan = lax.axis_size("chan"), lax.axis_index("chan")
    sibling = chan + 1 - 2 * lax.rem(chan, 2)
    across = lax.rem(chan + 2, 4)
    chunks = steps // CHUNK
    span = CHUNK * rows
    part = BLOCK * rows
    tiles = width // LANE
    blocks = CHUNK // BLOCK
    units = 3 * full // UNIT
    per_gate = full // UNIT

    def remote(src, dst, send, recv, target):
        return pltpu.make_async_remote_copy(src, dst, send, recv, device_id=target, device_id_type=MESH)

    def lanes(j):
        return slice(j * LANE, (j + 1) * LANE)

    def mine(ref, j):
        return ref[0:1, pl.ds(pl.multiple_of(chan * width + j * LANE, LANE), LANE)]

    def hat(at, j):
        return (own_tok[at, lanes(j)].astype(F32) - mean[at, :]) * inv[at, :]

    def normed(at, j):
        return hat(at, j) * mine(gain, j) + mine(shift, j)

    def rows_of(ch):
        return pl.ds(pl.multiple_of(ch * span, span), span)

    def raw_rows(ch, block, h0, h1):
        return pl.ds(pl.multiple_of((ch * chan_count + block) * span + h0 * part, part), (h1 - h0) * part)

    def token_copies(ch, h0, h1, copy):
        at = [pl.ds(pl.multiple_of(ch * CHUNK + h * BLOCK, BLOCK), BLOCK) for h in range(h0, h1)]
        return [
            copy(tokens.at[:, t, :], raw.at[raw_rows(ch, chan, h, h + 1)].reshape(rows, BLOCK, width), ch + h0)
            for h, t in zip(range(h0, h1), at)
        ]

    def own_move(src, dst, sem):
        return pltpu.make_async_copy(src, dst, own_sem)

    def x_move(src, dst, sem):
        return remote(src, dst, x_send, x_recv.at[sem], (tm, across))

    def s_move(src, dst, sem):
        return remote(src, dst, s_send, s_recv, (tm, sibling))

    def arrived(ch, block, h0, h1, copy):
        here = raw.at[raw_rows(ch, block, h0, h1)]
        return copy(here, here, ch + h0)

    def d_copy(ch, h0, h1):
        view = raw.at[raw_rows(ch, across, h0, h1)]
        return remote(view, view, d_send, d_recv.at[ch + h0], (tm, sibling))

    all_tokens = raw.at[pl.ds(0, steps * rows)]

    def cot_copy(ch):
        at = pl.ds(pl.multiple_of(ch * CHUNK, CHUNK), CHUNK)
        return pltpu.make_async_copy(cotangent.at[:, at, :], cot_raw.at[lax.rem(ch, 2)], cot_sem.at[lax.rem(ch, 2)])

    def act_copy(ch):
        at = pl.ds(pl.multiple_of(ch * CHUNK, CHUNK), CHUNK)
        return pltpu.make_async_copy(act_buf.at[lax.rem(ch, 2)], act.at[:, at, :], act_sem.at[lax.rem(ch, 2)])

    def tr_copy(ch):
        return pltpu.make_async_copy(low_t_buf, low_t.at[:, rows_of(ch)], tr_sem)

    def low_copy(u):
        at = pl.ds(pl.multiple_of(lax.rem(u, per_gate) * UNIT, UNIT), UNIT)
        return pltpu.make_async_copy(low_t.at[at], low.at[lax.rem(u, 2)], low_sem.at[lax.rem(u, 2)])

    w_copies = [pltpu.make_async_copy(weights.at[k], w_buf.at[k], w_sem.at[k]) for k in range(3)]

    barrier = pltpu.get_barrier_semaphore()
    for d in range(1, 4):
        pl.semaphore_signal(barrier, inc=1, device_id=(tm, lax.rem(chan + d, 4)), device_id_type=MESH)

    def greet(d, carry):
        pl.semaphore_signal(barrier, inc=1, device_id=(lax.rem(tm + d, tm_count), chan), device_id_type=MESH)
        return carry

    lax.fori_loop(1, tm_count, greet, 0)
    def start_own(ch, carry):
        for copy in token_copies(ch, 0, blocks, own_move):
            copy.start()
        return carry

    def start_sibling(ch, carry):
        for copy in token_copies(ch, 0, blocks, s_move):
            copy.start()
        return carry

    lax.fori_loop(0, chunks, start_own, 0)
    cot_copy(0).start()
    for copy in w_copies:
        copy.start()
    pl.semaphore_wait(barrier, tm_count + 2)
    for ch in range(AHEAD):
        for copy in token_copies(ch, 0, blocks, x_move):
            copy.start()
    lax.fori_loop(0, chunks, start_sibling, 0)

    count = resets.shape[1]
    for j in range(count):
        reset_rows[j] = jnp.broadcast_to(resets[:, j : j + 1], (rows, LANE))

    def mark(t, carry):
        at = tm * steps + t

        def compare(j, hit):
            return jnp.maximum(hit, jnp.where(reset_rows[j] == at, 1.0, 0.0))

        hit = lax.fori_loop(0, count, compare, jnp.zeros((rows, LANE), F32), unroll=16)
        keep_mask[pl.ds(pl.multiple_of(t * rows, rows), rows), :] = 1.0 - hit
        return carry

    lax.fori_loop(0, steps, mark, 0)
    for r in range(rows):
        entry[r : r + 1, :] = bank[pl.ds(selector[r], 1), :]

    def flip(ch):
        @pl.when(ch >= 1)
        def _():
            tr_copy(ch - 1).wait()

        def one(j, carry):
            cols = pl.ds(pl.multiple_of(j * 256, 256), 256)
            low_t_buf[cols, :] = jnp.transpose(low[lax.rem(ch, 2), :, cols])
            return carry

        lax.fori_loop(0, full // 256, one, 0, unroll=2)
        tr_copy(ch).start()

    def project_one(ch, k, h0, h1):
        at = pl.ds(pl.multiple_of(ch * span + h0 * part, part), (h1 - h0) * part)
        ref = (cand, forget, gate)[k]
        ref[at, :] = jnp.dot(low[lax.rem(ch, 2), h0 * part : h1 * part], w_buf[k], preferred_element_type=F32)

    def send_across(ch):
        for copy in token_copies(ch, 0, blocks, x_move):
            copy.start()

    def send_last():
        for h in range(blocks):
            for copy in token_copies(chunks - 1, h, h + 1, x_move):
                copy.start()

    def gates(b, carry):
        a_list, b_list = list(carry[0]), list(carry[1])
        at = pl.ds(pl.multiple_of(b * part, part), part)
        mask = keep_mask[at, :]
        for j in range(tiles):
            cols = lanes(j)
            nrm = normed(at, j)
            f = sigmoid(forget[at, cols] + mix_f[0:1, cols] * nrm + bias_f[0:1, cols])
            o = sigmoid(gate[at, cols] + mix_r[0:1, cols] * nrm + bias_r[0:1, cols])
            forget[at, cols] = f
            gate[at, cols] = o
            inject = (1.0 - f) * cand[at, cols]
            keep = f * mask
            for t in range(BLOCK):
                now = slice(t * rows, (t + 1) * rows)
                a_list[j] = a_list[j] * keep[now]
                b_list[j] = b_list[j] * keep[now] + inject[now]
        return tuple(a_list), tuple(b_list)

    def gather_step(ch, runs, h0=0, h1=blocks):
        entire = h1 - h0 == blocks
        if entire:
            pl.when(ch + AHEAD < chunks - 1)(lambda: send_across(ch + AHEAD))
            pl.when(ch + AHEAD == chunks - 1)(send_last)
            cot_copy(ch + 1).start()

        base = pl.multiple_of(ch * span, span)
        slot = lax.rem(ch, 2)

        arrived(ch, across, h0, h1, x_move).wait_recv()
        d_copy(ch, h0, h1).start()

        if entire:
            pl.when(ch >= 1)(lambda: project_one(ch - 1, 2, 0, blocks))
        elif h0 == 0:
            project_one(ch - 1, 2, 0, blocks)
        else:
            project_one(ch, 2, 0, h0)
        if h0 == 0:
            runs = lax.fori_loop(jnp.maximum(ch - 1, 0) * blocks, ch * blocks, gates, runs)
        else:
            runs = lax.fori_loop(ch * blocks, ch * blocks + h0, gates, runs)

        if h0 == 0:
            cot_copy(ch).wait()
            for h in range(blocks):
                for j in range(tiles):
                    v = cot_raw[slot, :, h * BLOCK : (h + 1) * BLOCK, lanes(j)].astype(F32).reshape(part, LANE)
                    at = pl.ds(pl.multiple_of(base + h * part, part), part)
                    cot[at, lanes(j)] = swapped(v, rows, BLOCK).astype(BF16)
        if entire:

            @pl.when(ch == 0)
            def _():
                own_move(all_tokens, all_tokens, 0).wait()
                s_move(all_tokens, all_tokens, 0).wait_recv()
                for copy in w_copies:
                    copy.wait()

        d_copy(ch, h0, h1).wait_recv()

        first = pl.multiple_of(ch * chan_count * span, span)

        def tokens_at(block, r, h, cols):
            at = pl.multiple_of(first + block * span + h * part + r * BLOCK, BLOCK)
            return raw[pl.ds(at, BLOCK), cols].astype(F32)

        def each(i, turn):
            r, h = lax.rem(i, rows), h0 + i // rows
            totals = [jnp.zeros((BLOCK, LANE), F32) for _ in range(chan_count)]
            for j in range(tiles):
                for b in range(chan_count):
                    totals[b] = totals[b] + turn(tokens_at(b, r, h, lanes(j)))
            while len(totals) > 1:
                totals = [a + b for a, b in zip(totals[::2], totals[1::2])]
            part_s[h, r] = totals[0]

        def sum_rows(i, carry):
            each(i, lambda v: v)
            return carry

        count = (h1 - h0) * rows
        stat = (h1 - h0,) + mean_s.shape[1:]
        lax.fori_loop(0, count, sum_rows, 0, unroll=2)
        total = jnp.sum(part_s[h0:h1], axis=-1, keepdims=True)
        mean_s[h0:h1] = jnp.broadcast_to(total * (1.0 / full), stat)

        def square_rows(i, carry):
            m = mean_s[h0 + i // rows, lax.rem(i, rows)]
            each(i, lambda v: (v - m) * (v - m))
            return carry

        lax.fori_loop(0, count, square_rows, 0, unroll=2)
        var = jnp.sum(part_s[h0:h1], axis=-1, keepdims=True) * (1.0 / full)
        inv_s[h0:h1] = jnp.broadcast_to(lax.rsqrt(var + EPSILON), stat)

        for h in range(h0, h1):
            mean_h = mean_s[h].reshape(part, LANE)
            inv_h = inv_s[h].reshape(part, LANE)

            def normalize(j, carry, h=h, mean_h=mean_h, inv_h=inv_h):
                cols = pl.ds(pl.multiple_of(j * LANE, LANE), LANE)
                inner = pl.ds(pl.multiple_of(lax.rem(j, tiles) * LANE, LANE), LANE)
                v = jnp.concatenate([tokens_at(j // tiles, r, h, inner) for r in range(rows)], axis=0)
                v = (v - mean_h) * inv_h * gain[0:1, cols] + shift[0:1, cols]
                low[slot, h * part : (h + 1) * part, cols] = swapped(v, rows, BLOCK).astype(BF16)
                return carry

            lax.fori_loop(0, full // LANE, normalize, 0, unroll=2)
            at = pl.ds(pl.multiple_of(base + h * part, part), part)
            mean[at, :] = swapped(mean_h, rows, BLOCK)
            inv[at, :] = swapped(inv_h, rows, BLOCK)
            for j in range(tiles):
                v = jnp.concatenate([tokens_at(chan, r, h, lanes(j)) for r in range(rows)], axis=0)
                own_tok[at, lanes(j)] = swapped(v, rows, BLOCK).astype(BF16)

        project_one(ch, 0, h0, h1)
        project_one(ch, 1, h0, h1)
        if entire:
            flip(ch)
        return runs

    ones = tuple(jnp.ones((rows, LANE), F32) for _ in range(tiles))
    zeros = tuple(jnp.zeros((rows, LANE), F32) for _ in range(tiles))
    runs = lax.fori_loop(0, chunks - 1, gather_step, (ones, zeros))
    for h in range(blocks):
        runs = gather_step(chunks - 1, runs, h, h + 1)
    project_one(chunks - 1, 2, blocks - 1, blocks)
    a_run, b_run = lax.fori_loop(chunks * blocks - 1, chunks * blocks, gates, runs)

    spans = jnp.where(reset_rows[0] >= tm_count * steps, 1.0, 0.0)
    last_tm = tm_count - 1

    def spanning(v):
        return jnp.sum(v * spans, axis=0, keepdims=True)

    def near_copy(way, target):
        return remote(near.at[way, 0], near.at[way, 1], near_send.at[way], near_recv.at[way], (target, chan))

    def far_copy(way, source, target):
        return remote(
            far.at[way, source], far.at[way, source], far_send.at[way], far_recv.at[way], (target, chan)
        )

    def far_all(way):
        maps = far.at[way, pl.ds(0, tm_count - 1)]
        return remote(maps, maps, far_send.at[way], far_recv.at[way], (tm, sibling))

    def last_copy(target):
        return remote(near.at[0, 0], near.at[0, 2], last_send, last_recv, (target, chan))

    def last_all():
        sent = sum_rx.at[pl.ds(0, tm_count - 1)]
        remote(sent, sent, last_send, last_recv, (tm, sibling)).wait_send()

    def sum_copy(source, target):
        return remote(sum_rx.at[source], sum_rx.at[source], sum_send, sum_recv, (target, chan))

    def peers(act_on):
        def one(d, carry):
            act_on(lax.rem(tm + d, tm_count))
            return carry

        lax.fori_loop(1, tm_count, one, 0)

    for j in range(tiles):
        near[0, 0, :, lanes(j)] = b_run[j]
        far[0, tm, j : j + 1, :] = spanning(a_run[j])
        far[0, tm, tiles + j : tiles + j + 1, :] = spanning(b_run[j])
    pl.when(tm < last_tm)(lambda: near_copy(0, tm + 1).start())
    peers(lambda p: far_copy(0, tm, p).start())
    pl.when(tm == last_tm)(lambda: peers(lambda p: last_copy(p).start()))
    flip(chunks - 1)
    far_all(0).wait_recv()
    pl.when(tm > 0)(lambda: near_copy(0, tm).wait_recv())

    def carry_on(d, carry):
        state, here = carry
        here = jnp.where(d == tm, state, here)
        return far[0, d, 0:tiles, :] * state + far[0, d, tiles : 2 * tiles, :], here

    lead = jnp.concatenate([spanning(entry[:, lanes(j)]) for j in range(tiles)], axis=0)
    last, here = lax.fori_loop(0, tm_count, carry_on, (lead, lead))
    states = []
    for j in range(tiles):
        row = jnp.broadcast_to(here[j : j + 1], (rows, LANE))
        others = jnp.where(tm == 0, entry[:, lanes(j)], near[0, 1, :, lanes(j)])
        states.append(jnp.where(spans > 0, row, others))
    tr_copy(chunks - 1).wait()
    low_copy(0).start()

    def forward(b, states):
        states = list(states)
        at = pl.ds(pl.multiple_of(b * part, part), part)
        mask = keep_mask[at, :]
        for j in range(tiles):
            cols = lanes(j)
            f = forget[at, cols]
            inject = (1.0 - f) * cand[at, cols]
            before, after = [], []
            c = states[j]
            for t in range(BLOCK):
                now = slice(t * rows, (t + 1) * rows)
                c = c * mask[now]
                before.append(c)
                c = f[now] * c + inject[now]
                after.append(c)
            states[j] = c
            masked[at, cols] = jnp.concatenate(before, axis=0)
            th = jnp.tanh(jnp.concatenate(after, axis=0))
            o = gate[at, cols]
            gate_grad = cot[at, cols].astype(F32) * (th - own_tok[at, cols].astype(F32))
            grad_buf[2, at, cols] = (gate_grad * o * (1.0 - o)).astype(BF16)
        return tuple(states)

    lax.fori_loop(0, steps // BLOCK, forward, tuple(states))

    def start_later():
        flow[0] = jnp.ones((rows, width), F32)
        flow[1] = jnp.zeros((rows, width), F32)

    def later(b, carry):
        at = pl.ds(pl.multiple_of(b * part, part), part)
        mask = keep_mask[at, :]
        for j in range(tiles):
            cols = lanes(j)
            f = forget[at, cols]
            th = jnp.tanh(f * masked[at, cols] + (1.0 - f) * cand[at, cols])
            o = gate[at, cols]
            direct = cot[at, cols].astype(F32) * o * (1.0 - th * th)
            side[at, cols] = jnp.where(o > 0.5, jnp.minimum(o - 1.0, -1e-30), o).astype(BF16)
            gate[at, cols] = direct
            keep = f * mask
            run, total = flow[0, :, cols], flow[1, :, cols]
            for t in range(BLOCK):
                now = slice(t * rows, (t + 1) * rows)
                run = run * keep[now]
                total = total + run * direct[now]
            flow[0, :, cols], flow[1, :, cols] = run, total
        return carry

    def output(b, carry):
        ch, h = b // blocks, lax.rem(b, blocks)
        slot = lax.rem(ch, 2)

        @pl.when(both(h == 0, ch >= 2))
        def _():
            act_copy(ch - 2).wait()

        at = pl.ds(pl.multiple_of(b * part, part), part)
        t0 = pl.multiple_of(h * BLOCK, BLOCK)
        for j in range(tiles):
            cols = lanes(j)
            f = forget[at, cols]
            th = jnp.tanh(f * masked[at, cols] + (1.0 - f) * cand[at, cols])
            q = side[at, cols].astype(F32)
            o = jnp.where(q < 0.0, 1.0 + q, q)
            rest = jnp.where(q < 0.0, -q, 1.0 - q)
            out = swapped(o * th + rest * own_tok[at, cols].astype(F32), BLOCK, rows).astype(BF16)
            act_buf[slot, :, pl.ds(t0, BLOCK), cols] = out.reshape(rows, BLOCK, LANE)
            side[at, cols] = (cot[at, cols].astype(F32) * rest).astype(BF16)

        @pl.when(h == blocks - 1)
        def _():
            act_copy(ch).start()

        return carry

    def end_output():
        for target in (sibling, across):
            pl.semaphore_signal(ready_sem, inc=1, device_id=(tm, target), device_id_type=MESH)

    def end_later():
        near[1, 0] = flow[1]
        for j in range(tiles):
            far[1, tm, j : j + 1, :] = spanning(flow[1, :, lanes(j)])
        pl.when(tm > 0)(lambda: near_copy(1, tm - 1).start())
        peers(lambda p: far_copy(1, tm, p).start())
        more[...] = jnp.zeros_like(more)

    remote(all_tokens, all_tokens, d_send, d_recv.at[0], (tm, sibling)).wait_send()

    n = tm_count // 2
    o, y = tm // 2, lax.rem(tm, 2)
    partner = (o * 2 + 1 - y, chan)
    left = (lax.rem(o - 1 + n, n) * 2 + y, chan)
    right = (lax.rem(o + 1, n) * 2 + y, chan)
    ring = ring_of(tm_count)
    ends, middle = (0, n - 1), (n // 2 - 1, n // 2)
    lines = [(0, middle[0] + y, n // 2, 1, None)]
    for l in (1, 2):
        if n == 4:
            lines += [(l, ends[l - 1], n - 1, 0, 0), (l, middle[l - 1], n // 2, 0, 1)]
        else:
            lines += [(l, middle[l - 1], n // 2, 0, None)]
    give_stage = 2 * (n // 2) + 2
    depth = LAG * max([give_stage] + [first + reach + (l > 0) + reach for l, c, reach, first, parity in lines])
    space = -(-depth // ring)

    def stage(s, number, parity=None):
        v = s - LAG * number
        u = v if space == 1 else v // space
        go = both(v >= 0, u < units)
        if space > 1:
            go = both(go, lax.rem(v, space) == 0)
        return u, go if parity is None else both(go, lax.rem(u, 2) == parity)

    def gate_of(u):
        return lax.rem(u // per_gate + 2, 3)

    def piece_of(l, mate=False):
        if l == 0:
            return (1 - y if mate else y) * PAIR, PAIR
        return 2 * PAIR + (l - 1) * LINE, LINE

    def wg_rows(l, u, mate=False):
        start, size = piece_of(l, mate)
        return pl.ds(pl.multiple_of(u * UNIT + start, 16), size)

    def fin_at(l, u):
        start, size = piece_of(l)
        return fin.at[pl.ds(pl.multiple_of((gate_of(u) * per_gate + lax.rem(u, per_gate)) * UNIT + start, 16), size)]

    def rx_rows(u, place, l):
        start = place * PAIR if l == 0 else 3 * PAIR + (place - 3) * LINE
        size = PAIR if l == 0 else LINE
        return pl.ds(pl.multiple_of(lax.rem(u, ring) * (3 * PAIR + 4 * LINE) + start, 16), size)

    def arrival(l, c, column, way, u):
        if l == 0:
            return 1 + way
        if l == 1:
            other = 6
        elif n == 4:
            other = jnp.where(column == jnp.where(lax.rem(u, 2) == 0, ends[0], middle[0]), 6, 3)
        else:
            other = jnp.where(column == middle[0], 6, 3)
        return jnp.where(column == c, 3 + way, other)

    def launch(make, u):
        @pl.when(u >= SENDS)
        def _():
            make(u - SENDS).wait_send()

        make(u).start()

    def rx_sem(u, place, l):
        if isinstance(place, int):
            which = (0, 1, 1, 2, 2, 3, 4)[place]
        else:
            which = jnp.where(place == 6, 4, 2)
        return rx_recv.at[lax.rem(u, ring), which]

    def to_rx(src, u, place, l, sem, target):
        return remote(src, rx.at[rx_rows(u, place, l)], sem, rx_sem(u, place, l), target)

    def pair_copy(u):
        return to_rx(raw.at[wg_rows(0, u, True)], u, 0, 0, pair_send.at[lax.rem(u, SENDS)], partner)

    def red_copy(l, c, u, to_right):
        way, column = (0, o + 1) if to_right else (1, o - 1)
        return to_rx(
            raw.at[wg_rows(l, u)], u, arrival(l, c, column, way, u), l, red_send.at[l, lax.rem(u, SENDS)],
            right if to_right else left,
        )

    def red_wait(l, c, u, way):
        place = arrival(l, c, o, way, u)
        at = rx_rows(u, place, l)
        to_rx(rx.at[at], u, place, l, red_send.at[l, 0], partner).wait_recv()
        return rx[at].astype(F32)

    def red_wait_both(l, u):
        place, size = (1, PAIR) if l == 0 else (3, LINE)
        start = rx_rows(u, place, l).start
        at = rx.at[pl.ds(start, 2 * size)]
        remote(at, at, red_send.at[l, 0], rx_sem(u, place, l), partner).wait_recv()
        return [rx[pl.ds(pl.multiple_of(start + i * size, 16), size)].astype(F32) for i in range(2)]

    def bc_copy(l, u, to_right, src):
        return remote(
            src, fin_at(l, u), bc_send.at[l, lax.rem(u, SENDS), 1 if to_right else 0], bc_recv.at[l, lax.rem(u, ring)],
            right if to_right else left,
        )

    def swap_copy(l, u):
        return to_rx(raw.at[wg_rows(l, u)], u, 5, l, swap_send.at[lax.rem(u, SENDS)], partner)

    def give_copy(u, src):
        return remote(src, fin_at(0, u), give_send.at[lax.rem(u, SENDS)], give_recv.at[lax.rem(u, ring)], partner)

    def local_copy(l, u):
        return pltpu.make_async_copy(raw.at[wg_rows(l, u)], fin_at(l, u), loc_sem.at[l, lax.rem(u, SENDS)])

    def add_to(l, u, *others):
        at = wg_rows(l, u)
        total = raw[at].astype(F32)
        for v in others:
            total = total + v
        raw[at] = total.astype(BF16)

    def red_start(l, c, u):
        pl.when(o < c)(lambda: launch(lambda v: red_copy(l, c, v, True), u))
        pl.when(o > c)(lambda: launch(lambda v: red_copy(l, c, v, False), u))

    def publish(l, u):
        @pl.when(u >= SENDS)
        def _():
            local_copy(l, u - SENDS).wait()

        local_copy(l, u).start()
        pl.when(o > 0)(lambda: launch(lambda v: bc_copy(l, v, False, raw.at[wg_rows(l, v)]), u))
        pl.when(o < n - 1)(lambda: launch(lambda v: bc_copy(l, v, True, raw.at[wg_rows(l, v)]), u))
        if l == 0:
            launch(lambda v: give_copy(v, raw.at[wg_rows(0, v)]), u)

    def block_cols(c):
        return pl.ds(pl.multiple_of(c * width, width), width)

    def sib_rows(ch, q):
        return pl.ds(pl.multiple_of(units * UNIT + (lax.rem(ch, 4) * 2 + q) * span, span), span)

    def sib_copy(ch, q):
        slot = lax.rem(ch, 2)
        cols = sibling if q == 0 else lax.rem(sibling + 2, 4)
        return remote(
            terms.at[slot, cols], raw.at[sib_rows(ch, q)], sib_send.at[q], sib_recv.at[lax.rem(ch, 4), q], (tm, sibling)
        )

    def acr_copy(ch):
        return remote(
            terms.at[lax.rem(ch, 2), across], cot.at[rows_of(ch)], acr_send.at[lax.rem(ch, 2)], acr_recv.at[ch], (tm, across)
        )

    def row_copy(ch, source, d):
        return remote(
            row_rx.at[ch, source], row_rx.at[ch, source], row_send.at[lax.rem(ch, 4)], row_recv.at[lax.rem(ch, 4)],
            (tm, lax.rem(chan + d, 4)),
        )

    def row_all(ch):
        sums = row_rx.at[ch, pl.ds(0, chan_count - 1)]
        return remote(sums, sums, row_send.at[lax.rem(ch, 4)], row_recv.at[lax.rem(ch, 4)], (tm, sibling))

    def out_copy(ch):
        at = pl.ds(pl.multiple_of(ch * CHUNK, CHUNK), CHUNK)
        return pltpu.make_async_copy(out_buf.at[lax.rem(ch, 2)], in_grad.at[:, at, :], out_sem.at[lax.rem(ch, 2)])

    def project(ch):
        at = rows_of(ch)
        slot = lax.rem(ch, 2)

        @pl.when(ch == 0)
        def _():
            pl.semaphore_wait(ready_sem, 2)

        @pl.when(ch >= 2)
        def _():
            acr_copy(ch - 2).wait_send()

        for b in range(chan_count):
            total = jnp.zeros((span, width), F32)
            for k in range(3):
                total = total + lax.dot_general(
                    grad_buf[k, at, :], w_buf[k, b * width : (b + 1) * width, :], (((1,), (1,)), ((), ())),
                    preferred_element_type=F32,
                )
            terms[slot, b] = total.astype(BF16)
        sib_copy(ch, 0).start()
        sib_copy(ch, 1).start()

    def chip_sum(ch):
        slot = lax.rem(ch, 2)
        for q in range(2):
            sib_copy(ch, q).wait_recv()
        there = terms[slot, across].astype(F32) + raw[sib_rows(ch, 1)].astype(F32)
        terms[slot, across] = there.astype(BF16)
        acr_copy(ch).start()
        here = terms[slot, chan].astype(F32) + raw[sib_rows(ch, 0)].astype(F32)
        cand[rows_of(ch), :] = here
        for q in range(2):
            sib_copy(ch, q).wait_send()

    def full_sum(ch):
        acr_copy(ch).wait_recv()
        at = rows_of(ch)
        total = jnp.zeros((8, span), F32)
        pick = lax.broadcasted_iota(jnp.int32, (8, LANE), 0)
        for j in range(tiles):
            cols = lanes(j)
            fp, rp = grad_buf[1, at, cols].astype(F32), grad_buf[2, at, cols].astype(F32)
            g = cand[at, cols] + cot[at, cols].astype(F32) + fp * mix_f[0:1, cols] + rp * mix_r[0:1, cols]
            cand[at, cols] = g
            h = hat(at, j)
            nrm = h * mine(gain, j) + mine(shift, j)
            weighted = g * h
            for i, v in enumerate((fp * nrm, rp * nrm, fp, rp, weighted, g)):
                more[i, :, cols] = more[i, :, cols] + jnp.sum(v.reshape(CHUNK, rows, LANE), axis=0)
            for i, v in enumerate((g * mine(gain, j), weighted * mine(gain, j))):
                lead = jnp.where(pick == i, 1.0, 0.0).astype(BF16)
                high = v.astype(BF16)
                low_part = (v - high.astype(F32)).astype(BF16)
                for p in (high, low_part):
                    total = total + lax.dot_general(lead, p, (((1,), (1,)), ((), ())), preferred_element_type=F32)
        row_rx[ch, chan] = total
        pl.when(ch >= 4)(lambda: row_all(ch - 4).wait_send())
        for d in range(1, 4):
            row_copy(ch, chan, d).start()

    def finish(ch):
        row_all(ch).wait_recv()

        @pl.when(ch >= 2)
        def _():
            out_copy(ch - 2).wait()

        at = rows_of(ch)
        total = (row_rx[ch, 0] + row_rx[ch, 1] + row_rx[ch, 2] + row_rx[ch, 3]) * (1.0 / full)
        columns = jnp.transpose(total)
        first = jnp.broadcast_to(columns[:, 0:1], (span, LANE))
        second = jnp.broadcast_to(columns[:, 1:2], (span, LANE))
        for j in range(tiles):
            cols = lanes(j)
            g = cand[at, cols] * mine(gain, j)
            v = inv[at, :] * (g - first - hat(at, j) * second) + side[at, cols].astype(F32)
            out_buf[lax.rem(ch, 2), :, :, cols] = swapped(v, CHUNK, rows).astype(BF16).reshape(rows, CHUNK, LANE)
        out_copy(ch).start()

    def share_sums():
        for i in range(6):
            sum_rx[tm, i : i + 1, :] = jnp.sum(more[i], axis=0, keepdims=True)
        sum_rx[tm, 6:8, :] = jnp.zeros((2, width), F32)
        peers(lambda p: sum_copy(tm, p).start())

    def start_backward():
        far_all(1).wait_recv()
        pl.when(tm < last_tm)(lambda: near_copy(1, tm).wait_recv())

        def carry_back(i, v):
            d = tm_count - 1 - i
            return jnp.where(d > tm, far[0, d, 0:tiles, :] * v + far[1, d, 0:tiles, :], v)

        inflow = lax.fori_loop(0, tm_count, carry_back, jnp.zeros((tiles, LANE), F32))
        for j in range(tiles):
            row = jnp.broadcast_to(inflow[j : j + 1], (rows, LANE))
            others = jnp.where(tm == last_tm, 0.0, near[1, 1, :, lanes(j)])
            flow[0, :, lanes(j)] = jnp.where(spans > 0, row, others)

    def backward(i, carry):
        b = steps // BLOCK - 1 - i
        at = pl.ds(pl.multiple_of(b * part, part), part)
        mask = keep_mask[at, :]
        for j in range(tiles):
            cols = lanes(j)
            f = forget[at, cols]
            keep = f * mask
            direct = gate[at, cols]
            g = flow[0, :, cols]
            adjoint = [None] * BLOCK
            for t in reversed(range(BLOCK)):
                now = slice(t * rows, (t + 1) * rows)
                adjoint[t] = direct[now] + g
                g = keep[now] * adjoint[t]
            flow[0, :, cols] = g
            cand_grad = jnp.concatenate(adjoint, axis=0) * (1.0 - f)
            forget_pre = cand_grad * (masked[at, cols] - cand[at, cols]) * f
            grad_buf[0, at, cols] = cand_grad.astype(BF16)
            grad_buf[1, at, cols] = forget_pre.astype(BF16)
        return carry

    def close_first():
        x_move(all_tokens, all_tokens, 0).wait_send()
        s_move(all_tokens, all_tokens, 0).wait_send()
        for way in range(2):
            far_all(way).wait_send()
        pl.when(tm < last_tm)(lambda: near_copy(0, tm).wait_send())
        pl.when(tm > 0)(lambda: near_copy(1, tm).wait_send())
        pl.when(tm == last_tm)(last_all)
        pl.when(tm != last_tm)(lambda: last_copy(tm).wait_recv())
        for ch in (chunks - 2, chunks - 1):
            act_copy(ch).wait()
        for j in range(tiles):
            row = jnp.broadcast_to(last[j : j + 1], (rows, LANE))
            others = jnp.where(tm == last_tm, near[0, 0, :, lanes(j)], near[0, 2, :, lanes(j)])
            final[:, lanes(j)] = jnp.where(spans > 0, row, others)

    def close_second():
        for ch in range(chunks - 4, chunks):
            row_all(ch).wait_send()
        for ch in (chunks - 2, chunks - 1):
            out_copy(ch).wait()
            acr_copy(ch).wait_send()
        sums = sum_rx.at[pl.ds(0, tm_count - 1)]
        remote(sums, sums, sum_send, sum_recv, (tm, sibling)).wait()
        totals[...] = lax.fori_loop(0, tm_count, lambda d, v: v + sum_rx[d], jnp.zeros(totals.shape, F32))

    def slot_step(s, carry):
        u, go = stage(s, give_stage)
        pl.when(go)(lambda: give_copy(u, raw.at[wg_rows(0, u)]).wait_recv())

        for l, c, reach, first, parity in lines:
            late = first + reach + (1 if l else 0)
            u, go = stage(s, late + jnp.abs(o - c), parity)

            @pl.when(both(o != c, go))
            def _(l=l, c=c, u=u):
                bc_copy(l, u, True, fin_at(l, u)).wait_recv()
                pl.when(both(o < c, o > 0))(lambda: launch(lambda v: bc_copy(l, v, False, fin_at(l, v)), u))
                pl.when(both(o > c, o < n - 1))(lambda: launch(lambda v: bc_copy(l, v, True, fin_at(l, v)), u))
                if l == 0:
                    launch(lambda v: give_copy(v, fin_at(0, v)), u)

        for l, c, reach, first, parity in lines[1:]:
            u, go = stage(s, reach + 1, parity)

            @pl.when(both(o == c, go))
            def _(l=l, u=u):
                swap_copy(l, u).wait()
                add_to(l, u, rx[rx_rows(u, 5, l)].astype(F32))
                publish(l, u)

        for l, c, reach, first, parity in lines:
            u, go = stage(s, first + reach, parity)

            @pl.when(both(o == c, go))
            def _(l=l, c=c, u=u):
                if l == 0 and n > 2:
                    add_to(l, u, *red_wait_both(l, u))
                elif l > 0 and 0 < c < n - 1:
                    add_to(l, u, *red_wait_both(l, u))
                else:
                    pl.when(o > 0)(lambda: add_to(l, u, red_wait(l, c, u, 0)))
                    pl.when(o < n - 1)(lambda: add_to(l, u, red_wait(l, c, u, 1)))
                if l == 0:
                    publish(l, u)
                else:
                    swap_copy(l, u).start()

        u0, go0 = stage(s, 0)

        @pl.when(go0)
        def _():
            pl.when(u0 + 1 < units)(lambda: low_copy(u0 + 1).start())
            low_copy(u0).wait()
            g = jnp.dot(low[lax.rem(u0, 2)], grad_buf[gate_of(u0)], preferred_element_type=F32)
            raw[pl.ds(pl.multiple_of(u0 * UNIT, UNIT), UNIT)] = g.astype(BF16)
            launch(pair_copy, u0)
            for l, c, reach, first, parity in lines[1:]:
                mine_now = jnp.logical_or(o == 0, o == n - 1)
                if parity is not None:
                    mine_now = both(mine_now, lax.rem(u0, 2) == parity)
                pl.when(mine_now)(lambda l=l, c=c: red_start(l, c, u0))

        for l, c, reach, first, parity in lines:
            u, go = stage(s, first + jnp.where(o < c, o, n - 1 - o), parity)

            @pl.when(both(o < c, o > 0, go))
            def _(l=l, c=c, u=u):
                add_to(l, u, red_wait(l, c, u, 0))
                launch(lambda v: red_copy(l, c, v, True), u)

            @pl.when(both(o > c, o < n - 1, go))
            def _(l=l, c=c, u=u):
                add_to(l, u, red_wait(l, c, u, 1))
                launch(lambda v: red_copy(l, c, v, False), u)

        u, go = stage(s, 1)

        @pl.when(go)
        def _():
            pair_copy(u).wait_recv()
            add_to(0, u, rx[rx_rows(u, 0, 0)].astype(F32))
            pl.when(jnp.logical_or(o == 0, o == n - 1))(lambda: red_start(0, lines[0][1], u))

        count = steps // BLOCK
        pl.when(s == 0)(start_later)
        share = -(-count // LATER)
        at = s * share

        @pl.when(s < LATER)
        def _():
            lax.fori_loop(at, jnp.minimum(at + share, count), later, 0)

        pl.when(s == LATER - 1)(end_later)
        pl.when(s == ADJOINT)(start_backward)
        share = -(-count // (OUTPUT - ADJOINT))
        at2 = (s - ADJOINT) * share

        @pl.when(both(s >= ADJOINT, s < OUTPUT))
        def _():
            lax.fori_loop(at2, jnp.minimum(at2 + share, count), backward, 0)

        share = -(-count // (FIRST - OUTPUT))
        at3 = (s - OUTPUT) * share

        @pl.when(both(s >= OUTPUT, s < FIRST))
        def _():
            lax.fori_loop(at3, jnp.minimum(at3 + share, count), output, 0)

        pl.when(s == FIRST - 1)(end_output)

        for job, offset in ((finish, 5), (full_sum, 3), (chip_sum, 1), (project, 0)):
            at = s - FIRST - offset
            pl.when(both(at >= 0, lax.rem(at, 2) == 0, at // 2 < chunks))(lambda job=job, at=at: job(at // 2))
        pl.when(s == FIRST + 3)(close_first)
        pl.when(s == FIRST + 2 * chunks + 2)(share_sums)
        pl.when(s == FIRST + 2 * chunks + 6)(close_second)
        return carry

    slots = max((units - 1) * space + depth + 1, FIRST + 2 * chunks + 7)
    lax.fori_loop(0, slots, slot_step, 0)

    def close_unit(u, carry):
        give_copy(u, raw.at[wg_rows(0, u)]).wait_send()
        pair_copy(u).wait_send()
        for l, c, reach, first, parity in lines:

            @pl.when(True if parity is None else lax.rem(u, 2) == parity)
            def _(l=l, c=c):
                src = raw.at[wg_rows(l, u)]
                pl.when(o != c)(lambda: red_copy(l, c, u, True).wait_send())
                pl.when(o == c)(lambda: local_copy(l, u).wait())
                pl.when(both(o <= c, o > 0))(lambda: bc_copy(l, u, False, src).wait_send())
                pl.when(both(o >= c, o < n - 1))(lambda: bc_copy(l, u, True, src).wait_send())

        return carry

    lax.fori_loop(units - SENDS, units, close_unit, 0)


def layer(tokens, weights, cotangent, gain, shift, mix_f, mix_r, bias_f, bias_r, bank, selector, resets):
    rows, steps, width = tokens.shape
    full = gain.shape[-1]
    tm_count, chan_count = lax.axis_size("tm"), lax.axis_size("chan")
    chunks = steps // CHUNK
    span = CHUNK * rows
    pieces = chunks - 1 + CHUNK // BLOCK
    count = steps * rows
    units = 3 * full // UNIT
    ring = ring_of(tm_count)
    hbm = pl.BlockSpec(memory_space=pl.ANY)
    vmem = pl.BlockSpec(memory_space=pltpu.VMEM)
    smem = pl.BlockSpec(memory_space=pltpu.SMEM)
    dma = pltpu.SemaphoreType.DMA
    stat = pltpu.VMEM((CHUNK // BLOCK, rows, BLOCK, LANE), F32)
    wide = pltpu.VMEM((count, width), F32)
    narrow = pltpu.VMEM((count, LANE), F32)
    short = pltpu.VMEM((count, width), BF16)
    return pl.pallas_call(
        layer_kernel,
        out_shape=(
            jax.ShapeDtypeStruct((units * UNIT, width), BF16),
            jax.ShapeDtypeStruct(tokens.shape, BF16),
            jax.ShapeDtypeStruct(tokens.shape, BF16),
            jax.ShapeDtypeStruct((full, count), BF16),
            jax.ShapeDtypeStruct((rows, width), F32),
            jax.ShapeDtypeStruct((8, width), F32),
        ),
        in_specs=[hbm, hbm, hbm] + [vmem] * 7 + [smem, vmem],
        out_specs=(hbm, hbm, hbm, hbm, vmem, vmem),
        scratch_shapes=[
            pltpu.VMEM((chunks * chan_count * span, width), BF16),
            pltpu.VMEM((ring * (3 * PAIR + 4 * LINE), width), BF16),
            pltpu.VMEM((2, span, full), BF16),
            pltpu.VMEM((full, span), BF16),
            pltpu.VMEM((3, full, width), BF16),
            wide, wide, wide, wide,
            short,
            pltpu.VMEM((2, rows, CHUNK, width), BF16),
            short,
            narrow, narrow, narrow,
            pltpu.VMEM((3, count, width), BF16),
            pltpu.VMEM((2, rows, CHUNK, width), BF16),
            short,
            pltpu.VMEM((2, chan_count, span, width), BF16),
            pltpu.VMEM((2, rows, CHUNK, width), BF16),
            pltpu.VMEM((chunks, 4, 8, span), F32),
            pltpu.VMEM((6, rows, width), F32),
            pltpu.VMEM((tm_count, 8, width), F32),
            stat, stat, stat,
            pltpu.VMEM((rows, width), F32),
            pltpu.VMEM((2, 3, rows, width), F32),
            pltpu.VMEM((2, tm_count, 8, LANE), F32),
            pltpu.VMEM((2, rows, width), F32),
            pltpu.VMEM((resets.shape[1], rows, LANE), jnp.int32),
            dma(()), dma((pieces,)), dma(()), dma(()), dma(()), dma((pieces,)), dma(()),
            dma((3,)), dma((2,)), dma((2,)), dma(()), dma((2,)),
            dma((2,)), dma((2,)), dma((2,)), dma((2,)), dma(()), dma(()),
            pltpu.SemaphoreType.REGULAR,
            dma((2,)), dma((3, SENDS)), dma((SENDS,)), dma((3, SENDS)), dma((3, SENDS, 2)), dma((3, ring)), dma((SENDS,)),
            dma((SENDS,)), dma((ring,)), dma((ring, 5)), dma((2,)), dma((4, 2)), dma((2,)), dma((chunks,)),
            dma((4,)), dma((4,)), dma(()), dma(()),
        ],
        compiler_params=pltpu.CompilerParams(collective_id=0, has_side_effects=True, vmem_limit_bytes=VMEM_BYTES),
        name="whole",
    )(tokens, weights, cotangent, gain, shift, mix_f, mix_r, bias_f, bias_r, bank, selector, resets)


def tail_kernel(
    fin, in_grad, act, final, totals, wide_out, in_out, act_out, final_out, s0, s1, s2, s3, s4, s5,
    fin_buf, wide_buf, in_buf, in_wide, act_buf, load_sem, store_sem,
):
    def move(src, dst, sem, i, n):
        at = pl.ds(i * n, n)
        return pltpu.make_async_copy(src.at[at], dst.at[at], sem)

    jobs = []

    def job(src, buf, wide, dst, parts):
        n = src.shape[0] // parts
        for i in range(parts):
            k = len(jobs)
            jobs.append((move(src, buf, load_sem.at[k], i, n), buf, wide, i * n, n, move(wide, dst, store_sem.at[k], i, n)))

    job(fin, fin_buf, wide_buf, wide_out, TAIL)
    job(in_grad, in_buf, in_wide, in_out, 2)
    job(act, act_buf, act_buf, act_out, 2)
    order = [0, 4, 1, 6, 2, 5, 3, 7] if TAIL == 4 else list(range(len(jobs)))
    for k in order:
        jobs[k][0].start()
    final_out[...] = final[...]
    for i, ref in enumerate((s0, s1, s2, s3, s4, s5)):
        ref[...] = totals[i : i + 1, :]
    for k in order:
        load, buf, wide, start, n, store = jobs[k]
        load.wait()
        if buf is not wide:
            step = 64 if len(buf.shape) == 2 else 1

            def cast(j, carry, buf=buf, wide=wide, start=start, step=step):
                at = pl.ds(start + j * step, step)
                wide[at] = buf[at].astype(F32)
                return carry

            lax.fori_loop(0, n // step, cast, 0, unroll=2)
        store.start()
    for k in order:
        jobs[k][-1].wait()


def tail(fin, in_grad, act, final, totals):
    width = fin.shape[-1]
    hbm = pl.BlockSpec(memory_space=pl.ANY)
    vmem = pl.BlockSpec(memory_space=pltpu.VMEM)
    dma = pltpu.SemaphoreType.DMA
    line = jax.ShapeDtypeStruct((1, width), F32)
    return pl.pallas_call(
        tail_kernel,
        out_shape=(
            jax.ShapeDtypeStruct(fin.shape, F32),
            jax.ShapeDtypeStruct(in_grad.shape, F32),
            jax.ShapeDtypeStruct(act.shape, BF16),
            jax.ShapeDtypeStruct(final.shape, F32),
        ) + (line,) * 6,
        in_specs=[hbm] * 3 + [vmem] * 2,
        out_specs=(hbm,) * 3 + (vmem,) * 7,
        scratch_shapes=[
            pltpu.VMEM(fin.shape, BF16), pltpu.VMEM(fin.shape, F32),
            pltpu.VMEM(in_grad.shape, BF16), pltpu.VMEM(in_grad.shape, F32), pltpu.VMEM(act.shape, BF16),
            dma((TAIL + 4,)), dma((TAIL + 4,)),
        ],
        compiler_params=pltpu.CompilerParams(vmem_limit_bytes=VMEM_BYTES),
        name="tail",
    )(fin, in_grad, act, final, totals)


def body(
    tokens, ln_gain, ln_bias, weights, mix_forget, mix_reset, bias_forget, bias_reset, state_bank, selector, resets, cotangent
):
    fin, in_grad, act, _, final, totals = layer(
        tokens, weights, cotangent, ln_gain[None], ln_bias[None], mix_forget[None], mix_reset[None], bias_forget[None],
        bias_reset[None], state_bank, selector, resets,
    )
    wide, in_grad, act, final, *sums = tail(fin, in_grad, act, final, totals)
    sums = [v[0] for v in sums]
    return act, final, in_grad, wide.reshape(weights.shape), sums[4], sums[5], sums[0], sums[1], sums[2], sums[3]


def solution(mesh):
    placed = (
        P(None, "tm", "chan"), P(), P(), P(None, None, "chan"), P("chan"), P("chan"), P("chan"), P("chan"),
        P(None, "chan"), P(), P(), P(None, "tm", "chan"),
    )
    return jax.shard_map(
        body,
        mesh=mesh,
        in_specs=placed,
        out_specs=(
            P(None, "tm", "chan"), P(None, "chan"), P(None, "tm", "chan"), P(None, None, "chan"),
            P("chan"), P("chan"), P("chan"), P("chan"), P("chan"), P("chan"),
        ),
        check_vma=False,
    )
```
